32 devices in a mesh: groups: 2 (over y), latent: 4 (over z), dp: 4 (over x, core).
Axes of the slice: x: 2, y: 2, z: 4, core: 2. Of those that a mesh axis runs over, the one named last changes fastest.
Arguments:
- activations: bfloat16 [3072, 2048], P(('groups', 'dp'), 'latent'), parts along dimension 0, may hold values from -40 to 40
- encoder: float32 [4096, 2048], P(('groups', 'dp'), 'latent'), parts along dimension 0, may hold values from -0.12 to 0.12
- enc_bias: float32 [4096], P(('groups', 'latent', 'dp')), parts along dimension 0, may hold values from -3 to 3
- decoder: float32 [4096, 2048], P(('groups', 'dp'), 'latent'), parts along dimension 0, may hold values from -1.2 to 1.2
- enc_moment: float32 [4096, 2048], P(('groups', 'dp'), 'latent'), parts along dimension 0, may hold values from -1.2 to 1.2
- enc_square: float32 [4096, 2048], P(('groups', 'dp'), 'latent'), parts along dimension 0, may hold values from 0.001 to 1
- bias_moment: float32 [4096], P(('groups', 'latent', 'dp')), parts along dimension 0, may hold values from -1.2 to 1.2
- bias_square: float32 [4096], P(('groups', 'latent', 'dp')), parts along dimension 0, may hold values from 0.001 to 1
- dec_moment: float32 [4096, 2048], P(('groups', 'dp'), 'latent'), parts along dimension 0, may hold values from -1.2 to 1.2
- dec_square: float32 [4096, 2048], P(('groups', 'dp'), 'latent'), parts along dimension 0, may hold values from 0.001 to 1
Outputs:
- error: bfloat16 [3072, 2048], P(('groups', 'dp'), 'latent'), parts along dimension 0
- new_encoder: float32 [4096, 2048], P(('groups', 'dp'), 'latent'), parts along dimension 0
- new_enc_bias: float32 [4096], P(('groups', 'latent', 'dp')), parts along dimension 0
- new_decoder: float32 [4096, 2048], P(('groups', 'dp'), 'latent'), parts along dimension 0
- new_enc_moment: float32 [4096, 2048], P(('groups', 'dp'), 'latent'), parts along dimension 0
- new_enc_square: float32 [4096, 2048], P(('groups', 'dp'), 'latent'), parts along dimension 0
- new_bias_moment: float32 [4096], P(('groups', 'latent', 'dp')), parts along dimension 0
- new_bias_square: float32 [4096], P(('groups', 'latent', 'dp')), parts along dimension 0
- new_dec_moment: float32 [4096, 2048], P(('groups', 'dp'), 'latent'), parts along dimension 0
- new_dec_square: float32 [4096, 2048], P(('groups', 'dp'), 'latent'), parts along dimension 0
The draws below stay inside these ranges and needn't reach their ends.
There are 2 independent parts, one for each index of `groups`. The reference program is written for one: setup_inputs(seed, part) draws one part's arguments, and reference() takes and returns one part's arrays. A program takes and returns all parts, laid end to end along the dimension named above; each array names one. Nothing has to cross between parts.
All inputs are finite; a program needn't handle non-finite values.
Results may differ from the reference program's by a relative error of at most 0.00055.
The reference program's roundings to bfloat16 on the way count: a program that leaves them out, or rounds other values in their place, can miss the bound.
Values may be sent and summed in bfloat16 or wider, within the bound.
No kernel may reach another device: no remote copies, remote signals or barrier semaphores. Data moves between devices by JAX's collectives and lax.ppermute only.
A program may use at most 64 MiB of HBM per device.

```python
import math
import jax
import jax.numpy as jnp
from jax import lax

D = 2048
ADAM_STEP = 1000
LATENTS = 2048
ROWS = 1536


def draw_activations(key, part):
    key = jax.random.fold_in(key, 11)
    keys = jax.random.split(key, 3)
    row_place = jnp.arange(ROWS, dtype=jnp.float32)[:, None] / ROWS - 0.5
    row_scale = jnp.exp(jax.random.uniform(keys[0], (ROWS, 1), jnp.float32, math.log(0.5), math.log(2.4)))
    col_scale = jnp.exp(jax.random.uniform(keys[1], (1, D), jnp.float32, math.log(0.5), math.log(2.0)))
    growth = jnp.exp(row_place * math.log(4.0))
    sample = jnp.clip(jax.random.normal(keys[2], (ROWS, D), jnp.float32), -4.0, 4.0)
    return (sample * row_scale * growth * col_scale).astype(jnp.bfloat16)


def draw_decoder(key, part):
    key = jax.random.fold_in(key, 23)
    keys = jax.random.split(key, 3)
    position = jnp.arange(D, dtype=jnp.float32)[:, None] / D - 0.5
    feature_scale = jnp.exp(jax.random.uniform(keys[0], (D, 1), jnp.float32, math.log(0.4), math.log(4.0)))
    latent_scale = jnp.exp(jax.random.uniform(keys[1], (1, LATENTS), jnp.float32, math.log(0.4), math.log(4.0)))
    rising = jnp.exp(position * math.log(3.0))
    sample = jnp.clip(jax.random.normal(keys[2], (D, LATENTS), jnp.float32), -4.0, 4.0)
    return (0.01 * sample * rising * feature_scale * latent_scale).astype(jnp.float32)


def shard_levels(key, dims, cuts, low, largest):
    def one(dim, blocks):
        steps = jax.random.uniform(jax.random.fold_in(jax.random.fold_in(key, 6), dim), (blocks,), jnp.float32, low / len(cuts), largest / len(cuts))
        return jnp.repeat(jnp.exp(steps), dims[dim] // blocks).reshape((-1,) + (1,) * (len(dims) - dim - 1))

    factor_of = one(*cuts[0])
    for cut in cuts[1:]:
        factor_of = factor_of * one(*cut)
    return factor_of


def scatter_about(own_key, extent, spread, limit, cuts=(), kind=jnp.bfloat16):
    entries = jax.random.normal(own_key, extent, jnp.float32) * spread
    if len(cuts) > 0:
        entries = shard_levels(own_key, extent, cuts, -0.22, 0.18) * entries
    return jnp.clip(entries, min=-limit, max=limit).astype(kind)


def setup_inputs(seed: int = 0, part: int = 0) -> dict:
    key_list = jax.random.split(jax.random.key(seed), 11)
    own_keys = jax.random.split(jax.random.fold_in(key_list[10], part), 11)
    return {
        "activations": draw_activations(jax.random.fold_in(jax.random.fold_in(key_list[10], part), 71), part),
        "encoder": scatter_about(own_keys[1], (D, LATENTS), 0.02, 0.12, ((0, 4), (1, 4)), jnp.float32),
        "enc_bias": scatter_about(own_keys[2], (LATENTS,), 0.5, 3.0, ((0, 16),), jnp.float32),
        "decoder": draw_decoder(jax.random.fold_in(jax.random.fold_in(key_list[10], part), 71), part),
        "enc_moment": scatter_about(own_keys[4], (D, LATENTS), 0.2, 1.2, ((0, 4), (1, 4)), jnp.float32),
        "enc_square": jnp.clip(jnp.exp(math.log(1.0) - 6.9077552 * jax.random.uniform(own_keys[5], (D, LATENTS), jnp.float32) ** shard_levels(own_keys[5], (D, LATENTS), ((0, 4), (1, 4)), -0.2, 0.2)), 0.001, 1.0),
        "bias_moment": scatter_about(own_keys[6], (LATENTS,), 0.2, 1.2, ((0, 16),), jnp.float32),
        "bias_square": jnp.clip(jnp.exp(math.log(1.0) - 6.9077552 * jax.random.uniform(own_keys[7], (LATENTS,), jnp.float32) ** shard_levels(own_keys[7], (LATENTS,), ((0, 16),), -0.2, 0.2)), 0.001, 1.0),
        "dec_moment": scatter_about(own_keys[8], (D, LATENTS), 0.2, 1.2, ((0, 4), (1, 4)), jnp.float32),
        "dec_square": jnp.clip(jnp.exp(math.log(1.0) - 6.9077552 * jax.random.uniform(own_keys[9], (D, LATENTS), jnp.float32) ** shard_levels(own_keys[9], (D, LATENTS), ((0, 4), (1, 4)), -0.2, 0.2)), 0.001, 1.0),
    }


first_decay = 0.9
second_decay = 0.999
learn_rate = 0.001
epsilon = 1e-08

def adam_update(param, grad, moment, square):
    moment_new = first_decay * moment + (1.0 - first_decay) * grad
    square_new = second_decay * square + (1.0 - second_decay) * grad * grad
    first_fix = 1.0 - first_decay ** ADAM_STEP
    second_fix = 1.0 - second_decay ** ADAM_STEP
    param_new = param - learn_rate * (moment_new / first_fix) / (jnp.sqrt(square_new / second_fix) + epsilon)
    return (param_new, moment_new, square_new)

def reference(activations, encoder, enc_bias, decoder, enc_moment, enc_square, bias_moment, bias_square, dec_moment, dec_square):
    row_count = activations.shape[0]
    loss_scale = 2.0 / row_count
    enc_low = encoder.astype(jnp.bfloat16)
    dec_low = decoder.astype(jnp.bfloat16)
    preact = jnp.dot(activations, enc_low, preferred_element_type=jnp.float32) + enc_bias
    latent_codes = jnp.maximum(preact, 0.0).astype(jnp.bfloat16)
    column_norms = jnp.sqrt(lax.optimization_barrier(jnp.sum(decoder * decoder, axis=0)) + 1e-06)
    rebuilt = lax.dot_general(latent_codes, dec_low, (((1,), (1,)), ((), ())), preferred_element_type=jnp.float32)
    error = (activations.astype(jnp.float32) - rebuilt).astype(jnp.bfloat16)
    active_sum = lax.optimization_barrier(jnp.sum(latent_codes.astype(jnp.float32), axis=0))
    grad_decoder = -loss_scale * lax.dot_general(error, latent_codes, (((0,), (0,)), ((), ())), preferred_element_type=jnp.float32) + decoder * (active_sum / column_norms) / row_count
    code_grad = -loss_scale * jnp.dot(error, dec_low, preferred_element_type=jnp.float32) + column_norms / row_count
    grad_preact = jnp.where(preact > 0.0, code_grad, 0.0)
    grad_encoder = lax.dot_general(activations, grad_preact.astype(jnp.bfloat16), (((0,), (0,)), ((), ())), preferred_element_type=jnp.float32)
    grad_bias = lax.optimization_barrier(jnp.sum(grad_preact, axis=0))
    new_encoder, new_enc_moment, new_enc_square = adam_update(encoder, grad_encoder, enc_moment, enc_square)
    new_enc_bias, new_bias_moment, new_bias_square = adam_update(enc_bias, grad_bias, bias_moment, bias_square)
    new_decoder, new_dec_moment, new_dec_square = adam_update(decoder, grad_decoder, dec_moment, dec_square)
    return (error, new_encoder, new_enc_bias, new_decoder, new_enc_moment, new_enc_square, new_bias_moment, new_bias_square, new_dec_moment, new_dec_square)
```

```python
import functools

import jax
import jax.numpy as jnp
from jax import lax
from jax.experimental import pallas as pl
from jax.experimental.pallas import tpu as pltpu
from jax.sharding import PartitionSpec as P

ADAM_STEP = 1000


first_decay = 0.9
second_decay = 0.999
learn_rate = 0.001
epsilon = 1e-08

F32 = jnp.float32
BF16 = jnp.bfloat16
CHUNKS = 2


def adam_update(param, grad, moment, square):
    moment_new = first_decay * moment + (1.0 - first_decay) * grad
    square_new = second_decay * square + (1.0 - second_decay) * grad * grad
    first_fix = 1.0 - first_decay**ADAM_STEP
    second_fix = 1.0 - second_decay**ADAM_STEP
    param_new = param - learn_rate * (moment_new / first_fix) / (
        jnp.sqrt(square_new / second_fix) + epsilon
    )
    return (param_new, moment_new, square_new)


def shards(
    activations,
    encoder,
    enc_bias,
    decoder,
    enc_moment,
    enc_square,
    bias_moment,
    bias_square,
    dec_moment,
    dec_square,
):
    row_count = activations.shape[0] * lax.axis_size("dp")
    loss_scale = 2.0 / row_count
    inputs = lax.all_gather(activations, "latent", axis=1, tiled=True)
    enc_low, dec_low = (
        lax.all_gather(encoder.astype(jnp.bfloat16), "dp", axis=0, tiled=True),
        lax.all_gather(decoder.astype(jnp.bfloat16), "dp", axis=0, tiled=True),
    )
    bias_full = lax.all_gather(enc_bias, "dp", axis=0, tiled=True)
    square_sums = lax.psum(jnp.sum(decoder * decoder, axis=0), "dp")
    column_norms = jnp.sqrt(square_sums + 1e-06)
    preact = jnp.dot(inputs, enc_low, preferred_element_type=jnp.float32) + bias_full
    latent_codes = jnp.maximum(preact, 0.0).astype(jnp.bfloat16)
    partial_sums = lax.dot_general(
        latent_codes, dec_low, (((1,), (1,)), ((), ())), preferred_element_type=jnp.float32
    )
    rebuilt = lax.psum_scatter(partial_sums, "latent", scatter_dimension=1, tiled=True)
    error = (activations.astype(jnp.float32) - rebuilt).astype(jnp.bfloat16)
    full_error = lax.all_gather(error, "latent", axis=1, tiled=True)
    active_sum = lax.psum(jnp.sum(latent_codes.astype(jnp.float32), axis=0), "dp")
    grad_dec_rows = -loss_scale * lax.dot_general(
        full_error, latent_codes, (((0,), (0,)), ((), ())), preferred_element_type=jnp.float32
    )
    code_grad = (
        -loss_scale * jnp.dot(full_error, dec_low, preferred_element_type=jnp.float32)
        + column_norms / row_count
    )
    grad_preact = jnp.where(preact > 0.0, code_grad, 0.0)
    grad_encoder = lax.dot_general(
        inputs,
        grad_preact.astype(jnp.bfloat16),
        (((0,), (0,)), ((), ())),
        preferred_element_type=jnp.float32,
    )
    grad_bias = jnp.sum(grad_preact, axis=0)
    grad_encoder, grad_dec_rows, grad_bias = (
        lax.psum_scatter(grad_encoder, "dp", scatter_dimension=0, tiled=True),
        lax.psum_scatter(grad_dec_rows, "dp", scatter_dimension=0, tiled=True),
        lax.psum_scatter(grad_bias, "dp", scatter_dimension=0, tiled=True),
    )
    grad_decoder = grad_dec_rows + decoder * (active_sum / column_norms) / row_count
    new_encoder, new_enc_moment, new_enc_square = adam_update(
        encoder, grad_encoder, enc_moment, enc_square
    )
    new_enc_bias, new_bias_moment, new_bias_square = adam_update(
        enc_bias, grad_bias, bias_moment, bias_square
    )
    new_decoder, new_dec_moment, new_dec_square = adam_update(
        decoder, grad_decoder, dec_moment, dec_square
    )
    return (
        error,
        new_encoder,
        new_enc_bias,
        new_decoder,
        new_enc_moment,
        new_enc_square,
        new_bias_moment,
        new_bias_square,
        new_dec_moment,
        new_dec_square,
    )


VMEM = pl.BlockSpec(memory_space=pltpu.VMEM)
SMEM = pl.BlockSpec(memory_space=pltpu.SMEM)


def local_kernel(body, outs, place, *args, flops):
    moved = sum(a.size * a.dtype.itemsize for a in args)
    moved += sum(o.size * jnp.dtype(o.dtype).itemsize for o in outs)
    return pl.pallas_call(
        body,
        out_shape=outs,
        in_specs=[SMEM] + [VMEM] * len(args),
        out_specs=[VMEM] * len(outs),
        compiler_params=pltpu.CompilerParams(vmem_limit_bytes=48 * 1024 * 1024),
        cost_estimate=pl.CostEstimate(flops=flops, bytes_accessed=moved, transcendentals=0),
    )(place, *args)


def shape(dims, dtype):
    return jax.ShapeDtypeStruct(dims, dtype)


def columns(start, width):
    return pl.ds(pl.multiple_of(start, width), width)


def codes_body(place, own, low, high, across, relay, enc, bias, codes, mask, full, active):
    z, i = place[0], place[1]
    width = own.shape[1]
    full[:, columns(z * width, width)] = own[...]
    full[:, columns(((z + 2) % 4) * width, width)] = across[...]

    @pl.when(z < 3)
    def _():
        full[:, columns((z + 1) * width, width)] = high[...]

    @pl.when(z == 3)
    def _():
        full[:, :width] = relay[...]

    @pl.when(z > 0)
    def _():
        full[:, columns((z - 1) * width, width)] = low[...]

    @pl.when(z == 0)
    def _():
        full[:, 3 * width :] = relay[...]

    total = jnp.zeros(codes.shape, F32)
    pieces = []
    for b in range(4):
        slot = b ^ i
        total += jnp.dot(
            full[:, b * width : (b + 1) * width],
            enc[columns(slot * width, width), :],
            preferred_element_type=F32,
        )
        pieces.append(bias[pl.ds(slot, 1), :])
    preact = total + jnp.concatenate(pieces, axis=1)
    low_codes = jnp.maximum(preact, 0.0).astype(BF16)
    codes[...] = low_codes
    mask[...] = (preact > 0.0).astype(F32).astype(BF16)
    active[...] = jnp.sum(low_codes.astype(F32), axis=0, keepdims=True)


def error_body(place, own, low, high, across, dec0, dec1, dec2, dec3, inputs, error):
    z, i = place[0], place[1]
    half = dec0.shape[0] // 4
    shift = jnp.where(z >= 2, half, 0)
    for t, dec in enumerate((dec0, dec1, dec2, dec3)):
        total = jnp.zeros((own.shape[0], half), F32)
        for m, codes in enumerate((own, low, high, across)):
            total += lax.dot_general(
                codes[...],
                dec[m * half : (m + 1) * half, :],
                (((1,), (1,)), ((), ())),
                preferred_element_type=F32,
            )
        q = i ^ t
        given = inputs[:, columns(q * 2 * half + shift, half)].astype(F32)
        error[:, columns(q * half, half)] = (given - total).astype(BF16)


def grad_code_body(
    rows, place, mine, swapped, passed, relayed, mask, dec, norms, grad_low, bias_sum, full, home
):
    z, i = place[0], place[1]
    half = mine.shape[1] // 4
    width = 2 * half
    for q in range(4):
        piece = slice(q * half, (q + 1) * half)
        first = slice(q * width, q * width + half)
        second = slice(q * width + half, (q + 1) * width)

        @pl.when(z == 0)
        def _():
            full[:, first] = passed[:, piece]
            full[:, second] = relayed[:, piece]

        @pl.when(z == 1)
        def _():
            full[:, first] = mine[:, piece]
            full[:, second] = swapped[:, piece]

        @pl.when(z == 2)
        def _():
            full[:, first] = swapped[:, piece]
            full[:, second] = mine[:, piece]

        @pl.when(z == 3)
        def _():
            full[:, first] = relayed[:, piece]
            full[:, second] = passed[:, piece]

    total = jnp.zeros(grad_low.shape, F32)
    for b in range(4):
        total += jnp.dot(
            full[:, b * width : (b + 1) * width],
            dec[columns((b ^ i) * width, width), :],
            preferred_element_type=F32,
        )
    code_grad = (-2.0 / rows) * total + norms[...] / rows
    grad = jnp.where(mask[...] > 0, code_grad, 0.0)
    grad_low[...] = grad.astype(BF16)
    bias_sum[...] = jnp.sum(grad, axis=0, keepdims=True)
    home[...] = full[:, columns(z * width, width)]


def grad_body(scale, slots, place, *refs):
    i = place[1]
    lefts, rights = refs[:CHUNKS], refs[CHUNKS : 2 * CHUNKS]
    outs = refs[2 * CHUNKS :]
    width = outs[0].shape[0]
    for slot, out in zip(slots, outs):
        total = jnp.zeros(out.shape, F32)
        for left, right in zip(lefts, rights):
            total += lax.dot_general(
                left[:, columns((i ^ slot) * width, width)],
                right[...],
                (((0,), (0,)), ((), ())),
                preferred_element_type=F32,
            )
        out[...] = scale * total


def line_shards(
    activations,
    encoder,
    enc_bias,
    decoder,
    enc_moment,
    enc_square,
    bias_moment,
    bias_square,
    dec_moment,
    dec_square,
):
    rows = activations.shape[0] * 4
    chunk = activations.shape[0] // CHUNKS
    width = activations.shape[1]
    latents = encoder.shape[1]
    half = width // 2
    features = 4 * width
    z, i = lax.axis_index("latent"), lax.axis_index("dp")
    place = jnp.stack([z, i]).astype(jnp.int32)

    def along(value, pairs):
        return lax.ppermute(value, "latent", pairs)

    def flip(value, bits):
        return lax.ppermute(value, "dp", [(k, k ^ bits) for k in range(4)])

    def sum_dp(value):
        return (value + flip(value, 1)) + (flip(value, 2) + flip(value, 3))

    def by_slot(value):
        core, chip = flip(value, 1), flip(value, 2)
        return [value, core, chip, flip(chip, 1)]

    up = [(0, 1), (1, 2), (2, 3)]
    down = [(1, 0), (2, 1), (3, 2)]
    two = [(0, 2), (1, 3), (2, 0), (3, 1)]

    parts = [activations[c * chunk : (c + 1) * chunk] for c in range(CHUNKS)]
    gathered = []
    for part in parts:
        low, high, across = along(part, up), along(part, down), along(part, two)
        relay = along(across, [(2, 3), (1, 0)])
        gathered.append((part, low, high, across, relay))

    enc_all = jnp.concatenate(by_slot(encoder.astype(BF16)), axis=0)
    bias_all = jnp.stack(by_slot(enc_bias), axis=0)
    dec_low = decoder.astype(BF16)
    dec_all = jnp.concatenate(by_slot(dec_low), axis=0)
    norms = jnp.sqrt(sum_dp(jnp.sum(decoder * decoder, axis=0, keepdims=True)) + 1e-06)

    first, second = dec_low[:half], dec_low[half:]
    mine = jnp.where(z >= 2, second, first)
    dec_rows = jnp.concatenate(
        [
            mine,
            along(jnp.where(z >= 1, second, first), [(0, 1), (1, 2)]),
            along(jnp.where(z >= 3, second, first), [(2, 1), (3, 2)]),
            along(jnp.where(z >= 2, first, second), [(0, 2), (3, 1)]),
        ],
        axis=0,
    )
    dec_rows = by_slot(dec_rows)

    flops = 2 * chunk * features * latents
    inputs, codes, masks, actives, errors = [], [], [], [], []
    for part in gathered:
        low_codes, mask, full, active = local_kernel(
            codes_body,
            [
                shape((chunk, latents), BF16),
                shape((chunk, latents), BF16),
                shape((chunk, features), BF16),
                shape((1, latents), F32),
            ],
            place,
            *part,
            enc_all,
            bias_all,
            flops=flops,
        )
        inputs.append(full)
        codes.append(low_codes)
        masks.append(mask)
        actives.append(active)
        low = along(low_codes, [(0, 1), (1, 2)])
        high = along(low_codes, [(2, 1), (3, 2)])
        across = along(low_codes, [(0, 2), (3, 1)])
        (own_error,) = local_kernel(
            error_body,
            [shape((chunk, features // 2), BF16)],
            place,
            low_codes,
            low,
            high,
            across,
            *dec_rows,
            full,
            flops=2 * flops,
        )
        passed = along(own_error, [(1, 0), (2, 3)])
        swapped = along(own_error, [(1, 2), (2, 1)])
        relayed = along(swapped, [(1, 0), (2, 3)])
        errors.append((own_error, swapped, passed, relayed))

    active_sum = sum_dp(functools.reduce(jnp.add, actives))

    grads, bias_sums, fulls, homes = [], [], [], []
    for error, mask in zip(errors, masks):
        grad_low, bias_sum, full, home = local_kernel(
            functools.partial(grad_code_body, rows),
            [
                shape((chunk, latents), BF16),
                shape((1, latents), F32),
                shape((chunk, features), BF16),
                shape((chunk, width), BF16),
            ],
            place,
            *error,
            mask,
            dec_all,
            norms,
            flops=flops,
        )
        grads.append(grad_low)
        bias_sums.append(bias_sum)
        fulls.append(full)
        homes.append(home)
    error = jnp.concatenate(homes, axis=0)

    def reduced(scale, lefts, rights):
        def slots(*which):
            return local_kernel(
                functools.partial(grad_body, scale, which),
                [shape((width, latents), F32)] * 2,
                place,
                *lefts,
                *rights,
                flops=CHUNKS * flops // 2,
            )

        send_far, send_near = slots(3, 1)
        keep_far, keep_near = slots(2, 0)
        far = keep_far + flip(send_far, 1)
        largest = jnp.maximum(jnp.max(jnp.abs(far), axis=0, keepdims=True), 1e-30)
        sent = (far * (16384.0 / largest)).astype(jnp.float16)
        near = keep_near + flip(send_near, 1)
        return near + flip(sent, 2).astype(F32) * (flip(largest, 2) / 16384.0)

    grad_dec_rows = reduced(-2.0 / rows, fulls, codes)
    grad_encoder = reduced(1.0, inputs, grads)
    grad_bias = sum_dp(functools.reduce(jnp.add, bias_sums))
    grad_bias = lax.dynamic_slice(
        grad_bias.reshape(latents), (i * enc_bias.shape[0],), (enc_bias.shape[0],)
    )
    grad_decoder = grad_dec_rows + decoder * (active_sum / norms) / rows

    new_decoder, new_dec_moment, new_dec_square = adam_update(
        decoder, grad_decoder, dec_moment, dec_square
    )
    new_enc_bias, new_bias_moment, new_bias_square = adam_update(
        enc_bias, grad_bias, bias_moment, bias_square
    )
    new_encoder, new_enc_moment, new_enc_square = adam_update(
        encoder, grad_encoder, enc_moment, enc_square
    )
    return (
        error,
        new_encoder,
        new_enc_bias,
        new_decoder,
        new_enc_moment,
        new_enc_square,
        new_bias_moment,
        new_bias_square,
        new_dec_moment,
        new_dec_square,
    )


def solution(mesh):
    in_specs = (
        P(("groups", "dp"), "latent"),
        P(("groups", "dp"), "latent"),
        P(("groups", "latent", "dp")),
        P(("groups", "dp"), "latent"),
        P(("groups", "dp"), "latent"),
        P(("groups", "dp"), "latent"),
        P(("groups", "latent", "dp")),
        P(("groups", "latent", "dp")),
        P(("groups", "dp"), "latent"),
        P(("groups", "dp"), "latent"),
    )
    out_specs = (
        P(("groups", "dp"), "latent"),
        P(("groups", "dp"), "latent"),
        P(("groups", "latent", "dp")),
        P(("groups", "dp"), "latent"),
        P(("groups", "dp"), "latent"),
        P(("groups", "dp"), "latent"),
        P(("groups", "latent", "dp")),
        P(("groups", "latent", "dp")),
        P(("groups", "dp"), "latent"),
        P(("groups", "dp"), "latent"),
    )
    line = mesh.shape["latent"] == 4 and mesh.shape["dp"] == 4
    plan = line_shards if line else shards
    return jax.shard_map(plan, mesh=mesh, in_specs=in_specs, out_specs=out_specs, check_vma=False)
```

```python
import functools

import jax
import jax.numpy as jnp
from jax import lax
from jax.experimental import pallas as pl
from jax.experimental.pallas import tpu as pltpu
from jax.sharding import PartitionSpec as P

ADAM_STEP = 1000


first_decay = 0.9
second_decay = 0.999
learn_rate = 0.001
epsilon = 1e-08

F32 = jnp.float32
BF16 = jnp.bfloat16
CHUNKS = 2


def adam_update(param, grad, moment, square):
    moment_new = first_decay * moment + (1.0 - first_decay) * grad
    square_new = second_decay * square + (1.0 - second_decay) * grad * grad
    first_fix = 1.0 - first_decay**ADAM_STEP
    second_fix = 1.0 - second_decay**ADAM_STEP
    param_new = param - learn_rate * (moment_new / first_fix) / (
        jnp.sqrt(square_new / second_fix) + epsilon
    )
    return (param_new, moment_new, square_new)


def shards(
    activations,
    encoder,
    enc_bias,
    decoder,
    enc_moment,
    enc_square,
    bias_moment,
    bias_square,
    dec_moment,
    dec_square,
):
    row_count = activations.shape[0] * lax.axis_size("dp")
    loss_scale = 2.0 / row_count
    inputs = lax.all_gather(activations, "latent", axis=1, tiled=True)
    enc_low, dec_low = (
        lax.all_gather(encoder.astype(jnp.bfloat16), "dp", axis=0, tiled=True),
        lax.all_gather(decoder.astype(jnp.bfloat16), "dp", axis=0, tiled=True),
    )
    bias_full = lax.all_gather(enc_bias, "dp", axis=0, tiled=True)
    square_sums = lax.psum(jnp.sum(decoder * decoder, axis=0), "dp")
    column_norms = jnp.sqrt(square_sums + 1e-06)
    preact = jnp.dot(inputs, enc_low, preferred_element_type=jnp.float32) + bias_full
    latent_codes = jnp.maximum(preact, 0.0).astype(jnp.bfloat16)
    partial_sums = lax.dot_general(
        latent_codes, dec_low, (((1,), (1,)), ((), ())), preferred_element_type=jnp.float32
    )
    rebuilt = lax.psum_scatter(partial_sums, "latent", scatter_dimension=1, tiled=True)
    error = (activations.astype(jnp.float32) - rebuilt).astype(jnp.bfloat16)
    full_error = lax.all_gather(error, "latent", axis=1, tiled=True)
    active_sum = lax.psum(jnp.sum(latent_codes.astype(jnp.float32), axis=0), "dp")
    grad_dec_rows = -loss_scale * lax.dot_general(
        full_error, latent_codes, (((0,), (0,)), ((), ())), preferred_element_type=jnp.float32
    )
    code_grad = (
        -loss_scale * jnp.dot(full_error, dec_low, preferred_element_type=jnp.float32)
        + column_norms / row_count
    )
    grad_preact = jnp.where(preact > 0.0, code_grad, 0.0)
    grad_encoder = lax.dot_general(
        inputs,
        grad_preact.astype(jnp.bfloat16),
        (((0,), (0,)), ((), ())),
        preferred_element_type=jnp.float32,
    )
    grad_bias = jnp.sum(grad_preact, axis=0)
    grad_encoder, grad_dec_rows, grad_bias = (
        lax.psum_scatter(grad_encoder, "dp", scatter_dimension=0, tiled=True),
        lax.psum_scatter(grad_dec_rows, "dp", scatter_dimension=0, tiled=True),
        lax.psum_scatter(grad_bias, "dp", scatter_dimension=0, tiled=True),
    )
    grad_decoder = grad_dec_rows + decoder * (active_sum / column_norms) / row_count
    new_encoder, new_enc_moment, new_enc_square = adam_update(
        encoder, grad_encoder, enc_moment, enc_square
    )
    new_enc_bias, new_bias_moment, new_bias_square = adam_update(
        enc_bias, grad_bias, bias_moment, bias_square
    )
    new_decoder, new_dec_moment, new_dec_square = adam_update(
        decoder, grad_decoder, dec_moment, dec_square
    )
    return (
        error,
        new_encoder,
        new_enc_bias,
        new_decoder,
        new_enc_moment,
        new_enc_square,
        new_bias_moment,
        new_bias_square,
        new_dec_moment,
        new_dec_square,
    )


VMEM = pl.BlockSpec(memory_space=pltpu.VMEM)
SMEM = pl.BlockSpec(memory_space=pltpu.SMEM)
ANY = pl.BlockSpec(memory_space=pl.ANY)
EXTRA = 16


def local_kernel(body, outs, place, *args, flops=0, after=(), scratch=()):
    moved = sum(a.size * a.dtype.itemsize for a in args)
    moved += sum(o.size * jnp.dtype(o.dtype).itemsize for o in outs)

    def run(place, *refs):
        body(place, *refs[: len(args)], *refs[len(args) + len(after) :])

    return pl.pallas_call(
        run,
        out_shape=outs,
        in_specs=[SMEM] + [VMEM] * len(args) + [ANY] * len(after),
        out_specs=[VMEM] * len(outs),
        scratch_shapes=scratch,
        compiler_params=pltpu.CompilerParams(vmem_limit_bytes=48 * 1024 * 1024),
        cost_estimate=pl.CostEstimate(flops=flops, bytes_accessed=moved, transcendentals=0),
    )(place, *args, *after)


def shape(dims, dtype):
    return jax.ShapeDtypeStruct(dims, dtype)


def columns(start, width):
    return pl.ds(pl.multiple_of(start, width), width)


def three_rows(row):
    high = row.astype(BF16).astype(F32)
    middle = (row - high).astype(BF16).astype(F32)
    low = row - high - middle
    at = lax.broadcasted_iota(jnp.int32, (EXTRA, row.shape[1]), 0)
    rows = jnp.where(at == 0, high, jnp.where(at == 1, middle, jnp.where(at == 2, low, 0.0)))
    return rows.astype(BF16)


def behind(value, *others):
    return lax.optimization_barrier((value, *others))[0]


def one_row(rows):
    return jnp.sum(rows.astype(F32), axis=0, keepdims=True)


def encoder_body(place, encoder, bias, out):
    depth = encoder.shape[0]
    out[:depth] = encoder[...].astype(BF16)
    out[depth:] = three_rows(jnp.concatenate([bias[...]] * 4, axis=1))


def decoder_body(place, decoder, out):
    depth = decoder.shape[0]
    value = decoder[...]
    out[:depth] = value.astype(BF16)
    out[depth:] = three_rows(jnp.sum(value * value, axis=0, keepdims=True))


def codes_body(
    place, own, low, high, across, relay, enc0, enc1, enc2, enc3, codes, mask, full, active, bias
):
    z, i = place[0], place[1]
    width = own.shape[1]
    full[:, columns(z * width, width)] = own[...]
    full[:, columns(((z + 2) % 4) * width, width)] = across[...]

    @pl.when(z < 3)
    def _():
        full[:, columns((z + 1) * width, width)] = high[...]

    @pl.when(z == 3)
    def _():
        full[:, :width] = relay[...]

    @pl.when(z > 0)
    def _():
        full[:, columns((z - 1) * width, width)] = low[...]

    @pl.when(z == 0)
    def _():
        full[:, 3 * width :] = relay[...]

    total = jnp.zeros(codes.shape, F32)
    piece = codes.shape[1] // 4
    for t, enc in enumerate((enc0, enc1, enc2, enc3)):
        b = i ^ t
        total += jnp.dot(
            full[:, columns(b * width, width)], enc[:width, :], preferred_element_type=F32
        )
        bias[:, columns(b * piece, piece)] = one_row(enc[width:, :piece])
    preact = total + bias[...]
    low_codes = jnp.maximum(preact, 0.0).astype(BF16)
    codes[...] = low_codes
    mask[...] = (preact > 0.0).astype(F32).astype(BF16)
    active[...] = jnp.sum(low_codes.astype(F32), axis=0, keepdims=True)


def error_body(
    place, own, low, high, across, dec0, dec1, dec2, dec3, row0, row1, row2, row3, inputs, error
):
    z, i = place[0], place[1]
    half = row0.shape[0] // 3
    shift = pl.multiple_of(jnp.where(z >= 2, half, 0), half)
    for t in range(4):
        dec, row = (dec0, dec1, dec2, dec3)[t], (row0, row1, row2, row3)[t]
        lefts = (own, low, high, across)
        rights = [dec[pl.ds(shift, half), :]] + [row[m * half : (m + 1) * half, :] for m in range(3)]
        total = jnp.zeros((own.shape[0], half), F32)
        for left, right in zip(lefts, rights):
            total += lax.dot_general(
                left[...], right, (((1,), (1,)), ((), ())), preferred_element_type=F32
            )
        q = i ^ t
        given = inputs[:, columns(q * 2 * half + shift, half)].astype(F32)
        error[:, columns(q * half, half)] = (given - total).astype(BF16)


def grad_code_body(
    rows,
    place,
    mine,
    swapped,
    passed,
    relayed,
    mask,
    dec0,
    dec1,
    dec2,
    dec3,
    grad_low,
    bias_sum,
    norms,
    full,
    home,
):
    z, i = place[0], place[1]
    half = mine.shape[1] // 4
    width = 2 * half
    for at, (near, far) in enumerate(
        ((passed, relayed), (mine, swapped), (swapped, mine), (relayed, passed))
    ):

        @pl.when(z == at)
        def _(near=near, far=far):
            for q in range(4):
                full[:, q * width : q * width + half] = near[:, q * half : (q + 1) * half]
                full[:, q * width + half : (q + 1) * width] = far[:, q * half : (q + 1) * half]

    total = jnp.zeros(grad_low.shape, F32)
    squares = jnp.zeros(bias_sum.shape, F32)
    for t, dec in enumerate((dec0, dec1, dec2, dec3)):
        total += jnp.dot(
            full[:, columns((i ^ t) * width, width)], dec[:width, :], preferred_element_type=F32
        )
        squares += one_row(dec[width:, :])
    column_norms = jnp.sqrt(squares + 1e-06)
    norms[...] = column_norms
    code_grad = (-2.0 / rows) * total + column_norms / rows
    grad = jnp.where(mask[...] > 0, code_grad, 0.0)
    grad_low[...] = grad.astype(BF16)
    bias_sum[...] = jnp.sum(grad, axis=0, keepdims=True)
    home[...] = full[:, columns(z * width, width)]


def grad_body(scale, slots, place, *refs):
    i = place[1]
    lefts, rights, sums = refs[:CHUNKS], refs[CHUNKS : 2 * CHUNKS], refs[2 * CHUNKS : 3 * CHUNKS]
    outs = refs[3 * CHUNKS :]
    width = lefts[0].shape[1] // 4
    for slot, out in zip(slots, outs):
        total = jnp.zeros((width, out.shape[1]), F32)
        for left, right in zip(lefts, rights):
            total += lax.dot_general(
                left[:, columns((i ^ slot) * width, width)],
                right[...],
                (((0,), (0,)), ((), ())),
                preferred_element_type=F32,
            )
        out[:width] = scale * total
    row = functools.reduce(jnp.add, [value[...] for value in sums])
    outs[0][width:] = jnp.broadcast_to(row, (outs[0].shape[0] - width, row.shape[1]))


def line_shards(
    activations,
    encoder,
    enc_bias,
    decoder,
    enc_moment,
    enc_square,
    bias_moment,
    bias_square,
    dec_moment,
    dec_square,
):
    rows = activations.shape[0] * 4
    chunk = activations.shape[0] // CHUNKS
    width = activations.shape[1]
    latents = encoder.shape[1]
    half = width // 2
    features = 4 * width
    z, i = lax.axis_index("latent"), lax.axis_index("dp")
    place = jnp.stack([z, i]).astype(jnp.int32)

    def along(value, pairs):
        return lax.ppermute(value, "latent", pairs)

    def flip(value, bits, planes=(0, 1, 2, 3)):
        pairs = [(4 * p + k, 4 * p + (k ^ bits)) for p in planes for k in range(4)]
        return lax.ppermute(value, ("latent", "dp"), pairs)

    up = [(0, 1), (1, 2), (2, 3)]
    down = [(1, 0), (2, 1), (3, 2)]
    two = [(0, 2), (1, 3), (2, 0), (3, 1)]

    (enc_own,) = local_kernel(
        encoder_body,
        [shape((width + EXTRA, latents), BF16)],
        place,
        encoder,
        enc_bias.reshape(1, -1),
    )

    parts = [activations[c * chunk : (c + 1) * chunk] for c in range(CHUNKS)]
    gathered = []
    for part in parts:
        part = behind(part, *(gathered[-1][1:4] if gathered else (enc_own,)))
        low, high, across = along(part, up), along(part, down), along(part, two)
        relay = along(across, [(2, 3), (1, 0)])
        gathered.append((part, low, high, across, relay))

    enc_chip, enc_core = flip(enc_own, 2), flip(enc_own, 1)
    enc = [enc_own, enc_core, enc_chip, flip(enc_chip, 1)]
    (dec_own,) = local_kernel(
        decoder_body,
        [shape((width + EXTRA, latents), BF16)],
        place,
        decoder,
        after=(enc_core, enc_chip, *gathered[0][1:4]),
    )
    dec_core, dec_chip = flip(dec_own, 1), flip(dec_own, 2)

    first, second = dec_own[:half], dec_own[half:width]
    dec_pieces = [
        along(jnp.where(z >= 1, second, first), [(0, 1), (1, 2)]),
        along(jnp.where(z >= 3, second, first), [(2, 1), (3, 2)]),
        along(jnp.where(z >= 2, first, second), [(0, 2), (3, 1)]),
    ]

    flops = 2 * chunk * features * latents
    inputs, codes, masks, actives = [], [], [], []
    for step, part in enumerate(gathered):
        low_codes, mask, full, active = local_kernel(
            codes_body,
            [
                shape((chunk, latents), BF16),
                shape((chunk, latents), BF16),
                shape((chunk, features), BF16),
                shape((1, latents), F32),
            ],
            place,
            *part,
            *enc,
            flops=flops,
            scratch=[pltpu.VMEM((1, latents), F32)],
        )
        if step == 0:
            dec = [dec_own, dec_core, dec_chip, flip(behind(dec_chip, low_codes), 1)]
            first_codes = low_codes
        inputs.append(full)
        codes.append(low_codes)
        masks.append(mask)
        actives.append(active)
    nearby = []
    for low_codes in codes:
        low = along(low_codes, [(0, 1), (1, 2)])
        high = along(low_codes, [(2, 1), (3, 2)])
        across = along(low_codes, [(0, 2), (3, 1)])
        nearby.append((low_codes, low, high, across))
    dec_pieces = [
        behind(piece, dec_chip, first_codes, *gathered[-1][1:3]) for piece in dec_pieces
    ]
    rows_own = jnp.concatenate(dec_pieces, axis=0)
    rows_chip, rows_core = flip(rows_own, 2, (1, 2)), flip(rows_own, 1, (1, 2))
    rows_both = flip(behind(rows_chip, *gathered[-1][3:], *nearby[0][1:]), 1, (1, 2))
    dec_rows = [rows_own, rows_core, rows_chip, rows_both]
    errors = []
    for step in range(CHUNKS):
        (own_error,) = local_kernel(
            error_body,
            [shape((chunk, features // 2), BF16)],
            place,
            *nearby[step],
            *dec,
            *dec_rows,
            inputs[step],
            flops=2 * flops,
            after=errors[-1][1:3] if errors else (),
        )
        passed = along(own_error, [(1, 0), (2, 3)])
        swapped = along(own_error, [(1, 2), (2, 1)])
        relayed = along(swapped, [(1, 0), (2, 3)])
        errors.append((own_error, swapped, passed, relayed))

    grads, bias_sums, fulls, homes = [], [], [], []
    for error, mask in zip(errors, masks):
        grad_low, bias_sum, norms, full, home = local_kernel(
            functools.partial(grad_code_body, rows),
            [
                shape((chunk, latents), BF16),
                shape((1, latents), F32),
                shape((1, latents), F32),
                shape((chunk, features), BF16),
                shape((chunk, width), BF16),
            ],
            place,
            *error,
            mask,
            *dec,
            flops=flops,
        )
        grads.append(grad_low)
        bias_sums.append(bias_sum)
        fulls.append(full)
        homes.append(home)
    error = jnp.concatenate(homes, axis=0)

    def reduced(scale, lefts, rights, sums):
        def slots(*which):
            return local_kernel(
                functools.partial(grad_body, scale, which),
                [shape((width + 8, latents), F32), shape((width, latents), F32)],
                place,
                *lefts,
                *rights,
                *sums,
                flops=CHUNKS * flops // 2,
            )

        send_far, send_near = slots(3, 1)
        keep_far, keep_near = slots(2, 0)
        far = keep_far + flip(send_far, 1)
        row = far[width : width + 1]
        far = far[:width]
        largest = jnp.maximum(jnp.max(jnp.abs(far), axis=0, keepdims=True), 1e-30)
        sent = (far * (16384.0 / largest)).astype(jnp.float16)
        near = keep_near + flip(send_near, 1)
        small = flip(jnp.concatenate([largest, row], axis=0), 2)
        block = near + flip(sent, 2).astype(F32) * (small[:1] / 16384.0)
        return block, row + small[1:]

    grad_dec_rows, active_sum = reduced(-2.0 / rows, fulls, codes, actives)
    grad_encoder, grad_bias = reduced(1.0, inputs, grads, bias_sums)
    grad_bias = lax.dynamic_slice(
        grad_bias.reshape(latents), (i * enc_bias.shape[0],), (enc_bias.shape[0],)
    )
    grad_decoder = grad_dec_rows + decoder * (active_sum / norms) / rows

    new_decoder, new_dec_moment, new_dec_square = adam_update(
        decoder, grad_decoder, dec_moment, dec_square
    )
    new_enc_bias, new_bias_moment, new_bias_square = adam_update(
        enc_bias, grad_bias, bias_moment, bias_square
    )
    new_encoder, new_enc_moment, new_enc_square = adam_update(
        encoder, grad_encoder, enc_moment, enc_square
    )
    return (
        error,
        new_encoder,
        new_enc_bias,
        new_decoder,
        new_enc_moment,
        new_enc_square,
        new_bias_moment,
        new_bias_square,
        new_dec_moment,
        new_dec_square,
    )


def solution(mesh):
    in_specs = (
        P(("groups", "dp"), "latent"),
        P(("groups", "dp"), "latent"),
        P(("groups", "latent", "dp")),
        P(("groups", "dp"), "latent"),
        P(("groups", "dp"), "latent"),
        P(("groups", "dp"), "latent"),
        P(("groups", "latent", "dp")),
        P(("groups", "latent", "dp")),
        P(("groups", "dp"), "latent"),
        P(("groups", "dp"), "latent"),
    )
    out_specs = (
        P(("groups", "dp"), "latent"),
        P(("groups", "dp"), "latent"),
        P(("groups", "latent", "dp")),
        P(("groups", "dp"), "latent"),
        P(("groups", "dp"), "latent"),
        P(("groups", "dp"), "latent"),
        P(("groups", "latent", "dp")),
        P(("groups", "latent", "dp")),
        P(("groups", "dp"), "latent"),
        P(("groups", "dp"), "latent"),
    )
    line = mesh.shape["latent"] == 4 and mesh.shape["dp"] == 4
    plan = line_shards if line else shards
    return jax.shard_map(plan, mesh=mesh, in_specs=in_specs, out_specs=out_specs, check_vma=False)
```

```python
import functools

import jax
import jax.numpy as jnp
from jax import lax
from jax.experimental import pallas as pl
from jax.experimental.pallas import tpu as pltpu
from jax.sharding import PartitionSpec as P

ADAM_STEP = 1000


first_decay = 0.9
second_decay = 0.999
learn_rate = 0.001
epsilon = 1e-08

F32 = jnp.float32
BF16 = jnp.bfloat16


def adam_update(param, grad, moment, square):
    moment_new = first_decay * moment + (1.0 - first_decay) * grad
    square_new = second_decay * square + (1.0 - second_decay) * grad * grad
    first_fix = 1.0 - first_decay**ADAM_STEP
    second_fix = 1.0 - second_decay**ADAM_STEP
    param_new = param - learn_rate * (moment_new / first_fix) / (
        jnp.sqrt(square_new / second_fix) + epsilon
    )
    return (param_new, moment_new, square_new)


def shards(
    activations,
    encoder,
    enc_bias,
    decoder,
    enc_moment,
    enc_square,
    bias_moment,
    bias_square,
    dec_moment,
    dec_square,
):
    row_count = activations.shape[0] * lax.axis_size("dp")
    loss_scale = 2.0 / row_count
    inputs = lax.all_gather(activations, "latent", axis=1, tiled=True)
    enc_low, dec_low = (
        lax.all_gather(encoder.astype(jnp.bfloat16), "dp", axis=0, tiled=True),
        lax.all_gather(decoder.astype(jnp.bfloat16), "dp", axis=0, tiled=True),
    )
    bias_full = lax.all_gather(enc_bias, "dp", axis=0, tiled=True)
    square_sums = lax.psum(jnp.sum(decoder * decoder, axis=0), "dp")
    column_norms = jnp.sqrt(square_sums + 1e-06)
    preact = jnp.dot(inputs, enc_low, preferred_element_type=jnp.float32) + bias_full
    latent_codes = jnp.maximum(preact, 0.0).astype(jnp.bfloat16)
    partial_sums = lax.dot_general(
        latent_codes, dec_low, (((1,), (1,)), ((), ())), preferred_element_type=jnp.float32
    )
    rebuilt = lax.psum_scatter(partial_sums, "latent", scatter_dimension=1, tiled=True)
    error = (activations.astype(jnp.float32) - rebuilt).astype(jnp.bfloat16)
    full_error = lax.all_gather(error, "latent", axis=1, tiled=True)
    active_sum = lax.psum(jnp.sum(latent_codes.astype(jnp.float32), axis=0), "dp")
    grad_dec_rows = -loss_scale * lax.dot_general(
        full_error, latent_codes, (((0,), (0,)), ((), ())), preferred_element_type=jnp.float32
    )
    code_grad = (
        -loss_scale * jnp.dot(full_error, dec_low, preferred_element_type=jnp.float32)
        + column_norms / row_count
    )
    grad_preact = jnp.where(preact > 0.0, code_grad, 0.0)
    grad_encoder = lax.dot_general(
        inputs,
        grad_preact.astype(jnp.bfloat16),
        (((0,), (0,)), ((), ())),
        preferred_element_type=jnp.float32,
    )
    grad_bias = jnp.sum(grad_preact, axis=0)
    grad_encoder, grad_dec_rows, grad_bias = (
        lax.psum_scatter(grad_encoder, "dp", scatter_dimension=0, tiled=True),
        lax.psum_scatter(grad_dec_rows, "dp", scatter_dimension=0, tiled=True),
        lax.psum_scatter(grad_bias, "dp", scatter_dimension=0, tiled=True),
    )
    grad_decoder = grad_dec_rows + decoder * (active_sum / column_norms) / row_count
    new_encoder, new_enc_moment, new_enc_square = adam_update(
        encoder, grad_encoder, enc_moment, enc_square
    )
    new_enc_bias, new_bias_moment, new_bias_square = adam_update(
        enc_bias, grad_bias, bias_moment, bias_square
    )
    new_decoder, new_dec_moment, new_dec_square = adam_update(
        decoder, grad_decoder, dec_moment, dec_square
    )
    return (
        error,
        new_encoder,
        new_enc_bias,
        new_decoder,
        new_enc_moment,
        new_enc_square,
        new_bias_moment,
        new_bias_square,
        new_dec_moment,
        new_dec_square,
    )


VMEM = pl.BlockSpec(memory_space=pltpu.VMEM)
SMEM = pl.BlockSpec(memory_space=pltpu.SMEM)
ANY = pl.BlockSpec(memory_space=pl.ANY)
EXTRA = 16


def local_kernel(body, outs, place, *args, flops=0, after=(), scratch=()):
    moved = sum(a.size * a.dtype.itemsize for a in args)
    moved += sum(o.size * jnp.dtype(o.dtype).itemsize for o in outs)

    def run(place, *refs):
        body(place, *refs[: len(args)], *refs[len(args) + len(after) :])

    return pl.pallas_call(
        run,
        out_shape=outs,
        in_specs=[SMEM] + [VMEM] * len(args) + [ANY] * len(after),
        out_specs=[VMEM] * len(outs),
        scratch_shapes=scratch,
        compiler_params=pltpu.CompilerParams(vmem_limit_bytes=48 * 1024 * 1024),
        cost_estimate=pl.CostEstimate(flops=flops, bytes_accessed=moved, transcendentals=0),
    )(place, *args, *after)


def shape(dims, dtype):
    return jax.ShapeDtypeStruct(dims, dtype)


def columns(start, width):
    return pl.ds(pl.multiple_of(start, width), width)


def three_rows(row):
    high = row.astype(BF16).astype(F32)
    middle = (row - high).astype(BF16).astype(F32)
    low = row - high - middle
    at = lax.broadcasted_iota(jnp.int32, (EXTRA, row.shape[1]), 0)
    rows = jnp.where(at == 0, high, jnp.where(at == 1, middle, jnp.where(at == 2, low, 0.0)))
    return rows.astype(BF16)


def behind(value, *others):
    return lax.optimization_barrier((value, *others))[0]


def one_row(rows):
    return jnp.sum(rows.astype(F32), axis=0, keepdims=True)


def encoder_body(place, encoder, bias, out):
    depth = encoder.shape[0]
    out[:depth] = encoder[...].astype(BF16)
    out[depth:] = three_rows(jnp.concatenate([bias[...]] * 4, axis=1))


def decoder_body(place, decoder, out):
    depth = decoder.shape[0]
    value = decoder[...]
    out[:depth] = value.astype(BF16)
    out[depth:] = three_rows(jnp.sum(value * value, axis=0, keepdims=True))


def codes_body(
    place,
    own,
    low,
    high,
    across,
    relay1,
    relay2,
    enc0,
    enc1,
    enc2,
    enc3,
    codes,
    mask,
    full,
    active,
    bias,
):
    z, i = place[0], place[1]
    width = own.shape[1]
    for at, blocks in enumerate(
        (
            (own, high, relay1, relay2),
            (low, own, high, across),
            (across, low, own, high),
            (relay2, relay1, low, own),
        )
    ):

        @pl.when(z == at)
        def _(blocks=blocks):
            for b, block in enumerate(blocks):
                full[:, b * width : (b + 1) * width] = block[...]

    total = jnp.zeros(codes.shape, F32)
    piece = codes.shape[1] // 4
    for t, enc in enumerate((enc0, enc1, enc2, enc3)):
        b = i ^ t
        total += jnp.dot(
            full[:, columns(b * width, width)], enc[:width, :], preferred_element_type=F32
        )
        bias[:, columns(b * piece, piece)] = one_row(enc[width:, :piece])
    preact = total + bias[...]
    low_codes = jnp.maximum(preact, 0.0).astype(BF16)
    codes[...] = low_codes
    mask[...] = (preact > 0.0).astype(F32).astype(BF16)
    active[...] = jnp.sum(low_codes.astype(F32), axis=0, keepdims=True)


def error_body(
    place, own, low, high, across, dec0, dec1, dec2, dec3, row0, row1, row2, row3, inputs, error
):
    z, i = place[0], place[1]
    half = row0.shape[0] // 3
    shift = pl.multiple_of(jnp.where(z >= 2, half, 0), half)
    for t in range(4):
        dec, row = (dec0, dec1, dec2, dec3)[t], (row0, row1, row2, row3)[t]
        lefts = (own, low, high, across)
        rights = [dec[pl.ds(shift, half), :]] + [row[m * half : (m + 1) * half, :] for m in range(3)]
        total = jnp.zeros((own.shape[0], half), F32)
        for left, right in zip(lefts, rights):
            total += lax.dot_general(
                left[...], right, (((1,), (1,)), ((), ())), preferred_element_type=F32
            )
        q = i ^ t
        given = inputs[:, columns(q * 2 * half + shift, half)].astype(F32)
        error[:, columns(q * half, half)] = (given - total).astype(BF16)


def grad_code_body(
    rows,
    place,
    mine,
    swapped,
    passed,
    relayed,
    mask,
    dec0,
    dec1,
    dec2,
    dec3,
    grad_low,
    bias_sum,
    norms,
    full,
    home,
):
    z, i = place[0], place[1]
    half = mine.shape[1] // 4
    width = 2 * half
    for at, (near, far) in enumerate(
        ((passed, relayed), (mine, swapped), (swapped, mine), (relayed, passed))
    ):

        @pl.when(z == at)
        def _(near=near, far=far):
            for q in range(4):
                full[:, q * width : q * width + half] = near[:, q * half : (q + 1) * half]
                full[:, q * width + half : (q + 1) * width] = far[:, q * half : (q + 1) * half]

    total = jnp.zeros(grad_low.shape, F32)
    squares = jnp.zeros(bias_sum.shape, F32)
    for t, dec in enumerate((dec0, dec1, dec2, dec3)):
        total += jnp.dot(
            full[:, columns((i ^ t) * width, width)], dec[:width, :], preferred_element_type=F32
        )
        squares += one_row(dec[width:, :])
    column_norms = jnp.sqrt(squares + 1e-06)
    norms[...] = column_norms
    code_grad = (-2.0 / rows) * total + column_norms / rows
    grad = jnp.where(mask[...] > 0, code_grad, 0.0)
    grad_low[...] = grad.astype(BF16)
    bias_sum[...] = jnp.sum(grad, axis=0, keepdims=True)
    home[...] = full[:, columns(z * width, width)]


def grad_body(scale, slots, place, left, right, row, *outs):
    i = place[1]
    width = left.shape[1] // 4
    for slot, out in zip(slots, outs):
        out[:width] = scale * lax.dot_general(
            left[:, columns((i ^ slot) * width, width)],
            right[...],
            (((0,), (0,)), ((), ())),
            preferred_element_type=F32,
        )
    outs[0][width:] = jnp.broadcast_to(row[...], (outs[0].shape[0] - width, row.shape[1]))


def far_body(place, kept, received, scaled, small):
    width = scaled.shape[0]
    total = kept[:width] + received[:width]
    largest = jnp.maximum(jnp.max(jnp.abs(total), axis=0, keepdims=True), 1e-30)
    scaled[...] = total * (16384.0 / largest)
    row = kept[width:] + received[width:]
    at = lax.broadcasted_iota(jnp.int32, row.shape, 0)
    small[...] = jnp.where(at == 0, largest * (1.0 / 16384.0), row)


def line_shards(
    activations,
    encoder,
    enc_bias,
    decoder,
    enc_moment,
    enc_square,
    bias_moment,
    bias_square,
    dec_moment,
    dec_square,
):
    rows = activations.shape[0] * 4
    count, width = activations.shape
    latents = encoder.shape[1]
    half = width // 2
    features = 4 * width
    z, i = lax.axis_index("latent"), lax.axis_index("dp")
    place = jnp.stack([z, i]).astype(jnp.int32)

    def along(value, pairs):
        return lax.ppermute(value, "latent", pairs)

    def flip(value, bits, planes=(0, 1, 2, 3)):
        pairs = [(4 * p + k, 4 * p + (k ^ bits)) for p in planes for k in range(4)]
        return lax.ppermute(value, ("latent", "dp"), pairs)

    low = along(activations, [(0, 1), (1, 2), (2, 3)])
    high = along(activations, [(1, 0), (2, 1), (3, 2)])
    across = along(activations, [(0, 2), (3, 1)])

    (enc_own,) = local_kernel(
        encoder_body,
        [shape((width + EXTRA, latents), BF16)],
        place,
        encoder,
        enc_bias.reshape(1, -1),
    )
    enc_chip, enc_core = flip(enc_own, 2), flip(enc_own, 1)
    (dec_own,) = local_kernel(
        decoder_body,
        [shape((width + EXTRA, latents), BF16)],
        place,
        decoder,
        after=(enc_core, enc_chip),
    )
    dec_chip, dec_core = flip(dec_own, 2), flip(dec_own, 1)
    relay1 = along(behind(jnp.where(z == 1, high, low), enc_core), [(1, 0), (2, 3)])
    relay2 = along(behind(across, relay1), [(1, 0), (2, 3)])
    enc = [enc_own, enc_core, enc_chip, flip(enc_chip, 1)]

    dec_late = behind(dec_own, across)
    first, second = dec_late[:half], dec_late[half:width]
    dec_pieces = [
        along(jnp.where(z >= 1, second, first), [(0, 1), (1, 2)]),
        along(jnp.where(z >= 3, second, first), [(2, 1), (3, 2)]),
        along(jnp.where(z >= 2, first, second), [(0, 2), (3, 1)]),
    ]
    dec_pieces = [behind(piece, dec_chip, relay2) for piece in dec_pieces]
    rows_own = jnp.concatenate(dec_pieces, axis=0)
    dec = [dec_own, dec_core, dec_chip, flip(dec_chip, 1)]
    rows_chip, rows_core = flip(rows_own, 2, (1, 2)), flip(rows_own, 1, (1, 2))

    flops = 2 * count * features * latents
    codes, mask, inputs, active = local_kernel(
        codes_body,
        [
            shape((count, latents), BF16),
            shape((count, latents), BF16),
            shape((count, features), BF16),
            shape((1, latents), F32),
        ],
        place,
        activations,
        low,
        high,
        across,
        relay1,
        relay2,
        *enc,
        flops=flops,
        after=(rows_core, dec[1], dec[3]),
        scratch=[pltpu.VMEM((1, latents), F32)],
    )
    codes_low = along(codes, [(0, 1), (1, 2)])
    codes_high = along(codes, [(2, 1), (3, 2)])
    codes_across = along(codes, [(0, 2), (3, 1)])
    rows_both = flip(behind(rows_chip, codes_low, codes_high, codes_across), 1, (1, 2))

    (own_error,) = local_kernel(
        error_body,
        [shape((count, features // 2), BF16)],
        place,
        codes,
        codes_low,
        codes_high,
        codes_across,
        *dec,
        rows_own,
        rows_core,
        rows_chip,
        rows_both,
        inputs,
        flops=2 * flops,
    )
    swapped = along(own_error, [(1, 2), (2, 1)])
    passed = along(own_error, [(1, 0), (2, 3)])
    relayed = along(swapped, [(1, 0), (2, 3)])

    grad_low, bias_sum, norms, full_error, error = local_kernel(
        functools.partial(grad_code_body, rows),
        [
            shape((count, latents), BF16),
            shape((1, latents), F32),
            shape((1, latents), F32),
            shape((count, features), BF16),
            shape((count, width), BF16),
        ],
        place,
        own_error,
        swapped,
        passed,
        relayed,
        mask,
        *dec,
        flops=flops,
    )

    def reduced(scale, left, right, row):
        def slots(*which):
            return local_kernel(
                functools.partial(grad_body, scale, which),
                [shape((width + 8, latents), F32), shape((width, latents), F32)],
                place,
                left,
                right,
                row,
                flops=flops // 2,
            )

        send_far, send_near = slots(3, 1)
        keep_far, keep_near = slots(2, 0)
        scaled, small = local_kernel(
            far_body,
            [shape((width, latents), F32), shape((8, latents), F32)],
            place,
            keep_far,
            flip(send_far, 1),
        )
        sent = scaled.astype(jnp.float16)
        received, small_received = flip(sent, 2), flip(small, 2)
        near = keep_near + flip(send_near, 1)
        block = near + received.astype(F32) * small_received[:1]
        return block, small[1] + small_received[1], sent

    grad_dec_rows, active_sum, dec_sent = reduced(-2.0 / rows, full_error, codes, active)
    grad_encoder, grad_bias, enc_sent = reduced(1.0, inputs, grad_low, bias_sum)
    grad_bias = lax.dynamic_slice(grad_bias, (i * enc_bias.shape[0],), (enc_bias.shape[0],))
    decoder, dec_moment, dec_square = lax.optimization_barrier(
        (decoder, dec_moment, dec_square, dec_sent)
    )[:3]
    encoder, enc_moment, enc_square = lax.optimization_barrier(
        (encoder, enc_moment, enc_square, enc_sent)
    )[:3]
    grad_decoder = grad_dec_rows + decoder * (active_sum / norms) / rows

    new_decoder, new_dec_moment, new_dec_square = adam_update(
        decoder, grad_decoder, dec_moment, dec_square
    )
    new_enc_bias, new_bias_moment, new_bias_square = adam_update(
        enc_bias, grad_bias, bias_moment, bias_square
    )
    new_encoder, new_enc_moment, new_enc_square = adam_update(
        encoder, grad_encoder, enc_moment, enc_square
    )
    return (
        error,
        new_encoder,
        new_enc_bias,
        new_decoder,
        new_enc_moment,
        new_enc_square,
        new_bias_moment,
        new_bias_square,
        new_dec_moment,
        new_dec_square,
    )


def solution(mesh):
    in_specs = (
        P(("groups", "dp"), "latent"),
        P(("groups", "dp"), "latent"),
        P(("groups", "latent", "dp")),
        P(("groups", "dp"), "latent"),
        P(("groups", "dp"), "latent"),
        P(("groups", "dp"), "latent"),
        P(("groups", "latent", "dp")),
        P(("groups", "latent", "dp")),
        P(("groups", "dp"), "latent"),
        P(("groups", "dp"), "latent"),
    )
    out_specs = (
        P(("groups", "dp"), "latent"),
        P(("groups", "dp"), "latent"),
        P(("groups", "latent", "dp")),
        P(("groups", "dp"), "latent"),
        P(("groups", "dp"), "latent"),
        P(("groups", "dp"), "latent"),
        P(("groups", "latent", "dp")),
        P(("groups", "latent", "dp")),
        P(("groups", "dp"), "latent"),
        P(("groups", "dp"), "latent"),
    )
    line = mesh.shape["latent"] == 4 and mesh.shape["dp"] == 4
    plan = line_shards if line else shards
    return jax.shard_map(plan, mesh=mesh, in_specs=in_specs, out_specs=out_specs, check_vma=False)
```

```python
import functools

import jax
import jax.numpy as jnp
from jax import lax
from jax.experimental import pallas as pl
from jax.experimental.pallas import tpu as pltpu
from jax.sharding import PartitionSpec as P

ADAM_STEP = 1000


first_decay = 0.9
second_decay = 0.999
learn_rate = 0.001
epsilon = 1e-08

F32 = jnp.float32
BF16 = jnp.bfloat16


def adam_update(param, grad, moment, square):
    moment_new = first_decay * moment + (1.0 - first_decay) * grad
    square_new = second_decay * square + (1.0 - second_decay) * grad * grad
    first_fix = 1.0 - first_decay**ADAM_STEP
    second_fix = 1.0 - second_decay**ADAM_STEP
    param_new = param - learn_rate * (moment_new / first_fix) / (
        jnp.sqrt(square_new / second_fix) + epsilon
    )
    return (param_new, moment_new, square_new)


def shards(
    activations,
    encoder,
    enc_bias,
    decoder,
    enc_moment,
    enc_square,
    bias_moment,
    bias_square,
    dec_moment,
    dec_square,
):
    row_count = activations.shape[0] * lax.axis_size("dp")
    loss_scale = 2.0 / row_count
    inputs = lax.all_gather(activations, "latent", axis=1, tiled=True)
    enc_low, dec_low = (
        lax.all_gather(encoder.astype(jnp.bfloat16), "dp", axis=0, tiled=True),
        lax.all_gather(decoder.astype(jnp.bfloat16), "dp", axis=0, tiled=True),
    )
    bias_full = lax.all_gather(enc_bias, "dp", axis=0, tiled=True)
    square_sums = lax.psum(jnp.sum(decoder * decoder, axis=0), "dp")
    column_norms = jnp.sqrt(square_sums + 1e-06)
    preact = jnp.dot(inputs, enc_low, preferred_element_type=jnp.float32) + bias_full
    latent_codes = jnp.maximum(preact, 0.0).astype(jnp.bfloat16)
    partial_sums = lax.dot_general(
        latent_codes, dec_low, (((1,), (1,)), ((), ())), preferred_element_type=jnp.float32
    )
    rebuilt = lax.psum_scatter(partial_sums, "latent", scatter_dimension=1, tiled=True)
    error = (activations.astype(jnp.float32) - rebuilt).astype(jnp.bfloat16)
    full_error = lax.all_gather(error, "latent", axis=1, tiled=True)
    active_sum = lax.psum(jnp.sum(latent_codes.astype(jnp.float32), axis=0), "dp")
    grad_dec_rows = -loss_scale * lax.dot_general(
        full_error, latent_codes, (((0,), (0,)), ((), ())), preferred_element_type=jnp.float32
    )
    code_grad = (
        -loss_scale * jnp.dot(full_error, dec_low, preferred_element_type=jnp.float32)
        + column_norms / row_count
    )
    grad_preact = jnp.where(preact > 0.0, code_grad, 0.0)
    grad_encoder = lax.dot_general(
        inputs,
        grad_preact.astype(jnp.bfloat16),
        (((0,), (0,)), ((), ())),
        preferred_element_type=jnp.float32,
    )
    grad_bias = jnp.sum(grad_preact, axis=0)
    grad_encoder, grad_dec_rows, grad_bias = (
        lax.psum_scatter(grad_encoder, "dp", scatter_dimension=0, tiled=True),
        lax.psum_scatter(grad_dec_rows, "dp", scatter_dimension=0, tiled=True),
        lax.psum_scatter(grad_bias, "dp", scatter_dimension=0, tiled=True),
    )
    grad_decoder = grad_dec_rows + decoder * (active_sum / column_norms) / row_count
    new_encoder, new_enc_moment, new_enc_square = adam_update(
        encoder, grad_encoder, enc_moment, enc_square
    )
    new_enc_bias, new_bias_moment, new_bias_square = adam_update(
        enc_bias, grad_bias, bias_moment, bias_square
    )
    new_decoder, new_dec_moment, new_dec_square = adam_update(
        decoder, grad_decoder, dec_moment, dec_square
    )
    return (
        error,
        new_encoder,
        new_enc_bias,
        new_decoder,
        new_enc_moment,
        new_enc_square,
        new_bias_moment,
        new_bias_square,
        new_dec_moment,
        new_dec_square,
    )


VMEM = pl.BlockSpec(memory_space=pltpu.VMEM)
SMEM = pl.BlockSpec(memory_space=pltpu.SMEM)
ANY = pl.BlockSpec(memory_space=pl.ANY)
EXTRA = 16


def local_kernel(body, outs, place, *args, after=(), scratch=()):
    def run(place, *refs):
        body(place, *refs[: len(args)], *refs[len(args) + len(after) :])

    return pl.pallas_call(
        run,
        out_shape=outs,
        in_specs=[SMEM] + [VMEM] * len(args) + [ANY] * len(after),
        out_specs=[VMEM] * len(outs),
        scratch_shapes=scratch,
        compiler_params=pltpu.CompilerParams(vmem_limit_bytes=24 * 1024 * 1024),
        cost_estimate=pl.CostEstimate(flops=1, bytes_accessed=1, transcendentals=0),
    )(place, *args, *after)


def shape(dims, dtype):
    return jax.ShapeDtypeStruct(dims, dtype)


def columns(start, width):
    return pl.ds(pl.multiple_of(start, width), width)


def three_rows(row):
    high = row.astype(BF16).astype(F32)
    middle = (row - high).astype(BF16).astype(F32)
    low = row - high - middle
    at = lax.broadcasted_iota(jnp.int32, (EXTRA, row.shape[1]), 0)
    rows = jnp.where(at == 0, high, jnp.where(at == 1, middle, jnp.where(at == 2, low, 0.0)))
    return rows.astype(BF16)


def behind(value, *others):
    return lax.optimization_barrier((value, *others))[0]


def one_row(rows):
    return jnp.sum(rows.astype(F32), axis=0, keepdims=True)


def encoder_body(place, encoder, bias, out):
    depth = encoder.shape[0]
    out[:depth] = encoder[...].astype(BF16)
    out[depth:] = three_rows(jnp.concatenate([bias[...]] * 4, axis=1))


def decoder_body(place, decoder, out):
    depth = decoder.shape[0]
    value = decoder[...]
    out[:depth] = value.astype(BF16)
    out[depth:] = three_rows(jnp.sum(value * value, axis=0, keepdims=True))


def codes_body(
    place, own, one, two, three, enc0, enc1, enc2, enc3, codes, mask, full, active, bias
):
    z, i = place[0], place[1]
    width = own.shape[1]
    for k, block in enumerate((own, one, two, three)):
        full[:, columns((z ^ k) * width, width)] = block[...]
    total = jnp.zeros(codes.shape, F32)
    piece = codes.shape[1] // 4
    for t, enc in enumerate((enc0, enc1, enc2, enc3)):
        b = i ^ t
        total += jnp.dot(
            full[:, columns(b * width, width)], enc[:width, :], preferred_element_type=F32
        )
        bias[:, columns(b * piece, piece)] = one_row(enc[width:, :piece])
    preact = total + bias[...]
    low_codes = jnp.maximum(preact, 0.0).astype(BF16)
    codes[...] = low_codes
    mask[...] = (preact > 0.0).astype(F32).astype(BF16)
    active[...] = jnp.sum(low_codes.astype(F32), axis=0, keepdims=True)


def turn_body(place, full, turned):
    turned[...] = full[...].T


def error_body(
    place, own, low, high, across, dec0, dec1, dec2, dec3, row0, row1, row2, row3, inputs, error
):
    z, i = place[0], place[1]
    half = row0.shape[0] // 3
    shift = pl.multiple_of(jnp.where(z >= 2, half, 0), half)
    for t in range(4):
        dec, row = (dec0, dec1, dec2, dec3)[t], (row0, row1, row2, row3)[t]
        lefts = (own, low, high, across)
        rights = [dec[pl.ds(shift, half), :]] + [row[m * half : (m + 1) * half, :] for m in range(3)]
        total = jnp.zeros((own.shape[0], half), F32)
        for left, right in zip(lefts, rights):
            total += lax.dot_general(
                left[...], right, (((1,), (1,)), ((), ())), preferred_element_type=F32
            )
        q = i ^ t
        given = inputs[:, columns(q * 2 * half + shift, half)].astype(F32)
        error[:, columns(q * half, half)] = (given - total).astype(BF16)


def pick(place, middle, end, out):
    z = place[0]
    is_middle = (z == 1) | (z == 2)

    @pl.when(is_middle)
    def _():
        out[...] = middle[...]

    @pl.when(jnp.logical_not(is_middle))
    def _():
        out[...] = end[...]


def decoder_grads(scale, i, error, codes, row, send, keep):
    half = error.shape[1] // 4
    for out, slots in ((send, (3, 1)), (keep, (2, 0))):
        for at, slot in enumerate(slots):
            out[at * half : (at + 1) * half] = scale * lax.dot_general(
                error[:, columns((i ^ slot) * half, half)],
                codes[...],
                (((0,), (0,)), ((), ())),
                preferred_element_type=F32,
            )
    send[2 * half :] = jnp.broadcast_to(row[...], (send.shape[0] - 2 * half, row.shape[1]))


def back_through(i, error, decs, shift):
    half = error.shape[1] // 4
    return functools.reduce(
        jnp.add,
        [
            jnp.dot(
                error[:, columns((i ^ t) * half, half)],
                dec[pl.ds(pl.multiple_of(shift, half), half), :],
                preferred_element_type=F32,
            )
            for t, dec in enumerate(decs)
        ],
    )


def near_body(
    rows, place, mine, passed, codes, active, dec0, dec1, dec2, dec3, part, send, keep, near
):
    z, i = place[0], place[1]
    half = mine.shape[1] // 4
    pick(place, mine, passed, near)
    decoder_grads(-2.0 / rows, i, near, codes, active, send, keep)
    part[...] = back_through(i, near, (dec0, dec1, dec2, dec3), jnp.where(z >= 2, half, 0))


def far_error_body(rows, place, swapped, direct, codes, active, send, keep, far):
    pick(place, swapped, direct, far)
    decoder_grads(-2.0 / rows, place[1], far, codes, active, send, keep)


def far_code_body(
    rows, place, near, far, part, mask, dec0, dec1, dec2, dec3, grad_low, bias_sum, norms, home
):
    z, i = place[0], place[1]
    half = far.shape[1] // 4
    width = 2 * half
    decs = (dec0, dec1, dec2, dec3)
    shift = jnp.where(z >= 2, 0, half)
    total = part[...] + back_through(i, far, decs, shift)
    squares = functools.reduce(jnp.add, [one_row(dec[width:, :]) for dec in decs])
    column_norms = jnp.sqrt(squares + 1e-06)
    norms[...] = column_norms
    code_grad = (-2.0 / rows) * total + column_norms / rows
    grad = jnp.where(mask[...] > 0, code_grad, 0.0)
    grad_low[...] = grad.astype(BF16)
    bias_sum[...] = jnp.sum(grad, axis=0, keepdims=True)
    home[:, columns(half - shift, half)] = near[:, columns(z * half, half)]
    home[:, columns(shift, half)] = far[:, columns(z * half, half)]


def encoder_grad_body(place, turned, grad_low, row, send_far, send_near, keep_far, keep_near):
    i = place[1]
    width = turned.shape[0] // 4
    for slot, out in ((3, send_far), (1, send_near), (2, keep_far), (0, keep_near)):
        at = pl.ds(pl.multiple_of((i ^ slot) * width, width), width)
        out[:width] = jnp.dot(turned[at, :], grad_low[...], preferred_element_type=F32)
    send_far[width:] = jnp.broadcast_to(row[...], (send_far.shape[0] - width, row.shape[1]))


def far_body(place, kept, received, row, scaled, small, *near):
    width = scaled.shape[0]
    total = kept[:width] + received[:width]
    largest = jnp.maximum(jnp.max(jnp.abs(total), axis=0, keepdims=True), 1e-30)
    scaled[...] = total * (16384.0 / largest)
    rows = received[received.shape[0] - small.shape[0] :] + row[...]
    at = lax.broadcasted_iota(jnp.int32, rows.shape, 0)
    small[...] = jnp.where(at == 0, largest * (1.0 / 16384.0), rows)
    for out in near:
        out[...] = kept[width:] + received[width : kept.shape[0]]


def line_shards(
    activations,
    encoder,
    enc_bias,
    decoder,
    enc_moment,
    enc_square,
    bias_moment,
    bias_square,
    dec_moment,
    dec_square,
):
    rows = activations.shape[0] * 4
    count, width = activations.shape
    latents = encoder.shape[1]
    half = width // 2
    features = 4 * width
    z, i = lax.axis_index("latent"), lax.axis_index("dp")
    place = jnp.stack([z, i]).astype(jnp.int32)

    def along(value, pairs):
        return lax.ppermute(value, "latent", pairs)

    def flip(value, bits, planes=(0, 1, 2, 3)):
        pairs = [(4 * p + k, 4 * p + (k ^ bits)) for p in planes for k in range(4)]
        return lax.ppermute(value, ("latent", "dp"), pairs)

    one, two, three = [along(activations, [(k, k ^ d) for k in range(4)]) for d in (1, 2, 3)]

    (enc_own,) = local_kernel(
        encoder_body,
        [shape((width + EXTRA, latents), BF16)],
        place,
        encoder,
        enc_bias.reshape(1, -1),
    )
    enc_chip, enc_core = flip(enc_own, 2), flip(enc_own, 1)
    (dec_own,) = local_kernel(
        decoder_body,
        [shape((width + EXTRA, latents), BF16)],
        place,
        decoder,
        after=(enc_core,),
    )
    dec_chip, dec_core = flip(behind(dec_own, enc_chip), 2), flip(dec_own, 1)
    enc = [enc_own, enc_core, enc_chip, flip(behind(enc_chip, one, two), 1)]

    dec_late = behind(dec_own, one, two)
    first, second = dec_late[:half], dec_late[half:width]
    dec_pieces = [
        along(jnp.where(z >= 1, second, first), [(0, 1), (1, 2)]),
        along(jnp.where(z >= 3, second, first), [(2, 1), (3, 2)]),
        along(jnp.where(z >= 2, first, second), [(0, 2), (3, 1)]),
    ]
    dec = [dec_own, dec_core, dec_chip, flip(dec_chip, 1)]

    codes, mask, inputs, active = local_kernel(
        codes_body,
        [
            shape((count, latents), BF16),
            shape((count, latents), BF16),
            shape((count, features), BF16),
            shape((1, latents), F32),
        ],
        place,
        activations,
        one,
        two,
        three,
        *enc,
        scratch=[pltpu.VMEM((1, latents), F32)],
    )
    codes_low = along(codes, [(0, 1), (1, 2)])
    codes_high = along(codes, [(2, 1), (3, 2)])
    codes_across = along(codes, [(0, 2), (3, 1)])
    dec_pieces = [behind(piece, codes, dec_chip) for piece in dec_pieces]
    rows_own = jnp.concatenate(dec_pieces, axis=0)
    (turned,) = local_kernel(turn_body, [shape((features, count), BF16)], place, inputs)
    rows_chip = flip(rows_own, 2, (1, 2))
    rows_core = flip(behind(rows_own, turned), 1, (1, 2))
    rows_both = flip(
        behind(rows_chip, codes_low, codes_high, codes_across, dec[1], dec[3]), 1, (1, 2)
    )

    (own_error,) = local_kernel(
        error_body,
        [shape((count, features // 2), BF16)],
        place,
        codes,
        codes_low,
        codes_high,
        codes_across,
        *dec,
        rows_own,
        rows_core,
        rows_chip,
        rows_both,
        inputs,
    )
    swapped = along(own_error, [(1, 2), (2, 1)])
    passed = along(own_error, [(1, 0), (2, 3)])
    direct = along(own_error, [(2, 0), (1, 3)])

    def across_chips(scaled, small):
        sent = scaled.astype(jnp.float16)
        received, small_received = flip(sent, 2), flip(small, 2)
        block = received.astype(F32) * small_received[:1]
        return received, block, small[1] + small_received[1]

    def decoder_half(send, keep, row):
        scaled, small, near = local_kernel(
            far_body,
            [shape((half, latents), F32), shape((8, latents), F32), shape((half, latents), F32)],
            place,
            keep,
            flip(send, 1),
            row,
        )
        received, block, row = across_chips(scaled, small)
        return scaled, received, near + block, row

    blocks = [shape((width + 8, latents), F32), shape((width, latents), F32)]
    part, send, keep, near = local_kernel(
        functools.partial(near_body, rows),
        [shape((count, latents), F32), *blocks, shape((count, features // 2), BF16)],
        place,
        own_error,
        passed,
        codes,
        active,
        *dec,
        after=(swapped,),
    )
    near_scaled, near_received, near_grad, active_sum = decoder_half(send, keep, active)
    send, keep, far = local_kernel(
        functools.partial(far_error_body, rows),
        [*blocks, shape((count, features // 2), BF16)],
        place,
        swapped,
        direct,
        codes,
        active,
        after=(near_scaled,),
    )
    _, _, far_grad, _ = decoder_half(send, keep, active)
    grad_low, bias_sum, norms, error = local_kernel(
        functools.partial(far_code_body, rows),
        [
            shape((count, latents), BF16),
            shape((1, latents), F32),
            shape((1, latents), F32),
            shape((count, width), BF16),
        ],
        place,
        near,
        far,
        behind(part, near_received),
        mask,
        *dec,
    )
    send_far, send_near, keep_far, keep_near = local_kernel(
        encoder_grad_body,
        [shape((width + 8, latents), F32)] + [shape((width, latents), F32)] * 3,
        place,
        turned,
        grad_low,
        bias_sum,
    )
    scaled, small = local_kernel(
        far_body,
        [shape((width, latents), F32), shape((8, latents), F32)],
        place,
        keep_far,
        flip(send_far, 1),
        bias_sum,
    )
    _, block, grad_bias = across_chips(scaled, small)
    grad_encoder = keep_near + flip(send_near, 1) + block
    grad_bias = lax.dynamic_slice(grad_bias, (i * enc_bias.shape[0],), (enc_bias.shape[0],))

    decoder, dec_moment, dec_square = lax.optimization_barrier(
        (decoder, dec_moment, dec_square, small)
    )[:3]
    encoder, enc_moment, enc_square = lax.optimization_barrier(
        (encoder, enc_moment, enc_square, small)
    )[:3]
    low_first = z < 2
    grad_dec_rows = jnp.concatenate(
        [
            jnp.where(low_first, near_grad, far_grad),
            jnp.where(low_first, far_grad, near_grad),
        ],
        axis=0,
    )
    grad_decoder = grad_dec_rows + decoder * (active_sum / norms) / rows

    new_decoder, new_dec_moment, new_dec_square = adam_update(
        decoder, grad_decoder, dec_moment, dec_square
    )
    new_enc_bias, new_bias_moment, new_bias_square = adam_update(
        enc_bias, grad_bias, bias_moment, bias_square
    )
    new_encoder, new_enc_moment, new_enc_square = adam_update(
        encoder, grad_encoder, enc_moment, enc_square
    )
    return (
        error,
        new_encoder,
        new_enc_bias,
        new_decoder,
        new_enc_moment,
        new_enc_square,
        new_bias_moment,
        new_bias_square,
        new_dec_moment,
        new_dec_square,
    )


def solution(mesh):
    in_specs = (
        P(("groups", "dp"), "latent"),
        P(("groups", "dp"), "latent"),
        P(("groups", "latent", "dp")),
        P(("groups", "dp"), "latent"),
        P(("groups", "dp"), "latent"),
        P(("groups", "dp"), "latent"),
        P(("groups", "latent", "dp")),
        P(("groups", "latent", "dp")),
        P(("groups", "dp"), "latent"),
        P(("groups", "dp"), "latent"),
    )
    out_specs = (
        P(("groups", "dp"), "latent"),
        P(("groups", "dp"), "latent"),
        P(("groups", "latent", "dp")),
        P(("groups", "dp"), "latent"),
        P(("groups", "dp"), "latent"),
        P(("groups", "dp"), "latent"),
        P(("groups", "latent", "dp")),
        P(("groups", "latent", "dp")),
        P(("groups", "dp"), "latent"),
        P(("groups", "dp"), "latent"),
    )
    line = mesh.shape["latent"] == 4 and mesh.shape["dp"] == 4
    plan = line_shards if line else shards
    return jax.shard_map(plan, mesh=mesh, in_specs=in_specs, out_specs=out_specs, check_vma=False)
```

```python
import functools

import jax
import jax.numpy as jnp
from jax import lax
from jax.experimental import pallas as pl
from jax.experimental.pallas import tpu as pltpu
from jax.sharding import PartitionSpec as P

ADAM_STEP = 1000


first_decay = 0.9
second_decay = 0.999
learn_rate = 0.001
epsilon = 1e-08

F32 = jnp.float32
BF16 = jnp.bfloat16


def adam_update(param, grad, moment, square):
    moment_new = first_decay * moment + (1.0 - first_decay) * grad
    square_new = second_decay * square + (1.0 - second_decay) * grad * grad
    first_fix = 1.0 - first_decay**ADAM_STEP
    second_fix = 1.0 - second_decay**ADAM_STEP
    param_new = param - learn_rate * (moment_new / first_fix) / (
        jnp.sqrt(square_new / second_fix) + epsilon
    )
    return (param_new, moment_new, square_new)


def shards(
    activations,
    encoder,
    enc_bias,
    decoder,
    enc_moment,
    enc_square,
    bias_moment,
    bias_square,
    dec_moment,
    dec_square,
):
    row_count = activations.shape[0] * lax.axis_size("dp")
    loss_scale = 2.0 / row_count
    inputs = lax.all_gather(activations, "latent", axis=1, tiled=True)
    enc_low, dec_low = (
        lax.all_gather(encoder.astype(jnp.bfloat16), "dp", axis=0, tiled=True),
        lax.all_gather(decoder.astype(jnp.bfloat16), "dp", axis=0, tiled=True),
    )
    bias_full = lax.all_gather(enc_bias, "dp", axis=0, tiled=True)
    square_sums = lax.psum(jnp.sum(decoder * decoder, axis=0), "dp")
    column_norms = jnp.sqrt(square_sums + 1e-06)
    preact = jnp.dot(inputs, enc_low, preferred_element_type=jnp.float32) + bias_full
    latent_codes = jnp.maximum(preact, 0.0).astype(jnp.bfloat16)
    partial_sums = lax.dot_general(
        latent_codes, dec_low, (((1,), (1,)), ((), ())), preferred_element_type=jnp.float32
    )
    rebuilt = lax.psum_scatter(partial_sums, "latent", scatter_dimension=1, tiled=True)
    error = (activations.astype(jnp.float32) - rebuilt).astype(jnp.bfloat16)
    full_error = lax.all_gather(error, "latent", axis=1, tiled=True)
    active_sum = lax.psum(jnp.sum(latent_codes.astype(jnp.float32), axis=0), "dp")
    grad_dec_rows = -loss_scale * lax.dot_general(
        full_error, latent_codes, (((0,), (0,)), ((), ())), preferred_element_type=jnp.float32
    )
    code_grad = (
        -loss_scale * jnp.dot(full_error, dec_low, preferred_element_type=jnp.float32)
        + column_norms / row_count
    )
    grad_preact = jnp.where(preact > 0.0, code_grad, 0.0)
    grad_encoder = lax.dot_general(
        inputs,
        grad_preact.astype(jnp.bfloat16),
        (((0,), (0,)), ((), ())),
        preferred_element_type=jnp.float32,
    )
    grad_bias = jnp.sum(grad_preact, axis=0)
    grad_encoder, grad_dec_rows, grad_bias = (
        lax.psum_scatter(grad_encoder, "dp", scatter_dimension=0, tiled=True),
        lax.psum_scatter(grad_dec_rows, "dp", scatter_dimension=0, tiled=True),
        lax.psum_scatter(grad_bias, "dp", scatter_dimension=0, tiled=True),
    )
    grad_decoder = grad_dec_rows + decoder * (active_sum / column_norms) / row_count
    new_encoder, new_enc_moment, new_enc_square = adam_update(
        encoder, grad_encoder, enc_moment, enc_square
    )
    new_enc_bias, new_bias_moment, new_bias_square = adam_update(
        enc_bias, grad_bias, bias_moment, bias_square
    )
    new_decoder, new_dec_moment, new_dec_square = adam_update(
        decoder, grad_decoder, dec_moment, dec_square
    )
    return (
        error,
        new_encoder,
        new_enc_bias,
        new_decoder,
        new_enc_moment,
        new_enc_square,
        new_bias_moment,
        new_bias_square,
        new_dec_moment,
        new_dec_square,
    )


VMEM = pl.BlockSpec(memory_space=pltpu.VMEM)
SMEM = pl.BlockSpec(memory_space=pltpu.SMEM)
ANY = pl.BlockSpec(memory_space=pl.ANY)
EXTRA = 16


def local_kernel(body, outs, place, *args, after=(), scratch=()):
    def run(place, *refs):
        body(place, *refs[: len(args)], *refs[len(args) + len(after) :])

    return pl.pallas_call(
        run,
        out_shape=outs,
        in_specs=[SMEM] + [VMEM] * len(args) + [ANY] * len(after),
        out_specs=[VMEM] * len(outs),
        scratch_shapes=scratch,
        compiler_params=pltpu.CompilerParams(vmem_limit_bytes=24 * 1024 * 1024),
        cost_estimate=pl.CostEstimate(flops=1, bytes_accessed=1, transcendentals=0),
    )(place, *args, *after)


def shape(dims, dtype):
    return jax.ShapeDtypeStruct(dims, dtype)


def columns(start, width):
    return pl.ds(pl.multiple_of(start, width), width)


def three_rows(row):
    high = row.astype(BF16).astype(F32)
    middle = (row - high).astype(BF16).astype(F32)
    low = row - high - middle
    at = lax.broadcasted_iota(jnp.int32, (EXTRA, row.shape[1]), 0)
    rows = jnp.where(at == 0, high, jnp.where(at == 1, middle, jnp.where(at == 2, low, 0.0)))
    return rows.astype(BF16)


def behind(value, *others):
    return lax.optimization_barrier((value, *others))[0]


def one_row(rows):
    return jnp.sum(rows.astype(F32), axis=0, keepdims=True)


def encoder_body(place, encoder, bias, out):
    depth = encoder.shape[0]
    out[:depth] = encoder[...].astype(BF16)
    out[depth:] = three_rows(jnp.concatenate([bias[...]] * 4, axis=1))


def decoder_body(place, decoder, out):
    depth = decoder.shape[0]
    value = decoder[...]
    out[:depth] = value.astype(BF16)
    out[depth:] = three_rows(jnp.sum(value * value, axis=0, keepdims=True))


def codes_body(
    place,
    own,
    low,
    high,
    across,
    relay1,
    relay2,
    enc0,
    enc1,
    enc2,
    enc3,
    codes,
    mask,
    full,
    active,
    bias,
):
    z, i = place[0], place[1]
    width = own.shape[1]
    for at, blocks in enumerate(
        (
            (own, high, relay1, relay2),
            (low, own, high, across),
            (across, low, own, high),
            (relay2, relay1, low, own),
        )
    ):

        @pl.when(z == at)
        def _(blocks=blocks):
            for b, block in enumerate(blocks):
                full[:, b * width : (b + 1) * width] = block[...]

    total = jnp.zeros(codes.shape, F32)
    piece = codes.shape[1] // 4
    for t, enc in enumerate((enc0, enc1, enc2, enc3)):
        b = i ^ t
        total += jnp.dot(
            full[:, columns(b * width, width)], enc[:width, :], preferred_element_type=F32
        )
        bias[:, columns(b * piece, piece)] = one_row(enc[width:, :piece])
    preact = total + bias[...]
    low_codes = jnp.maximum(preact, 0.0).astype(BF16)
    codes[...] = low_codes
    mask[...] = (preact > 0.0).astype(F32).astype(BF16)
    active[...] = jnp.sum(low_codes.astype(F32), axis=0, keepdims=True)


def onward_body(place, low, high, out):
    @pl.when(place[0] == 1)
    def _():
        out[...] = high[...]

    @pl.when(place[0] != 1)
    def _():
        out[...] = low[...]


def pieces_body(place, dec, up, down, across):
    z = place[0]
    half = up.shape[0]
    for out, second in ((up, z >= 1), (down, z >= 3), (across, z < 2)):
        out[...] = dec[pl.ds(pl.multiple_of(jnp.where(second, half, 0), half), half), :]


def turn_body(place, full, turned):
    turned[...] = full[...].T


def error_body(
    place, own, low, high, across, dec0, dec1, dec2, dec3, row0, row1, row2, row3, inputs, error
):
    z, i = place[0], place[1]
    half = row0.shape[0] // 3
    shift = pl.multiple_of(jnp.where(z >= 2, half, 0), half)
    for t in range(4):
        dec, row = (dec0, dec1, dec2, dec3)[t], (row0, row1, row2, row3)[t]
        lefts = (own, low, high, across)
        rights = [dec[pl.ds(shift, half), :]] + [row[m * half : (m + 1) * half, :] for m in range(3)]
        total = jnp.zeros((own.shape[0], half), F32)
        for left, right in zip(lefts, rights):
            total += lax.dot_general(
                left[...], right, (((1,), (1,)), ((), ())), preferred_element_type=F32
            )
        q = i ^ t
        given = inputs[:, columns(q * 2 * half + shift, half)].astype(F32)
        error[:, columns(q * half, half)] = (given - total).astype(BF16)


def pick(place, middle, end, out):
    z = place[0]
    is_middle = (z == 1) | (z == 2)

    @pl.when(is_middle)
    def _():
        out[...] = middle[...]

    @pl.when(jnp.logical_not(is_middle))
    def _():
        out[...] = end[...]


def decoder_grads(scale, i, error, codes, row, outs):
    half = error.shape[1] // 4
    for out, slot in zip(outs, (3, 1, 2, 0)):
        out[:half] = scale * lax.dot_general(
            error[:, columns((i ^ slot) * half, half)],
            codes[...],
            (((0,), (0,)), ((), ())),
            preferred_element_type=F32,
        )
    outs[0][half:] = jnp.broadcast_to(row[...], (outs[0].shape[0] - half, row.shape[1]))


def back_through(i, error, decs, shift):
    half = error.shape[1] // 4
    return functools.reduce(
        jnp.add,
        [
            jnp.dot(
                error[:, columns((i ^ t) * half, half)],
                dec[pl.ds(pl.multiple_of(shift, half), half), :],
                preferred_element_type=F32,
            )
            for t, dec in enumerate(decs)
        ],
    )


def near_body(rows, place, mine, passed, codes, active, dec0, dec1, dec2, dec3, part, near, *outs):
    z, i = place[0], place[1]
    half = mine.shape[1] // 4
    pick(place, mine, passed, near)
    decoder_grads(-2.0 / rows, i, near, codes, active, outs)
    part[...] = back_through(i, near, (dec0, dec1, dec2, dec3), jnp.where(z >= 2, half, 0))


def far_error_body(rows, place, swapped, direct, codes, active, far, *outs):
    pick(place, swapped, direct, far)
    decoder_grads(-2.0 / rows, place[1], far, codes, active, outs)


def far_code_body(
    rows, place, near, far, part, mask, dec0, dec1, dec2, dec3, grad_low, bias_sum, norms, home
):
    z, i = place[0], place[1]
    half = far.shape[1] // 4
    width = 2 * half
    decs = (dec0, dec1, dec2, dec3)
    shift = jnp.where(z >= 2, 0, half)
    total = part[...] + back_through(i, far, decs, shift)
    squares = functools.reduce(jnp.add, [one_row(dec[width:, :]) for dec in decs])
    column_norms = jnp.sqrt(squares + 1e-06)
    norms[...] = column_norms
    code_grad = (-2.0 / rows) * total + column_norms / rows
    grad = jnp.where(mask[...] > 0, code_grad, 0.0)
    grad_low[...] = grad.astype(BF16)
    bias_sum[...] = jnp.sum(grad, axis=0, keepdims=True)
    home[:, columns(half - shift, half)] = near[:, columns(z * half, half)]
    home[:, columns(shift, half)] = far[:, columns(z * half, half)]


def encoder_grad_body(place, turned, grad_low, row, send_far, send_near, keep_far, keep_near):
    i = place[1]
    width = turned.shape[0] // 4
    for slot, out in ((3, send_far), (1, send_near), (2, keep_far), (0, keep_near)):
        at = pl.ds(pl.multiple_of((i ^ slot) * width, width), width)
        out[:width] = jnp.dot(turned[at, :], grad_low[...], preferred_element_type=F32)
    send_far[width:] = jnp.broadcast_to(row[...], (send_far.shape[0] - width, row.shape[1]))


def far_body(place, kept, received, row, *refs):
    scaled, small = refs[-2:]
    width = scaled.shape[0]
    total = kept[...] + received[:width]
    largest = jnp.maximum(jnp.max(jnp.abs(total), axis=0, keepdims=True), 1e-30)
    scaled[...] = total * (16384.0 / largest)
    rows = received[width:] + row[...]
    at = lax.broadcasted_iota(jnp.int32, rows.shape, 0)
    small[:8] = jnp.where(at == 0, largest * (1.0 / 16384.0), rows)
    for other in refs[:-2]:
        small[8:] = other[...]


def decoder_step_body(
    rows, place, param, moment, square, near, far, active, norms, param_out, moment_out, square_out
):
    is_near = (pl.program_id(0) < pl.num_programs(0) // 2) == (place[0] < 2)
    grad = jnp.where(is_near, near[...], far[...])
    grad += param[...] * (active[...] / norms[...]) / rows
    param_out[...], moment_out[...], square_out[...] = adam_update(
        param[...], grad, moment[...], square[...]
    )


def line_shards(
    activations,
    encoder,
    enc_bias,
    decoder,
    enc_moment,
    enc_square,
    bias_moment,
    bias_square,
    dec_moment,
    dec_square,
):
    rows = activations.shape[0] * 4
    count, width = activations.shape
    latents = encoder.shape[1]
    half = width // 2
    features = 4 * width
    z, i = lax.axis_index("latent"), lax.axis_index("dp")
    place = jnp.stack([z, i]).astype(jnp.int32)

    def along(value, pairs):
        return lax.ppermute(value, "latent", pairs)

    def flip(value, bits, planes=(0, 1, 2, 3)):
        pairs = [(4 * p + k, 4 * p + (k ^ bits)) for p in planes for k in range(4)]
        return lax.ppermute(value, ("latent", "dp"), pairs)

    ends = [(1, 0), (2, 3)]
    low = along(activations, [(0, 1), (1, 2), (2, 3)])
    high = along(activations, [(1, 0), (2, 1), (3, 2)])
    across = along(activations, [(0, 2), (3, 1)])

    (enc_own,) = local_kernel(
        encoder_body,
        [shape((width + EXTRA, latents), BF16)],
        place,
        encoder,
        enc_bias.reshape(1, -1),
    )
    enc_chip, enc_core = flip(enc_own, 2), flip(enc_own, 1)
    (dec_own,) = local_kernel(
        decoder_body,
        [shape((width + EXTRA, latents), BF16)],
        place,
        decoder,
        after=(enc_core,),
    )
    dec_chip, dec_core = flip(behind(dec_own, enc_chip), 2), flip(dec_own, 1)
    (onward,) = local_kernel(
        onward_body, [shape((count, width), BF16)], place, low, high, after=(dec_core,)
    )
    relay1 = along(onward, ends)
    relay2 = along(across, ends)
    enc = [enc_own, enc_core, enc_chip, flip(behind(enc_chip, onward), 1)]

    up, down, beyond = local_kernel(
        pieces_body, [shape((half, latents), BF16)] * 3, place, dec_own, after=(onward,)
    )
    dec_pieces = [
        along(up, [(0, 1), (1, 2)]),
        along(down, [(2, 1), (3, 2)]),
        along(beyond, [(0, 2), (3, 1)]),
    ]
    dec = [dec_own, dec_core, dec_chip, flip(dec_chip, 1)]

    codes, mask, inputs, active = local_kernel(
        codes_body,
        [
            shape((count, latents), BF16),
            shape((count, latents), BF16),
            shape((count, features), BF16),
            shape((1, latents), F32),
        ],
        place,
        activations,
        low,
        high,
        across,
        relay1,
        relay2,
        *enc,
        scratch=[pltpu.VMEM((1, latents), F32)],
    )
    codes_low = along(codes, [(0, 1), (1, 2)])
    codes_high = along(codes, [(2, 1), (3, 2)])
    codes_across = along(codes, [(0, 2), (3, 1)])
    dec_pieces = [behind(piece, codes, dec_chip) for piece in dec_pieces]
    rows_own = jnp.concatenate(dec_pieces, axis=0)
    (turned,) = local_kernel(turn_body, [shape((features, count), BF16)], place, inputs)
    rows_chip = flip(rows_own, 2, (1, 2))
    rows_core = flip(behind(rows_own, turned), 1, (1, 2))
    rows_both = flip(
        behind(rows_chip, codes_low, codes_high, codes_across, dec[1], dec[3]), 1, (1, 2)
    )

    (own_error,) = local_kernel(
        error_body,
        [shape((count, features // 2), BF16)],
        place,
        codes,
        codes_low,
        codes_high,
        codes_across,
        *dec,
        rows_own,
        rows_core,
        rows_chip,
        rows_both,
        inputs,
    )
    swapped = along(own_error, [(1, 2), (2, 1)])
    passed = along(own_error, [(1, 0), (2, 3)])
    direct = along(own_error, [(2, 0), (1, 3)])

    def across_chips(scaled, small):
        return flip(scaled.astype(jnp.float16), 2), flip(small, 2)

    def decoder_half(send_far, send_near, keep_far, keep_near):
        scaled, small = local_kernel(
            far_body,
            [shape((half, latents), F32), shape((8, latents), F32)],
            place,
            keep_far,
            flip(send_far, 1),
            active,
        )
        return scaled, small, (keep_near, flip(send_near, 1))

    blocks = [shape((half + 8, latents), F32)] + [shape((half, latents), F32)] * 3
    part, near, *near_blocks = local_kernel(
        functools.partial(near_body, rows),
        [shape((count, latents), F32), shape((count, features // 2), BF16), *blocks],
        place,
        own_error,
        passed,
        codes,
        active,
        *dec,
        after=(swapped,),
    )
    near_scaled, near_small, near_kept = decoder_half(*near_blocks)
    far, *far_blocks = local_kernel(
        functools.partial(far_error_body, rows),
        [shape((count, features // 2), BF16), *blocks],
        place,
        swapped,
        direct,
        codes,
        active,
        after=(near_scaled,),
    )
    near_received = across_chips(near_scaled, behind(near_small, far))
    far_scaled, far_small, far_kept = decoder_half(*far_blocks)
    far_received = flip(far_scaled.astype(jnp.float16), 2)
    grad_low, bias_sum, norms, error = local_kernel(
        functools.partial(far_code_body, rows),
        [
            shape((count, latents), BF16),
            shape((1, latents), F32),
            shape((1, latents), F32),
            shape((count, width), BF16),
        ],
        place,
        near,
        far,
        behind(part, *near_received),
        mask,
        *dec,
    )
    send_far, send_near, keep_far, keep_near = local_kernel(
        encoder_grad_body,
        [shape((width + 8, latents), F32)] + [shape((width, latents), F32)] * 3,
        place,
        turned,
        grad_low,
        bias_sum,
    )
    scaled, small = local_kernel(
        far_body,
        [shape((width, latents), F32), shape((16, latents), F32)],
        place,
        keep_far,
        flip(send_far, 1),
        bias_sum,
        far_small,
    )
    enc_received, enc_small = across_chips(scaled, small)

    decoder, dec_moment, dec_square, encoder, enc_moment, enc_square = lax.optimization_barrier(
        (decoder, dec_moment, dec_square, encoder, enc_moment, enc_square, small)
    )[:6]

    def added(kept, received):
        return kept[0] + kept[1] + received[0].astype(F32) * received[1][:1]

    near_grad = added(near_kept, near_received)
    far_grad = added(far_kept, (far_received, enc_small[8:]))
    active_sum = near_small[1] + near_received[1][1]
    grad_encoder = added((keep_near, flip(send_near, 1)), (enc_received, enc_small))
    grad_bias = small[1] + enc_small[1]
    grad_bias = lax.dynamic_slice(grad_bias, (i * enc_bias.shape[0],), (enc_bias.shape[0],))
    step = width // 4
    block = pl.BlockSpec((step, latents), lambda r: (r, 0))
    in_half = pl.BlockSpec((step, latents), lambda r: (r % 2, 0))
    row = pl.BlockSpec((1, latents), lambda r: (0, 0))
    new_decoder, new_dec_moment, new_dec_square = pl.pallas_call(
        functools.partial(decoder_step_body, rows),
        grid=(4,),
        out_shape=[shape((width, latents), F32)] * 3,
        in_specs=[SMEM, block, block, block, in_half, in_half, row, row],
        out_specs=[block] * 3,
        compiler_params=pltpu.CompilerParams(vmem_limit_bytes=24 * 1024 * 1024),
        cost_estimate=pl.CostEstimate(flops=1, bytes_accessed=1, transcendentals=0),
    )(place, decoder, dec_moment, dec_square, near_grad, far_grad, active_sum[None], norms)
    new_enc_bias, new_bias_moment, new_bias_square = adam_update(
        enc_bias, grad_bias, bias_moment, bias_square
    )
    new_encoder, new_enc_moment, new_enc_square = adam_update(
        encoder, grad_encoder, enc_moment, enc_square
    )
    return (
        error,
        new_encoder,
        new_enc_bias,
        new_decoder,
        new_enc_moment,
        new_enc_square,
        new_bias_moment,
        new_bias_square,
        new_dec_moment,
        new_dec_square,
    )


def solution(mesh):
    in_specs = (
        P(("groups", "dp"), "latent"),
        P(("groups", "dp"), "latent"),
        P(("groups", "latent", "dp")),
        P(("groups", "dp"), "latent"),
        P(("groups", "dp"), "latent"),
        P(("groups", "dp"), "latent"),
        P(("groups", "latent", "dp")),
        P(("groups", "latent", "dp")),
        P(("groups", "dp"), "latent"),
        P(("groups", "dp"), "latent"),
    )
    out_specs = (
        P(("groups", "dp"), "latent"),
        P(("groups", "dp"), "latent"),
        P(("groups", "latent", "dp")),
        P(("groups", "dp"), "latent"),
        P(("groups", "dp"), "latent"),
        P(("groups", "dp"), "latent"),
        P(("groups", "latent", "dp")),
        P(("groups", "latent", "dp")),
        P(("groups", "dp"), "latent"),
        P(("groups", "dp"), "latent"),
    )
    line = mesh.shape["latent"] == 4 and mesh.shape["dp"] == 4
    plan = line_shards if line else shards
    return jax.shard_map(plan, mesh=mesh, in_specs=in_specs, out_specs=out_specs, check_vma=False)
```

```python
import functools

import jax
import jax.numpy as jnp
from jax import lax
from jax.experimental import pallas as pl
from jax.experimental.pallas import tpu as pltpu
from jax.sharding import PartitionSpec as P

ADAM_STEP = 1000


first_decay = 0.9
second_decay = 0.999
learn_rate = 0.001
epsilon = 1e-08

F32 = jnp.float32
BF16 = jnp.bfloat16


def adam_update(param, grad, moment, square):
    moment_new = first_decay * moment + (1.0 - first_decay) * grad
    square_new = second_decay * square + (1.0 - second_decay) * grad * grad
    first_fix = 1.0 - first_decay**ADAM_STEP
    second_fix = 1.0 - second_decay**ADAM_STEP
    param_new = param - learn_rate * (moment_new / first_fix) / (
        jnp.sqrt(square_new / second_fix) + epsilon
    )
    return (param_new, moment_new, square_new)


def shards(
    activations,
    encoder,
    enc_bias,
    decoder,
    enc_moment,
    enc_square,
    bias_moment,
    bias_square,
    dec_moment,
    dec_square,
):
    row_count = activations.shape[0] * lax.axis_size("dp")
    loss_scale = 2.0 / row_count
    inputs = lax.all_gather(activations, "latent", axis=1, tiled=True)
    enc_low, dec_low = (
        lax.all_gather(encoder.astype(jnp.bfloat16), "dp", axis=0, tiled=True),
        lax.all_gather(decoder.astype(jnp.bfloat16), "dp", axis=0, tiled=True),
    )
    bias_full = lax.all_gather(enc_bias, "dp", axis=0, tiled=True)
    square_sums = lax.psum(jnp.sum(decoder * decoder, axis=0), "dp")
    column_norms = jnp.sqrt(square_sums + 1e-06)
    preact = jnp.dot(inputs, enc_low, preferred_element_type=jnp.float32) + bias_full
    latent_codes = jnp.maximum(preact, 0.0).astype(jnp.bfloat16)
    partial_sums = lax.dot_general(
        latent_codes, dec_low, (((1,), (1,)), ((), ())), preferred_element_type=jnp.float32
    )
    rebuilt = lax.psum_scatter(partial_sums, "latent", scatter_dimension=1, tiled=True)
    error = (activations.astype(jnp.float32) - rebuilt).astype(jnp.bfloat16)
    full_error = lax.all_gather(error, "latent", axis=1, tiled=True)
    active_sum = lax.psum(jnp.sum(latent_codes.astype(jnp.float32), axis=0), "dp")
    grad_dec_rows = -loss_scale * lax.dot_general(
        full_error, latent_codes, (((0,), (0,)), ((), ())), preferred_element_type=jnp.float32
    )
    code_grad = (
        -loss_scale * jnp.dot(full_error, dec_low, preferred_element_type=jnp.float32)
        + column_norms / row_count
    )
    grad_preact = jnp.where(preact > 0.0, code_grad, 0.0)
    grad_encoder = lax.dot_general(
        inputs,
        grad_preact.astype(jnp.bfloat16),
        (((0,), (0,)), ((), ())),
        preferred_element_type=jnp.float32,
    )
    grad_bias = jnp.sum(grad_preact, axis=0)
    grad_encoder, grad_dec_rows, grad_bias = (
        lax.psum_scatter(grad_encoder, "dp", scatter_dimension=0, tiled=True),
        lax.psum_scatter(grad_dec_rows, "dp", scatter_dimension=0, tiled=True),
        lax.psum_scatter(grad_bias, "dp", scatter_dimension=0, tiled=True),
    )
    grad_decoder = grad_dec_rows + decoder * (active_sum / column_norms) / row_count
    new_encoder, new_enc_moment, new_enc_square = adam_update(
        encoder, grad_encoder, enc_moment, enc_square
    )
    new_enc_bias, new_bias_moment, new_bias_square = adam_update(
        enc_bias, grad_bias, bias_moment, bias_square
    )
    new_decoder, new_dec_moment, new_dec_square = adam_update(
        decoder, grad_decoder, dec_moment, dec_square
    )
    return (
        error,
        new_encoder,
        new_enc_bias,
        new_decoder,
        new_enc_moment,
        new_enc_square,
        new_bias_moment,
        new_bias_square,
        new_dec_moment,
        new_dec_square,
    )


VMEM = pl.BlockSpec(memory_space=pltpu.VMEM)
SMEM = pl.BlockSpec(memory_space=pltpu.SMEM)
ANY = pl.BlockSpec(memory_space=pl.ANY)
EXTRA = 16


def local_kernel(body, outs, place, *args, after=(), scratch=()):
    def run(place, *refs):
        body(place, *refs[: len(args)], *refs[len(args) + len(after) :])

    held = sum(a.size * jnp.dtype(a.dtype).itemsize for a in (*args, *outs))
    return pl.pallas_call(
        run,
        out_shape=outs,
        in_specs=[SMEM] + [VMEM] * len(args) + [ANY] * len(after),
        out_specs=[VMEM] * len(outs),
        scratch_shapes=scratch,
        compiler_params=pltpu.CompilerParams(vmem_limit_bytes=held + 6 * 1024 * 1024),
        cost_estimate=pl.CostEstimate(flops=1, bytes_accessed=1, transcendentals=0),
    )(place, *args, *after)


def shape(dims, dtype):
    return jax.ShapeDtypeStruct(dims, dtype)


def columns(start, width):
    return pl.ds(pl.multiple_of(start, width), width)


def three_rows(row):
    high = row.astype(BF16).astype(F32)
    middle = (row - high).astype(BF16).astype(F32)
    low = row - high - middle
    at = lax.broadcasted_iota(jnp.int32, (EXTRA, row.shape[1]), 0)
    rows = jnp.where(at == 0, high, jnp.where(at == 1, middle, jnp.where(at == 2, low, 0.0)))
    return rows.astype(BF16)


def behind(value, *others):
    return lax.optimization_barrier((value, *others))[0]


def one_row(rows):
    return jnp.sum(rows.astype(F32), axis=0, keepdims=True)


def encoder_body(place, encoder, bias, out):
    depth = encoder.shape[0]
    out[:depth] = encoder[...].astype(BF16)
    out[depth:] = three_rows(jnp.concatenate([bias[...]] * 4, axis=1))


def decoder_body(place, decoder, out):
    depth = decoder.shape[0]
    value = decoder[...]
    out[:depth] = value.astype(BF16)
    out[depth:] = three_rows(jnp.sum(value * value, axis=0, keepdims=True))


def codes_body(
    place,
    own,
    low,
    high,
    across,
    relay1,
    relay2,
    enc0,
    enc1,
    enc2,
    enc3,
    codes,
    mask,
    full,
    active,
    bias,
):
    z, i = place[0], place[1]
    width = own.shape[1]
    for at, blocks in enumerate(
        (
            (own, high, relay1, relay2),
            (low, own, high, across),
            (across, low, own, high),
            (relay2, relay1, low, own),
        )
    ):

        @pl.when(z == at)
        def _(blocks=blocks):
            for b, block in enumerate(blocks):
                full[:, b * width : (b + 1) * width] = block[...]

    total = jnp.zeros(codes.shape, F32)
    piece = codes.shape[1] // 4
    for t, enc in enumerate((enc0, enc1, enc2, enc3)):
        b = i ^ t
        total += jnp.dot(
            full[:, columns(b * width, width)], enc[:width, :], preferred_element_type=F32
        )
        bias[:, columns(b * piece, piece)] = one_row(enc[width:, :piece])
    preact = total + bias[...]
    low_codes = jnp.maximum(preact, 0.0).astype(BF16)
    codes[...] = low_codes
    mask[...] = (preact > 0.0).astype(F32).astype(BF16)
    active[...] = jnp.sum(low_codes.astype(F32), axis=0, keepdims=True)


def onward_body(place, low, high, out):
    @pl.when(place[0] == 1)
    def _():
        out[...] = high[...]

    @pl.when(place[0] != 1)
    def _():
        out[...] = low[...]


def pieces_body(place, dec, up, down, across):
    z = place[0]
    half = up.shape[0]
    for out, second in ((up, z >= 1), (down, z >= 3), (across, z < 2)):
        out[...] = dec[pl.ds(pl.multiple_of(jnp.where(second, half, 0), half), half), :]


def turn_body(place, full, turned):
    turned[...] = full[...].T


def error_body(
    place, own, low, high, across, dec0, dec1, dec2, dec3, row0, row1, row2, row3, inputs, error
):
    z, i = place[0], place[1]
    half = row0.shape[0] // 3
    shift = pl.multiple_of(jnp.where(z >= 2, half, 0), half)
    for t in range(4):
        dec, row = (dec0, dec1, dec2, dec3)[t], (row0, row1, row2, row3)[t]
        lefts = (own, low, high, across)
        rights = [dec[pl.ds(shift, half), :]] + [row[m * half : (m + 1) * half, :] for m in range(3)]
        total = jnp.zeros((own.shape[0], half), F32)
        for left, right in zip(lefts, rights):
            total += lax.dot_general(
                left[...], right, (((1,), (1,)), ((), ())), preferred_element_type=F32
            )
        q = i ^ t
        given = inputs[:, columns(q * 2 * half + shift, half)].astype(F32)
        error[:, columns(q * half, half)] = (given - total).astype(BF16)


def pick(place, middle, end, out):
    z = place[0]
    is_middle = (z == 1) | (z == 2)

    @pl.when(is_middle)
    def _():
        out[...] = middle[...]

    @pl.when(jnp.logical_not(is_middle))
    def _():
        out[...] = end[...]


def decoder_grads(scale, i, error, codes, outs):
    half = error.shape[1] // 4
    for out, slot in zip(outs, (3, 1, 2, 0)):
        out[:half] = scale * lax.dot_general(
            error[:, columns((i ^ slot) * half, half)],
            codes[...],
            (((0,), (0,)), ((), ())),
            preferred_element_type=F32,
        )


def back_through(i, error, decs, shift):
    half = error.shape[1] // 4
    return functools.reduce(
        jnp.add,
        [
            jnp.dot(
                error[:, columns((i ^ t) * half, half)],
                dec[pl.ds(pl.multiple_of(shift, half), half), :],
                preferred_element_type=F32,
            )
            for t, dec in enumerate(decs)
        ],
    )


def near_body(rows, place, mine, passed, codes, active, dec0, dec1, dec2, dec3, part, near, *outs):
    z, i = place[0], place[1]
    half = mine.shape[1] // 4
    pick(place, mine, passed, near)
    decoder_grads(-2.0 / rows, i, near, codes, outs)
    outs[0][half:] = jnp.broadcast_to(active[...], (outs[0].shape[0] - half, active.shape[1]))
    part[...] = back_through(i, near, (dec0, dec1, dec2, dec3), jnp.where(z >= 2, half, 0))


def code_grad_body(
    rows,
    place,
    swapped,
    direct,
    part,
    mask,
    dec0,
    dec1,
    dec2,
    dec3,
    turned,
    far,
    grad_low,
    bias_sum,
    norms,
    send_far,
):
    z, i = place[0], place[1]
    half = far.shape[1] // 4
    width = 2 * half
    decs = (dec0, dec1, dec2, dec3)
    pick(place, swapped, direct, far)
    total = part[...] + back_through(i, far, decs, jnp.where(z >= 2, 0, half))
    squares = functools.reduce(jnp.add, [one_row(dec[width:, :]) for dec in decs])
    column_norms = jnp.sqrt(squares + 1e-06)
    norms[...] = column_norms
    code_grad = (-2.0 / rows) * total + column_norms / rows
    grad = jnp.where(mask[...] > 0, code_grad, 0.0)
    grad_low[...] = grad.astype(BF16)
    row = jnp.sum(grad, axis=0, keepdims=True)
    bias_sum[...] = row
    encoder_grads(i, turned, grad_low, (3,), (send_far,))
    send_far[width:] = jnp.broadcast_to(row, (send_far.shape[0] - width, row.shape[1]))


def encoder_grads(i, turned, grad_low, slots, outs):
    width = turned.shape[0] // 4
    for slot, out in zip(slots, outs):
        at = pl.ds(pl.multiple_of((i ^ slot) * width, width), width)
        out[:width] = jnp.dot(turned[at, :], grad_low[...], preferred_element_type=F32)


def rest_body(rows, place, turned, grad_low, near, far, codes, home, send, kept_far, kept, *outs):
    z, i = place[0], place[1]
    half = far.shape[1] // 4
    shift = jnp.where(z >= 2, 0, half)
    encoder_grads(i, turned, grad_low, (2, 1, 0), (kept_far, send, kept))
    decoder_grads(-2.0 / rows, i, far, codes, outs)
    home[:, columns(half - shift, half)] = near[:, columns(z * half, half)]
    home[:, columns(shift, half)] = far[:, columns(z * half, half)]


def far_body(place, kept, received, row, *refs):
    scaled, small = refs[-2:]
    width = scaled.shape[0]
    total = kept[...] + received[:width]
    largest = jnp.maximum(jnp.max(jnp.abs(total), axis=0, keepdims=True), 1e-30)
    scaled[...] = total * (16384.0 / largest)
    rows = jnp.broadcast_to(row[...], (8, row.shape[1]))
    if received.shape[0] > width:
        rows += received[width:]
    at = lax.broadcasted_iota(jnp.int32, rows.shape, 0)
    small[:8] = jnp.where(at == 0, largest * (1.0 / 16384.0), rows)
    for other in refs[:-2]:
        small[8:] = other[...]


def decoder_step_body(
    rows, place, param, moment, square, near, far, active, norms, param_out, moment_out, square_out
):
    is_near = (pl.program_id(0) < pl.num_programs(0) // 2) == (place[0] < 2)
    grad = jnp.where(is_near, near[...], far[...])
    grad += param[...] * (active[...] / norms[...]) / rows
    param_out[...], moment_out[...], square_out[...] = adam_update(
        param[...], grad, moment[...], square[...]
    )


def line_shards(
    activations,
    encoder,
    enc_bias,
    decoder,
    enc_moment,
    enc_square,
    bias_moment,
    bias_square,
    dec_moment,
    dec_square,
):
    rows = activations.shape[0] * 4
    count, width = activations.shape
    latents = encoder.shape[1]
    half = width // 2
    features = 4 * width
    z, i = lax.axis_index("latent"), lax.axis_index("dp")
    place = jnp.stack([z, i]).astype(jnp.int32)

    def along(value, pairs):
        return lax.ppermute(value, "latent", pairs)

    def flip(value, bits, planes=(0, 1, 2, 3)):
        pairs = [(4 * p + k, 4 * p + (k ^ bits)) for p in planes for k in range(4)]
        return lax.ppermute(value, ("latent", "dp"), pairs)

    ends = [(1, 0), (2, 3)]
    low = along(activations, [(0, 1), (1, 2), (2, 3)])
    high = along(activations, [(1, 0), (2, 1), (3, 2)])
    across = along(activations, [(0, 2), (3, 1)])

    (enc_own,) = local_kernel(
        encoder_body,
        [shape((width + EXTRA, latents), BF16)],
        place,
        encoder,
        enc_bias.reshape(1, -1),
    )
    enc_chip, enc_core = flip(enc_own, 2), flip(enc_own, 1)
    (dec_own,) = local_kernel(
        decoder_body,
        [shape((width + EXTRA, latents), BF16)],
        place,
        decoder,
        after=(enc_core,),
    )
    dec_chip, dec_core = flip(dec_own, 2), flip(dec_own, 1)
    (onward,) = local_kernel(
        onward_body, [shape((count, width), BF16)], place, low, high
    )
    relay1 = along(onward, ends)
    relay2 = along(across, ends)
    enc = [enc_own, enc_core, enc_chip, flip(behind(enc_chip, relay1), 1)]

    up, down, beyond = local_kernel(
        pieces_body, [shape((half, latents), BF16)] * 3, place, dec_own
    )
    dec_pieces = [
        along(up, [(0, 1), (1, 2)]),
        along(down, [(2, 1), (3, 2)]),
        along(beyond, [(0, 2), (3, 1)]),
    ]
    dec = [dec_own, dec_core, dec_chip, flip(dec_chip, 1)]

    rows_own = jnp.concatenate([behind(piece, dec_chip) for piece in dec_pieces], axis=0)
    codes, mask, inputs, active = local_kernel(
        codes_body,
        [
            shape((count, latents), BF16),
            shape((count, latents), BF16),
            shape((count, features), BF16),
            shape((1, latents), F32),
        ],
        place,
        activations,
        low,
        high,
        across,
        relay1,
        relay2,
        *enc,
        after=(rows_own,),
        scratch=[pltpu.VMEM((1, latents), F32)],
    )
    codes_low = along(codes, [(0, 1), (1, 2)])
    codes_high = along(codes, [(2, 1), (3, 2)])
    codes_across = along(codes, [(0, 2), (3, 1)])
    (turned,) = local_kernel(turn_body, [shape((features, count), BF16)], place, inputs)
    rows_chip = flip(rows_own, 2, (1, 2))
    rows_core = flip(behind(rows_own, turned), 1, (1, 2))
    rows_both = flip(
        behind(rows_chip, codes_low, codes_high, codes_across, dec[1], dec[3]), 1, (1, 2)
    )

    (own_error,) = local_kernel(
        error_body,
        [shape((count, features // 2), BF16)],
        place,
        codes,
        codes_low,
        codes_high,
        codes_across,
        *dec,
        rows_own,
        rows_core,
        rows_chip,
        rows_both,
        inputs,
    )
    swapped = along(own_error, [(1, 2), (2, 1)])
    passed = along(own_error, [(1, 0), (2, 3)])
    direct = along(own_error, [(2, 0), (1, 3)])

    def decoder_half(send_far, send_near, keep_far, keep_near, *others, after=()):
        scaled, small = local_kernel(
            far_body,
            [shape((half, latents), F32), shape((8 + 8 * len(others), latents), F32)],
            place,
            keep_far,
            flip(send_far, 1),
            active,
            *others,
            after=after,
        )
        return scaled, small, (keep_near, flip(send_near, 1))

    blocks = [shape((half + 8, latents), F32)] + [shape((half, latents), F32)] * 3
    part, near, *near_blocks = local_kernel(
        functools.partial(near_body, rows),
        [shape((count, latents), F32), shape((count, features // 2), BF16), *blocks],
        place,
        own_error,
        passed,
        codes,
        active,
        *dec,
        after=(swapped,),
    )
    near_scaled, near_small, near_kept = decoder_half(*near_blocks)
    near_received = flip(near_scaled.astype(jnp.float16), 2)
    far, grad_low, bias_sum, norms, send_far = local_kernel(
        functools.partial(code_grad_body, rows),
        [
            shape((count, features // 2), BF16),
            shape((count, latents), BF16),
            shape((1, latents), F32),
            shape((1, latents), F32),
            shape((width + 8, latents), F32),
        ],
        place,
        swapped,
        direct,
        behind(part, near_received),
        mask,
        *dec,
        turned,
    )
    error, send_near, keep_far, keep_near, *far_blocks = local_kernel(
        functools.partial(rest_body, rows),
        [shape((count, width), BF16)]
        + [shape((width, latents), F32)] * 3
        + [shape((half, latents), F32)] * 4,
        place,
        turned,
        grad_low,
        near,
        far,
        codes,
    )
    near_small_received = flip(behind(near_small, far), 2)
    scaled, small = local_kernel(
        far_body,
        [shape((width, latents), F32), shape((8, latents), F32)],
        place,
        keep_far,
        flip(send_far, 1),
        bias_sum,
    )
    enc_received = flip(scaled.astype(jnp.float16), 2)
    far_scaled, small, far_kept = decoder_half(*far_blocks, small, after=(scaled,))
    far_received = flip(far_scaled.astype(jnp.float16), 2)
    small_received = behind(flip(small, 2), enc_received)

    decoder, dec_moment, dec_square, encoder, enc_moment, enc_square = lax.optimization_barrier(
        (decoder, dec_moment, dec_square, encoder, enc_moment, enc_square, small)
    )[:6]

    def added(kept, received, scale):
        return kept[0] + kept[1] + received.astype(F32) * scale

    near_received, near_small_received = lax.optimization_barrier(
        (near_received, near_small_received, enc_received)
    )[:2]
    near_grad = added(near_kept, near_received, near_small_received[:1])
    active_sum = near_small[1] + near_small_received[1]
    grad_encoder = added((keep_near, flip(send_near, 1)), enc_received, small_received[8:9])
    grad_bias = small[9] + small_received[9]
    grad_bias = lax.dynamic_slice(grad_bias, (i * enc_bias.shape[0],), (enc_bias.shape[0],))
    new_enc_bias, new_bias_moment, new_bias_square = adam_update(
        enc_bias, grad_bias, bias_moment, bias_square
    )
    new_encoder, new_enc_moment, new_enc_square = adam_update(
        encoder, grad_encoder, enc_moment, enc_square
    )
    far_received, new_encoder, near_grad = lax.optimization_barrier(
        (far_received, new_encoder, near_grad)
    )
    far_grad = added(far_kept, far_received, small_received[:1])
    step = width // 4
    block = pl.BlockSpec((step, latents), lambda r: (r, 0))
    in_half = pl.BlockSpec((step, latents), lambda r: (r % 2, 0))
    row = pl.BlockSpec((1, latents), lambda r: (0, 0))
    new_decoder, new_dec_moment, new_dec_square = pl.pallas_call(
        functools.partial(decoder_step_body, rows),
        grid=(4,),
        out_shape=[shape((width, latents), F32)] * 3,
        in_specs=[SMEM, block, block, block, in_half, in_half, row, row],
        out_specs=[block] * 3,
        compiler_params=pltpu.CompilerParams(vmem_limit_bytes=12 * 1024 * 1024),
        cost_estimate=pl.CostEstimate(flops=1, bytes_accessed=1, transcendentals=0),
    )(place, decoder, dec_moment, dec_square, near_grad, far_grad, active_sum[None], norms)
    return (
        error,
        new_encoder,
        new_enc_bias,
        new_decoder,
        new_enc_moment,
        new_enc_square,
        new_bias_moment,
        new_bias_square,
        new_dec_moment,
        new_dec_square,
    )


def solution(mesh):
    in_specs = (
        P(("groups", "dp"), "latent"),
        P(("groups", "dp"), "latent"),
        P(("groups", "latent", "dp")),
        P(("groups", "dp"), "latent"),
        P(("groups", "dp"), "latent"),
        P(("groups", "dp"), "latent"),
        P(("groups", "latent", "dp")),
        P(("groups", "latent", "dp")),
        P(("groups", "dp"), "latent"),
        P(("groups", "dp"), "latent"),
    )
    out_specs = (
        P(("groups", "dp"), "latent"),
        P(("groups", "dp"), "latent"),
        P(("groups", "latent", "dp")),
        P(("groups", "dp"), "latent"),
        P(("groups", "dp"), "latent"),
        P(("groups", "dp"), "latent"),
        P(("groups", "latent", "dp")),
        P(("groups", "latent", "dp")),
        P(("groups", "dp"), "latent"),
        P(("groups", "dp"), "latent"),
    )
    line = mesh.shape["latent"] == 4 and mesh.shape["dp"] == 4
    plan = line_shards if line else shards
    return jax.shard_map(plan, mesh=mesh, in_specs=in_specs, out_specs=out_specs, check_vma=False)
```

```python
import functools
import math

import jax
import jax.numpy as jnp
from jax import lax
from jax.experimental import pallas as pl
from jax.experimental.pallas import tpu as pltpu
from jax.sharding import PartitionSpec as P

ADAM_STEP = 1000


first_decay = 0.9
second_decay = 0.999
learn_rate = 0.001
epsilon = 1e-08

F32 = jnp.float32
BF16 = jnp.bfloat16


def adam_update(param, grad, moment, square):
    moment_new = first_decay * moment + (1.0 - first_decay) * grad
    square_new = second_decay * square + (1.0 - second_decay) * grad * grad
    first_fix = 1.0 - first_decay**ADAM_STEP
    second_fix = 1.0 - second_decay**ADAM_STEP
    param_new = param - learn_rate * (moment_new / first_fix) / (
        jnp.sqrt(square_new / second_fix) + epsilon
    )
    return (param_new, moment_new, square_new)


def shards(
    activations,
    encoder,
    enc_bias,
    decoder,
    enc_moment,
    enc_square,
    bias_moment,
    bias_square,
    dec_moment,
    dec_square,
):
    row_count = activations.shape[0] * lax.axis_size("dp")
    loss_scale = 2.0 / row_count
    inputs = lax.all_gather(activations, "latent", axis=1, tiled=True)
    enc_low, dec_low = (
        lax.all_gather(encoder.astype(jnp.bfloat16), "dp", axis=0, tiled=True),
        lax.all_gather(decoder.astype(jnp.bfloat16), "dp", axis=0, tiled=True),
    )
    bias_full = lax.all_gather(enc_bias, "dp", axis=0, tiled=True)
    square_sums = lax.psum(jnp.sum(decoder * decoder, axis=0), "dp")
    column_norms = jnp.sqrt(square_sums + 1e-06)
    preact = jnp.dot(inputs, enc_low, preferred_element_type=jnp.float32) + bias_full
    latent_codes = jnp.maximum(preact, 0.0).astype(jnp.bfloat16)
    partial_sums = lax.dot_general(
        latent_codes, dec_low, (((1,), (1,)), ((), ())), preferred_element_type=jnp.float32
    )
    rebuilt = lax.psum_scatter(partial_sums, "latent", scatter_dimension=1, tiled=True)
    error = (activations.astype(jnp.float32) - rebuilt).astype(jnp.bfloat16)
    full_error = lax.all_gather(error, "latent", axis=1, tiled=True)
    active_sum = lax.psum(jnp.sum(latent_codes.astype(jnp.float32), axis=0), "dp")
    grad_dec_rows = -loss_scale * lax.dot_general(
        full_error, latent_codes, (((0,), (0,)), ((), ())), preferred_element_type=jnp.float32
    )
    code_grad = (
        -loss_scale * jnp.dot(full_error, dec_low, preferred_element_type=jnp.float32)
        + column_norms / row_count
    )
    grad_preact = jnp.where(preact > 0.0, code_grad, 0.0)
    grad_encoder = lax.dot_general(
        inputs,
        grad_preact.astype(jnp.bfloat16),
        (((0,), (0,)), ((), ())),
        preferred_element_type=jnp.float32,
    )
    grad_bias = jnp.sum(grad_preact, axis=0)
    grad_encoder, grad_dec_rows, grad_bias = (
        lax.psum_scatter(grad_encoder, "dp", scatter_dimension=0, tiled=True),
        lax.psum_scatter(grad_dec_rows, "dp", scatter_dimension=0, tiled=True),
        lax.psum_scatter(grad_bias, "dp", scatter_dimension=0, tiled=True),
    )
    grad_decoder = grad_dec_rows + decoder * (active_sum / column_norms) / row_count
    new_encoder, new_enc_moment, new_enc_square = adam_update(
        encoder, grad_encoder, enc_moment, enc_square
    )
    new_enc_bias, new_bias_moment, new_bias_square = adam_update(
        enc_bias, grad_bias, bias_moment, bias_square
    )
    new_decoder, new_dec_moment, new_dec_square = adam_update(
        decoder, grad_decoder, dec_moment, dec_square
    )
    return (
        error,
        new_encoder,
        new_enc_bias,
        new_decoder,
        new_enc_moment,
        new_enc_square,
        new_bias_moment,
        new_bias_square,
        new_dec_moment,
        new_dec_square,
    )


VMEM = pl.BlockSpec(memory_space=pltpu.VMEM)
SMEM = pl.BlockSpec(memory_space=pltpu.SMEM)
ANY = pl.BlockSpec(memory_space=pl.ANY)
EXTRA = 16
NOTABLE = 10**10


def local_kernel(body, outs, place, *args, after=(), scratch=(), cost=1):
    def run(place, *refs):
        body(place, *refs[: len(args)], *refs[len(args) + len(after) :])

    held = sum(a.size * jnp.dtype(a.dtype).itemsize for a in (*args, *outs))
    return pl.pallas_call(
        run,
        out_shape=outs,
        in_specs=[SMEM] + [VMEM] * len(args) + [ANY] * len(after),
        out_specs=[VMEM] * len(outs),
        scratch_shapes=scratch,
        compiler_params=pltpu.CompilerParams(vmem_limit_bytes=held + 6 * 1024 * 1024),
        cost_estimate=pl.CostEstimate(flops=cost, bytes_accessed=1, transcendentals=0),
    )(place, *args, *after)


def shape(dims, dtype):
    return jax.ShapeDtypeStruct(dims, dtype)


def columns(start, width):
    return pl.ds(pl.multiple_of(start, width), width)


def three_rows(row):
    high = row.astype(BF16).astype(F32)
    middle = (row - high).astype(BF16).astype(F32)
    low = row - high - middle
    at = lax.broadcasted_iota(jnp.int32, (EXTRA, row.shape[1]), 0)
    rows = jnp.where(at == 0, high, jnp.where(at == 1, middle, jnp.where(at == 2, low, 0.0)))
    return rows.astype(BF16)


def behind(value, *others):
    return lax.optimization_barrier((value, *others))[0]


def one_row(rows):
    return jnp.sum(rows.astype(F32), axis=0, keepdims=True)


def encoder_body(place, encoder, bias, out):
    depth = encoder.shape[0]
    out[:depth] = encoder[...].astype(BF16)
    out[depth:] = three_rows(jnp.concatenate([bias[...]] * 4, axis=1))


def decoder_body(place, decoder, out):
    depth = decoder.shape[0]
    value = decoder[...]
    out[:depth] = value.astype(BF16)
    out[depth:] = three_rows(jnp.sum(value * value, axis=0, keepdims=True))


def codes_body(
    place,
    own,
    low,
    high,
    across,
    relay1,
    relay2,
    enc0,
    enc1,
    enc2,
    enc3,
    codes,
    mask,
    full,
    active,
    bias,
):
    z, i = place[0], place[1]
    width = own.shape[1]
    for at, blocks in enumerate(
        (
            (own, high, relay1, relay2),
            (low, own, high, across),
            (across, low, own, high),
            (relay2, relay1, low, own),
        )
    ):

        @pl.when(z == at)
        def _(blocks=blocks):
            for b, block in enumerate(blocks):
                full[:, b * width : (b + 1) * width] = block[...]

    total = jnp.zeros(codes.shape, F32)
    piece = codes.shape[1] // 4
    for t, enc in enumerate((enc0, enc1, enc2, enc3)):
        b = i ^ t
        total += jnp.dot(
            full[:, columns(b * width, width)], enc[:width, :], preferred_element_type=F32
        )
        bias[:, columns(b * piece, piece)] = one_row(enc[width:, :piece])
    preact = total + bias[...]
    low_codes = jnp.maximum(preact, 0.0).astype(BF16)
    codes[...] = low_codes
    mask[...] = (preact > 0.0).astype(F32).astype(BF16)
    active[...] = jnp.sum(low_codes.astype(F32), axis=0, keepdims=True)


def onward_body(place, low, high, out):
    @pl.when(place[0] == 1)
    def _():
        out[...] = high[...]

    @pl.when(place[0] != 1)
    def _():
        out[...] = low[...]


def pieces_body(place, dec, up, down, across):
    z = place[0]
    half = up.shape[0]
    for out, second in ((up, z >= 1), (down, z >= 3), (across, z < 2)):
        out[...] = dec[pl.ds(pl.multiple_of(jnp.where(second, half, 0), half), half), :]


def turn_body(place, full, turned):
    turned[...] = full[...].T


def error_body(
    place, own, low, high, across, dec0, dec1, dec2, dec3, row0, row1, row2, row3, inputs, error
):
    z, i = place[0], place[1]
    half = row0.shape[0] // 3
    shift = pl.multiple_of(jnp.where(z >= 2, half, 0), half)
    for t in range(4):
        dec, row = (dec0, dec1, dec2, dec3)[t], (row0, row1, row2, row3)[t]
        lefts = (own, low, high, across)
        rights = [dec[pl.ds(shift, half), :]] + [row[m * half : (m + 1) * half, :] for m in range(3)]
        total = jnp.zeros((own.shape[0], half), F32)
        for left, right in zip(lefts, rights):
            total += lax.dot_general(
                left[...], right, (((1,), (1,)), ((), ())), preferred_element_type=F32
            )
        q = i ^ t
        given = inputs[:, columns(q * 2 * half + shift, half)].astype(F32)
        error[:, columns(q * half, half)] = (given - total).astype(BF16)


def pick(place, middle, end, out):
    z = place[0]
    is_middle = (z == 1) | (z == 2)

    @pl.when(is_middle)
    def _():
        out[...] = middle[...]

    @pl.when(jnp.logical_not(is_middle))
    def _():
        out[...] = end[...]


def decoder_grads(scale, i, error, codes, slots, outs):
    half = error.shape[1] // 4
    for slot, out in zip(slots, outs):
        out[:half] = scale * lax.dot_general(
            error[:, columns((i ^ slot) * half, half)],
            codes[...],
            (((0,), (0,)), ((), ())),
            preferred_element_type=F32,
        )


def back_through(i, error, decs, shift):
    half = error.shape[1] // 4
    return functools.reduce(
        jnp.add,
        [
            jnp.dot(
                error[:, columns((i ^ t) * half, half)],
                dec[pl.ds(pl.multiple_of(shift, half), half), :],
                preferred_element_type=F32,
            )
            for t, dec in enumerate(decs)
        ],
    )


def near_body(rows, place, mine, passed, codes, active, dec0, dec1, dec2, dec3, part, near, *outs):
    z, i = place[0], place[1]
    half = mine.shape[1] // 4
    pick(place, mine, passed, near)
    decoder_grads(-2.0 / rows, i, near, codes, (3, 1, 2, 0), outs)
    outs[0][half:] = jnp.broadcast_to(active[...], (outs[0].shape[0] - half, active.shape[1]))
    part[...] = back_through(i, near, (dec0, dec1, dec2, dec3), jnp.where(z >= 2, half, 0))


def far_error_body(rows, place, swapped, direct, codes, far, send):
    pick(place, swapped, direct, far)
    decoder_grads(-2.0 / rows, place[1], far, codes, (3,), (send,))


def code_grad_body(
    rows, place, far, part, mask, dec0, dec1, dec2, dec3, turned, grad_low, bias_sum, norms, send_far
):
    z, i = place[0], place[1]
    half = far.shape[1] // 4
    width = 2 * half
    decs = (dec0, dec1, dec2, dec3)
    total = part[...] + back_through(i, far, decs, jnp.where(z >= 2, 0, half))
    squares = functools.reduce(jnp.add, [one_row(dec[width:, :]) for dec in decs])
    column_norms = jnp.sqrt(squares + 1e-06)
    norms[...] = column_norms
    code_grad = (-2.0 / rows) * total + column_norms / rows
    grad = jnp.where(mask[...] > 0, code_grad, 0.0)
    grad_low[...] = grad.astype(BF16)
    row = jnp.sum(grad, axis=0, keepdims=True)
    bias_sum[...] = row
    encoder_grads(i, turned, grad_low, (3,), (send_far,))
    send_far[width:] = jnp.broadcast_to(row, (send_far.shape[0] - width, row.shape[1]))


def encoder_grads(i, turned, grad_low, slots, outs):
    width = turned.shape[0] // 4
    for slot, out in zip(slots, outs):
        at = pl.ds(pl.multiple_of((i ^ slot) * width, width), width)
        out[:width] = jnp.dot(turned[at, :], grad_low[...], preferred_element_type=F32)


def rest_body(rows, place, turned, grad_low, near, far, codes, home, send, kept_far, kept, *outs):
    z, i = place[0], place[1]
    half = far.shape[1] // 4
    shift = jnp.where(z >= 2, 0, half)
    encoder_grads(i, turned, grad_low, (2, 1, 0), (kept_far, send, kept))
    decoder_grads(-2.0 / rows, i, far, codes, (1, 2, 0), outs)
    home[:, columns(half - shift, half)] = near[:, columns(z * half, half)]
    home[:, columns(shift, half)] = far[:, columns(z * half, half)]


def power(values):
    largest = jnp.max(jnp.abs(values), axis=0, keepdims=True)
    return jnp.ceil(jnp.log(jnp.maximum(largest, 1e-30)) * (1.0 / math.log(2.0)))


def scale_of(exponent):
    return jnp.exp(exponent * math.log(2.0))


def pack_body(place, kept, received, row, packed, row_sum):
    width = kept.shape[0]
    total = kept[...] + received[:width]
    exponent = power(total)
    packed[:width] = total * scale_of(14.0 - exponent)
    sums = row[...]
    if received.shape[0] > width:
        sums += received[width : width + 1]
    row_sum[...] = sums
    row_exponent = power(sums)
    parts = three_rows(sums * scale_of(14.0 - row_exponent)).astype(F32)
    at = lax.broadcasted_iota(jnp.int32, parts.shape, 0)
    parts = jnp.where(at == 3, exponent, jnp.where(at == 4, row_exponent, parts))
    packed[width:] = parts


def unpack(packed):
    width = packed.shape[0] - EXTRA
    rows = packed[width:].astype(F32)
    block = packed[:width].astype(F32) * scale_of(rows[3:4] - 14.0)
    row = (rows[0:1] + rows[1:2] + rows[2:3]) * scale_of(rows[4:5] - 14.0)
    return block, row


def decoder_step_body(
    rows, place, param, moment, square, near, far, active, norms, param_out, moment_out, square_out
):
    is_near = (pl.program_id(0) < pl.num_programs(0) // 2) == (place[0] < 2)
    grad = jnp.where(is_near, near[...], far[...])
    grad += param[...] * (active[...] / norms[...]) / rows
    param_out[...], moment_out[...], square_out[...] = adam_update(
        param[...], grad, moment[...], square[...]
    )


def line_shards(
    activations,
    encoder,
    enc_bias,
    decoder,
    enc_moment,
    enc_square,
    bias_moment,
    bias_square,
    dec_moment,
    dec_square,
):
    rows = activations.shape[0] * 4
    count, width = activations.shape
    latents = encoder.shape[1]
    half = width // 2
    features = 4 * width
    z, i = lax.axis_index("latent"), lax.axis_index("dp")
    place = jnp.stack([z, i]).astype(jnp.int32)

    def along(value, pairs):
        return lax.ppermute(value, "latent", pairs)

    def flip(value, bits, planes=(0, 1, 2, 3)):
        pairs = [(4 * p + k, 4 * p + (k ^ bits)) for p in planes for k in range(4)]
        return lax.ppermute(value, ("latent", "dp"), pairs)

    ends = [(1, 0), (2, 3)]
    low = along(activations, [(0, 1), (1, 2), (2, 3)])
    high = along(activations, [(1, 0), (2, 1), (3, 2)])
    across = along(activations, [(0, 2), (3, 1)])

    (enc_own,) = local_kernel(
        encoder_body,
        [shape((width + EXTRA, latents), BF16)],
        place,
        encoder,
        enc_bias.reshape(1, -1),
    )
    enc_chip, enc_core = flip(enc_own, 2), flip(enc_own, 1)
    (dec_own,) = local_kernel(
        decoder_body,
        [shape((width + EXTRA, latents), BF16)],
        place,
        decoder,
        after=(enc_core,),
    )
    dec_chip, dec_core = flip(dec_own, 2), flip(dec_own, 1)
    (onward,) = local_kernel(
        onward_body, [shape((count, width), BF16)], place, low, high
    )
    relay1 = along(onward, ends)
    relay2 = along(across, ends)
    enc = [enc_own, enc_core, enc_chip, flip(behind(enc_chip, relay2), 1)]

    up, down, beyond = local_kernel(
        pieces_body, [shape((half, latents), BF16)] * 3, place, dec_own
    )
    dec_pieces = [
        along(up, [(0, 1), (1, 2)]),
        along(down, [(2, 1), (3, 2)]),
        along(beyond, [(0, 2), (3, 1)]),
    ]
    dec = [dec_own, dec_core, dec_chip, flip(dec_chip, 1)]

    rows_own = jnp.concatenate([behind(piece, dec_chip) for piece in dec_pieces], axis=0)
    codes, mask, inputs, active = local_kernel(
        codes_body,
        [
            shape((count, latents), BF16),
            shape((count, latents), BF16),
            shape((count, features), BF16),
            shape((1, latents), F32),
        ],
        place,
        activations,
        low,
        high,
        across,
        relay1,
        relay2,
        *enc,
        after=(rows_own,),
        scratch=[pltpu.VMEM((1, latents), F32)],
    )
    codes_low = along(codes, [(0, 1), (1, 2)])
    codes_high = along(codes, [(2, 1), (3, 2)])
    codes_across = along(codes, [(0, 2), (3, 1)])
    (turned,) = local_kernel(turn_body, [shape((features, count), BF16)], place, inputs)
    rows_chip = flip(rows_own, 2, (1, 2))
    rows_core = flip(behind(rows_own, turned), 1, (1, 2))
    rows_both = flip(
        behind(rows_chip, codes_low, codes_high, codes_across, dec[1], dec[3]), 1, (1, 2)
    )

    (own_error,) = local_kernel(
        error_body,
        [shape((count, features // 2), BF16)],
        place,
        codes,
        codes_low,
        codes_high,
        codes_across,
        *dec,
        rows_own,
        rows_core,
        rows_chip,
        rows_both,
        inputs,
    )
    swapped = along(own_error, [(1, 2), (2, 1)])
    passed = along(own_error, [(1, 0), (2, 3)])
    direct = along(own_error, [(2, 0), (1, 3)])

    def across_chips(kept, send, row):
        packed, row_sum = local_kernel(
            pack_body,
            [shape((kept.shape[0] + EXTRA, latents), F32), shape((1, latents), F32)],
            place,
            kept,
            flip(send, 1),
            row,
        )
        return packed, flip(packed.astype(jnp.float16), 2), row_sum

    blocks = [shape((half + 8, latents), F32)] + [shape((half, latents), F32)] * 3
    part, near, *near_blocks = local_kernel(
        functools.partial(near_body, rows),
        [shape((count, latents), F32), shape((count, features // 2), BF16), *blocks],
        place,
        own_error,
        passed,
        codes,
        active,
        *dec,
        after=(swapped,),
    )
    send_far, send_near, keep_far, keep_near = near_blocks
    near_packed, near_received, active_sum = across_chips(keep_far, send_far, active)
    near_kept = keep_near, flip(send_near, 1)
    far, far_send = local_kernel(
        functools.partial(far_error_body, rows),
        [shape((count, features // 2), BF16), shape((half, latents), F32)],
        place,
        swapped,
        direct,
        codes,
        after=(near_packed,),
        cost=NOTABLE,
    )
    grad_low, bias_sum, norms, send_far_enc = local_kernel(
        functools.partial(code_grad_body, rows),
        [
            shape((count, latents), BF16),
            shape((1, latents), F32),
            shape((1, latents), F32),
            shape((width + 8, latents), F32),
        ],
        place,
        far,
        behind(part, near_received),
        mask,
        *dec,
        turned,
    )
    error, enc_send_near, enc_keep_far, enc_keep_near, *far_blocks = local_kernel(
        functools.partial(rest_body, rows),
        [shape((count, width), BF16)]
        + [shape((width, latents), F32)] * 3
        + [shape((half, latents), F32)] * 3,
        place,
        turned,
        grad_low,
        near,
        far,
        codes,
    )
    send_near, keep_far, keep_near = far_blocks
    far_packed, far_received, _ = across_chips(keep_far, far_send, active)
    far_kept = keep_near, flip(send_near, 1)
    enc_packed, enc_received, bias_here = across_chips(
        behind(enc_keep_far, far_packed), send_far_enc, bias_sum
    )
    enc_kept = enc_keep_near, flip(enc_send_near, 1)

    decoder, dec_moment, dec_square, encoder, enc_moment, enc_square = lax.optimization_barrier(
        (decoder, dec_moment, dec_square, encoder, enc_moment, enc_square, enc_packed)
    )[:6]
    near_block, active_there = unpack(near_received)
    far_block, _ = unpack(far_received)
    enc_block, bias_there = unpack(enc_received)
    near_grad = near_kept[0] + near_kept[1] + near_block
    far_grad = far_kept[0] + far_kept[1] + far_block
    active_sum = active_sum + active_there
    grad_encoder = enc_kept[0] + enc_kept[1] + enc_block
    grad_bias = (bias_here + bias_there).reshape(latents)
    grad_bias = lax.dynamic_slice(grad_bias, (i * enc_bias.shape[0],), (enc_bias.shape[0],))
    new_enc_bias, new_bias_moment, new_bias_square = adam_update(
        enc_bias, grad_bias, bias_moment, bias_square
    )
    new_encoder, new_enc_moment, new_enc_square = adam_update(
        encoder, grad_encoder, enc_moment, enc_square
    )
    step = width // 4
    block = pl.BlockSpec((step, latents), lambda r: (r, 0))
    in_half = pl.BlockSpec((step, latents), lambda r: (r % 2, 0))
    row = pl.BlockSpec((1, latents), lambda r: (0, 0))
    new_decoder, new_dec_moment, new_dec_square = pl.pallas_call(
        functools.partial(decoder_step_body, rows),
        grid=(4,),
        out_shape=[shape((width, latents), F32)] * 3,
        in_specs=[SMEM, block, block, block, in_half, in_half, row, row],
        out_specs=[block] * 3,
        compiler_params=pltpu.CompilerParams(vmem_limit_bytes=12 * 1024 * 1024),
        cost_estimate=pl.CostEstimate(flops=1, bytes_accessed=1, transcendentals=0),
    )(place, decoder, dec_moment, dec_square, near_grad, far_grad, active_sum, norms)
    return (
        error,
        new_encoder,
        new_enc_bias,
        new_decoder,
        new_enc_moment,
        new_enc_square,
        new_bias_moment,
        new_bias_square,
        new_dec_moment,
        new_dec_square,
    )


def solution(mesh):
    in_specs = (
        P(("groups", "dp"), "latent"),
        P(("groups", "dp"), "latent"),
        P(("groups", "latent", "dp")),
        P(("groups", "dp"), "latent"),
        P(("groups", "dp"), "latent"),
        P(("groups", "dp"), "latent"),
        P(("groups", "latent", "dp")),
        P(("groups", "latent", "dp")),
        P(("groups", "dp"), "latent"),
        P(("groups", "dp"), "latent"),
    )
    out_specs = (
        P(("groups", "dp"), "latent"),
        P(("groups", "dp"), "latent"),
        P(("groups", "latent", "dp")),
        P(("groups", "dp"), "latent"),
        P(("groups", "dp"), "latent"),
        P(("groups", "dp"), "latent"),
        P(("groups", "latent", "dp")),
        P(("groups", "latent", "dp")),
        P(("groups", "dp"), "latent"),
        P(("groups", "dp"), "latent"),
    )
    line = mesh.shape["latent"] == 4 and mesh.shape["dp"] == 4
    plan = line_shards if line else shards
    return jax.shard_map(plan, mesh=mesh, in_specs=in_specs, out_specs=out_specs, check_vma=False)
```

```python
import functools
import math

import jax
import jax.numpy as jnp
from jax import lax
from jax.experimental import pallas as pl
from jax.experimental.pallas import tpu as pltpu
from jax.sharding import PartitionSpec as P

ADAM_STEP = 1000


first_decay = 0.9
second_decay = 0.999
learn_rate = 0.001
epsilon = 1e-08

F32 = jnp.float32
BF16 = jnp.bfloat16


def adam_update(param, grad, moment, square):
    moment_new = first_decay * moment + (1.0 - first_decay) * grad
    square_new = second_decay * square + (1.0 - second_decay) * grad * grad
    first_fix = 1.0 - first_decay**ADAM_STEP
    second_fix = 1.0 - second_decay**ADAM_STEP
    param_new = param - learn_rate * (moment_new / first_fix) / (
        jnp.sqrt(square_new / second_fix) + epsilon
    )
    return (param_new, moment_new, square_new)


def shards(
    activations,
    encoder,
    enc_bias,
    decoder,
    enc_moment,
    enc_square,
    bias_moment,
    bias_square,
    dec_moment,
    dec_square,
):
    row_count = activations.shape[0] * lax.axis_size("dp")
    loss_scale = 2.0 / row_count
    inputs = lax.all_gather(activations, "latent", axis=1, tiled=True)
    enc_low, dec_low = (
        lax.all_gather(encoder.astype(jnp.bfloat16), "dp", axis=0, tiled=True),
        lax.all_gather(decoder.astype(jnp.bfloat16), "dp", axis=0, tiled=True),
    )
    bias_full = lax.all_gather(enc_bias, "dp", axis=0, tiled=True)
    square_sums = lax.psum(jnp.sum(decoder * decoder, axis=0), "dp")
    column_norms = jnp.sqrt(square_sums + 1e-06)
    preact = jnp.dot(inputs, enc_low, preferred_element_type=jnp.float32) + bias_full
    latent_codes = jnp.maximum(preact, 0.0).astype(jnp.bfloat16)
    partial_sums = lax.dot_general(
        latent_codes, dec_low, (((1,), (1,)), ((), ())), preferred_element_type=jnp.float32
    )
    rebuilt = lax.psum_scatter(partial_sums, "latent", scatter_dimension=1, tiled=True)
    error = (activations.astype(jnp.float32) - rebuilt).astype(jnp.bfloat16)
    full_error = lax.all_gather(error, "latent", axis=1, tiled=True)
    active_sum = lax.psum(jnp.sum(latent_codes.astype(jnp.float32), axis=0), "dp")
    grad_dec_rows = -loss_scale * lax.dot_general(
        full_error, latent_codes, (((0,), (0,)), ((), ())), preferred_element_type=jnp.float32
    )
    code_grad = (
        -loss_scale * jnp.dot(full_error, dec_low, preferred_element_type=jnp.float32)
        + column_norms / row_count
    )
    grad_preact = jnp.where(preact > 0.0, code_grad, 0.0)
    grad_encoder = lax.dot_general(
        inputs,
        grad_preact.astype(jnp.bfloat16),
        (((0,), (0,)), ((), ())),
        preferred_element_type=jnp.float32,
    )
    grad_bias = jnp.sum(grad_preact, axis=0)
    grad_encoder, grad_dec_rows, grad_bias = (
        lax.psum_scatter(grad_encoder, "dp", scatter_dimension=0, tiled=True),
        lax.psum_scatter(grad_dec_rows, "dp", scatter_dimension=0, tiled=True),
        lax.psum_scatter(grad_bias, "dp", scatter_dimension=0, tiled=True),
    )
    grad_decoder = grad_dec_rows + decoder * (active_sum / column_norms) / row_count
    new_encoder, new_enc_moment, new_enc_square = adam_update(
        encoder, grad_encoder, enc_moment, enc_square
    )
    new_enc_bias, new_bias_moment, new_bias_square = adam_update(
        enc_bias, grad_bias, bias_moment, bias_square
    )
    new_decoder, new_dec_moment, new_dec_square = adam_update(
        decoder, grad_decoder, dec_moment, dec_square
    )
    return (
        error,
        new_encoder,
        new_enc_bias,
        new_decoder,
        new_enc_moment,
        new_enc_square,
        new_bias_moment,
        new_bias_square,
        new_dec_moment,
        new_dec_square,
    )


VMEM = pl.BlockSpec(memory_space=pltpu.VMEM)
SMEM = pl.BlockSpec(memory_space=pltpu.SMEM)
ANY = pl.BlockSpec(memory_space=pl.ANY)
EXTRA = 16
NOTABLE = 10**10


def local_kernel(body, outs, place, *args, after=(), scratch=(), cost=1):
    def run(place, *refs):
        body(place, *refs[: len(args)], *refs[len(args) + len(after) :])

    held = sum(a.size * jnp.dtype(a.dtype).itemsize for a in (*args, *outs))
    return pl.pallas_call(
        run,
        out_shape=outs,
        in_specs=[SMEM] + [VMEM] * len(args) + [ANY] * len(after),
        out_specs=[VMEM] * len(outs),
        scratch_shapes=scratch,
        compiler_params=pltpu.CompilerParams(vmem_limit_bytes=held + 6 * 1024 * 1024),
        cost_estimate=pl.CostEstimate(flops=cost, bytes_accessed=1, transcendentals=0),
    )(place, *args, *after)


def shape(dims, dtype):
    return jax.ShapeDtypeStruct(dims, dtype)


def columns(start, width):
    return pl.ds(pl.multiple_of(start, width), width)


def three_rows(row):
    high = row.astype(BF16).astype(F32)
    middle = (row - high).astype(BF16).astype(F32)
    low = row - high - middle
    at = lax.broadcasted_iota(jnp.int32, (EXTRA, row.shape[1]), 0)
    rows = jnp.where(at == 0, high, jnp.where(at == 1, middle, jnp.where(at == 2, low, 0.0)))
    return rows.astype(BF16)


def behind(value, *others):
    return lax.optimization_barrier((value, *others))[0]


def one_row(rows):
    return jnp.sum(rows.astype(F32), axis=0, keepdims=True)


def encoder_body(place, encoder, bias, out):
    depth = encoder.shape[0]
    out[:depth] = encoder[...].astype(BF16)
    out[depth:] = three_rows(jnp.concatenate([bias[...]] * 4, axis=1))


def decoder_body(place, decoder, out):
    depth = decoder.shape[0]
    value = decoder[...]
    out[:depth] = value.astype(BF16)
    out[depth:] = three_rows(jnp.sum(value * value, axis=0, keepdims=True))


def codes_body(
    place,
    own,
    low,
    high,
    across,
    relay1,
    relay2,
    enc0,
    enc1,
    enc2,
    enc3,
    codes,
    mask,
    full,
    active,
    bias,
):
    z, i = place[0], place[1]
    width = own.shape[1]
    for at, blocks in enumerate(
        (
            (own, high, relay1, relay2),
            (low, own, high, across),
            (across, low, own, high),
            (relay2, relay1, low, own),
        )
    ):

        @pl.when(z == at)
        def _(blocks=blocks):
            for b, block in enumerate(blocks):
                full[:, b * width : (b + 1) * width] = block[...]

    total = jnp.zeros(codes.shape, F32)
    piece = codes.shape[1] // 4
    for t, enc in enumerate((enc0, enc1, enc2, enc3)):
        b = i ^ t
        total += jnp.dot(
            full[:, columns(b * width, width)], enc[:width, :], preferred_element_type=F32
        )
        bias[:, columns(b * piece, piece)] = one_row(enc[width:, :piece])
    preact = total + bias[...]
    low_codes = jnp.maximum(preact, 0.0).astype(BF16)
    codes[...] = low_codes
    mask[...] = (preact > 0.0).astype(F32).astype(BF16)
    active[...] = jnp.sum(low_codes.astype(F32), axis=0, keepdims=True)


def onward_body(place, low, high, out):
    @pl.when(place[0] == 1)
    def _():
        out[...] = high[...]

    @pl.when(place[0] != 1)
    def _():
        out[...] = low[...]


def pieces_body(place, dec, up, down, across):
    z = place[0]
    half = up.shape[0]
    for out, second in ((up, z >= 1), (down, z >= 3), (across, z < 2)):
        out[...] = dec[pl.ds(pl.multiple_of(jnp.where(second, half, 0), half), half), :]


def turn_body(place, full, turned):
    turned[...] = full[...].T


def error_body(
    place, own, low, high, across, dec0, dec1, dec2, dec3, row0, row1, row2, row3, inputs, error
):
    z, i = place[0], place[1]
    half = row0.shape[0] // 3
    shift = pl.multiple_of(jnp.where(z >= 2, half, 0), half)
    for t in range(4):
        dec, row = (dec0, dec1, dec2, dec3)[t], (row0, row1, row2, row3)[t]
        lefts = (own, low, high, across)
        rights = [dec[pl.ds(shift, half), :]] + [row[m * half : (m + 1) * half, :] for m in range(3)]
        total = jnp.zeros((own.shape[0], half), F32)
        for left, right in zip(lefts, rights):
            total += lax.dot_general(
                left[...], right, (((1,), (1,)), ((), ())), preferred_element_type=F32
            )
        q = i ^ t
        given = inputs[:, columns(q * 2 * half + shift, half)].astype(F32)
        error[:, columns(q * half, half)] = (given - total).astype(BF16)


def pick(place, middle, end, out):
    z = place[0]
    is_middle = (z == 1) | (z == 2)

    @pl.when(is_middle)
    def _():
        out[...] = middle[...]

    @pl.when(jnp.logical_not(is_middle))
    def _():
        out[...] = end[...]


def decoder_grads(scale, i, error, codes, slots, outs):
    half = error.shape[1] // 4
    for slot, out in zip(slots, outs):
        out[:half] = scale * lax.dot_general(
            error[:, columns((i ^ slot) * half, half)],
            codes[...],
            (((0,), (0,)), ((), ())),
            preferred_element_type=F32,
        )


def back_through(i, error, decs, shift):
    half = error.shape[1] // 4
    return functools.reduce(
        jnp.add,
        [
            jnp.dot(
                error[:, columns((i ^ t) * half, half)],
                dec[pl.ds(pl.multiple_of(shift, half), half), :],
                preferred_element_type=F32,
            )
            for t, dec in enumerate(decs)
        ],
    )


def near_body(rows, place, mine, passed, codes, active, dec0, dec1, dec2, dec3, part, near, *outs):
    z, i = place[0], place[1]
    half = mine.shape[1] // 4
    pick(place, mine, passed, near)
    decoder_grads(-2.0 / rows, i, near, codes, (3, 1, 2, 0), outs)
    outs[0][half:] = jnp.broadcast_to(active[...], (outs[0].shape[0] - half, active.shape[1]))
    part[...] = back_through(i, near, (dec0, dec1, dec2, dec3), jnp.where(z >= 2, half, 0))


def far_error_body(rows, place, swapped, direct, codes, far, send):
    pick(place, swapped, direct, far)
    decoder_grads(-2.0 / rows, place[1], far, codes, (3,), (send,))


def code_grad_body(
    rows, place, far, part, mask, dec0, dec1, dec2, dec3, turned, grad_low, bias_sum, norms, send_far
):
    z, i = place[0], place[1]
    half = far.shape[1] // 4
    width = 2 * half
    decs = (dec0, dec1, dec2, dec3)
    total = part[...] + back_through(i, far, decs, jnp.where(z >= 2, 0, half))
    squares = functools.reduce(jnp.add, [one_row(dec[width:, :]) for dec in decs])
    column_norms = jnp.sqrt(squares + 1e-06)
    norms[...] = column_norms
    code_grad = (-2.0 / rows) * total + column_norms / rows
    grad = jnp.where(mask[...] > 0, code_grad, 0.0)
    grad_low[...] = grad.astype(BF16)
    row = jnp.sum(grad, axis=0, keepdims=True)
    bias_sum[...] = row
    encoder_grads(i, turned, grad_low, (3,), (send_far,))
    send_far[width:] = jnp.broadcast_to(row, (send_far.shape[0] - width, row.shape[1]))


def encoder_grads(i, turned, grad_low, slots, outs):
    width = turned.shape[0] // 4
    for slot, out in zip(slots, outs):
        at = pl.ds(pl.multiple_of((i ^ slot) * width, width), width)
        out[:width] = jnp.dot(turned[at, :], grad_low[...], preferred_element_type=F32)


def rest_body(rows, place, turned, grad_low, near, far, codes, home, send, kept_far, kept, *outs):
    z, i = place[0], place[1]
    half = far.shape[1] // 4
    shift = jnp.where(z >= 2, 0, half)
    encoder_grads(i, turned, grad_low, (2, 1, 0), (kept_far, send, kept))
    decoder_grads(-2.0 / rows, i, far, codes, (1, 2, 0), outs)
    home[:, columns(half - shift, half)] = near[:, columns(z * half, half)]
    home[:, columns(shift, half)] = far[:, columns(z * half, half)]


def power(values):
    largest = jnp.max(jnp.abs(values), axis=0, keepdims=True)
    return jnp.ceil(jnp.log(jnp.maximum(largest, 1e-30)) * (1.0 / math.log(2.0)))


def scale_of(exponent):
    return jnp.exp(exponent * math.log(2.0))


def pack_body(place, kept, received, row, packed, row_sum):
    width = kept.shape[0]
    total = kept[...] + received[:width]
    exponent = power(total)
    packed[:width] = total * scale_of(14.0 - exponent)
    sums = row[...]
    if received.shape[0] > width:
        sums += received[width : width + 1]
    row_sum[...] = sums
    row_exponent = power(sums)
    parts = three_rows(sums * scale_of(14.0 - row_exponent)).astype(F32)
    at = lax.broadcasted_iota(jnp.int32, parts.shape, 0)
    parts = jnp.where(at == 3, exponent, jnp.where(at == 4, row_exponent, parts))
    packed[width:] = parts


def unpack(packed):
    width = packed.shape[0] - EXTRA
    rows = packed[width:].astype(F32)
    block = packed[:width].astype(F32) * scale_of(rows[3:4] - 14.0)
    row = (rows[0:1] + rows[1:2] + rows[2:3]) * scale_of(rows[4:5] - 14.0)
    return block, row


def bias_step_body(place, param, moment, square, here, there, param_out, moment_out, square_out):
    width = param.shape[1]
    grad = here[...] + there[...]
    pieces = [grad[:, b * width : (b + 1) * width] for b in range(4)]
    own = functools.reduce(
        jnp.add, [jnp.where(place[1] == b, piece, 0.0) for b, piece in enumerate(pieces)]
    )
    param_out[...], moment_out[...], square_out[...] = adam_update(
        param[...], own, moment[...], square[...]
    )


def decoder_step_body(
    rows, place, param, moment, square, near, far, active, norms, param_out, moment_out, square_out
):
    is_near = (pl.program_id(0) < pl.num_programs(0) // 2) == (place[0] < 2)
    grad = jnp.where(is_near, near[...], far[...])
    grad += param[...] * (active[...] / norms[...]) / rows
    param_out[...], moment_out[...], square_out[...] = adam_update(
        param[...], grad, moment[...], square[...]
    )


def line_shards(
    activations,
    encoder,
    enc_bias,
    decoder,
    enc_moment,
    enc_square,
    bias_moment,
    bias_square,
    dec_moment,
    dec_square,
):
    rows = activations.shape[0] * 4
    count, width = activations.shape
    latents = encoder.shape[1]
    half = width // 2
    features = 4 * width
    z, i = lax.axis_index("latent"), lax.axis_index("dp")
    place = jnp.stack([z, i]).astype(jnp.int32)

    def along(value, pairs):
        return lax.ppermute(value, "latent", pairs)

    def flip(value, bits, planes=(0, 1, 2, 3)):
        pairs = [(4 * p + k, 4 * p + (k ^ bits)) for p in planes for k in range(4)]
        return lax.ppermute(value, ("latent", "dp"), pairs)

    ends = [(1, 0), (2, 3)]
    low = along(activations, [(0, 1), (1, 2), (2, 3)])
    high = along(activations, [(1, 0), (2, 1), (3, 2)])
    across = along(activations, [(0, 2), (3, 1)])

    (enc_own,) = local_kernel(
        encoder_body,
        [shape((width + EXTRA, latents), BF16)],
        place,
        encoder,
        enc_bias.reshape(1, -1),
    )
    enc_chip, enc_core = flip(enc_own, 2), flip(enc_own, 1)
    (dec_own,) = local_kernel(
        decoder_body,
        [shape((width + EXTRA, latents), BF16)],
        place,
        decoder,
        after=(enc_core,),
    )
    dec_chip, dec_core = flip(dec_own, 2), flip(dec_own, 1)
    (onward,) = local_kernel(
        onward_body, [shape((count, width), BF16)], place, low, high
    )
    relay1 = along(onward, ends)
    relay2 = along(across, ends)
    enc = [enc_own, enc_core, enc_chip, flip(behind(enc_chip, relay2), 1)]

    up, down, beyond = local_kernel(
        pieces_body, [shape((half, latents), BF16)] * 3, place, dec_own
    )
    dec_pieces = [
        along(up, [(0, 1), (1, 2)]),
        along(down, [(2, 1), (3, 2)]),
        along(beyond, [(0, 2), (3, 1)]),
    ]
    dec = [dec_own, dec_core, dec_chip, flip(dec_chip, 1)]

    rows_own = jnp.concatenate([behind(piece, dec_chip) for piece in dec_pieces], axis=0)
    codes, mask, inputs, active = local_kernel(
        codes_body,
        [
            shape((count, latents), BF16),
            shape((count, latents), BF16),
            shape((count, features), BF16),
            shape((1, latents), F32),
        ],
        place,
        activations,
        low,
        high,
        across,
        relay1,
        relay2,
        *enc,
        after=(rows_own,),
        scratch=[pltpu.VMEM((1, latents), F32)],
    )
    codes_low = along(codes, [(0, 1), (1, 2)])
    codes_high = along(codes, [(2, 1), (3, 2)])
    codes_across = along(codes, [(0, 2), (3, 1)])
    (turned,) = local_kernel(turn_body, [shape((features, count), BF16)], place, inputs)
    rows_chip = flip(rows_own, 2, (1, 2))
    rows_core = flip(behind(rows_own, turned), 1, (1, 2))
    rows_both = flip(
        behind(rows_chip, codes_low, codes_high, codes_across, dec[1], dec[3]), 1, (1, 2)
    )

    (own_error,) = local_kernel(
        error_body,
        [shape((count, features // 2), BF16)],
        place,
        codes,
        codes_low,
        codes_high,
        codes_across,
        *dec,
        rows_own,
        rows_core,
        rows_chip,
        rows_both,
        inputs,
    )
    swapped = along(own_error, [(1, 2), (2, 1)])
    passed = along(own_error, [(1, 0), (2, 3)])
    direct = along(own_error, [(2, 0), (1, 3)])

    def across_chips(kept, send, row):
        packed, row_sum = local_kernel(
            pack_body,
            [shape((kept.shape[0] + EXTRA, latents), F32), shape((1, latents), F32)],
            place,
            kept,
            flip(send, 1),
            row,
        )
        return packed, flip(packed.astype(jnp.float16), 2), row_sum

    blocks = [shape((half + 8, latents), F32)] + [shape((half, latents), F32)] * 3
    part, near, *near_blocks = local_kernel(
        functools.partial(near_body, rows),
        [shape((count, latents), F32), shape((count, features // 2), BF16), *blocks],
        place,
        own_error,
        passed,
        codes,
        active,
        *dec,
        after=(swapped,),
    )
    send_far, send_near, keep_far, keep_near = near_blocks
    near_packed, near_received, active_sum = across_chips(keep_far, send_far, active)
    near_kept = keep_near, flip(send_near, 1)
    far, far_send = local_kernel(
        functools.partial(far_error_body, rows),
        [shape((count, features // 2), BF16), shape((half, latents), F32)],
        place,
        swapped,
        direct,
        codes,
        after=(near_packed,),
        cost=NOTABLE,
    )
    grad_low, bias_sum, norms, send_far_enc = local_kernel(
        functools.partial(code_grad_body, rows),
        [
            shape((count, latents), BF16),
            shape((1, latents), F32),
            shape((1, latents), F32),
            shape((width + 8, latents), F32),
        ],
        place,
        far,
        behind(part, near_received),
        mask,
        *dec,
        turned,
    )
    error, enc_send_near, enc_keep_far, enc_keep_near, *far_blocks = local_kernel(
        functools.partial(rest_body, rows),
        [shape((count, width), BF16)]
        + [shape((width, latents), F32)] * 3
        + [shape((half, latents), F32)] * 3,
        place,
        turned,
        grad_low,
        near,
        far,
        codes,
    )
    send_near, keep_far, keep_near = far_blocks
    far_packed, far_received, _ = across_chips(keep_far, far_send, active)
    far_kept = keep_near, flip(send_near, 1)
    enc_packed, enc_received, bias_here = across_chips(
        behind(enc_keep_far, far_packed), send_far_enc, bias_sum
    )
    enc_kept = enc_keep_near, flip(enc_send_near, 1)

    decoder, dec_moment, dec_square, encoder, enc_moment, enc_square = lax.optimization_barrier(
        (decoder, dec_moment, dec_square, encoder, enc_moment, enc_square, enc_packed)
    )[:6]
    near_block, active_there = unpack(near_received)
    far_block, _ = unpack(far_received)
    enc_block, bias_there = unpack(enc_received)
    near_grad = near_kept[0] + near_kept[1] + near_block
    far_grad = far_kept[0] + far_kept[1] + far_block
    active_sum = active_sum + active_there
    grad_encoder = enc_kept[0] + enc_kept[1] + enc_block
    new_enc_bias, new_bias_moment, new_bias_square = [
        value.reshape(-1)
        for value in local_kernel(
            bias_step_body,
            [shape((1, enc_bias.shape[0]), F32)] * 3,
            place,
            enc_bias.reshape(1, -1),
            bias_moment.reshape(1, -1),
            bias_square.reshape(1, -1),
            bias_here,
            bias_there,
        )
    ]
    new_encoder, new_enc_moment, new_enc_square = adam_update(
        encoder, grad_encoder, enc_moment, enc_square
    )
    step = width // 4
    block = pl.BlockSpec((step, latents), lambda r: (r, 0))
    in_half = pl.BlockSpec((step, latents), lambda r: (r % 2, 0))
    row = pl.BlockSpec((1, latents), lambda r: (0, 0))
    new_decoder, new_dec_moment, new_dec_square = pl.pallas_call(
        functools.partial(decoder_step_body, rows),
        grid=(4,),
        out_shape=[shape((width, latents), F32)] * 3,
        in_specs=[SMEM, block, block, block, in_half, in_half, row, row],
        out_specs=[block] * 3,
        compiler_params=pltpu.CompilerParams(vmem_limit_bytes=12 * 1024 * 1024),
        cost_estimate=pl.CostEstimate(flops=1, bytes_accessed=1, transcendentals=0),
    )(place, decoder, dec_moment, dec_square, near_grad, far_grad, active_sum, norms)
    return (
        error,
        new_encoder,
        new_enc_bias,
        new_decoder,
        new_enc_moment,
        new_enc_square,
        new_bias_moment,
        new_bias_square,
        new_dec_moment,
        new_dec_square,
    )


def solution(mesh):
    in_specs = (
        P(("groups", "dp"), "latent"),
        P(("groups", "dp"), "latent"),
        P(("groups", "latent", "dp")),
        P(("groups", "dp"), "latent"),
        P(("groups", "dp"), "latent"),
        P(("groups", "dp"), "latent"),
        P(("groups", "latent", "dp")),
        P(("groups", "latent", "dp")),
        P(("groups", "dp"), "latent"),
        P(("groups", "dp"), "latent"),
    )
    out_specs = (
        P(("groups", "dp"), "latent"),
        P(("groups", "dp"), "latent"),
        P(("groups", "latent", "dp")),
        P(("groups", "dp"), "latent"),
        P(("groups", "dp"), "latent"),
        P(("groups", "dp"), "latent"),
        P(("groups", "latent", "dp")),
        P(("groups", "latent", "dp")),
        P(("groups", "dp"), "latent"),
        P(("groups", "dp"), "latent"),
    )
    line = mesh.shape["latent"] == 4 and mesh.shape["dp"] == 4
    plan = line_shards if line else shards
    return jax.shard_map(plan, mesh=mesh, in_specs=in_specs, out_specs=out_specs, check_vma=False)
```

```python
import functools
import math

import jax
import jax.numpy as jnp
from jax import lax
from jax.experimental import pallas as pl
from jax.experimental.pallas import tpu as pltpu
from jax.sharding import PartitionSpec as P

ADAM_STEP = 1000


first_decay = 0.9
second_decay = 0.999
learn_rate = 0.001
epsilon = 1e-08

F32 = jnp.float32
BF16 = jnp.bfloat16


def adam_update(param, grad, moment, square):
    moment_new = first_decay * moment + (1.0 - first_decay) * grad
    square_new = second_decay * square + (1.0 - second_decay) * grad * grad
    first_fix = 1.0 - first_decay**ADAM_STEP
    second_fix = 1.0 - second_decay**ADAM_STEP
    param_new = param - learn_rate * (moment_new / first_fix) / (
        jnp.sqrt(square_new / second_fix) + epsilon
    )
    return (param_new, moment_new, square_new)


def shards(
    activations,
    encoder,
    enc_bias,
    decoder,
    enc_moment,
    enc_square,
    bias_moment,
    bias_square,
    dec_moment,
    dec_square,
):
    row_count = activations.shape[0] * lax.axis_size("dp")
    loss_scale = 2.0 / row_count
    inputs = lax.all_gather(activations, "latent", axis=1, tiled=True)
    enc_low, dec_low = (
        lax.all_gather(encoder.astype(jnp.bfloat16), "dp", axis=0, tiled=True),
        lax.all_gather(decoder.astype(jnp.bfloat16), "dp", axis=0, tiled=True),
    )
    bias_full = lax.all_gather(enc_bias, "dp", axis=0, tiled=True)
    square_sums = lax.psum(jnp.sum(decoder * decoder, axis=0), "dp")
    column_norms = jnp.sqrt(square_sums + 1e-06)
    preact = jnp.dot(inputs, enc_low, preferred_element_type=jnp.float32) + bias_full
    latent_codes = jnp.maximum(preact, 0.0).astype(jnp.bfloat16)
    partial_sums = lax.dot_general(
        latent_codes, dec_low, (((1,), (1,)), ((), ())), preferred_element_type=jnp.float32
    )
    rebuilt = lax.psum_scatter(partial_sums, "latent", scatter_dimension=1, tiled=True)
    error = (activations.astype(jnp.float32) - rebuilt).astype(jnp.bfloat16)
    full_error = lax.all_gather(error, "latent", axis=1, tiled=True)
    active_sum = lax.psum(jnp.sum(latent_codes.astype(jnp.float32), axis=0), "dp")
    grad_dec_rows = -loss_scale * lax.dot_general(
        full_error, latent_codes, (((0,), (0,)), ((), ())), preferred_element_type=jnp.float32
    )
    code_grad = (
        -loss_scale * jnp.dot(full_error, dec_low, preferred_element_type=jnp.float32)
        + column_norms / row_count
    )
    grad_preact = jnp.where(preact > 0.0, code_grad, 0.0)
    grad_encoder = lax.dot_general(
        inputs,
        grad_preact.astype(jnp.bfloat16),
        (((0,), (0,)), ((), ())),
        preferred_element_type=jnp.float32,
    )
    grad_bias = jnp.sum(grad_preact, axis=0)
    grad_encoder, grad_dec_rows, grad_bias = (
        lax.psum_scatter(grad_encoder, "dp", scatter_dimension=0, tiled=True),
        lax.psum_scatter(grad_dec_rows, "dp", scatter_dimension=0, tiled=True),
        lax.psum_scatter(grad_bias, "dp", scatter_dimension=0, tiled=True),
    )
    grad_decoder = grad_dec_rows + decoder * (active_sum / column_norms) / row_count
    new_encoder, new_enc_moment, new_enc_square = adam_update(
        encoder, grad_encoder, enc_moment, enc_square
    )
    new_enc_bias, new_bias_moment, new_bias_square = adam_update(
        enc_bias, grad_bias, bias_moment, bias_square
    )
    new_decoder, new_dec_moment, new_dec_square = adam_update(
        decoder, grad_decoder, dec_moment, dec_square
    )
    return (
        error,
        new_encoder,
        new_enc_bias,
        new_decoder,
        new_enc_moment,
        new_enc_square,
        new_bias_moment,
        new_bias_square,
        new_dec_moment,
        new_dec_square,
    )


VMEM = pl.BlockSpec(memory_space=pltpu.VMEM)
SMEM = pl.BlockSpec(memory_space=pltpu.SMEM)
ANY = pl.BlockSpec(memory_space=pl.ANY)
EXTRA = 16
NOTABLE = 10**10


def local_kernel(body, outs, place, *args, after=(), scratch=(), cost=1):
    def run(place, *refs):
        body(place, *refs[: len(args)], *refs[len(args) + len(after) :])

    held = sum(a.size * jnp.dtype(a.dtype).itemsize for a in (*args, *outs))
    return pl.pallas_call(
        run,
        out_shape=outs,
        in_specs=[SMEM] + [VMEM] * len(args) + [ANY] * len(after),
        out_specs=[VMEM] * len(outs),
        scratch_shapes=scratch,
        compiler_params=pltpu.CompilerParams(vmem_limit_bytes=held + 6 * 1024 * 1024),
        cost_estimate=pl.CostEstimate(flops=cost, bytes_accessed=1, transcendentals=0),
    )(place, *args, *after)


def shape(dims, dtype):
    return jax.ShapeDtypeStruct(dims, dtype)


def columns(start, width):
    return pl.ds(pl.multiple_of(start, width), width)


def three_rows(row):
    high = row.astype(BF16).astype(F32)
    middle = (row - high).astype(BF16).astype(F32)
    low = row - high - middle
    at = lax.broadcasted_iota(jnp.int32, (EXTRA, row.shape[1]), 0)
    rows = jnp.where(at == 0, high, jnp.where(at == 1, middle, jnp.where(at == 2, low, 0.0)))
    return rows.astype(BF16)


def behind(value, *others):
    return lax.optimization_barrier((value, *others))[0]


def one_row(rows):
    return jnp.sum(rows.astype(F32), axis=0, keepdims=True)


def encoder_body(place, encoder, bias, out):
    depth = encoder.shape[0]
    out[:depth] = encoder[...].astype(BF16)
    out[depth:] = three_rows(jnp.concatenate([bias[...]] * 4, axis=1))


def decoder_body(place, decoder, out):
    depth = decoder.shape[0]
    value = decoder[...]
    out[:depth] = value.astype(BF16)
    out[depth:] = three_rows(jnp.sum(value * value, axis=0, keepdims=True))


def codes_body(
    place,
    own,
    low,
    high,
    across,
    relay1,
    relay2,
    enc0,
    enc1,
    enc2,
    enc3,
    codes,
    mask,
    full,
    active,
    bias,
):
    z, i = place[0], place[1]
    width = own.shape[1]
    for at, blocks in enumerate(
        (
            (own, high, relay1, relay2),
            (low, own, high, across),
            (across, low, own, high),
            (relay2, relay1, low, own),
        )
    ):

        @pl.when(z == at)
        def _(blocks=blocks):
            for b, block in enumerate(blocks):
                full[:, b * width : (b + 1) * width] = block[...]

    total = jnp.zeros(codes.shape, F32)
    piece = codes.shape[1] // 4
    for t, enc in enumerate((enc0, enc1, enc2, enc3)):
        b = i ^ t
        total += jnp.dot(
            full[:, columns(b * width, width)], enc[:width, :], preferred_element_type=F32
        )
        bias[:, columns(b * piece, piece)] = one_row(enc[width:, :piece])
    preact = total + bias[...]
    low_codes = jnp.maximum(preact, 0.0).astype(BF16)
    codes[...] = low_codes
    mask[...] = (preact > 0.0).astype(F32).astype(BF16)
    active[...] = jnp.sum(low_codes.astype(F32), axis=0, keepdims=True)


def onward_body(place, low, high, out):
    @pl.when(place[0] == 1)
    def _():
        out[...] = high[...]

    @pl.when(place[0] != 1)
    def _():
        out[...] = low[...]


def pieces_body(place, dec, up, down, across):
    z = place[0]
    half = up.shape[0]
    for out, second in ((up, z >= 1), (down, z >= 3), (across, z < 2)):
        out[...] = dec[pl.ds(pl.multiple_of(jnp.where(second, half, 0), half), half), :]


def turn_body(place, full, turned):
    turned[...] = full[...].T


def error_body(
    place, own, low, high, across, dec0, dec1, dec2, dec3, row0, row1, row2, row3, inputs, error
):
    z, i = place[0], place[1]
    half = row0.shape[0] // 3
    shift = pl.multiple_of(jnp.where(z >= 2, half, 0), half)
    for t in range(4):
        dec, row = (dec0, dec1, dec2, dec3)[t], (row0, row1, row2, row3)[t]
        lefts = (own, low, high, across)
        rights = [dec[pl.ds(shift, half), :]] + [row[m * half : (m + 1) * half, :] for m in range(3)]
        total = jnp.zeros((own.shape[0], half), F32)
        for left, right in zip(lefts, rights):
            total += lax.dot_general(
                left[...], right, (((1,), (1,)), ((), ())), preferred_element_type=F32
            )
        q = i ^ t
        given = inputs[:, columns(q * 2 * half + shift, half)].astype(F32)
        error[:, columns(q * half, half)] = (given - total).astype(BF16)


def pick(place, middle, end, out):
    z = place[0]
    is_middle = (z == 1) | (z == 2)

    @pl.when(is_middle)
    def _():
        out[...] = middle[...]

    @pl.when(jnp.logical_not(is_middle))
    def _():
        out[...] = end[...]


def decoder_grads(scale, i, error, codes, slots, outs):
    half = error.shape[1] // 4
    for slot, out in zip(slots, outs):
        out[:half] = scale * lax.dot_general(
            error[:, columns((i ^ slot) * half, half)],
            codes[...],
            (((0,), (0,)), ((), ())),
            preferred_element_type=F32,
        )


def back_through(i, error, decs, shift):
    half = error.shape[1] // 4
    return functools.reduce(
        jnp.add,
        [
            jnp.dot(
                error[:, columns((i ^ t) * half, half)],
                dec[pl.ds(pl.multiple_of(shift, half), half), :],
                preferred_element_type=F32,
            )
            for t, dec in enumerate(decs)
        ],
    )


def near_body(rows, place, mine, passed, codes, active, dec0, dec1, dec2, dec3, part, near, *outs):
    z, i = place[0], place[1]
    half = mine.shape[1] // 4
    pick(place, mine, passed, near)
    decoder_grads(-2.0 / rows, i, near, codes, (3, 1, 2, 0), outs)
    outs[0][half:] = jnp.broadcast_to(active[...], (outs[0].shape[0] - half, active.shape[1]))
    part[...] = back_through(i, near, (dec0, dec1, dec2, dec3), jnp.where(z >= 2, half, 0))


def far_error_body(rows, place, swapped, direct, codes, far, send, kept):
    pick(place, swapped, direct, far)
    decoder_grads(-2.0 / rows, place[1], far, codes, (3, 2), (send, kept))


def code_grad_body(
    rows, place, far, part, mask, dec0, dec1, dec2, dec3, turned, grad_low, bias_sum, norms, *sends
):
    z, i = place[0], place[1]
    half = far.shape[1] // 4
    width = 2 * half
    decs = (dec0, dec1, dec2, dec3)
    total = part[...] + back_through(i, far, decs, jnp.where(z >= 2, 0, half))
    squares = functools.reduce(jnp.add, [one_row(dec[width:, :]) for dec in decs])
    column_norms = jnp.sqrt(squares + 1e-06)
    norms[...] = column_norms
    code_grad = (-2.0 / rows) * total + column_norms / rows
    grad = jnp.where(mask[...] > 0, code_grad, 0.0)
    grad_low[...] = grad.astype(BF16)
    row = jnp.sum(grad, axis=0, keepdims=True)
    bias_sum[...] = row
    at = pl.multiple_of((i ^ 3) * width, width)
    block = jnp.dot(turned[pl.ds(at, width), :], grad_low[...], preferred_element_type=F32)
    sends[0][:half] = block[:half]
    sends[0][half:] = jnp.broadcast_to(row, (sends[0].shape[0] - half, row.shape[1]))
    sends[1][...] = block[half:]


def encoder_grads(i, turned, grad_low, slots, outs):
    width = turned.shape[0] // 4
    for slot, out in zip(slots, outs):
        at = pl.ds(pl.multiple_of((i ^ slot) * width, width), width)
        out[:width] = jnp.dot(turned[at, :], grad_low[...], preferred_element_type=F32)


def rest_body(rows, place, turned, grad_low, near, far, codes, home, send, kept_far, kept, *outs):
    z, i = place[0], place[1]
    half = far.shape[1] // 4
    shift = jnp.where(z >= 2, 0, half)
    encoder_grads(i, turned, grad_low, (2, 1, 0), (kept_far, send, kept))
    decoder_grads(-2.0 / rows, i, far, codes, (1, 0), outs)
    home[:, columns(half - shift, half)] = near[:, columns(z * half, half)]
    home[:, columns(shift, half)] = far[:, columns(z * half, half)]


def power(values):
    largest = jnp.max(jnp.abs(values), axis=0, keepdims=True)
    return jnp.ceil(jnp.log(jnp.maximum(largest, 1e-30)) * (1.0 / math.log(2.0)))


def scale_of(exponent):
    return jnp.exp(exponent * math.log(2.0))


def pack_body(place, kept, row, *refs):
    received, (packed, row_sum) = refs[:-2], refs[-2:]
    width = kept.shape[0]
    block = width // len(received)
    total = jnp.concatenate([piece[:block] for piece in received], axis=0) + kept[...]
    exponent = power(total)
    packed[:width] = total * scale_of(14.0 - exponent)
    sums = row[...]
    if received[0].shape[0] > block:
        sums += received[0][block : block + 1]
    row_sum[...] = sums
    row_exponent = power(sums)
    parts = three_rows(sums * scale_of(14.0 - row_exponent)).astype(F32)
    at = lax.broadcasted_iota(jnp.int32, parts.shape, 0)
    parts = jnp.where(at == 3, exponent, jnp.where(at == 4, row_exponent, parts))
    packed[width:] = parts


def unpack(packed):
    width = packed.shape[0] - EXTRA
    rows = packed[width:].astype(F32)
    block = packed[:width].astype(F32) * scale_of(rows[3:4] - 14.0)
    row = (rows[0:1] + rows[1:2] + rows[2:3]) * scale_of(rows[4:5] - 14.0)
    return block, row


def bias_step_body(place, param, moment, square, here, there, param_out, moment_out, square_out):
    width = param.shape[1]
    grad = here[...] + there[...]
    pieces = [grad[:, b * width : (b + 1) * width] for b in range(4)]
    own = functools.reduce(
        jnp.add, [jnp.where(place[1] == b, piece, 0.0) for b, piece in enumerate(pieces)]
    )
    param_out[...], moment_out[...], square_out[...] = adam_update(
        param[...], own, moment[...], square[...]
    )


def decoder_step_body(
    rows, place, param, moment, square, near, far, active, norms, param_out, moment_out, square_out
):
    is_near = (pl.program_id(0) < pl.num_programs(0) // 2) == (place[0] < 2)
    grad = jnp.where(is_near, near[...], far[...])
    grad += param[...] * (active[...] / norms[...]) / rows
    param_out[...], moment_out[...], square_out[...] = adam_update(
        param[...], grad, moment[...], square[...]
    )


def line_shards(
    activations,
    encoder,
    enc_bias,
    decoder,
    enc_moment,
    enc_square,
    bias_moment,
    bias_square,
    dec_moment,
    dec_square,
):
    rows = activations.shape[0] * 4
    count, width = activations.shape
    latents = encoder.shape[1]
    half = width // 2
    features = 4 * width
    z, i = lax.axis_index("latent"), lax.axis_index("dp")
    place = jnp.stack([z, i]).astype(jnp.int32)

    def along(value, pairs):
        return lax.ppermute(value, "latent", pairs)

    def flip(value, bits, planes=(0, 1, 2, 3)):
        pairs = [(4 * p + k, 4 * p + (k ^ bits)) for p in planes for k in range(4)]
        return lax.ppermute(value, ("latent", "dp"), pairs)

    ends = [(1, 0), (2, 3)]
    low = along(activations, [(0, 1), (1, 2), (2, 3)])
    high = along(activations, [(1, 0), (2, 1), (3, 2)])
    across = along(activations, [(0, 2), (3, 1)])

    (enc_own,) = local_kernel(
        encoder_body,
        [shape((width + EXTRA, latents), BF16)],
        place,
        encoder,
        enc_bias.reshape(1, -1),
    )
    enc_chip, enc_core = flip(enc_own, 2), flip(enc_own, 1)
    (dec_own,) = local_kernel(
        decoder_body,
        [shape((width + EXTRA, latents), BF16)],
        place,
        decoder,
        after=(enc_core,),
    )
    dec_chip, dec_core = flip(dec_own, 2), flip(dec_own, 1)
    (onward,) = local_kernel(
        onward_body, [shape((count, width), BF16)], place, low, high
    )
    relay1 = along(onward, ends)
    relay2 = along(across, ends)
    enc = [enc_own, enc_core, enc_chip, flip(behind(enc_chip, relay2), 1)]

    up, down, beyond = local_kernel(
        pieces_body, [shape((half, latents), BF16)] * 3, place, dec_own
    )
    dec_pieces = [
        along(up, [(0, 1), (1, 2)]),
        along(down, [(2, 1), (3, 2)]),
        along(beyond, [(0, 2), (3, 1)]),
    ]
    dec = [dec_own, dec_core, dec_chip, flip(dec_chip, 1)]

    rows_own = jnp.concatenate([behind(piece, dec_chip) for piece in dec_pieces], axis=0)
    codes, mask, inputs, active = local_kernel(
        codes_body,
        [
            shape((count, latents), BF16),
            shape((count, latents), BF16),
            shape((count, features), BF16),
            shape((1, latents), F32),
        ],
        place,
        activations,
        low,
        high,
        across,
        relay1,
        relay2,
        *enc,
        after=(rows_own,),
        scratch=[pltpu.VMEM((1, latents), F32)],
    )
    codes_low = along(codes, [(0, 1), (1, 2)])
    codes_high = along(codes, [(2, 1), (3, 2)])
    codes_across = along(codes, [(0, 2), (3, 1)])
    (turned,) = local_kernel(
        turn_body, [shape((features, count), BF16)], place, inputs
    )
    rows_chip = flip(rows_own, 2, (1, 2))
    rows_core = flip(behind(rows_own, turned), 1, (1, 2))
    rows_both = flip(
        behind(rows_chip, codes_low, codes_high, codes_across, dec[1], dec[3]), 1, (1, 2)
    )

    (own_error,) = local_kernel(
        error_body,
        [shape((count, features // 2), BF16)],
        place,
        codes,
        codes_low,
        codes_high,
        codes_across,
        *dec,
        rows_own,
        rows_core,
        rows_chip,
        rows_both,
        inputs,
    )
    swapped = along(own_error, [(1, 2), (2, 1)])
    passed = along(own_error, [(1, 0), (2, 3)])
    direct = along(own_error, [(2, 0), (1, 3)])

    def across_chips(kept, row, *send):
        packed, row_sum = local_kernel(
            pack_body,
            [shape((kept.shape[0] + EXTRA, latents), F32), shape((1, latents), F32)],
            place,
            kept,
            row,
            *[flip(piece, 1) for piece in send],
        )
        return packed, flip(packed.astype(jnp.float16), 2), row_sum

    blocks = [shape((half + 8, latents), F32)] + [shape((half, latents), F32)] * 3
    part, near, *near_blocks = local_kernel(
        functools.partial(near_body, rows),
        [shape((count, latents), F32), shape((count, features // 2), BF16), *blocks],
        place,
        own_error,
        passed,
        codes,
        active,
        *dec,
        after=(swapped,),
    )
    send_far, send_near, keep_far, keep_near = near_blocks
    near_packed, near_received, active_sum = across_chips(keep_far, active, send_far)
    near_kept = keep_near, flip(send_near, 1)
    far, far_send, far_keep = local_kernel(
        functools.partial(far_error_body, rows),
        [shape((count, features // 2), BF16)] + [shape((half, latents), F32)] * 2,
        place,
        swapped,
        direct,
        codes,
        after=(near_packed,),
        cost=NOTABLE,
    )
    grad_low, bias_sum, norms, *send_far_enc = local_kernel(
        functools.partial(code_grad_body, rows),
        [
            shape((count, latents), BF16),
            shape((1, latents), F32),
            shape((1, latents), F32),
            shape((half + 8, latents), F32),
            shape((half, latents), F32),
        ],
        place,
        far,
        behind(part, near_received),
        mask,
        *dec,
        turned,
        cost=NOTABLE,
    )
    far_packed, far_received, _ = across_chips(far_keep, active, far_send)
    error, enc_send_near, enc_keep_far, enc_keep_near, send_near, keep_near = local_kernel(
        functools.partial(rest_body, rows),
        [shape((count, width), BF16)]
        + [shape((width, latents), F32)] * 3
        + [shape((half, latents), F32)] * 2,
        place,
        turned,
        grad_low,
        near,
        far,
        codes,
        after=(far_packed,),
    )
    far_kept = keep_near, flip(send_near, 1)
    enc_packed, enc_received, bias_here = across_chips(enc_keep_far, bias_sum, *send_far_enc)
    enc_kept = enc_keep_near, flip(enc_send_near, 1)

    decoder, dec_moment, dec_square, encoder, enc_moment, enc_square = lax.optimization_barrier(
        (decoder, dec_moment, dec_square, encoder, enc_moment, enc_square, enc_packed)
    )[:6]
    near_block, active_there = unpack(near_received)
    far_block, _ = unpack(far_received)
    enc_block, bias_there = unpack(enc_received)
    near_grad = near_kept[0] + near_kept[1] + near_block
    far_grad = far_kept[0] + far_kept[1] + far_block
    active_sum = active_sum + active_there
    grad_encoder = enc_kept[0] + enc_kept[1] + enc_block
    new_enc_bias, new_bias_moment, new_bias_square = [
        value.reshape(-1)
        for value in local_kernel(
            bias_step_body,
            [shape((1, enc_bias.shape[0]), F32)] * 3,
            place,
            enc_bias.reshape(1, -1),
            bias_moment.reshape(1, -1),
            bias_square.reshape(1, -1),
            bias_here,
            bias_there,
        )
    ]
    new_encoder, new_enc_moment, new_enc_square = adam_update(
        encoder, grad_encoder, enc_moment, enc_square
    )
    step = width // 4
    block = pl.BlockSpec((step, latents), lambda r: (r, 0))
    in_half = pl.BlockSpec((step, latents), lambda r: (r % 2, 0))
    row = pl.BlockSpec((1, latents), lambda r: (0, 0))
    new_decoder, new_dec_moment, new_dec_square = pl.pallas_call(
        functools.partial(decoder_step_body, rows),
        grid=(4,),
        out_shape=[shape((width, latents), F32)] * 3,
        in_specs=[SMEM, block, block, block, in_half, in_half, row, row],
        out_specs=[block] * 3,
        compiler_params=pltpu.CompilerParams(vmem_limit_bytes=12 * 1024 * 1024),
        cost_estimate=pl.CostEstimate(flops=1, bytes_accessed=1, transcendentals=0),
    )(place, decoder, dec_moment, dec_square, near_grad, far_grad, active_sum, norms)
    return (
        error,
        new_encoder,
        new_enc_bias,
        new_decoder,
        new_enc_moment,
        new_enc_square,
        new_bias_moment,
        new_bias_square,
        new_dec_moment,
        new_dec_square,
    )


def solution(mesh):
    in_specs = (
        P(("groups", "dp"), "latent"),
        P(("groups", "dp"), "latent"),
        P(("groups", "latent", "dp")),
        P(("groups", "dp"), "latent"),
        P(("groups", "dp"), "latent"),
        P(("groups", "dp"), "latent"),
        P(("groups", "latent", "dp")),
        P(("groups", "latent", "dp")),
        P(("groups", "dp"), "latent"),
        P(("groups", "dp"), "latent"),
    )
    out_specs = (
        P(("groups", "dp"), "latent"),
        P(("groups", "dp"), "latent"),
        P(("groups", "latent", "dp")),
        P(("groups", "dp"), "latent"),
        P(("groups", "dp"), "latent"),
        P(("groups", "dp"), "latent"),
        P(("groups", "latent", "dp")),
        P(("groups", "latent", "dp")),
        P(("groups", "dp"), "latent"),
        P(("groups", "dp"), "latent"),
    )
    line = mesh.shape["latent"] == 4 and mesh.shape["dp"] == 4
    plan = line_shards if line else shards
    return jax.shard_map(plan, mesh=mesh, in_specs=in_specs, out_specs=out_specs, check_vma=False)
```

```python
import functools
import math

import jax
import jax.numpy as jnp
from jax import lax
from jax.experimental import pallas as pl
from jax.experimental.pallas import tpu as pltpu
from jax.sharding import PartitionSpec as P

ADAM_STEP = 1000


first_decay = 0.9
second_decay = 0.999
learn_rate = 0.001
epsilon = 1e-08

F32 = jnp.float32
BF16 = jnp.bfloat16


def adam_update(param, grad, moment, square):
    moment_new = first_decay * moment + (1.0 - first_decay) * grad
    square_new = second_decay * square + (1.0 - second_decay) * grad * grad
    first_fix = 1.0 - first_decay**ADAM_STEP
    second_fix = 1.0 - second_decay**ADAM_STEP
    param_new = param - learn_rate * (moment_new / first_fix) / (
        jnp.sqrt(square_new / second_fix) + epsilon
    )
    return (param_new, moment_new, square_new)


def shards(
    activations,
    encoder,
    enc_bias,
    decoder,
    enc_moment,
    enc_square,
    bias_moment,
    bias_square,
    dec_moment,
    dec_square,
):
    row_count = activations.shape[0] * lax.axis_size("dp")
    loss_scale = 2.0 / row_count
    inputs = lax.all_gather(activations, "latent", axis=1, tiled=True)
    enc_low, dec_low = (
        lax.all_gather(encoder.astype(jnp.bfloat16), "dp", axis=0, tiled=True),
        lax.all_gather(decoder.astype(jnp.bfloat16), "dp", axis=0, tiled=True),
    )
    bias_full = lax.all_gather(enc_bias, "dp", axis=0, tiled=True)
    square_sums = lax.psum(jnp.sum(decoder * decoder, axis=0), "dp")
    column_norms = jnp.sqrt(square_sums + 1e-06)
    preact = jnp.dot(inputs, enc_low, preferred_element_type=jnp.float32) + bias_full
    latent_codes = jnp.maximum(preact, 0.0).astype(jnp.bfloat16)
    partial_sums = lax.dot_general(
        latent_codes, dec_low, (((1,), (1,)), ((), ())), preferred_element_type=jnp.float32
    )
    rebuilt = lax.psum_scatter(partial_sums, "latent", scatter_dimension=1, tiled=True)
    error = (activations.astype(jnp.float32) - rebuilt).astype(jnp.bfloat16)
    full_error = lax.all_gather(error, "latent", axis=1, tiled=True)
    active_sum = lax.psum(jnp.sum(latent_codes.astype(jnp.float32), axis=0), "dp")
    grad_dec_rows = -loss_scale * lax.dot_general(
        full_error, latent_codes, (((0,), (0,)), ((), ())), preferred_element_type=jnp.float32
    )
    code_grad = (
        -loss_scale * jnp.dot(full_error, dec_low, preferred_element_type=jnp.float32)
        + column_norms / row_count
    )
    grad_preact = jnp.where(preact > 0.0, code_grad, 0.0)
    grad_encoder = lax.dot_general(
        inputs,
        grad_preact.astype(jnp.bfloat16),
        (((0,), (0,)), ((), ())),
        preferred_element_type=jnp.float32,
    )
    grad_bias = jnp.sum(grad_preact, axis=0)
    grad_encoder, grad_dec_rows, grad_bias = (
        lax.psum_scatter(grad_encoder, "dp", scatter_dimension=0, tiled=True),
        lax.psum_scatter(grad_dec_rows, "dp", scatter_dimension=0, tiled=True),
        lax.psum_scatter(grad_bias, "dp", scatter_dimension=0, tiled=True),
    )
    grad_decoder = grad_dec_rows + decoder * (active_sum / column_norms) / row_count
    new_encoder, new_enc_moment, new_enc_square = adam_update(
        encoder, grad_encoder, enc_moment, enc_square
    )
    new_enc_bias, new_bias_moment, new_bias_square = adam_update(
        enc_bias, grad_bias, bias_moment, bias_square
    )
    new_decoder, new_dec_moment, new_dec_square = adam_update(
        decoder, grad_decoder, dec_moment, dec_square
    )
    return (
        error,
        new_encoder,
        new_enc_bias,
        new_decoder,
        new_enc_moment,
        new_enc_square,
        new_bias_moment,
        new_bias_square,
        new_dec_moment,
        new_dec_square,
    )


VMEM = pl.BlockSpec(memory_space=pltpu.VMEM)
SMEM = pl.BlockSpec(memory_space=pltpu.SMEM)
ANY = pl.BlockSpec(memory_space=pl.ANY)
EXTRA = 16
NOTABLE = 10**10


def local_kernel(body, outs, place, *args, after=(), scratch=(), cost=1):
    def run(place, *refs):
        body(place, *refs[: len(args)], *refs[len(args) + len(after) :])

    held = sum(a.size * jnp.dtype(a.dtype).itemsize for a in (*args, *outs))
    return pl.pallas_call(
        run,
        out_shape=outs,
        in_specs=[SMEM] + [VMEM] * len(args) + [ANY] * len(after),
        out_specs=[VMEM] * len(outs),
        scratch_shapes=scratch,
        compiler_params=pltpu.CompilerParams(vmem_limit_bytes=held + 6 * 1024 * 1024),
        cost_estimate=pl.CostEstimate(flops=cost, bytes_accessed=1, transcendentals=0),
    )(place, *args, *after)


def shape(dims, dtype):
    return jax.ShapeDtypeStruct(dims, dtype)


def columns(start, width):
    return pl.ds(pl.multiple_of(start, width), width)


def three_rows(row):
    high = row.astype(BF16).astype(F32)
    middle = (row - high).astype(BF16).astype(F32)
    low = row - high - middle
    at = lax.broadcasted_iota(jnp.int32, (EXTRA, row.shape[1]), 0)
    rows = jnp.where(at == 0, high, jnp.where(at == 1, middle, jnp.where(at == 2, low, 0.0)))
    return rows.astype(BF16)


def behind(value, *others):
    return lax.optimization_barrier((value, *others))[0]


def one_row(rows):
    return jnp.sum(rows.astype(F32), axis=0, keepdims=True)


def encoder_body(place, encoder, bias, out):
    depth = encoder.shape[0]
    out[:depth] = encoder[...].astype(BF16)
    out[depth:] = three_rows(jnp.concatenate([bias[...]] * 4, axis=1))


def decoder_body(place, decoder, out):
    depth = decoder.shape[0]
    value = decoder[...]
    out[:depth] = value.astype(BF16)
    out[depth:] = three_rows(jnp.sum(value * value, axis=0, keepdims=True))


def codes_body(
    place,
    own,
    low,
    high,
    across,
    relay1,
    relay2,
    enc0,
    enc1,
    enc2,
    enc3,
    codes,
    mask,
    full,
    active,
    bias,
):
    z, i = place[0], place[1]
    width = own.shape[1]
    for at, blocks in enumerate(
        (
            (own, high, relay1, relay2),
            (low, own, high, across),
            (across, low, own, high),
            (relay2, relay1, low, own),
        )
    ):

        @pl.when(z == at)
        def _(blocks=blocks):
            for b, block in enumerate(blocks):
                full[:, b * width : (b + 1) * width] = block[...]

    total = jnp.zeros(codes.shape, F32)
    piece = codes.shape[1] // 4
    for t, enc in enumerate((enc0, enc1, enc2, enc3)):
        b = i ^ t
        total += jnp.dot(
            full[:, columns(b * width, width)], enc[:width, :], preferred_element_type=F32
        )
        bias[:, columns(b * piece, piece)] = one_row(enc[width:, :piece])
    preact = total + bias[...]
    low_codes = jnp.maximum(preact, 0.0).astype(BF16)
    codes[...] = low_codes
    mask[...] = (preact > 0.0).astype(F32).astype(BF16)
    active[...] = jnp.sum(low_codes.astype(F32), axis=0, keepdims=True)


def onward_body(place, low, high, out):
    @pl.when(place[0] == 1)
    def _():
        out[...] = high[...]

    @pl.when(place[0] != 1)
    def _():
        out[...] = low[...]


def pieces_body(place, dec, up, down, across):
    z = place[0]
    half = up.shape[0]
    for out, second in ((up, z >= 1), (down, z >= 3), (across, z < 2)):
        out[...] = dec[pl.ds(pl.multiple_of(jnp.where(second, half, 0), half), half), :]


def split_body(place, rows, first, second):
    edge = first.shape[0]
    first[...] = rows[:edge]
    second[...] = rows[edge:]


def turn_body(place, full, turned):
    turned[...] = full[...].T


def error_body(
    place, own, low, high, across, dec0, dec1, dec2, dec3, row0, row1, row2, *refs
):
    first, second, inputs, error = refs
    z, i = place[0], place[1]
    half = row0.shape[0] // 3
    edge = first.shape[0]
    shift = pl.multiple_of(jnp.where(z >= 2, half, 0), half)
    for t in range(4):
        dec = (dec0, dec1, dec2, dec3)[t]
        lefts = (own, low, high, across)
        if t < 3:
            row = (row0, row1, row2)[t]
            rights = [row[m * half : (m + 1) * half, :] for m in range(3)]
        else:
            middle = jnp.concatenate([first[half:], second[: edge - half]], axis=0)
            rights = [first[:half], middle, second[edge - half :]]
        rights = [dec[pl.ds(shift, half), :]] + rights
        total = jnp.zeros((own.shape[0], half), F32)
        for left, right in zip(lefts, rights):
            total += lax.dot_general(
                left[...], right, (((1,), (1,)), ((), ())), preferred_element_type=F32
            )
        q = i ^ t
        given = inputs[:, columns(q * 2 * half + shift, half)].astype(F32)
        error[:, columns(q * half, half)] = (given - total).astype(BF16)


def pick(place, middle, end, out):
    z = place[0]
    is_middle = (z == 1) | (z == 2)

    @pl.when(is_middle)
    def _():
        out[...] = middle[...]

    @pl.when(jnp.logical_not(is_middle))
    def _():
        out[...] = end[...]


def decoder_grads(scale, i, error, codes, slots, outs):
    half = error.shape[1] // 4
    for slot, out in zip(slots, outs):
        out[:half] = scale * lax.dot_general(
            error[:, columns((i ^ slot) * half, half)],
            codes[...],
            (((0,), (0,)), ((), ())),
            preferred_element_type=F32,
        )


def back_through(i, error, decs, shift):
    half = error.shape[1] // 4
    return functools.reduce(
        jnp.add,
        [
            jnp.dot(
                error[:, columns((i ^ t) * half, half)],
                dec[pl.ds(pl.multiple_of(shift, half), half), :],
                preferred_element_type=F32,
            )
            for t, dec in enumerate(decs)
        ],
    )


def near_body(rows, place, mine, passed, codes, active, dec0, dec1, dec2, dec3, part, near, *outs):
    z, i = place[0], place[1]
    half = mine.shape[1] // 4
    pick(place, mine, passed, near)
    decoder_grads(-2.0 / rows, i, near, codes, (3, 1, 2, 0), outs)
    outs[0][half:] = jnp.broadcast_to(active[...], (outs[0].shape[0] - half, active.shape[1]))
    part[...] = back_through(i, near, (dec0, dec1, dec2, dec3), jnp.where(z >= 2, half, 0))


def far_error_body(rows, place, swapped, direct, codes, far, send, kept):
    pick(place, swapped, direct, far)
    decoder_grads(-2.0 / rows, place[1], far, codes, (3, 2), (send, kept))


def code_grad_body(
    rows, place, far, part, mask, dec0, dec1, dec2, dec3, turned, grad_low, bias_sum, norms, *sends
):
    z, i = place[0], place[1]
    half = far.shape[1] // 4
    width = 2 * half
    decs = (dec0, dec1, dec2, dec3)
    total = part[...] + back_through(i, far, decs, jnp.where(z >= 2, 0, half))
    squares = functools.reduce(jnp.add, [one_row(dec[width:, :]) for dec in decs])
    column_norms = jnp.sqrt(squares + 1e-06)
    norms[...] = column_norms
    code_grad = (-2.0 / rows) * total + column_norms / rows
    grad = jnp.where(mask[...] > 0, code_grad, 0.0)
    grad_low[...] = grad.astype(BF16)
    row = jnp.sum(grad, axis=0, keepdims=True)
    bias_sum[...] = row
    at = pl.multiple_of((i ^ 3) * width, width)
    block = jnp.dot(turned[pl.ds(at, width), :], grad_low[...], preferred_element_type=F32)
    sends[0][:half] = block[:half]
    sends[0][half:] = jnp.broadcast_to(row, (sends[0].shape[0] - half, row.shape[1]))
    sends[1][...] = block[half:]


def encoder_grads(i, turned, grad_low, slots, outs):
    width = turned.shape[0] // 4
    for slot, out in zip(slots, outs):
        at = pl.ds(pl.multiple_of((i ^ slot) * width, width), width)
        out[:width] = jnp.dot(turned[at, :], grad_low[...], preferred_element_type=F32)


def rest_body(rows, place, turned, grad_low, near, far, codes, home, send, kept_far, kept, *outs):
    z, i = place[0], place[1]
    half = far.shape[1] // 4
    shift = jnp.where(z >= 2, 0, half)
    encoder_grads(i, turned, grad_low, (2, 1, 0), (kept_far, send, kept))
    decoder_grads(-2.0 / rows, i, far, codes, (1, 0), outs)
    home[:, columns(half - shift, half)] = near[:, columns(z * half, half)]
    home[:, columns(shift, half)] = far[:, columns(z * half, half)]


def power(values):
    largest = jnp.max(jnp.abs(values), axis=0, keepdims=True)
    return jnp.ceil(jnp.log(jnp.maximum(largest, 1e-30)) * (1.0 / math.log(2.0)))


def scale_of(exponent):
    return jnp.exp(exponent * math.log(2.0))


def pack_body(place, kept, row, *refs):
    received, (packed, row_sum) = refs[:-2], refs[-2:]
    width = kept.shape[0]
    block = width // len(received)
    total = jnp.concatenate([piece[:block] for piece in received], axis=0) + kept[...]
    exponent = power(total)
    packed[:width] = total * scale_of(14.0 - exponent)
    sums = row[...]
    if received[0].shape[0] > block:
        sums += received[0][block : block + 1]
    row_sum[...] = sums
    row_exponent = power(sums)
    parts = three_rows(sums * scale_of(14.0 - row_exponent)).astype(F32)
    at = lax.broadcasted_iota(jnp.int32, parts.shape, 0)
    parts = jnp.where(at == 3, exponent, jnp.where(at == 4, row_exponent, parts))
    packed[width:] = parts


def unpack(packed):
    width = packed.shape[0] - EXTRA
    rows = packed[width:].astype(F32)
    block = packed[:width].astype(F32) * scale_of(rows[3:4] - 14.0)
    row = (rows[0:1] + rows[1:2] + rows[2:3]) * scale_of(rows[4:5] - 14.0)
    return block, row


def bias_step_body(place, param, moment, square, here, there, param_out, moment_out, square_out):
    width = param.shape[1]
    grad = here[...] + there[...]
    pieces = [grad[:, b * width : (b + 1) * width] for b in range(4)]
    own = functools.reduce(
        jnp.add, [jnp.where(place[1] == b, piece, 0.0) for b, piece in enumerate(pieces)]
    )
    param_out[...], moment_out[...], square_out[...] = adam_update(
        param[...], own, moment[...], square[...]
    )


def decoder_step_body(
    rows, place, param, moment, square, near, far, active, norms, param_out, moment_out, square_out
):
    is_near = (pl.program_id(0) < pl.num_programs(0) // 2) == (place[0] < 2)
    grad = jnp.where(is_near, near[...], far[...])
    grad += param[...] * (active[...] / norms[...]) / rows
    param_out[...], moment_out[...], square_out[...] = adam_update(
        param[...], grad, moment[...], square[...]
    )


def line_shards(
    activations,
    encoder,
    enc_bias,
    decoder,
    enc_moment,
    enc_square,
    bias_moment,
    bias_square,
    dec_moment,
    dec_square,
):
    rows = activations.shape[0] * 4
    count, width = activations.shape
    latents = encoder.shape[1]
    half = width // 2
    features = 4 * width
    z, i = lax.axis_index("latent"), lax.axis_index("dp")
    place = jnp.stack([z, i]).astype(jnp.int32)

    def along(value, pairs):
        return lax.ppermute(value, "latent", pairs)

    def flip(value, bits, planes=(0, 1, 2, 3)):
        pairs = [(4 * p + k, 4 * p + (k ^ bits)) for p in planes for k in range(4)]
        return lax.ppermute(value, ("latent", "dp"), pairs)

    ends = [(1, 0), (2, 3)]
    low = along(activations, [(0, 1), (1, 2), (2, 3)])
    high = along(activations, [(1, 0), (2, 1), (3, 2)])
    across = along(activations, [(0, 2), (3, 1)])

    (enc_own,) = local_kernel(
        encoder_body,
        [shape((width + EXTRA, latents), BF16)],
        place,
        encoder,
        enc_bias.reshape(1, -1),
    )
    enc_chip, enc_core = flip(enc_own, 2), flip(enc_own, 1)
    (dec_own,) = local_kernel(
        decoder_body,
        [shape((width + EXTRA, latents), BF16)],
        place,
        decoder,
        after=(enc_core,),
    )
    dec_chip, dec_core = flip(dec_own, 2), flip(dec_own, 1)
    (onward,) = local_kernel(
        onward_body, [shape((count, width), BF16)], place, low, high
    )
    relay1 = along(onward, ends)
    relay2 = along(across, ends)
    enc = [enc_own, enc_core, enc_chip, flip(behind(enc_chip, relay2), 1)]

    up, down, beyond = local_kernel(
        pieces_body, [shape((half, latents), BF16)] * 3, place, dec_own
    )
    dec_pieces = [
        along(up, [(0, 1), (1, 2)]),
        along(down, [(2, 1), (3, 2)]),
        along(beyond, [(0, 2), (3, 1)]),
    ]
    dec = [dec_own, dec_core, dec_chip, flip(dec_chip, 1)]

    rows_own = jnp.concatenate([behind(piece, dec_chip) for piece in dec_pieces], axis=0)
    codes, mask, inputs, active = local_kernel(
        codes_body,
        [
            shape((count, latents), BF16),
            shape((count, latents), BF16),
            shape((count, features), BF16),
            shape((1, latents), F32),
        ],
        place,
        activations,
        low,
        high,
        across,
        relay1,
        relay2,
        *enc,
        after=(rows_own, dec[1], dec[3]),
        scratch=[pltpu.VMEM((1, latents), F32)],
    )
    codes_low = along(codes, [(0, 1), (1, 2)])
    codes_high = along(codes, [(2, 1), (3, 2)])
    codes_across = along(codes, [(0, 2), (3, 1)])
    (turned,) = local_kernel(
        turn_body, [shape((features, count), BF16)], place, inputs
    )
    rows_chip = flip(rows_own, 2, (1, 2))
    rows_core = flip(behind(rows_own, turned), 1, (1, 2))
    halves = local_kernel(
        split_body,
        [shape((3 * half // 2, latents), BF16)] * 2,
        place,
        rows_chip,
        after=(codes_across,),
    )
    rows_both = [flip(piece, 1, (1, 2)) for piece in halves]

    (own_error,) = local_kernel(
        error_body,
        [shape((count, features // 2), BF16)],
        place,
        codes,
        codes_low,
        codes_high,
        codes_across,
        *dec,
        rows_own,
        rows_core,
        rows_chip,
        *rows_both,
        inputs,
    )
    swapped = along(own_error, [(1, 2), (2, 1)])
    passed = along(own_error, [(1, 0), (2, 3)])
    direct = along(own_error, [(2, 0), (1, 3)])

    def across_chips(kept, row, *send):
        packed, row_sum = local_kernel(
            pack_body,
            [shape((kept.shape[0] + EXTRA, latents), F32), shape((1, latents), F32)],
            place,
            kept,
            row,
            *[flip(piece, 1) for piece in send],
        )
        return packed, flip(packed.astype(jnp.float16), 2), row_sum

    blocks = [shape((half + 8, latents), F32)] + [shape((half, latents), F32)] * 3
    part, near, *near_blocks = local_kernel(
        functools.partial(near_body, rows),
        [shape((count, latents), F32), shape((count, features // 2), BF16), *blocks],
        place,
        own_error,
        passed,
        codes,
        active,
        *dec,
        after=(swapped,),
    )
    send_far, send_near, keep_far, keep_near = near_blocks
    near_packed, near_received, active_sum = across_chips(keep_far, active, send_far)
    near_kept = keep_near, flip(send_near, 1)
    far, far_send, far_keep = local_kernel(
        functools.partial(far_error_body, rows),
        [shape((count, features // 2), BF16)] + [shape((half, latents), F32)] * 2,
        place,
        swapped,
        direct,
        codes,
        after=(near_packed,),
        cost=NOTABLE,
    )
    grad_low, bias_sum, norms, *send_far_enc = local_kernel(
        functools.partial(code_grad_body, rows),
        [
            shape((count, latents), BF16),
            shape((1, latents), F32),
            shape((1, latents), F32),
            shape((half + 8, latents), F32),
            shape((half, latents), F32),
        ],
        place,
        far,
        behind(part, near_received),
        mask,
        *dec,
        turned,
        cost=NOTABLE,
    )
    far_packed, far_received, _ = across_chips(far_keep, active, far_send)
    error, enc_send_near, enc_keep_far, enc_keep_near, send_near, keep_near = local_kernel(
        functools.partial(rest_body, rows),
        [shape((count, width), BF16)]
        + [shape((width, latents), F32)] * 3
        + [shape((half, latents), F32)] * 2,
        place,
        turned,
        grad_low,
        near,
        far,
        codes,
        after=(far_packed,),
    )
    far_kept = keep_near, flip(send_near, 1)
    enc_packed, enc_received, bias_here = across_chips(enc_keep_far, bias_sum, *send_far_enc)
    enc_kept = enc_keep_near, flip(enc_send_near, 1)

    decoder, dec_moment, dec_square, encoder, enc_moment, enc_square = lax.optimization_barrier(
        (decoder, dec_moment, dec_square, encoder, enc_moment, enc_square, enc_packed)
    )[:6]
    near_block, active_there = unpack(near_received)
    far_block, _ = unpack(far_received)
    enc_block, bias_there = unpack(enc_received)
    near_grad = near_kept[0] + near_kept[1] + near_block
    far_grad = far_kept[0] + far_kept[1] + far_block
    active_sum = active_sum + active_there
    grad_encoder = enc_kept[0] + enc_kept[1] + enc_block
    new_enc_bias, new_bias_moment, new_bias_square = [
        value.reshape(-1)
        for value in local_kernel(
            bias_step_body,
            [shape((1, enc_bias.shape[0]), F32)] * 3,
            place,
            enc_bias.reshape(1, -1),
            bias_moment.reshape(1, -1),
            bias_square.reshape(1, -1),
            bias_here,
            bias_there,
        )
    ]
    new_encoder, new_enc_moment, new_enc_square = adam_update(
        encoder, grad_encoder, enc_moment, enc_square
    )
    step = width // 4
    block = pl.BlockSpec((step, latents), lambda r: (r, 0))
    in_half = pl.BlockSpec((step, latents), lambda r: (r % 2, 0))
    row = pl.BlockSpec((1, latents), lambda r: (0, 0))
    new_decoder, new_dec_moment, new_dec_square = pl.pallas_call(
        functools.partial(decoder_step_body, rows),
        grid=(4,),
        out_shape=[shape((width, latents), F32)] * 3,
        in_specs=[SMEM, block, block, block, in_half, in_half, row, row],
        out_specs=[block] * 3,
        compiler_params=pltpu.CompilerParams(vmem_limit_bytes=12 * 1024 * 1024),
        cost_estimate=pl.CostEstimate(flops=1, bytes_accessed=1, transcendentals=0),
    )(place, decoder, dec_moment, dec_square, near_grad, far_grad, active_sum, norms)
    return (
        error,
        new_encoder,
        new_enc_bias,
        new_decoder,
        new_enc_moment,
        new_enc_square,
        new_bias_moment,
        new_bias_square,
        new_dec_moment,
        new_dec_square,
    )


def solution(mesh):
    in_specs = (
        P(("groups", "dp"), "latent"),
        P(("groups", "dp"), "latent"),
        P(("groups", "latent", "dp")),
        P(("groups", "dp"), "latent"),
        P(("groups", "dp"), "latent"),
        P(("groups", "dp"), "latent"),
        P(("groups", "latent", "dp")),
        P(("groups", "latent", "dp")),
        P(("groups", "dp"), "latent"),
        P(("groups", "dp"), "latent"),
    )
    out_specs = (
        P(("groups", "dp"), "latent"),
        P(("groups", "dp"), "latent"),
        P(("groups", "latent", "dp")),
        P(("groups", "dp"), "latent"),
        P(("groups", "dp"), "latent"),
        P(("groups", "dp"), "latent"),
        P(("groups", "latent", "dp")),
        P(("groups", "latent", "dp")),
        P(("groups", "dp"), "latent"),
        P(("groups", "dp"), "latent"),
    )
    line = mesh.shape["latent"] == 4 and mesh.shape["dp"] == 4
    plan = line_shards if line else shards
    return jax.shard_map(plan, mesh=mesh, in_specs=in_specs, out_specs=out_specs, check_vma=False)
```

```python
import functools
import math

import jax
import jax.numpy as jnp
from jax import lax
from jax.experimental import pallas as pl
from jax.experimental.pallas import tpu as pltpu
from jax.sharding import PartitionSpec as P

ADAM_STEP = 1000


first_decay = 0.9
second_decay = 0.999
learn_rate = 0.001
epsilon = 1e-08

F32 = jnp.float32
BF16 = jnp.bfloat16


def adam_update(param, grad, moment, square):
    moment_new = first_decay * moment + (1.0 - first_decay) * grad
    square_new = second_decay * square + (1.0 - second_decay) * grad * grad
    first_fix = 1.0 - first_decay**ADAM_STEP
    second_fix = 1.0 - second_decay**ADAM_STEP
    param_new = param - learn_rate * (moment_new / first_fix) / (
        jnp.sqrt(square_new / second_fix) + epsilon
    )
    return (param_new, moment_new, square_new)


def shards(
    activations,
    encoder,
    enc_bias,
    decoder,
    enc_moment,
    enc_square,
    bias_moment,
    bias_square,
    dec_moment,
    dec_square,
):
    row_count = activations.shape[0] * lax.axis_size("dp")
    loss_scale = 2.0 / row_count
    inputs = lax.all_gather(activations, "latent", axis=1, tiled=True)
    enc_low, dec_low = (
        lax.all_gather(encoder.astype(jnp.bfloat16), "dp", axis=0, tiled=True),
        lax.all_gather(decoder.astype(jnp.bfloat16), "dp", axis=0, tiled=True),
    )
    bias_full = lax.all_gather(enc_bias, "dp", axis=0, tiled=True)
    square_sums = lax.psum(jnp.sum(decoder * decoder, axis=0), "dp")
    column_norms = jnp.sqrt(square_sums + 1e-06)
    preact = jnp.dot(inputs, enc_low, preferred_element_type=jnp.float32) + bias_full
    latent_codes = jnp.maximum(preact, 0.0).astype(jnp.bfloat16)
    partial_sums = lax.dot_general(
        latent_codes, dec_low, (((1,), (1,)), ((), ())), preferred_element_type=jnp.float32
    )
    rebuilt = lax.psum_scatter(partial_sums, "latent", scatter_dimension=1, tiled=True)
    error = (activations.astype(jnp.float32) - rebuilt).astype(jnp.bfloat16)
    full_error = lax.all_gather(error, "latent", axis=1, tiled=True)
    active_sum = lax.psum(jnp.sum(latent_codes.astype(jnp.float32), axis=0), "dp")
    grad_dec_rows = -loss_scale * lax.dot_general(
        full_error, latent_codes, (((0,), (0,)), ((), ())), preferred_element_type=jnp.float32
    )
    code_grad = (
        -loss_scale * jnp.dot(full_error, dec_low, preferred_element_type=jnp.float32)
        + column_norms / row_count
    )
    grad_preact = jnp.where(preact > 0.0, code_grad, 0.0)
    grad_encoder = lax.dot_general(
        inputs,
        grad_preact.astype(jnp.bfloat16),
        (((0,), (0,)), ((), ())),
        preferred_element_type=jnp.float32,
    )
    grad_bias = jnp.sum(grad_preact, axis=0)
    grad_encoder, grad_dec_rows, grad_bias = (
        lax.psum_scatter(grad_encoder, "dp", scatter_dimension=0, tiled=True),
        lax.psum_scatter(grad_dec_rows, "dp", scatter_dimension=0, tiled=True),
        lax.psum_scatter(grad_bias, "dp", scatter_dimension=0, tiled=True),
    )
    grad_decoder = grad_dec_rows + decoder * (active_sum / column_norms) / row_count
    new_encoder, new_enc_moment, new_enc_square = adam_update(
        encoder, grad_encoder, enc_moment, enc_square
    )
    new_enc_bias, new_bias_moment, new_bias_square = adam_update(
        enc_bias, grad_bias, bias_moment, bias_square
    )
    new_decoder, new_dec_moment, new_dec_square = adam_update(
        decoder, grad_decoder, dec_moment, dec_square
    )
    return (
        error,
        new_encoder,
        new_enc_bias,
        new_decoder,
        new_enc_moment,
        new_enc_square,
        new_bias_moment,
        new_bias_square,
        new_dec_moment,
        new_dec_square,
    )


VMEM = pl.BlockSpec(memory_space=pltpu.VMEM)
SMEM = pl.BlockSpec(memory_space=pltpu.SMEM)
ANY = pl.BlockSpec(memory_space=pl.ANY)
EXTRA = 16
NOTABLE = 10**10


def local_kernel(body, outs, place, *args, after=(), scratch=(), cost=1):
    def run(place, *refs):
        body(place, *refs[: len(args)], *refs[len(args) + len(after) :])

    held = sum(a.size * jnp.dtype(a.dtype).itemsize for a in (*args, *outs))
    return pl.pallas_call(
        run,
        out_shape=outs,
        in_specs=[SMEM] + [VMEM] * len(args) + [ANY] * len(after),
        out_specs=[VMEM] * len(outs),
        scratch_shapes=scratch,
        compiler_params=pltpu.CompilerParams(vmem_limit_bytes=held + 6 * 1024 * 1024),
        cost_estimate=pl.CostEstimate(flops=cost, bytes_accessed=1, transcendentals=0),
    )(place, *args, *after)


def shape(dims, dtype):
    return jax.ShapeDtypeStruct(dims, dtype)


def columns(start, width):
    return pl.ds(pl.multiple_of(start, width), width)


def three_rows(row):
    high = row.astype(BF16).astype(F32)
    middle = (row - high).astype(BF16).astype(F32)
    low = row - high - middle
    at = lax.broadcasted_iota(jnp.int32, (EXTRA, row.shape[1]), 0)
    rows = jnp.where(at == 0, high, jnp.where(at == 1, middle, jnp.where(at == 2, low, 0.0)))
    return rows.astype(BF16)


def behind(value, *others):
    return lax.optimization_barrier((value, *others))[0]


def one_row(rows):
    return jnp.sum(rows.astype(F32), axis=0, keepdims=True)


def encoder_body(place, encoder, bias, out):
    depth = encoder.shape[0]
    out[:depth] = encoder[...].astype(BF16)
    out[depth:] = three_rows(jnp.concatenate([bias[...]] * 4, axis=1))


def decoder_body(place, decoder, out):
    depth = decoder.shape[0]
    value = decoder[...]
    out[:depth] = value.astype(BF16)
    out[depth:] = three_rows(jnp.sum(value * value, axis=0, keepdims=True))


def codes_body(
    place,
    own,
    low,
    high,
    across,
    relay1,
    relay2,
    enc0,
    enc1,
    enc2,
    enc3,
    codes,
    mask,
    full,
    active,
    bias,
):
    z, i = place[0], place[1]
    width = own.shape[1]
    for at, blocks in enumerate(
        (
            (own, high, relay1, relay2),
            (low, own, high, across),
            (across, low, own, high),
            (relay2, relay1, low, own),
        )
    ):

        @pl.when(z == at)
        def _(blocks=blocks):
            for b, block in enumerate(blocks):
                full[:, b * width : (b + 1) * width] = block[...]

    total = jnp.zeros(codes.shape, F32)
    piece = codes.shape[1] // 4
    for t, enc in enumerate((enc0, enc1, enc2, enc3)):
        b = i ^ t
        total += jnp.dot(
            full[:, columns(b * width, width)], enc[:width, :], preferred_element_type=F32
        )
        bias[:, columns(b * piece, piece)] = one_row(enc[width:, :piece])
    preact = total + bias[...]
    low_codes = jnp.maximum(preact, 0.0).astype(BF16)
    codes[...] = low_codes
    mask[...] = (preact > 0.0).astype(F32).astype(BF16)
    active[...] = jnp.sum(low_codes.astype(F32), axis=0, keepdims=True)


def onward_body(place, low, high, out):
    @pl.when(place[0] == 1)
    def _():
        out[...] = high[...]

    @pl.when(place[0] != 1)
    def _():
        out[...] = low[...]


def pieces_body(place, dec, up, down, across):
    z = place[0]
    half = up.shape[0]
    for out, second in ((up, z >= 1), (down, z >= 3), (across, z < 2)):
        out[...] = dec[pl.ds(pl.multiple_of(jnp.where(second, half, 0), half), half), :]


def stack_body(place, piece0, piece1, piece2, first, second):
    size = piece0.shape[0]
    edge = first.shape[0]
    first[:size] = piece0[...]
    first[size:] = piece1[: edge - size]
    second[: edge - size] = piece1[edge - size :]
    second[edge - size :] = piece2[...]


def turn_body(place, full, turned):
    turned[...] = full[...].T


def error_body(place, own, low, high, across, dec0, dec1, dec2, dec3, *refs):
    *rows, inputs, error = refs
    z, i = place[0], place[1]
    edge = rows[0].shape[0]
    half = 2 * edge // 3
    shift = pl.multiple_of(jnp.where(z >= 2, half, 0), half)
    for t, dec in enumerate((dec0, dec1, dec2, dec3)):
        first, second = rows[2 * t], rows[2 * t + 1]
        between = jnp.concatenate([first[half:], second[: edge - half]], axis=0)
        lefts = (own, low, high, across)
        rights = [dec[pl.ds(shift, half), :], first[:half], between, second[edge - half :]]
        total = jnp.zeros((own.shape[0], half), F32)
        for left, right in zip(lefts, rights):
            total += lax.dot_general(
                left[...], right, (((1,), (1,)), ((), ())), preferred_element_type=F32
            )
        q = i ^ t
        given = inputs[:, columns(q * 2 * half + shift, half)].astype(F32)
        error[:, columns(q * half, half)] = (given - total).astype(BF16)


def pick(place, middle, end, out):
    z = place[0]
    is_middle = (z == 1) | (z == 2)

    @pl.when(is_middle)
    def _():
        out[...] = middle[...]

    @pl.when(jnp.logical_not(is_middle))
    def _():
        out[...] = end[...]


def decoder_grads(scale, i, error, codes, slots, outs):
    half = error.shape[1] // 4
    for slot, out in zip(slots, outs):
        out[:half] = scale * lax.dot_general(
            error[:, columns((i ^ slot) * half, half)],
            codes[...],
            (((0,), (0,)), ((), ())),
            preferred_element_type=F32,
        )


def back_through(i, error, decs, shift):
    half = error.shape[1] // 4
    return functools.reduce(
        jnp.add,
        [
            jnp.dot(
                error[:, columns((i ^ t) * half, half)],
                dec[pl.ds(pl.multiple_of(shift, half), half), :],
                preferred_element_type=F32,
            )
            for t, dec in enumerate(decs)
        ],
    )


def near_body(rows, place, mine, passed, codes, active, dec0, dec1, dec2, dec3, part, near, *outs):
    z, i = place[0], place[1]
    half = mine.shape[1] // 4
    pick(place, mine, passed, near)
    decoder_grads(-2.0 / rows, i, near, codes, (3, 1, 2, 0), outs)
    outs[0][half:] = jnp.broadcast_to(active[...], (outs[0].shape[0] - half, active.shape[1]))
    part[...] = back_through(i, near, (dec0, dec1, dec2, dec3), jnp.where(z >= 2, half, 0))


def far_error_body(rows, place, swapped, direct, codes, far, send, kept):
    pick(place, swapped, direct, far)
    decoder_grads(-2.0 / rows, place[1], far, codes, (3, 2), (send, kept))


def code_grad_body(
    rows, place, far, part, mask, dec0, dec1, dec2, dec3, turned, grad_low, bias_sum, norms, *sends
):
    z, i = place[0], place[1]
    half = far.shape[1] // 4
    width = 2 * half
    decs = (dec0, dec1, dec2, dec3)
    total = part[...] + back_through(i, far, decs, jnp.where(z >= 2, 0, half))
    squares = functools.reduce(jnp.add, [one_row(dec[width:, :]) for dec in decs])
    column_norms = jnp.sqrt(squares + 1e-06)
    norms[...] = column_norms
    code_grad = (-2.0 / rows) * total + column_norms / rows
    grad = jnp.where(mask[...] > 0, code_grad, 0.0)
    grad_low[...] = grad.astype(BF16)
    row = jnp.sum(grad, axis=0, keepdims=True)
    bias_sum[...] = row
    at = pl.multiple_of((i ^ 3) * width, width)
    block = jnp.dot(turned[pl.ds(at, width), :], grad_low[...], preferred_element_type=F32)
    sends[0][:half] = block[:half]
    sends[0][half:] = jnp.broadcast_to(row, (sends[0].shape[0] - half, row.shape[1]))
    sends[1][...] = block[half:]


def encoder_grads(i, turned, grad_low, slots, outs):
    width = turned.shape[0] // 4
    for slot, out in zip(slots, outs):
        at = pl.ds(pl.multiple_of((i ^ slot) * width, width), width)
        out[:width] = jnp.dot(turned[at, :], grad_low[...], preferred_element_type=F32)


def rest_body(rows, place, turned, grad_low, near, far, codes, home, send, kept_far, kept, *outs):
    z, i = place[0], place[1]
    half = far.shape[1] // 4
    shift = jnp.where(z >= 2, 0, half)
    encoder_grads(i, turned, grad_low, (2, 1, 0), (kept_far, send, kept))
    decoder_grads(-2.0 / rows, i, far, codes, (1, 0), outs)
    home[:, columns(half - shift, half)] = near[:, columns(z * half, half)]
    home[:, columns(shift, half)] = far[:, columns(z * half, half)]


def power(values):
    largest = jnp.max(jnp.abs(values), axis=0, keepdims=True)
    return jnp.ceil(jnp.log(jnp.maximum(largest, 1e-30)) * (1.0 / math.log(2.0)))


def scale_of(exponent):
    return jnp.exp(exponent * math.log(2.0))


def pack_body(place, kept, row, *refs):
    received, (packed, row_sum) = refs[:-2], refs[-2:]
    width = kept.shape[0]
    block = width // len(received)
    total = jnp.concatenate([piece[:block] for piece in received], axis=0) + kept[...]
    exponent = power(total)
    packed[:width] = total * scale_of(14.0 - exponent)
    sums = row[...]
    if received[0].shape[0] > block:
        sums += received[0][block : block + 1]
    row_sum[...] = sums
    row_exponent = power(sums)
    parts = three_rows(sums * scale_of(14.0 - row_exponent)).astype(F32)
    at = lax.broadcasted_iota(jnp.int32, parts.shape, 0)
    parts = jnp.where(at == 3, exponent, jnp.where(at == 4, row_exponent, parts))
    packed[width:] = parts


def unpack(packed):
    width = packed.shape[0] - EXTRA
    rows = packed[width:].astype(F32)
    block = packed[:width].astype(F32) * scale_of(rows[3:4] - 14.0)
    row = (rows[0:1] + rows[1:2] + rows[2:3]) * scale_of(rows[4:5] - 14.0)
    return block, row


def bias_step_body(place, param, moment, square, here, there, param_out, moment_out, square_out):
    width = param.shape[1]
    grad = here[...] + there[...]
    pieces = [grad[:, b * width : (b + 1) * width] for b in range(4)]
    own = functools.reduce(
        jnp.add, [jnp.where(place[1] == b, piece, 0.0) for b, piece in enumerate(pieces)]
    )
    param_out[...], moment_out[...], square_out[...] = adam_update(
        param[...], own, moment[...], square[...]
    )


def decoder_step_body(
    rows, place, param, moment, square, near, far, active, norms, param_out, moment_out, square_out
):
    is_near = (pl.program_id(0) < pl.num_programs(0) // 2) == (place[0] < 2)
    grad = jnp.where(is_near, near[...], far[...])
    grad += param[...] * (active[...] / norms[...]) / rows
    param_out[...], moment_out[...], square_out[...] = adam_update(
        param[...], grad, moment[...], square[...]
    )


def line_shards(
    activations,
    encoder,
    enc_bias,
    decoder,
    enc_moment,
    enc_square,
    bias_moment,
    bias_square,
    dec_moment,
    dec_square,
):
    rows = activations.shape[0] * 4
    count, width = activations.shape
    latents = encoder.shape[1]
    half = width // 2
    features = 4 * width
    z, i = lax.axis_index("latent"), lax.axis_index("dp")
    place = jnp.stack([z, i]).astype(jnp.int32)

    def along(value, pairs):
        return lax.ppermute(value, "latent", pairs)

    def flip(value, bits, planes=(0, 1, 2, 3)):
        pairs = [(4 * p + k, 4 * p + (k ^ bits)) for p in planes for k in range(4)]
        return lax.ppermute(value, ("latent", "dp"), pairs)

    ends = [(1, 0), (2, 3)]
    low = along(activations, [(0, 1), (1, 2), (2, 3)])
    high = along(activations, [(1, 0), (2, 1), (3, 2)])
    across = along(activations, [(0, 2), (3, 1)])

    (enc_own,) = local_kernel(
        encoder_body,
        [shape((width + EXTRA, latents), BF16)],
        place,
        encoder,
        enc_bias.reshape(1, -1),
    )
    enc_chip, enc_core = flip(enc_own, 2), flip(enc_own, 1)
    (dec_own,) = local_kernel(
        decoder_body,
        [shape((width + EXTRA, latents), BF16)],
        place,
        decoder,
        after=(enc_core,),
    )
    dec_late = behind(dec_own, enc_chip)
    dec_chip, dec_core = flip(dec_late, 2), flip(dec_late, 1)
    (onward,) = local_kernel(
        onward_body, [shape((count, width), BF16)], place, low, high
    )
    relay1 = along(onward, ends)
    relay2 = along(across, ends)

    up, down, beyond = local_kernel(
        pieces_body, [shape((half, latents), BF16)] * 3, place, dec_own
    )
    dec_pieces = [
        along(up, [(0, 1), (1, 2)]),
        along(down, [(2, 1), (3, 2)]),
        along(beyond, [(0, 2), (3, 1)]),
    ]
    enc_both = flip(behind(enc_chip, relay1, relay2, *dec_pieces), 1)
    enc = [enc_own, enc_core, enc_chip, enc_both]
    dec = [dec_own, dec_core, dec_chip, flip(dec_chip, 1)]

    rows_own = local_kernel(
        stack_body,
        [shape((3 * half // 2, latents), BF16)] * 2,
        place,
        *dec_pieces,
        after=(dec_chip,),
    )
    rows_chip = [flip(piece, 2, (1, 2)) for piece in rows_own]
    codes, mask, inputs, active = local_kernel(
        codes_body,
        [
            shape((count, latents), BF16),
            shape((count, latents), BF16),
            shape((count, features), BF16),
            shape((1, latents), F32),
        ],
        place,
        activations,
        low,
        high,
        across,
        relay1,
        relay2,
        *enc,
        after=(*rows_own, dec[1], dec[3]),
        scratch=[pltpu.VMEM((1, latents), F32)],
    )
    codes_low = along(codes, [(0, 1), (1, 2)])
    codes_high = along(codes, [(2, 1), (3, 2)])
    codes_across = along(codes, [(0, 2), (3, 1)])
    (turned,) = local_kernel(
        turn_body, [shape((features, count), BF16)], place, inputs
    )
    rows_core = [flip(behind(piece, turned), 1, (1, 2)) for piece in rows_own]
    rows_both = [flip(behind(piece, codes_across), 1, (1, 2)) for piece in rows_chip]

    (own_error,) = local_kernel(
        error_body,
        [shape((count, features // 2), BF16)],
        place,
        codes,
        codes_low,
        codes_high,
        codes_across,
        *dec,
        *rows_own,
        *rows_core,
        *rows_chip,
        *rows_both,
        inputs,
    )
    swapped = along(own_error, [(1, 2), (2, 1)])
    passed = along(own_error, [(1, 0), (2, 3)])
    direct = along(own_error, [(2, 0), (1, 3)])

    def across_chips(kept, row, *send):
        packed, row_sum = local_kernel(
            pack_body,
            [shape((kept.shape[0] + EXTRA, latents), F32), shape((1, latents), F32)],
            place,
            kept,
            row,
            *[flip(piece, 1) for piece in send],
        )
        return packed, flip(packed.astype(jnp.float16), 2), row_sum

    blocks = [shape((half + 8, latents), F32)] + [shape((half, latents), F32)] * 3
    part, near, *near_blocks = local_kernel(
        functools.partial(near_body, rows),
        [shape((count, latents), F32), shape((count, features // 2), BF16), *blocks],
        place,
        own_error,
        passed,
        codes,
        active,
        *dec,
        after=(swapped,),
    )
    send_far, send_near, keep_far, keep_near = near_blocks
    near_packed, near_received, active_sum = across_chips(keep_far, active, send_far)
    near_kept = keep_near, flip(send_near, 1)
    far, far_send, far_keep = local_kernel(
        functools.partial(far_error_body, rows),
        [shape((count, features // 2), BF16)] + [shape((half, latents), F32)] * 2,
        place,
        swapped,
        direct,
        codes,
        after=(near_packed,),
        cost=NOTABLE,
    )
    grad_low, bias_sum, norms, *send_far_enc = local_kernel(
        functools.partial(code_grad_body, rows),
        [
            shape((count, latents), BF16),
            shape((1, latents), F32),
            shape((1, latents), F32),
            shape((half + 8, latents), F32),
            shape((half, latents), F32),
        ],
        place,
        far,
        behind(part, near_received),
        mask,
        *dec,
        turned,
        cost=NOTABLE,
    )
    far_packed, far_received, _ = across_chips(far_keep, active, far_send)
    error, enc_send_near, enc_keep_far, enc_keep_near, send_near, keep_near = local_kernel(
        functools.partial(rest_body, rows),
        [shape((count, width), BF16)]
        + [shape((width, latents), F32)] * 3
        + [shape((half, latents), F32)] * 2,
        place,
        turned,
        grad_low,
        near,
        far,
        codes,
        after=(far_packed,),
    )
    far_kept = keep_near, flip(send_near, 1)
    enc_packed, enc_received, bias_here = across_chips(enc_keep_far, bias_sum, *send_far_enc)
    enc_kept = enc_keep_near, flip(enc_send_near, 1)

    decoder, dec_moment, dec_square, encoder, enc_moment, enc_square = lax.optimization_barrier(
        (decoder, dec_moment, dec_square, encoder, enc_moment, enc_square, enc_packed)
    )[:6]
    near_block, active_there = unpack(near_received)
    far_block, _ = unpack(far_received)
    enc_block, bias_there = unpack(enc_received)
    near_grad = near_kept[0] + near_kept[1] + near_block
    far_grad = far_kept[0] + far_kept[1] + far_block
    active_sum = active_sum + active_there
    grad_encoder = enc_kept[0] + enc_kept[1] + enc_block
    new_enc_bias, new_bias_moment, new_bias_square = [
        value.reshape(-1)
        for value in local_kernel(
            bias_step_body,
            [shape((1, enc_bias.shape[0]), F32)] * 3,
            place,
            enc_bias.reshape(1, -1),
            bias_moment.reshape(1, -1),
            bias_square.reshape(1, -1),
            bias_here,
            bias_there,
        )
    ]
    new_encoder, new_enc_moment, new_enc_square = adam_update(
        encoder, grad_encoder, enc_moment, enc_square
    )
    step = width // 4
    block = pl.BlockSpec((step, latents), lambda r: (r, 0))
    in_half = pl.BlockSpec((step, latents), lambda r: (r % 2, 0))
    row = pl.BlockSpec((1, latents), lambda r: (0, 0))
    new_decoder, new_dec_moment, new_dec_square = pl.pallas_call(
        functools.partial(decoder_step_body, rows),
        grid=(4,),
        out_shape=[shape((width, latents), F32)] * 3,
        in_specs=[SMEM, block, block, block, in_half, in_half, row, row],
        out_specs=[block] * 3,
        compiler_params=pltpu.CompilerParams(vmem_limit_bytes=12 * 1024 * 1024),
        cost_estimate=pl.CostEstimate(flops=1, bytes_accessed=1, transcendentals=0),
    )(place, decoder, dec_moment, dec_square, near_grad, far_grad, active_sum, norms)
    return (
        error,
        new_encoder,
        new_enc_bias,
        new_decoder,
        new_enc_moment,
        new_enc_square,
        new_bias_moment,
        new_bias_square,
        new_dec_moment,
        new_dec_square,
    )


def solution(mesh):
    in_specs = (
        P(("groups", "dp"), "latent"),
        P(("groups", "dp"), "latent"),
        P(("groups", "latent", "dp")),
        P(("groups", "dp"), "latent"),
        P(("groups", "dp"), "latent"),
        P(("groups", "dp"), "latent"),
        P(("groups", "latent", "dp")),
        P(("groups", "latent", "dp")),
        P(("groups", "dp"), "latent"),
        P(("groups", "dp"), "latent"),
    )
    out_specs = (
        P(("groups", "dp"), "latent"),
        P(("groups", "dp"), "latent"),
        P(("groups", "latent", "dp")),
        P(("groups", "dp"), "latent"),
        P(("groups", "dp"), "latent"),
        P(("groups", "dp"), "latent"),
        P(("groups", "latent", "dp")),
        P(("groups", "latent", "dp")),
        P(("groups", "dp"), "latent"),
        P(("groups", "dp"), "latent"),
    )
    line = mesh.shape["latent"] == 4 and mesh.shape["dp"] == 4
    plan = line_shards if line else shards
    return jax.shard_map(plan, mesh=mesh, in_specs=in_specs, out_specs=out_specs, check_vma=False)
```

```python
import functools
import math

import jax
import jax.numpy as jnp
from jax import lax
from jax.experimental import pallas as pl
from jax.experimental.pallas import tpu as pltpu
from jax.sharding import PartitionSpec as P

ADAM_STEP = 1000


first_decay = 0.9
second_decay = 0.999
learn_rate = 0.001
epsilon = 1e-08

F32 = jnp.float32
BF16 = jnp.bfloat16


def adam_update(param, grad, moment, square):
    moment_new = first_decay * moment + (1.0 - first_decay) * grad
    square_new = second_decay * square + (1.0 - second_decay) * grad * grad
    first_fix = 1.0 - first_decay**ADAM_STEP
    second_fix = 1.0 - second_decay**ADAM_STEP
    param_new = param - learn_rate * (moment_new / first_fix) / (
        jnp.sqrt(square_new / second_fix) + epsilon
    )
    return (param_new, moment_new, square_new)


def shards(
    activations,
    encoder,
    enc_bias,
    decoder,
    enc_moment,
    enc_square,
    bias_moment,
    bias_square,
    dec_moment,
    dec_square,
):
    row_count = activations.shape[0] * lax.axis_size("dp")
    loss_scale = 2.0 / row_count
    inputs = lax.all_gather(activations, "latent", axis=1, tiled=True)
    enc_low, dec_low = (
        lax.all_gather(encoder.astype(jnp.bfloat16), "dp", axis=0, tiled=True),
        lax.all_gather(decoder.astype(jnp.bfloat16), "dp", axis=0, tiled=True),
    )
    bias_full = lax.all_gather(enc_bias, "dp", axis=0, tiled=True)
    square_sums = lax.psum(jnp.sum(decoder * decoder, axis=0), "dp")
    column_norms = jnp.sqrt(square_sums + 1e-06)
    preact = jnp.dot(inputs, enc_low, preferred_element_type=jnp.float32) + bias_full
    latent_codes = jnp.maximum(preact, 0.0).astype(jnp.bfloat16)
    partial_sums = lax.dot_general(
        latent_codes, dec_low, (((1,), (1,)), ((), ())), preferred_element_type=jnp.float32
    )
    rebuilt = lax.psum_scatter(partial_sums, "latent", scatter_dimension=1, tiled=True)
    error = (activations.astype(jnp.float32) - rebuilt).astype(jnp.bfloat16)
    full_error = lax.all_gather(error, "latent", axis=1, tiled=True)
    active_sum = lax.psum(jnp.sum(latent_codes.astype(jnp.float32), axis=0), "dp")
    grad_dec_rows = -loss_scale * lax.dot_general(
        full_error, latent_codes, (((0,), (0,)), ((), ())), preferred_element_type=jnp.float32
    )
    code_grad = (
        -loss_scale * jnp.dot(full_error, dec_low, preferred_element_type=jnp.float32)
        + column_norms / row_count
    )
    grad_preact = jnp.where(preact > 0.0, code_grad, 0.0)
    grad_encoder = lax.dot_general(
        inputs,
        grad_preact.astype(jnp.bfloat16),
        (((0,), (0,)), ((), ())),
        preferred_element_type=jnp.float32,
    )
    grad_bias = jnp.sum(grad_preact, axis=0)
    grad_encoder, grad_dec_rows, grad_bias = (
        lax.psum_scatter(grad_encoder, "dp", scatter_dimension=0, tiled=True),
        lax.psum_scatter(grad_dec_rows, "dp", scatter_dimension=0, tiled=True),
        lax.psum_scatter(grad_bias, "dp", scatter_dimension=0, tiled=True),
    )
    grad_decoder = grad_dec_rows + decoder * (active_sum / column_norms) / row_count
    new_encoder, new_enc_moment, new_enc_square = adam_update(
        encoder, grad_encoder, enc_moment, enc_square
    )
    new_enc_bias, new_bias_moment, new_bias_square = adam_update(
        enc_bias, grad_bias, bias_moment, bias_square
    )
    new_decoder, new_dec_moment, new_dec_square = adam_update(
        decoder, grad_decoder, dec_moment, dec_square
    )
    return (
        error,
        new_encoder,
        new_enc_bias,
        new_decoder,
        new_enc_moment,
        new_enc_square,
        new_bias_moment,
        new_bias_square,
        new_dec_moment,
        new_dec_square,
    )


VMEM = pl.BlockSpec(memory_space=pltpu.VMEM)
SMEM = pl.BlockSpec(memory_space=pltpu.SMEM)
ANY = pl.BlockSpec(memory_space=pl.ANY)
EXTRA = 16
NOTABLE = 10**10


def local_kernel(body, outs, place, *args, after=(), scratch=(), cost=1):
    def run(place, *refs):
        body(place, *refs[: len(args)], *refs[len(args) + len(after) :])

    held = sum(a.size * jnp.dtype(a.dtype).itemsize for a in (*args, *outs))
    return pl.pallas_call(
        run,
        out_shape=outs,
        in_specs=[SMEM] + [VMEM] * len(args) + [ANY] * len(after),
        out_specs=[VMEM] * len(outs),
        scratch_shapes=scratch,
        compiler_params=pltpu.CompilerParams(vmem_limit_bytes=held + 6 * 1024 * 1024),
        cost_estimate=pl.CostEstimate(flops=cost, bytes_accessed=1, transcendentals=0),
    )(place, *args, *after)


def shape(dims, dtype):
    return jax.ShapeDtypeStruct(dims, dtype)


def columns(start, width):
    return pl.ds(pl.multiple_of(start, width), width)


def three_rows(row):
    high = row.astype(BF16).astype(F32)
    middle = (row - high).astype(BF16).astype(F32)
    low = row - high - middle
    at = lax.broadcasted_iota(jnp.int32, (EXTRA, row.shape[1]), 0)
    rows = jnp.where(at == 0, high, jnp.where(at == 1, middle, jnp.where(at == 2, low, 0.0)))
    return rows.astype(BF16)


def behind(value, *others):
    return lax.optimization_barrier((value, *others))[0]


def one_row(rows):
    return jnp.sum(rows.astype(F32), axis=0, keepdims=True)


def encoder_body(place, encoder, bias, out):
    depth = encoder.shape[0]
    out[:depth] = encoder[...].astype(BF16)
    out[depth:] = three_rows(jnp.concatenate([bias[...]] * 4, axis=1))


def decoder_body(place, decoder, out):
    depth = decoder.shape[0]
    value = decoder[...]
    out[:depth] = value.astype(BF16)
    out[depth:] = three_rows(jnp.sum(value * value, axis=0, keepdims=True))


def codes_body(place, full, enc0, enc1, enc2, enc3, codes, mask, active, bias):
    i = place[1]
    width = full.shape[1] // 4
    total = jnp.zeros(codes.shape, F32)
    piece = codes.shape[1] // 4
    for t, enc in enumerate((enc0, enc1, enc2, enc3)):
        b = i ^ t
        total += jnp.dot(
            full[:, columns(b * width, width)], enc[:width, :], preferred_element_type=F32
        )
        bias[:, columns(b * piece, piece)] = one_row(enc[width:, :piece])
    preact = total + bias[...]
    low_codes = jnp.maximum(preact, 0.0).astype(BF16)
    codes[...] = low_codes
    mask[...] = (preact > 0.0).astype(F32).astype(BF16)
    active[...] = jnp.sum(low_codes.astype(F32), axis=0, keepdims=True)


def pieces_body(place, dec, up, down, across):
    z = place[0]
    half = up.shape[0]
    for out, second in ((up, z >= 1), (down, z >= 3), (across, z < 2)):
        out[...] = dec[pl.ds(pl.multiple_of(jnp.where(second, half, 0), half), half), :]


def stack_body(place, *refs):
    *pieces, out = refs
    size = pieces[0].shape[0]
    for k, piece in enumerate(pieces):
        out[k * size : (k + 1) * size] = piece[...]


def turn_body(place, full, turned):
    turned[...] = full[...].T


def error_body(place, own, low, high, across, dec0, dec1, dec2, dec3, *refs):
    *rows, inputs, error = refs
    z, i = place[0], place[1]
    half = rows[0].shape[0] // 3
    shift = pl.multiple_of(jnp.where(z >= 2, half, 0), half)
    for t, dec in enumerate((dec0, dec1, dec2, dec3)):
        lefts = (own, low, high, across)
        rights = [rows[t][m * half : (m + 1) * half, :] for m in range(3)]
        total = jnp.zeros((own.shape[0], half), F32)
        for left, right in zip(lefts, [dec[pl.ds(shift, half), :]] + rights):
            total += lax.dot_general(
                left[...], right, (((1,), (1,)), ((), ())), preferred_element_type=F32
            )
        q = i ^ t
        given = inputs[:, columns(q * 2 * half + shift, half)].astype(F32)
        error[:, columns(q * half, half)] = (given - total).astype(BF16)


def pick(place, middle, end, out):
    z = place[0]
    is_middle = (z == 1) | (z == 2)

    @pl.when(is_middle)
    def _():
        out[...] = middle[...]

    @pl.when(jnp.logical_not(is_middle))
    def _():
        out[...] = end[...]


def decoder_grads(scale, i, error, codes, slots, outs):
    half = error.shape[1] // 4
    for slot, out in zip(slots, outs):
        out[:half] = scale * lax.dot_general(
            error[:, columns((i ^ slot) * half, half)],
            codes[...],
            (((0,), (0,)), ((), ())),
            preferred_element_type=F32,
        )


def back_through(i, error, decs, shift):
    half = error.shape[1] // 4
    return functools.reduce(
        jnp.add,
        [
            jnp.dot(
                error[:, columns((i ^ t) * half, half)],
                dec[pl.ds(pl.multiple_of(shift, half), half), :],
                preferred_element_type=F32,
            )
            for t, dec in enumerate(decs)
        ],
    )


def near_body(rows, place, mine, passed, codes, active, dec0, dec1, dec2, dec3, part, near, *outs):
    z, i = place[0], place[1]
    half = mine.shape[1] // 4
    pick(place, mine, passed, near)
    decoder_grads(-2.0 / rows, i, near, codes, (3, 1, 2, 0), outs)
    outs[0][half:] = jnp.broadcast_to(active[...], (outs[0].shape[0] - half, active.shape[1]))
    part[...] = back_through(i, near, (dec0, dec1, dec2, dec3), jnp.where(z >= 2, half, 0))


def far_error_body(rows, place, swapped, direct, codes, far, send, kept):
    pick(place, swapped, direct, far)
    decoder_grads(-2.0 / rows, place[1], far, codes, (3, 2), (send, kept))


def code_grad_body(
    rows, place, far, part, mask, dec0, dec1, dec2, dec3, turned, grad_low, bias_sum, norms, *sends
):
    z, i = place[0], place[1]
    half = far.shape[1] // 4
    width = 2 * half
    decs = (dec0, dec1, dec2, dec3)
    total = part[...] + back_through(i, far, decs, jnp.where(z >= 2, 0, half))
    squares = functools.reduce(jnp.add, [one_row(dec[width:, :]) for dec in decs])
    column_norms = jnp.sqrt(squares + 1e-06)
    norms[...] = column_norms
    code_grad = (-2.0 / rows) * total + column_norms / rows
    grad = jnp.where(mask[...] > 0, code_grad, 0.0)
    grad_low[...] = grad.astype(BF16)
    row = jnp.sum(grad, axis=0, keepdims=True)
    bias_sum[...] = row
    at = pl.multiple_of((i ^ 3) * width, width)
    block = jnp.dot(turned[pl.ds(at, width), :], grad_low[...], preferred_element_type=F32)
    sends[0][:half] = block[:half]
    sends[0][half:] = jnp.broadcast_to(row, (sends[0].shape[0] - half, row.shape[1]))
    sends[1][...] = block[half:]


def encoder_grads(i, turned, grad_low, slots, outs):
    width = turned.shape[0] // 4
    for slot, out in zip(slots, outs):
        at = pl.ds(pl.multiple_of((i ^ slot) * width, width), width)
        out[:width] = jnp.dot(turned[at, :], grad_low[...], preferred_element_type=F32)


def rest_body(rows, place, turned, grad_low, near, far, codes, home, send, kept_far, kept, *outs):
    z, i = place[0], place[1]
    half = far.shape[1] // 4
    shift = jnp.where(z >= 2, 0, half)
    encoder_grads(i, turned, grad_low, (2, 1, 0), (kept_far, send, kept))
    decoder_grads(-2.0 / rows, i, far, codes, (1, 0), outs)
    home[:, columns(half - shift, half)] = near[:, columns(z * half, half)]
    home[:, columns(shift, half)] = far[:, columns(z * half, half)]


def power(values):
    largest = jnp.max(jnp.abs(values), axis=0, keepdims=True)
    return jnp.ceil(jnp.log(jnp.maximum(largest, 1e-30)) * (1.0 / math.log(2.0)))


def scale_of(exponent):
    return jnp.exp(exponent * math.log(2.0))


def pack_body(place, kept, row, *refs):
    received, (packed, row_sum) = refs[:-2], refs[-2:]
    width = kept.shape[0]
    block = width // len(received)
    total = jnp.concatenate([piece[:block] for piece in received], axis=0) + kept[...]
    exponent = power(total)
    packed[:width] = total * scale_of(14.0 - exponent)
    sums = row[...]
    if received[0].shape[0] > block:
        sums += received[0][block : block + 1]
    row_sum[...] = sums
    row_exponent = power(sums)
    parts = three_rows(sums * scale_of(14.0 - row_exponent)).astype(F32)
    at = lax.broadcasted_iota(jnp.int32, parts.shape, 0)
    parts = jnp.where(at == 3, exponent, jnp.where(at == 4, row_exponent, parts))
    packed[width:] = parts


def unpack(packed):
    width = packed.shape[0] - EXTRA
    rows = packed[width:].astype(F32)
    block = packed[:width].astype(F32) * scale_of(rows[3:4] - 14.0)
    row = (rows[0:1] + rows[1:2] + rows[2:3]) * scale_of(rows[4:5] - 14.0)
    return block, row


def bias_step_body(place, param, moment, square, here, there, param_out, moment_out, square_out):
    width = param.shape[1]
    grad = here[...] + there[...]
    pieces = [grad[:, b * width : (b + 1) * width] for b in range(4)]
    own = functools.reduce(
        jnp.add, [jnp.where(place[1] == b, piece, 0.0) for b, piece in enumerate(pieces)]
    )
    param_out[...], moment_out[...], square_out[...] = adam_update(
        param[...], own, moment[...], square[...]
    )


def decoder_step_body(
    rows, place, param, moment, square, near, far, active, norms, param_out, moment_out, square_out
):
    is_near = (pl.program_id(0) < pl.num_programs(0) // 2) == (place[0] < 2)
    grad = jnp.where(is_near, near[...], far[...])
    grad += param[...] * (active[...] / norms[...]) / rows
    param_out[...], moment_out[...], square_out[...] = adam_update(
        param[...], grad, moment[...], square[...]
    )


def line_shards(
    activations,
    encoder,
    enc_bias,
    decoder,
    enc_moment,
    enc_square,
    bias_moment,
    bias_square,
    dec_moment,
    dec_square,
):
    rows = activations.shape[0] * 4
    count, width = activations.shape
    latents = encoder.shape[1]
    half = width // 2
    features = 4 * width
    z, i = lax.axis_index("latent"), lax.axis_index("dp")
    place = jnp.stack([z, i]).astype(jnp.int32)

    def along(value, pairs):
        return lax.ppermute(value, "latent", pairs)

    def flip(value, bits, planes=(0, 1, 2, 3)):
        pairs = [(4 * p + k, 4 * p + (k ^ bits)) for p in planes for k in range(4)]
        return lax.ppermute(value, ("latent", "dp"), pairs)

    inputs = lax.all_gather(activations, "latent", axis=1, tiled=True)

    (dec_own,) = local_kernel(
        decoder_body, [shape((width + EXTRA, latents), BF16)], place, decoder
    )
    pieces = local_kernel(pieces_body, [shape((half, latents), BF16)] * 3, place, dec_own)
    dec_pieces = [
        along(pieces[0], [(0, 1), (1, 2)]),
        along(pieces[1], [(2, 1), (3, 2)]),
        along(pieces[2], [(0, 2), (3, 1)]),
    ]
    (enc_own,) = local_kernel(
        encoder_body,
        [shape((width + EXTRA, latents), BF16)],
        place,
        encoder,
        enc_bias.reshape(1, -1),
        after=(pieces[0],),
    )
    enc_chip, enc_core = flip(enc_own, 2), flip(enc_own, 1)
    enc = [enc_own, enc_core, enc_chip, flip(enc_chip, 1)]
    (rows_own,) = local_kernel(
        stack_body, [shape((3 * half, latents), BF16)], place, *dec_pieces, after=(enc_chip,)
    )
    rows_chip, rows_core = flip(rows_own, 2, (1, 2)), flip(rows_own, 1, (1, 2))
    dec_late = behind(dec_own, rows_core)
    dec_chip, dec_core = flip(dec_late, 2), flip(dec_late, 1)
    dec = [dec_own, dec_core, dec_chip, flip(dec_chip, 1)]
    rows_both = flip(rows_chip, 1, (1, 2))

    codes, mask, active = local_kernel(
        codes_body,
        [
            shape((count, latents), BF16),
            shape((count, latents), BF16),
            shape((1, latents), F32),
        ],
        place,
        inputs,
        *enc,
        after=(rows_both,),
        scratch=[pltpu.VMEM((1, latents), F32)],
    )
    codes_low = along(codes, [(0, 1), (1, 2)])
    codes_high = along(codes, [(2, 1), (3, 2)])
    codes_across = along(codes, [(0, 2), (3, 1)])
    (turned,) = local_kernel(
        turn_body, [shape((features, count), BF16)], place, inputs
    )
    (own_error,) = local_kernel(
        error_body,
        [shape((count, features // 2), BF16)],
        place,
        codes,
        codes_low,
        codes_high,
        codes_across,
        *dec,
        rows_own,
        rows_core,
        rows_chip,
        rows_both,
        inputs,
    )
    swapped = along(own_error, [(1, 2), (2, 1)])
    passed = along(own_error, [(1, 0), (2, 3)])
    direct = along(own_error, [(2, 0), (1, 3)])

    def across_chips(kept, row, *send):
        packed, row_sum = local_kernel(
            pack_body,
            [shape((kept.shape[0] + EXTRA, latents), F32), shape((1, latents), F32)],
            place,
            kept,
            row,
            *[flip(piece, 1) for piece in send],
        )
        return packed, flip(packed.astype(jnp.float16), 2), row_sum

    blocks = [shape((half + 8, latents), F32)] + [shape((half, latents), F32)] * 3
    part, near, *near_blocks = local_kernel(
        functools.partial(near_body, rows),
        [shape((count, latents), F32), shape((count, features // 2), BF16), *blocks],
        place,
        own_error,
        passed,
        codes,
        active,
        *dec,
        after=(swapped,),
    )
    send_far, send_near, keep_far, keep_near = near_blocks
    near_packed, near_received, active_sum = across_chips(keep_far, active, send_far)
    near_kept = keep_near, flip(send_near, 1)
    far, far_send, far_keep = local_kernel(
        functools.partial(far_error_body, rows),
        [shape((count, features // 2), BF16)] + [shape((half, latents), F32)] * 2,
        place,
        swapped,
        direct,
        codes,
        after=(near_packed,),
        cost=NOTABLE,
    )
    grad_low, bias_sum, norms, *send_far_enc = local_kernel(
        functools.partial(code_grad_body, rows),
        [
            shape((count, latents), BF16),
            shape((1, latents), F32),
            shape((1, latents), F32),
            shape((half + 8, latents), F32),
            shape((half, latents), F32),
        ],
        place,
        far,
        behind(part, near_received),
        mask,
        *dec,
        turned,
        cost=NOTABLE,
    )
    far_packed, far_received, _ = across_chips(far_keep, active, far_send)
    error, enc_send_near, enc_keep_far, enc_keep_near, send_near, keep_near = local_kernel(
        functools.partial(rest_body, rows),
        [shape((count, width), BF16)]
        + [shape((width, latents), F32)] * 3
        + [shape((half, latents), F32)] * 2,
        place,
        turned,
        grad_low,
        near,
        far,
        codes,
        after=(far_packed,),
    )
    far_kept = keep_near, flip(send_near, 1)
    enc_packed, enc_received, bias_here = across_chips(enc_keep_far, bias_sum, *send_far_enc)
    enc_kept = enc_keep_near, flip(enc_send_near, 1)

    decoder, dec_moment, dec_square, encoder, enc_moment, enc_square = lax.optimization_barrier(
        (decoder, dec_moment, dec_square, encoder, enc_moment, enc_square, enc_packed)
    )[:6]
    near_block, active_there = unpack(near_received)
    far_block, _ = unpack(far_received)
    enc_block, bias_there = unpack(enc_received)
    near_grad = near_kept[0] + near_kept[1] + near_block
    far_grad = far_kept[0] + far_kept[1] + far_block
    active_sum = active_sum + active_there
    grad_encoder = enc_kept[0] + enc_kept[1] + enc_block
    new_enc_bias, new_bias_moment, new_bias_square = [
        value.reshape(-1)
        for value in local_kernel(
            bias_step_body,
            [shape((1, enc_bias.shape[0]), F32)] * 3,
            place,
            enc_bias.reshape(1, -1),
            bias_moment.reshape(1, -1),
            bias_square.reshape(1, -1),
            bias_here,
            bias_there,
        )
    ]
    new_encoder, new_enc_moment, new_enc_square = adam_update(
        encoder, grad_encoder, enc_moment, enc_square
    )
    step = width // 4
    block = pl.BlockSpec((step, latents), lambda r: (r, 0))
    in_half = pl.BlockSpec((step, latents), lambda r: (r % 2, 0))
    row = pl.BlockSpec((1, latents), lambda r: (0, 0))
    new_decoder, new_dec_moment, new_dec_square = pl.pallas_call(
        functools.partial(decoder_step_body, rows),
        grid=(4,),
        out_shape=[shape((width, latents), F32)] * 3,
        in_specs=[SMEM, block, block, block, in_half, in_half, row, row],
        out_specs=[block] * 3,
        compiler_params=pltpu.CompilerParams(vmem_limit_bytes=12 * 1024 * 1024),
        cost_estimate=pl.CostEstimate(flops=1, bytes_accessed=1, transcendentals=0),
    )(place, decoder, dec_moment, dec_square, near_grad, far_grad, active_sum, norms)
    return (
        error,
        new_encoder,
        new_enc_bias,
        new_decoder,
        new_enc_moment,
        new_enc_square,
        new_bias_moment,
        new_bias_square,
        new_dec_moment,
        new_dec_square,
    )


def solution(mesh):
    in_specs = (
        P(("groups", "dp"), "latent"),
        P(("groups", "dp"), "latent"),
        P(("groups", "latent", "dp")),
        P(("groups", "dp"), "latent"),
        P(("groups", "dp"), "latent"),
        P(("groups", "dp"), "latent"),
        P(("groups", "latent", "dp")),
        P(("groups", "latent", "dp")),
        P(("groups", "dp"), "latent"),
        P(("groups", "dp"), "latent"),
    )
    out_specs = (
        P(("groups", "dp"), "latent"),
        P(("groups", "dp"), "latent"),
        P(("groups", "latent", "dp")),
        P(("groups", "dp"), "latent"),
        P(("groups", "dp"), "latent"),
        P(("groups", "dp"), "latent"),
        P(("groups", "latent", "dp")),
        P(("groups", "latent", "dp")),
        P(("groups", "dp"), "latent"),
        P(("groups", "dp"), "latent"),
    )
    line = mesh.shape["latent"] == 4 and mesh.shape["dp"] == 4
    plan = line_shards if line else shards
    return jax.shard_map(plan, mesh=mesh, in_specs=in_specs, out_specs=out_specs, check_vma=False)
```

```python
import functools
import math

import jax
import jax.numpy as jnp
from jax import lax
from jax.experimental import pallas as pl
from jax.experimental.pallas import tpu as pltpu
from jax.sharding import PartitionSpec as P

ADAM_STEP = 1000


first_decay = 0.9
second_decay = 0.999
learn_rate = 0.001
epsilon = 1e-08

F32 = jnp.float32
BF16 = jnp.bfloat16


def adam_update(param, grad, moment, square):
    moment_new = first_decay * moment + (1.0 - first_decay) * grad
    square_new = second_decay * square + (1.0 - second_decay) * grad * grad
    first_fix = 1.0 - first_decay**ADAM_STEP
    second_fix = 1.0 - second_decay**ADAM_STEP
    param_new = param - learn_rate * (moment_new / first_fix) / (
        jnp.sqrt(square_new / second_fix) + epsilon
    )
    return (param_new, moment_new, square_new)


def shards(
    activations,
    encoder,
    enc_bias,
    decoder,
    enc_moment,
    enc_square,
    bias_moment,
    bias_square,
    dec_moment,
    dec_square,
):
    row_count = activations.shape[0] * lax.axis_size("dp")
    loss_scale = 2.0 / row_count
    inputs = lax.all_gather(activations, "latent", axis=1, tiled=True)
    enc_low, dec_low = (
        lax.all_gather(encoder.astype(jnp.bfloat16), "dp", axis=0, tiled=True),
        lax.all_gather(decoder.astype(jnp.bfloat16), "dp", axis=0, tiled=True),
    )
    bias_full = lax.all_gather(enc_bias, "dp", axis=0, tiled=True)
    square_sums = lax.psum(jnp.sum(decoder * decoder, axis=0), "dp")
    column_norms = jnp.sqrt(square_sums + 1e-06)
    preact = jnp.dot(inputs, enc_low, preferred_element_type=jnp.float32) + bias_full
    latent_codes = jnp.maximum(preact, 0.0).astype(jnp.bfloat16)
    partial_sums = lax.dot_general(
        latent_codes, dec_low, (((1,), (1,)), ((), ())), preferred_element_type=jnp.float32
    )
    rebuilt = lax.psum_scatter(partial_sums, "latent", scatter_dimension=1, tiled=True)
    error = (activations.astype(jnp.float32) - rebuilt).astype(jnp.bfloat16)
    full_error = lax.all_gather(error, "latent", axis=1, tiled=True)
    active_sum = lax.psum(jnp.sum(latent_codes.astype(jnp.float32), axis=0), "dp")
    grad_dec_rows = -loss_scale * lax.dot_general(
        full_error, latent_codes, (((0,), (0,)), ((), ())), preferred_element_type=jnp.float32
    )
    code_grad = (
        -loss_scale * jnp.dot(full_error, dec_low, preferred_element_type=jnp.float32)
        + column_norms / row_count
    )
    grad_preact = jnp.where(preact > 0.0, code_grad, 0.0)
    grad_encoder = lax.dot_general(
        inputs,
        grad_preact.astype(jnp.bfloat16),
        (((0,), (0,)), ((), ())),
        preferred_element_type=jnp.float32,
    )
    grad_bias = jnp.sum(grad_preact, axis=0)
    grad_encoder, grad_dec_rows, grad_bias = (
        lax.psum_scatter(grad_encoder, "dp", scatter_dimension=0, tiled=True),
        lax.psum_scatter(grad_dec_rows, "dp", scatter_dimension=0, tiled=True),
        lax.psum_scatter(grad_bias, "dp", scatter_dimension=0, tiled=True),
    )
    grad_decoder = grad_dec_rows + decoder * (active_sum / column_norms) / row_count
    new_encoder, new_enc_moment, new_enc_square = adam_update(
        encoder, grad_encoder, enc_moment, enc_square
    )
    new_enc_bias, new_bias_moment, new_bias_square = adam_update(
        enc_bias, grad_bias, bias_moment, bias_square
    )
    new_decoder, new_dec_moment, new_dec_square = adam_update(
        decoder, grad_decoder, dec_moment, dec_square
    )
    return (
        error,
        new_encoder,
        new_enc_bias,
        new_decoder,
        new_enc_moment,
        new_enc_square,
        new_bias_moment,
        new_bias_square,
        new_dec_moment,
        new_dec_square,
    )


VMEM = pl.BlockSpec(memory_space=pltpu.VMEM)
SMEM = pl.BlockSpec(memory_space=pltpu.SMEM)
ANY = pl.BlockSpec(memory_space=pl.ANY)
EXTRA = 16
NOTABLE = 10**10


def local_kernel(body, outs, place, *args, after=(), scratch=(), cost=1):
    def run(place, *refs):
        body(place, *refs[: len(args)], *refs[len(args) + len(after) :])

    held = sum(a.size * jnp.dtype(a.dtype).itemsize for a in (*args, *outs))
    return pl.pallas_call(
        run,
        out_shape=outs,
        in_specs=[SMEM] + [VMEM] * len(args) + [ANY] * len(after),
        out_specs=[VMEM] * len(outs),
        scratch_shapes=scratch,
        compiler_params=pltpu.CompilerParams(vmem_limit_bytes=held + 6 * 1024 * 1024),
        cost_estimate=pl.CostEstimate(flops=cost, bytes_accessed=1, transcendentals=0),
    )(place, *args, *after)


def shape(dims, dtype):
    return jax.ShapeDtypeStruct(dims, dtype)


def columns(start, width):
    return pl.ds(pl.multiple_of(start, width), width)


def three_rows(row):
    high = row.astype(BF16).astype(F32)
    middle = (row - high).astype(BF16).astype(F32)
    low = row - high - middle
    at = lax.broadcasted_iota(jnp.int32, (EXTRA, row.shape[1]), 0)
    rows = jnp.where(at == 0, high, jnp.where(at == 1, middle, jnp.where(at == 2, low, 0.0)))
    return rows.astype(BF16)


def behind(value, *others):
    return lax.optimization_barrier((value, *others))[0]


def one_row(rows):
    return jnp.sum(rows.astype(F32), axis=0, keepdims=True)


def encoder_body(place, encoder, bias, out):
    depth = encoder.shape[0]
    out[:depth] = encoder[...].astype(BF16)
    out[depth:] = three_rows(jnp.concatenate([bias[...]] * 4, axis=1))


def decoder_body(place, decoder, out):
    depth = decoder.shape[0]
    value = decoder[...]
    out[:depth] = value.astype(BF16)
    out[depth:] = three_rows(jnp.sum(value * value, axis=0, keepdims=True))


def codes_body(
    place,
    own,
    low,
    high,
    across,
    relay1,
    relay2,
    enc0,
    enc1,
    enc2,
    enc3,
    codes,
    mask,
    full,
    active,
    bias,
):
    z, i = place[0], place[1]
    width = own.shape[1]
    for at, blocks in enumerate(
        (
            (own, high, relay1, relay2),
            (low, own, high, across),
            (across, low, own, high),
            (relay2, relay1, low, own),
        )
    ):

        @pl.when(z == at)
        def _(blocks=blocks):
            for b, block in enumerate(blocks):
                full[:, b * width : (b + 1) * width] = block[...]

    total = jnp.zeros(codes.shape, F32)
    piece = codes.shape[1] // 4
    for t, enc in enumerate((enc0, enc1, enc2, enc3)):
        b = i ^ t
        total += jnp.dot(
            full[:, columns(b * width, width)], enc[:width, :], preferred_element_type=F32
        )
        bias[:, columns(b * piece, piece)] = one_row(enc[width:, :piece])
    preact = total + bias[...]
    low_codes = jnp.maximum(preact, 0.0).astype(BF16)
    codes[...] = low_codes
    mask[...] = (preact > 0.0).astype(F32).astype(BF16)
    active[...] = jnp.sum(low_codes.astype(F32), axis=0, keepdims=True)


def onward_body(place, low, high, out):
    @pl.when(place[0] == 1)
    def _():
        out[...] = high[...]

    @pl.when(place[0] != 1)
    def _():
        out[...] = low[...]


def pieces_body(place, dec, up, down, across):
    z = place[0]
    half = up.shape[0]
    for out, second in ((up, z >= 1), (down, z >= 3), (across, z < 2)):
        out[...] = dec[pl.ds(pl.multiple_of(jnp.where(second, half, 0), half), half), :]


def split_body(place, rows, first, second):
    edge = first.shape[0]
    first[...] = rows[:edge]
    second[...] = rows[edge:]


def turn_body(place, full, turned):
    turned[...] = full[...].T


def error_body(
    place, own, low, high, across, dec0, dec1, dec2, dec3, row0, row1, row2, *refs
):
    first, second, inputs, error = refs
    z, i = place[0], place[1]
    half = row0.shape[0] // 3
    edge = first.shape[0]
    shift = pl.multiple_of(jnp.where(z >= 2, half, 0), half)
    for t in range(4):
        dec = (dec0, dec1, dec2, dec3)[t]
        lefts = (own, low, high, across)
        if t < 3:
            row = (row0, row1, row2)[t]
            rights = [row[m * half : (m + 1) * half, :] for m in range(3)]
        else:
            middle = jnp.concatenate([first[half:], second[: edge - half]], axis=0)
            rights = [first[:half], middle, second[edge - half :]]
        rights = [dec[pl.ds(shift, half), :]] + rights
        total = jnp.zeros((own.shape[0], half), F32)
        for left, right in zip(lefts, rights):
            total += lax.dot_general(
                left[...], right, (((1,), (1,)), ((), ())), preferred_element_type=F32
            )
        q = i ^ t
        given = inputs[:, columns(q * 2 * half + shift, half)].astype(F32)
        error[:, columns(q * half, half)] = (given - total).astype(BF16)


def pick(place, middle, end, out):
    z = place[0]
    is_middle = (z == 1) | (z == 2)

    @pl.when(is_middle)
    def _():
        out[...] = middle[...]

    @pl.when(jnp.logical_not(is_middle))
    def _():
        out[...] = end[...]


def decoder_grads(scale, i, error, codes, slots, outs):
    half = error.shape[1] // 4
    for slot, out in zip(slots, outs):
        out[:half] = scale * lax.dot_general(
            error[:, columns((i ^ slot) * half, half)],
            codes[...],
            (((0,), (0,)), ((), ())),
            preferred_element_type=F32,
        )


def back_through(i, error, decs, shift):
    half = error.shape[1] // 4
    return functools.reduce(
        jnp.add,
        [
            jnp.dot(
                error[:, columns((i ^ t) * half, half)],
                dec[pl.ds(pl.multiple_of(shift, half), half), :],
                preferred_element_type=F32,
            )
            for t, dec in enumerate(decs)
        ],
    )


def near_body(rows, place, mine, passed, codes, active, dec0, dec1, dec2, dec3, part, near, *outs):
    z, i = place[0], place[1]
    half = mine.shape[1] // 4
    pick(place, mine, passed, near)
    decoder_grads(-2.0 / rows, i, near, codes, (3, 1, 2, 0), outs)
    outs[0][half:] = jnp.broadcast_to(active[...], (outs[0].shape[0] - half, active.shape[1]))
    part[...] = back_through(i, near, (dec0, dec1, dec2, dec3), jnp.where(z >= 2, half, 0))


def far_error_body(rows, place, swapped, direct, codes, far, send, kept):
    pick(place, swapped, direct, far)
    decoder_grads(-2.0 / rows, place[1], far, codes, (3, 2), (send, kept))


def code_grad_body(
    rows, place, far, part, mask, dec0, dec1, dec2, dec3, turned, grad_low, bias_sum, norms, *sends
):
    z, i = place[0], place[1]
    half = far.shape[1] // 4
    width = 2 * half
    decs = (dec0, dec1, dec2, dec3)
    total = part[...] + back_through(i, far, decs, jnp.where(z >= 2, 0, half))
    squares = functools.reduce(jnp.add, [one_row(dec[width:, :]) for dec in decs])
    column_norms = jnp.sqrt(squares + 1e-06)
    norms[...] = column_norms
    code_grad = (-2.0 / rows) * total + column_norms / rows
    grad = jnp.where(mask[...] > 0, code_grad, 0.0)
    grad_low[...] = grad.astype(BF16)
    row = jnp.sum(grad, axis=0, keepdims=True)
    bias_sum[...] = row
    at = pl.multiple_of((i ^ 3) * width, width)
    block = jnp.dot(turned[pl.ds(at, width), :], grad_low[...], preferred_element_type=F32)
    sends[0][:half] = block[:half]
    sends[0][half:] = jnp.broadcast_to(row, (sends[0].shape[0] - half, row.shape[1]))
    sends[1][...] = block[half:]


def encoder_grads(i, turned, grad_low, slots, outs):
    width = turned.shape[0] // 4
    for slot, out in zip(slots, outs):
        at = pl.ds(pl.multiple_of((i ^ slot) * width, width), width)
        out[:width] = jnp.dot(turned[at, :], grad_low[...], preferred_element_type=F32)


def rest_body(rows, place, turned, grad_low, near, far, codes, home, send, kept_far, kept, *outs):
    z, i = place[0], place[1]
    half = far.shape[1] // 4
    shift = jnp.where(z >= 2, 0, half)
    encoder_grads(i, turned, grad_low, (2, 1, 0), (kept_far, send, kept))
    decoder_grads(-2.0 / rows, i, far, codes, (1, 0), outs)
    home[:, columns(half - shift, half)] = near[:, columns(z * half, half)]
    home[:, columns(shift, half)] = far[:, columns(z * half, half)]


def power(values):
    largest = jnp.max(jnp.abs(values), axis=0, keepdims=True)
    return jnp.ceil(jnp.log(jnp.maximum(largest, 1e-30)) * (1.0 / math.log(2.0)))


def scale_of(exponent):
    return jnp.exp(exponent * math.log(2.0))


def pack_body(place, kept, row, *refs):
    width = kept.shape[0]
    at = [ref.shape[0] == width + EXTRA for ref in refs].index(True)
    received, packed, row_sums = refs[:at], refs[at], refs[at + 1 :]
    block = width // len(received)
    total = jnp.concatenate([piece[:block] for piece in received], axis=0) + kept[...]
    exponent = power(total)
    packed[:width] = total * scale_of(14.0 - exponent)
    sums = row[...]
    if received[0].shape[0] > block:
        sums += received[0][block : block + 1]
    for row_sum in row_sums:
        row_sum[...] = sums
    row_exponent = power(sums)
    parts = three_rows(sums * scale_of(14.0 - row_exponent)).astype(F32)
    at = lax.broadcasted_iota(jnp.int32, parts.shape, 0)
    parts = jnp.where(at == 3, exponent, jnp.where(at == 4, row_exponent, parts))
    packed[width:] = parts


def unpack(packed):
    width = packed.shape[0] - EXTRA
    rows = packed[width:].astype(F32)
    block = packed[:width].astype(F32) * scale_of(rows[3:4] - 14.0)
    row = (rows[0:1] + rows[1:2] + rows[2:3]) * scale_of(rows[4:5] - 14.0)
    return block, row


def bias_step_body(place, param, moment, square, here, there, param_out, moment_out, square_out):
    width = param.shape[1]
    grad = here[...] + there[...]
    pieces = [grad[:, b * width : (b + 1) * width] for b in range(4)]
    own = functools.reduce(
        jnp.add, [jnp.where(place[1] == b, piece, 0.0) for b, piece in enumerate(pieces)]
    )
    param_out[...], moment_out[...], square_out[...] = adam_update(
        param[...], own, moment[...], square[...]
    )


def decoder_step_body(
    rows, place, param, moment, square, near, far, active, norms, param_out, moment_out, square_out
):
    is_near = (pl.program_id(0) < pl.num_programs(0) // 2) == (place[0] < 2)
    grad = jnp.where(is_near, near[...], far[...])
    grad += param[...] * (active[...] / norms[...]) / rows
    param_out[...], moment_out[...], square_out[...] = adam_update(
        param[...], grad, moment[...], square[...]
    )


def line_shards(
    activations,
    encoder,
    enc_bias,
    decoder,
    enc_moment,
    enc_square,
    bias_moment,
    bias_square,
    dec_moment,
    dec_square,
):
    rows = activations.shape[0] * 4
    count, width = activations.shape
    latents = encoder.shape[1]
    half = width // 2
    features = 4 * width
    z, i = lax.axis_index("latent"), lax.axis_index("dp")
    place = jnp.stack([z, i]).astype(jnp.int32)

    def along(value, pairs):
        return lax.ppermute(value, "latent", pairs)

    def flip(value, bits, planes=(0, 1, 2, 3)):
        pairs = [(4 * p + k, 4 * p + (k ^ bits)) for p in planes for k in range(4)]
        return lax.ppermute(value, ("latent", "dp"), pairs)

    ends = [(1, 0), (2, 3)]
    low = along(activations, [(0, 1), (1, 2), (2, 3)])
    high = along(activations, [(1, 0), (2, 1), (3, 2)])
    across = along(activations, [(0, 2), (3, 1)])

    (enc_own,) = local_kernel(
        encoder_body,
        [shape((width + EXTRA, latents), BF16)],
        place,
        encoder,
        enc_bias.reshape(1, -1),
    )
    enc_chip, enc_core = flip(enc_own, 2), flip(enc_own, 1)
    (dec_own,) = local_kernel(
        decoder_body,
        [shape((width + EXTRA, latents), BF16)],
        place,
        decoder,
        after=(enc_core,),
    )
    dec_chip, dec_core = flip(dec_own, 2), flip(dec_own, 1)
    (onward,) = local_kernel(
        onward_body, [shape((count, width), BF16)], place, low, high
    )
    relay1 = along(onward, ends)
    relay2 = along(across, ends)
    enc = [enc_own, enc_core, enc_chip, flip(behind(enc_chip, relay2), 1)]

    up, down, beyond = local_kernel(
        pieces_body, [shape((half, latents), BF16)] * 3, place, dec_own
    )
    dec_pieces = [
        along(up, [(0, 1), (1, 2)]),
        along(down, [(2, 1), (3, 2)]),
        along(beyond, [(0, 2), (3, 1)]),
    ]
    dec = [dec_own, dec_core, dec_chip, flip(dec_chip, 1)]

    rows_own = jnp.concatenate([behind(piece, dec_chip) for piece in dec_pieces], axis=0)
    codes, mask, inputs, active = local_kernel(
        codes_body,
        [
            shape((count, latents), BF16),
            shape((count, latents), BF16),
            shape((count, features), BF16),
            shape((1, latents), F32),
        ],
        place,
        activations,
        low,
        high,
        across,
        relay1,
        relay2,
        *enc,
        after=(rows_own, dec[1], dec[3]),
        scratch=[pltpu.VMEM((1, latents), F32)],
    )
    codes_low = along(codes, [(0, 1), (1, 2)])
    codes_high = along(codes, [(2, 1), (3, 2)])
    codes_across = along(codes, [(0, 2), (3, 1)])
    (turned,) = local_kernel(
        turn_body, [shape((features, count), BF16)], place, inputs, after=(codes_across,)
    )
    rows_chip = flip(rows_own, 2, (1, 2))
    rows_core = flip(behind(rows_own, codes), 1, (1, 2))
    halves = local_kernel(
        split_body,
        [shape((3 * half // 2, latents), BF16)] * 2,
        place,
        rows_chip,
        after=(codes_across,),
    )
    rows_both = [flip(piece, 1, (1, 2)) for piece in halves]

    (own_error,) = local_kernel(
        error_body,
        [shape((count, features // 2), BF16)],
        place,
        codes,
        codes_low,
        codes_high,
        codes_across,
        *dec,
        rows_own,
        rows_core,
        rows_chip,
        *rows_both,
        inputs,
    )
    swapped = along(own_error, [(1, 2), (2, 1)])
    passed = along(own_error, [(1, 0), (2, 3)])
    direct = along(own_error, [(2, 0), (1, 3)])

    def across_chips(kept, row, *send, keep_row=True):
        packed, *row_sum = local_kernel(
            pack_body,
            [shape((kept.shape[0] + EXTRA, latents), F32)] + [shape((1, latents), F32)] * keep_row,
            place,
            kept,
            row,
            *[flip(piece, 1) for piece in send],
        )
        return packed, flip(packed.astype(jnp.float16), 2), *row_sum

    blocks = [shape((half + 8, latents), F32)] + [shape((half, latents), F32)] * 3
    part, near, *near_blocks = local_kernel(
        functools.partial(near_body, rows),
        [shape((count, latents), F32), shape((count, features // 2), BF16), *blocks],
        place,
        own_error,
        passed,
        codes,
        active,
        *dec,
        after=(swapped,),
    )
    send_far, send_near, keep_far, keep_near = near_blocks
    near_packed, near_received, active_sum = across_chips(keep_far, active, send_far)
    near_kept = keep_near, flip(send_near, 1)
    far, far_send, far_keep = local_kernel(
        functools.partial(far_error_body, rows),
        [shape((count, features // 2), BF16)] + [shape((half, latents), F32)] * 2,
        place,
        swapped,
        direct,
        codes,
        after=(near_packed, near_kept[1]),
        cost=NOTABLE,
    )
    grad_low, bias_sum, norms, *send_far_enc = local_kernel(
        functools.partial(code_grad_body, rows),
        [
            shape((count, latents), BF16),
            shape((1, latents), F32),
            shape((1, latents), F32),
            shape((half + 8, latents), F32),
            shape((half, latents), F32),
        ],
        place,
        far,
        behind(part, near_received),
        mask,
        *dec,
        turned,
        cost=NOTABLE,
    )
    far_packed, far_received = across_chips(far_keep, active, far_send, keep_row=False)
    error, enc_send_near, enc_keep_far, enc_keep_near, send_near, keep_near = local_kernel(
        functools.partial(rest_body, rows),
        [shape((count, width), BF16)]
        + [shape((width, latents), F32)] * 3
        + [shape((half, latents), F32)] * 2,
        place,
        turned,
        grad_low,
        near,
        far,
        codes,
        after=(far_packed,),
    )
    far_kept = keep_near, flip(send_near, 1)
    enc_packed, enc_received, bias_here = across_chips(enc_keep_far, bias_sum, *send_far_enc)
    enc_kept = enc_keep_near, flip(enc_send_near, 1)

    decoder, dec_moment, dec_square, encoder, enc_moment, enc_square = lax.optimization_barrier(
        (decoder, dec_moment, dec_square, encoder, enc_moment, enc_square, enc_packed)
    )[:6]
    near_block, active_there = unpack(near_received)
    far_block, _ = unpack(far_received)
    enc_block, bias_there = unpack(enc_received)
    near_grad = near_kept[0] + near_kept[1] + near_block
    far_grad = far_kept[0] + far_kept[1] + far_block
    active_sum = active_sum + active_there
    grad_encoder = enc_kept[0] + enc_kept[1] + enc_block
    new_enc_bias, new_bias_moment, new_bias_square = [
        value.reshape(-1)
        for value in local_kernel(
            bias_step_body,
            [shape((1, enc_bias.shape[0]), F32)] * 3,
            place,
            enc_bias.reshape(1, -1),
            bias_moment.reshape(1, -1),
            bias_square.reshape(1, -1),
            bias_here,
            bias_there,
        )
    ]
    new_encoder, new_enc_moment, new_enc_square = adam_update(
        encoder, grad_encoder, enc_moment, enc_square
    )
    step = width // 4
    block = pl.BlockSpec((step, latents), lambda r: (r, 0))
    in_half = pl.BlockSpec((step, latents), lambda r: (r % 2, 0))
    row = pl.BlockSpec((1, latents), lambda r: (0, 0))
    new_decoder, new_dec_moment, new_dec_square = pl.pallas_call(
        functools.partial(decoder_step_body, rows),
        grid=(4,),
        out_shape=[shape((width, latents), F32)] * 3,
        in_specs=[SMEM, block, block, block, in_half, in_half, row, row],
        out_specs=[block] * 3,
        compiler_params=pltpu.CompilerParams(vmem_limit_bytes=12 * 1024 * 1024),
        cost_estimate=pl.CostEstimate(flops=1, bytes_accessed=1, transcendentals=0),
    )(place, decoder, dec_moment, dec_square, near_grad, far_grad, active_sum, norms)
    return (
        error,
        new_encoder,
        new_enc_bias,
        new_decoder,
        new_enc_moment,
        new_enc_square,
        new_bias_moment,
        new_bias_square,
        new_dec_moment,
        new_dec_square,
    )


def solution(mesh):
    in_specs = (
        P(("groups", "dp"), "latent"),
        P(("groups", "dp"), "latent"),
        P(("groups", "latent", "dp")),
        P(("groups", "dp"), "latent"),
        P(("groups", "dp"), "latent"),
        P(("groups", "dp"), "latent"),
        P(("groups", "latent", "dp")),
        P(("groups", "latent", "dp")),
        P(("groups", "dp"), "latent"),
        P(("groups", "dp"), "latent"),
    )
    out_specs = (
        P(("groups", "dp"), "latent"),
        P(("groups", "dp"), "latent"),
        P(("groups", "latent", "dp")),
        P(("groups", "dp"), "latent"),
        P(("groups", "dp"), "latent"),
        P(("groups", "dp"), "latent"),
        P(("groups", "latent", "dp")),
        P(("groups", "latent", "dp")),
        P(("groups", "dp"), "latent"),
        P(("groups", "dp"), "latent"),
    )
    line = mesh.shape["latent"] == 4 and mesh.shape["dp"] == 4
    plan = line_shards if line else shards
    return jax.shard_map(plan, mesh=mesh, in_specs=in_specs, out_specs=out_specs, check_vma=False)
```

```python
import functools
import math

import jax
import jax.numpy as jnp
from jax import lax
from jax.experimental import pallas as pl
from jax.experimental.pallas import tpu as pltpu
from jax.sharding import PartitionSpec as P

ADAM_STEP = 1000


first_decay = 0.9
second_decay = 0.999
learn_rate = 0.001
epsilon = 1e-08

F32 = jnp.float32
BF16 = jnp.bfloat16


def adam_update(param, grad, moment, square):
    moment_new = first_decay * moment + (1.0 - first_decay) * grad
    square_new = second_decay * square + (1.0 - second_decay) * grad * grad
    first_fix = 1.0 - first_decay**ADAM_STEP
    second_fix = 1.0 - second_decay**ADAM_STEP
    param_new = param - learn_rate * (moment_new / first_fix) / (
        jnp.sqrt(square_new / second_fix) + epsilon
    )
    return (param_new, moment_new, square_new)


def shards(
    activations,
    encoder,
    enc_bias,
    decoder,
    enc_moment,
    enc_square,
    bias_moment,
    bias_square,
    dec_moment,
    dec_square,
):
    row_count = activations.shape[0] * lax.axis_size("dp")
    loss_scale = 2.0 / row_count
    inputs = lax.all_gather(activations, "latent", axis=1, tiled=True)
    enc_low, dec_low = (
        lax.all_gather(encoder.astype(jnp.bfloat16), "dp", axis=0, tiled=True),
        lax.all_gather(decoder.astype(jnp.bfloat16), "dp", axis=0, tiled=True),
    )
    bias_full = lax.all_gather(enc_bias, "dp", axis=0, tiled=True)
    square_sums = lax.psum(jnp.sum(decoder * decoder, axis=0), "dp")
    column_norms = jnp.sqrt(square_sums + 1e-06)
    preact = jnp.dot(inputs, enc_low, preferred_element_type=jnp.float32) + bias_full
    latent_codes = jnp.maximum(preact, 0.0).astype(jnp.bfloat16)
    partial_sums = lax.dot_general(
        latent_codes, dec_low, (((1,), (1,)), ((), ())), preferred_element_type=jnp.float32
    )
    rebuilt = lax.psum_scatter(partial_sums, "latent", scatter_dimension=1, tiled=True)
    error = (activations.astype(jnp.float32) - rebuilt).astype(jnp.bfloat16)
    full_error = lax.all_gather(error, "latent", axis=1, tiled=True)
    active_sum = lax.psum(jnp.sum(latent_codes.astype(jnp.float32), axis=0), "dp")
    grad_dec_rows = -loss_scale * lax.dot_general(
        full_error, latent_codes, (((0,), (0,)), ((), ())), preferred_element_type=jnp.float32
    )
    code_grad = (
        -loss_scale * jnp.dot(full_error, dec_low, preferred_element_type=jnp.float32)
        + column_norms / row_count
    )
    grad_preact = jnp.where(preact > 0.0, code_grad, 0.0)
    grad_encoder = lax.dot_general(
        inputs,
        grad_preact.astype(jnp.bfloat16),
        (((0,), (0,)), ((), ())),
        preferred_element_type=jnp.float32,
    )
    grad_bias = jnp.sum(grad_preact, axis=0)
    grad_encoder, grad_dec_rows, grad_bias = (
        lax.psum_scatter(grad_encoder, "dp", scatter_dimension=0, tiled=True),
        lax.psum_scatter(grad_dec_rows, "dp", scatter_dimension=0, tiled=True),
        lax.psum_scatter(grad_bias, "dp", scatter_dimension=0, tiled=True),
    )
    grad_decoder = grad_dec_rows + decoder * (active_sum / column_norms) / row_count
    new_encoder, new_enc_moment, new_enc_square = adam_update(
        encoder, grad_encoder, enc_moment, enc_square
    )
    new_enc_bias, new_bias_moment, new_bias_square = adam_update(
        enc_bias, grad_bias, bias_moment, bias_square
    )
    new_decoder, new_dec_moment, new_dec_square = adam_update(
        decoder, grad_decoder, dec_moment, dec_square
    )
    return (
        error,
        new_encoder,
        new_enc_bias,
        new_decoder,
        new_enc_moment,
        new_enc_square,
        new_bias_moment,
        new_bias_square,
        new_dec_moment,
        new_dec_square,
    )


VMEM = pl.BlockSpec(memory_space=pltpu.VMEM)
SMEM = pl.BlockSpec(memory_space=pltpu.SMEM)
ANY = pl.BlockSpec(memory_space=pl.ANY)
EXTRA = 16
NOTABLE = 10**10


def local_kernel(body, outs, place, *args, after=(), scratch=(), cost=1):
    def run(place, *refs):
        body(place, *refs[: len(args)], *refs[len(args) + len(after) :])

    held = sum(a.size * jnp.dtype(a.dtype).itemsize for a in (*args, *outs))
    return pl.pallas_call(
        run,
        out_shape=outs,
        in_specs=[SMEM] + [VMEM] * len(args) + [ANY] * len(after),
        out_specs=[VMEM] * len(outs),
        scratch_shapes=scratch,
        compiler_params=pltpu.CompilerParams(vmem_limit_bytes=held + 6 * 1024 * 1024),
        cost_estimate=pl.CostEstimate(flops=cost, bytes_accessed=1, transcendentals=0),
    )(place, *args, *after)


def shape(dims, dtype):
    return jax.ShapeDtypeStruct(dims, dtype)


def columns(start, width):
    return pl.ds(pl.multiple_of(start, width), width)


def three_rows(row):
    high = row.astype(BF16).astype(F32)
    middle = (row - high).astype(BF16).astype(F32)
    low = row - high - middle
    at = lax.broadcasted_iota(jnp.int32, (EXTRA, row.shape[1]), 0)
    rows = jnp.where(at == 0, high, jnp.where(at == 1, middle, jnp.where(at == 2, low, 0.0)))
    return rows.astype(BF16)


def behind(value, *others):
    return lax.optimization_barrier((value, *others))[0]


def one_row(rows):
    return jnp.sum(rows.astype(F32), axis=0, keepdims=True)


def encoder_body(place, encoder, bias, out):
    depth = encoder.shape[0]
    out[:depth] = encoder[...].astype(BF16)
    out[depth:] = three_rows(jnp.concatenate([bias[...]] * 4, axis=1))


def decoder_body(place, decoder, out):
    depth = decoder.shape[0]
    value = decoder[...]
    out[:depth] = value.astype(BF16)
    out[depth:] = three_rows(jnp.sum(value * value, axis=0, keepdims=True))


def codes_body(
    place,
    own,
    low,
    high,
    across,
    relay1,
    relay2,
    enc0,
    enc1,
    enc2,
    enc3,
    codes,
    mask,
    full,
    active,
    bias,
):
    z, i = place[0], place[1]
    width = own.shape[1]
    for at, blocks in enumerate(
        (
            (own, high, relay1, relay2),
            (low, own, high, across),
            (across, low, own, high),
            (relay2, relay1, low, own),
        )
    ):

        @pl.when(z == at)
        def _(blocks=blocks):
            for b, block in enumerate(blocks):
                full[:, b * width : (b + 1) * width] = block[...]

    total = jnp.zeros(codes.shape, F32)
    piece = codes.shape[1] // 4
    for t, enc in enumerate((enc0, enc1, enc2, enc3)):
        b = i ^ t
        total += jnp.dot(
            full[:, columns(b * width, width)], enc[:width, :], preferred_element_type=F32
        )
        bias[:, columns(b * piece, piece)] = one_row(enc[width:, :piece])
    preact = total + bias[...]
    low_codes = jnp.maximum(preact, 0.0).astype(BF16)
    codes[...] = low_codes
    mask[...] = (preact > 0.0).astype(F32).astype(BF16)
    active[...] = jnp.sum(low_codes.astype(F32), axis=0, keepdims=True)


def onward_body(place, low, high, out):
    @pl.when(place[0] == 1)
    def _():
        out[...] = high[...]

    @pl.when(place[0] != 1)
    def _():
        out[...] = low[...]


def pieces_body(place, dec, up, down, across):
    z = place[0]
    half = up.shape[0]
    for out, second in ((up, z >= 1), (down, z >= 3), (across, z < 2)):
        out[...] = dec[pl.ds(pl.multiple_of(jnp.where(second, half, 0), half), half), :]


def turn_body(place, full, turned):
    turned[...] = full[...].T


def rebuilt_error(place, t, codes, dec, row, inputs):
    z, i = place[0], place[1]
    half = row.shape[0] // 3
    shift = pl.multiple_of(jnp.where(z >= 2, half, 0), half)
    rights = [dec[pl.ds(shift, half), :]] + [row[m * half : (m + 1) * half, :] for m in range(3)]
    total = jnp.zeros((codes[0].shape[0], half), F32)
    for left, right in zip(codes, rights):
        total += lax.dot_general(
            left[...], right, (((1,), (1,)), ((), ())), preferred_element_type=F32
        )
    given = inputs[:, columns((i ^ t) * 2 * half + shift, half)].astype(F32)
    return (given - total).astype(BF16)


def own_error_body(place, own, low, high, across, dec0, dec2, row0, row2, inputs, out):
    half = out.shape[1] // 2
    codes = (own, low, high, across)
    out[:, :half] = rebuilt_error(place, 0, codes, dec0, row0, inputs)
    out[:, half:] = rebuilt_error(place, 2, codes, dec2, row2, inputs)


def error_body(place, own, low, high, across, dec1, dec3, row1, row3, inputs, made, error):
    i = place[1]
    half = error.shape[1] // 4
    codes = (own, low, high, across)
    error[:, columns(i * half, half)] = made[:, :half]
    error[:, columns((i ^ 2) * half, half)] = made[:, half:]
    error[:, columns((i ^ 1) * half, half)] = rebuilt_error(place, 1, codes, dec1, row1, inputs)
    error[:, columns((i ^ 3) * half, half)] = rebuilt_error(place, 3, codes, dec3, row3, inputs)


def pick(place, middle, end, out):
    z = place[0]
    is_middle = (z == 1) | (z == 2)

    @pl.when(is_middle)
    def _():
        out[...] = middle[...]

    @pl.when(jnp.logical_not(is_middle))
    def _():
        out[...] = end[...]


def decoder_grads(scale, i, error, codes, slots, outs):
    half = error.shape[1] // 4
    for slot, out in zip(slots, outs):
        out[:half] = scale * lax.dot_general(
            error[:, columns((i ^ slot) * half, half)],
            codes[...],
            (((0,), (0,)), ((), ())),
            preferred_element_type=F32,
        )


def back_through(i, error, decs, shift):
    half = error.shape[1] // 4
    return functools.reduce(
        jnp.add,
        [
            jnp.dot(
                error[:, columns((i ^ t) * half, half)],
                dec[pl.ds(pl.multiple_of(shift, half), half), :],
                preferred_element_type=F32,
            )
            for t, dec in enumerate(decs)
        ],
    )


def near_body(rows, place, mine, passed, codes, active, dec0, dec1, dec2, dec3, part, near, *outs):
    z, i = place[0], place[1]
    half = mine.shape[1] // 4
    pick(place, mine, passed, near)
    decoder_grads(-2.0 / rows, i, near, codes, (3, 1, 2, 0), outs)
    outs[0][half:] = jnp.broadcast_to(active[...], (outs[0].shape[0] - half, active.shape[1]))
    part[...] = back_through(i, near, (dec0, dec1, dec2, dec3), jnp.where(z >= 2, half, 0))


def far_error_body(rows, place, swapped, direct, codes, far, send, kept):
    pick(place, swapped, direct, far)
    decoder_grads(-2.0 / rows, place[1], far, codes, (3, 2), (send, kept))


def code_grad_body(
    rows, place, far, part, mask, dec0, dec1, dec2, dec3, turned, grad_low, bias_sum, norms, *sends
):
    z, i = place[0], place[1]
    half = far.shape[1] // 4
    width = 2 * half
    decs = (dec0, dec1, dec2, dec3)
    total = part[...] + back_through(i, far, decs, jnp.where(z >= 2, 0, half))
    squares = functools.reduce(jnp.add, [one_row(dec[width:, :]) for dec in decs])
    column_norms = jnp.sqrt(squares + 1e-06)
    norms[...] = column_norms
    code_grad = (-2.0 / rows) * total + column_norms / rows
    grad = jnp.where(mask[...] > 0, code_grad, 0.0)
    grad_low[...] = grad.astype(BF16)
    row = jnp.sum(grad, axis=0, keepdims=True)
    bias_sum[...] = row
    at = pl.multiple_of((i ^ 3) * width, width)
    block = jnp.dot(turned[pl.ds(at, width), :], grad_low[...], preferred_element_type=F32)
    sends[0][:half] = block[:half]
    sends[0][half:] = jnp.broadcast_to(row, (sends[0].shape[0] - half, row.shape[1]))
    sends[1][...] = block[half:]


def encoder_grads(i, turned, grad_low, slots, outs):
    width = turned.shape[0] // 4
    for slot, out in zip(slots, outs):
        at = pl.ds(pl.multiple_of((i ^ slot) * width, width), width)
        out[:width] = jnp.dot(turned[at, :], grad_low[...], preferred_element_type=F32)


def rest_body(rows, place, turned, grad_low, near, far, codes, home, send, kept_far, kept, *outs):
    z, i = place[0], place[1]
    half = far.shape[1] // 4
    shift = jnp.where(z >= 2, 0, half)
    encoder_grads(i, turned, grad_low, (2, 1, 0), (kept_far, send, kept))
    decoder_grads(-2.0 / rows, i, far, codes, (1, 0), outs)
    home[:, columns(half - shift, half)] = near[:, columns(z * half, half)]
    home[:, columns(shift, half)] = far[:, columns(z * half, half)]


def power(values):
    largest = jnp.max(jnp.abs(values), axis=0, keepdims=True)
    return jnp.ceil(jnp.log(jnp.maximum(largest, 1e-30)) * (1.0 / math.log(2.0)))


def scale_of(exponent):
    return jnp.exp(exponent * math.log(2.0))


def pack_body(place, kept, row, *refs):
    width = kept.shape[0]
    at = [ref.shape[0] == width + EXTRA for ref in refs].index(True)
    received, packed, row_sums = refs[:at], refs[at], refs[at + 1 :]
    block = width // len(received)
    total = jnp.concatenate([piece[:block] for piece in received], axis=0) + kept[...]
    exponent = power(total)
    packed[:width] = total * scale_of(14.0 - exponent)
    sums = row[...]
    if received[0].shape[0] > block:
        sums += received[0][block : block + 1]
    for row_sum in row_sums:
        row_sum[...] = sums
    row_exponent = power(sums)
    parts = three_rows(sums * scale_of(14.0 - row_exponent)).astype(F32)
    at = lax.broadcasted_iota(jnp.int32, parts.shape, 0)
    parts = jnp.where(at == 3, exponent, jnp.where(at == 4, row_exponent, parts))
    packed[width:] = parts


def unpack(packed):
    width = packed.shape[0] - EXTRA
    rows = packed[width:].astype(F32)
    block = packed[:width].astype(F32) * scale_of(rows[3:4] - 14.0)
    row = (rows[0:1] + rows[1:2] + rows[2:3]) * scale_of(rows[4:5] - 14.0)
    return block, row


def bias_step_body(place, param, moment, square, here, there, param_out, moment_out, square_out):
    width = param.shape[1]
    grad = here[...] + there[...]
    pieces = [grad[:, b * width : (b + 1) * width] for b in range(4)]
    own = functools.reduce(
        jnp.add, [jnp.where(place[1] == b, piece, 0.0) for b, piece in enumerate(pieces)]
    )
    param_out[...], moment_out[...], square_out[...] = adam_update(
        param[...], own, moment[...], square[...]
    )


def decoder_step_body(
    rows, place, param, moment, square, near, far, active, norms, param_out, moment_out, square_out
):
    is_near = (pl.program_id(0) < pl.num_programs(0) // 2) == (place[0] < 2)
    grad = jnp.where(is_near, near[...], far[...])
    grad += param[...] * (active[...] / norms[...]) / rows
    param_out[...], moment_out[...], square_out[...] = adam_update(
        param[...], grad, moment[...], square[...]
    )


def line_shards(
    activations,
    encoder,
    enc_bias,
    decoder,
    enc_moment,
    enc_square,
    bias_moment,
    bias_square,
    dec_moment,
    dec_square,
):
    rows = activations.shape[0] * 4
    count, width = activations.shape
    latents = encoder.shape[1]
    half = width // 2
    features = 4 * width
    z, i = lax.axis_index("latent"), lax.axis_index("dp")
    place = jnp.stack([z, i]).astype(jnp.int32)

    def along(value, pairs):
        return lax.ppermute(value, "latent", pairs)

    def flip(value, bits, planes=(0, 1, 2, 3)):
        pairs = [(4 * p + k, 4 * p + (k ^ bits)) for p in planes for k in range(4)]
        return lax.ppermute(value, ("latent", "dp"), pairs)

    ends = [(1, 0), (2, 3)]
    low = along(activations, [(0, 1), (1, 2), (2, 3)])
    high = along(activations, [(1, 0), (2, 1), (3, 2)])
    across = along(activations, [(0, 2), (3, 1)])

    (enc_own,) = local_kernel(
        encoder_body,
        [shape((width + EXTRA, latents), BF16)],
        place,
        encoder,
        enc_bias.reshape(1, -1),
    )
    enc_chip, enc_core = flip(enc_own, 2), flip(enc_own, 1)
    (dec_own,) = local_kernel(
        decoder_body,
        [shape((width + EXTRA, latents), BF16)],
        place,
        decoder,
        after=(enc_core,),
    )
    dec_chip, dec_core = flip(dec_own, 2), flip(dec_own, 1)
    (onward,) = local_kernel(
        onward_body, [shape((count, width), BF16)], place, low, high
    )
    relay1 = along(onward, ends)
    relay2 = along(across, ends)
    enc = [enc_own, enc_core, enc_chip, flip(behind(enc_chip, relay2), 1)]

    up, down, beyond = local_kernel(
        pieces_body, [shape((half, latents), BF16)] * 3, place, dec_own
    )
    dec_pieces = [
        along(up, [(0, 1), (1, 2)]),
        along(down, [(2, 1), (3, 2)]),
        along(beyond, [(0, 2), (3, 1)]),
    ]
    dec = [dec_own, dec_core, dec_chip, flip(dec_chip, 1)]

    rows_own = jnp.concatenate([behind(piece, dec_chip) for piece in dec_pieces], axis=0)
    codes, mask, inputs, active = local_kernel(
        codes_body,
        [
            shape((count, latents), BF16),
            shape((count, latents), BF16),
            shape((count, features), BF16),
            shape((1, latents), F32),
        ],
        place,
        activations,
        low,
        high,
        across,
        relay1,
        relay2,
        *enc,
        after=(rows_own, dec[1], dec[3]),
        scratch=[pltpu.VMEM((1, latents), F32)],
    )
    codes_low = along(codes, [(0, 1), (1, 2)])
    codes_high = along(codes, [(2, 1), (3, 2)])
    codes_across = along(codes, [(0, 2), (3, 1)])
    (turned,) = local_kernel(
        turn_body, [shape((features, count), BF16)], place, inputs, after=(codes_across,)
    )
    rows_chip = flip(rows_own, 2, (1, 2))
    rows_core = flip(behind(rows_own, codes), 1, (1, 2))
    rows_both = flip(behind(rows_chip, codes_across), 1, (1, 2))

    all_codes = codes, codes_low, codes_high, codes_across
    (made,) = local_kernel(
        own_error_body,
        [shape((count, features // 4), BF16)],
        place,
        *all_codes,
        dec[0],
        dec[2],
        rows_own,
        rows_chip,
        inputs,
        cost=NOTABLE,
    )
    (own_error,) = local_kernel(
        error_body,
        [shape((count, features // 2), BF16)],
        place,
        *all_codes,
        dec[1],
        dec[3],
        rows_core,
        rows_both,
        inputs,
        made,
    )
    swapped = along(own_error, [(1, 2), (2, 1)])
    passed = along(own_error, [(1, 0), (2, 3)])
    direct = along(own_error, [(2, 0), (1, 3)])

    def across_chips(kept, row, *send, keep_row=True):
        packed, *row_sum = local_kernel(
            pack_body,
            [shape((kept.shape[0] + EXTRA, latents), F32)] + [shape((1, latents), F32)] * keep_row,
            place,
            kept,
            row,
            *[flip(piece, 1) for piece in send],
        )
        return packed, flip(packed.astype(jnp.float16), 2), *row_sum

    blocks = [shape((half + 8, latents), F32)] + [shape((half, latents), F32)] * 3
    part, near, *near_blocks = local_kernel(
        functools.partial(near_body, rows),
        [shape((count, latents), F32), shape((count, features // 2), BF16), *blocks],
        place,
        own_error,
        passed,
        codes,
        active,
        *dec,
        after=(swapped,),
    )
    send_far, send_near, keep_far, keep_near = near_blocks
    near_packed, near_received, active_sum = across_chips(keep_far, active, send_far)
    near_kept = keep_near, flip(send_near, 1)
    far, far_send, far_keep = local_kernel(
        functools.partial(far_error_body, rows),
        [shape((count, features // 2), BF16)] + [shape((half, latents), F32)] * 2,
        place,
        swapped,
        direct,
        codes,
        after=(near_packed, near_kept[1]),
        cost=NOTABLE,
    )
    grad_low, bias_sum, norms, *send_far_enc = local_kernel(
        functools.partial(code_grad_body, rows),
        [
            shape((count, latents), BF16),
            shape((1, latents), F32),
            shape((1, latents), F32),
            shape((half + 8, latents), F32),
            shape((half, latents), F32),
        ],
        place,
        far,
        behind(part, near_received),
        mask,
        *dec,
        turned,
        cost=NOTABLE,
    )
    far_packed, far_received = across_chips(far_keep, active, far_send, keep_row=False)
    error, enc_send_near, enc_keep_far, enc_keep_near, send_near, keep_near = local_kernel(
        functools.partial(rest_body, rows),
        [shape((count, width), BF16)]
        + [shape((width, latents), F32)] * 3
        + [shape((half, latents), F32)] * 2,
        place,
        turned,
        grad_low,
        near,
        far,
        codes,
        after=(far_packed,),
    )
    far_kept = keep_near, flip(send_near, 1)
    enc_packed, enc_received, bias_here = across_chips(enc_keep_far, bias_sum, *send_far_enc)
    enc_kept = enc_keep_near, flip(enc_send_near, 1)

    decoder, dec_moment, dec_square, encoder, enc_moment, enc_square = lax.optimization_barrier(
        (decoder, dec_moment, dec_square, encoder, enc_moment, enc_square, enc_packed)
    )[:6]
    near_block, active_there = unpack(near_received)
    far_block, _ = unpack(far_received)
    enc_block, bias_there = unpack(enc_received)
    near_grad = near_kept[0] + near_kept[1] + near_block
    far_grad = far_kept[0] + far_kept[1] + far_block
    active_sum = active_sum + active_there
    grad_encoder = enc_kept[0] + enc_kept[1] + enc_block
    new_enc_bias, new_bias_moment, new_bias_square = [
        value.reshape(-1)
        for value in local_kernel(
            bias_step_body,
            [shape((1, enc_bias.shape[0]), F32)] * 3,
            place,
            enc_bias.reshape(1, -1),
            bias_moment.reshape(1, -1),
            bias_square.reshape(1, -1),
            bias_here,
            bias_there,
        )
    ]
    new_encoder, new_enc_moment, new_enc_square = adam_update(
        encoder, grad_encoder, enc_moment, enc_square
    )
    step = width // 4
    block = pl.BlockSpec((step, latents), lambda r: (r, 0))
    in_half = pl.BlockSpec((step, latents), lambda r: (r % 2, 0))
    row = pl.BlockSpec((1, latents), lambda r: (0, 0))
    new_decoder, new_dec_moment, new_dec_square = pl.pallas_call(
        functools.partial(decoder_step_body, rows),
        grid=(4,),
        out_shape=[shape((width, latents), F32)] * 3,
        in_specs=[SMEM, block, block, block, in_half, in_half, row, row],
        out_specs=[block] * 3,
        compiler_params=pltpu.CompilerParams(vmem_limit_bytes=12 * 1024 * 1024),
        cost_estimate=pl.CostEstimate(flops=1, bytes_accessed=1, transcendentals=0),
    )(place, decoder, dec_moment, dec_square, near_grad, far_grad, active_sum, norms)
    return (
        error,
        new_encoder,
        new_enc_bias,
        new_decoder,
        new_enc_moment,
        new_enc_square,
        new_bias_moment,
        new_bias_square,
        new_dec_moment,
        new_dec_square,
    )


def solution(mesh):
    in_specs = (
        P(("groups", "dp"), "latent"),
        P(("groups", "dp"), "latent"),
        P(("groups", "latent", "dp")),
        P(("groups", "dp"), "latent"),
        P(("groups", "dp"), "latent"),
        P(("groups", "dp"), "latent"),
        P(("groups", "latent", "dp")),
        P(("groups", "latent", "dp")),
        P(("groups", "dp"), "latent"),
        P(("groups", "dp"), "latent"),
    )
    out_specs = (
        P(("groups", "dp"), "latent"),
        P(("groups", "dp"), "latent"),
        P(("groups", "latent", "dp")),
        P(("groups", "dp"), "latent"),
        P(("groups", "dp"), "latent"),
        P(("groups", "dp"), "latent"),
        P(("groups", "latent", "dp")),
        P(("groups", "latent", "dp")),
        P(("groups", "dp"), "latent"),
        P(("groups", "dp"), "latent"),
    )
    line = mesh.shape["latent"] == 4 and mesh.shape["dp"] == 4
    plan = line_shards if line else shards
    return jax.shard_map(plan, mesh=mesh, in_specs=in_specs, out_specs=out_specs, check_vma=False)
```

```python
import functools
import math

import jax
import jax.numpy as jnp
from jax import lax
from jax.experimental import pallas as pl
from jax.experimental.pallas import tpu as pltpu
from jax.sharding import PartitionSpec as P

ADAM_STEP = 1000


first_decay = 0.9
second_decay = 0.999
learn_rate = 0.001
epsilon = 1e-08

F32 = jnp.float32
BF16 = jnp.bfloat16


def adam_update(param, grad, moment, square):
    moment_new = first_decay * moment + (1.0 - first_decay) * grad
    square_new = second_decay * square + (1.0 - second_decay) * grad * grad
    first_fix = 1.0 - first_decay**ADAM_STEP
    second_fix = 1.0 - second_decay**ADAM_STEP
    param_new = param - learn_rate * (moment_new / first_fix) / (
        jnp.sqrt(square_new / second_fix) + epsilon
    )
    return (param_new, moment_new, square_new)


def shards(
    activations,
    encoder,
    enc_bias,
    decoder,
    enc_moment,
    enc_square,
    bias_moment,
    bias_square,
    dec_moment,
    dec_square,
):
    row_count = activations.shape[0] * lax.axis_size("dp")
    loss_scale = 2.0 / row_count
    inputs = lax.all_gather(activations, "latent", axis=1, tiled=True)
    enc_low, dec_low = (
        lax.all_gather(encoder.astype(jnp.bfloat16), "dp", axis=0, tiled=True),
        lax.all_gather(decoder.astype(jnp.bfloat16), "dp", axis=0, tiled=True),
    )
    bias_full = lax.all_gather(enc_bias, "dp", axis=0, tiled=True)
    square_sums = lax.psum(jnp.sum(decoder * decoder, axis=0), "dp")
    column_norms = jnp.sqrt(square_sums + 1e-06)
    preact = jnp.dot(inputs, enc_low, preferred_element_type=jnp.float32) + bias_full
    latent_codes = jnp.maximum(preact, 0.0).astype(jnp.bfloat16)
    partial_sums = lax.dot_general(
        latent_codes, dec_low, (((1,), (1,)), ((), ())), preferred_element_type=jnp.float32
    )
    rebuilt = lax.psum_scatter(partial_sums, "latent", scatter_dimension=1, tiled=True)
    error = (activations.astype(jnp.float32) - rebuilt).astype(jnp.bfloat16)
    full_error = lax.all_gather(error, "latent", axis=1, tiled=True)
    active_sum = lax.psum(jnp.sum(latent_codes.astype(jnp.float32), axis=0), "dp")
    grad_dec_rows = -loss_scale * lax.dot_general(
        full_error, latent_codes, (((0,), (0,)), ((), ())), preferred_element_type=jnp.float32
    )
    code_grad = (
        -loss_scale * jnp.dot(full_error, dec_low, preferred_element_type=jnp.float32)
        + column_norms / row_count
    )
    grad_preact = jnp.where(preact > 0.0, code_grad, 0.0)
    grad_encoder = lax.dot_general(
        inputs,
        grad_preact.astype(jnp.bfloat16),
        (((0,), (0,)), ((), ())),
        preferred_element_type=jnp.float32,
    )
    grad_bias = jnp.sum(grad_preact, axis=0)
    grad_encoder, grad_dec_rows, grad_bias = (
        lax.psum_scatter(grad_encoder, "dp", scatter_dimension=0, tiled=True),
        lax.psum_scatter(grad_dec_rows, "dp", scatter_dimension=0, tiled=True),
        lax.psum_scatter(grad_bias, "dp", scatter_dimension=0, tiled=True),
    )
    grad_decoder = grad_dec_rows + decoder * (active_sum / column_norms) / row_count
    new_encoder, new_enc_moment, new_enc_square = adam_update(
        encoder, grad_encoder, enc_moment, enc_square
    )
    new_enc_bias, new_bias_moment, new_bias_square = adam_update(
        enc_bias, grad_bias, bias_moment, bias_square
    )
    new_decoder, new_dec_moment, new_dec_square = adam_update(
        decoder, grad_decoder, dec_moment, dec_square
    )
    return (
        error,
        new_encoder,
        new_enc_bias,
        new_decoder,
        new_enc_moment,
        new_enc_square,
        new_bias_moment,
        new_bias_square,
        new_dec_moment,
        new_dec_square,
    )


VMEM = pl.BlockSpec(memory_space=pltpu.VMEM)
SMEM = pl.BlockSpec(memory_space=pltpu.SMEM)
ANY = pl.BlockSpec(memory_space=pl.ANY)
EXTRA = 16
NOTABLE = 10**10


def local_kernel(body, outs, place, *args, after=(), scratch=(), cost=1):
    def run(place, *refs):
        body(place, *refs[: len(args)], *refs[len(args) + len(after) :])

    held = sum(a.size * jnp.dtype(a.dtype).itemsize for a in (*args, *outs))
    return pl.pallas_call(
        run,
        out_shape=outs,
        in_specs=[SMEM] + [VMEM] * len(args) + [ANY] * len(after),
        out_specs=[VMEM] * len(outs),
        scratch_shapes=scratch,
        compiler_params=pltpu.CompilerParams(vmem_limit_bytes=held + 6 * 1024 * 1024),
        cost_estimate=pl.CostEstimate(flops=cost, bytes_accessed=1, transcendentals=0),
    )(place, *args, *after)


def shape(dims, dtype):
    return jax.ShapeDtypeStruct(dims, dtype)


def columns(start, width):
    return pl.ds(pl.multiple_of(start, width), width)


def three_rows(row):
    high = row.astype(BF16).astype(F32)
    middle = (row - high).astype(BF16).astype(F32)
    low = row - high - middle
    at = lax.broadcasted_iota(jnp.int32, (EXTRA, row.shape[1]), 0)
    rows = jnp.where(at == 0, high, jnp.where(at == 1, middle, jnp.where(at == 2, low, 0.0)))
    return rows.astype(BF16)


def behind(value, *others):
    return lax.optimization_barrier((value, *others))[0]


def one_row(rows):
    return jnp.sum(rows.astype(F32), axis=0, keepdims=True)


def encoder_body(place, encoder, bias, out):
    depth = encoder.shape[0]
    out[:depth] = encoder[...].astype(BF16)
    out[depth:] = three_rows(jnp.concatenate([bias[...]] * 4, axis=1))


def decoder_body(place, decoder, out):
    depth = decoder.shape[0]
    value = decoder[...]
    out[:depth] = value.astype(BF16)
    out[depth:] = three_rows(jnp.sum(value * value, axis=0, keepdims=True))


def codes_body(
    place,
    own,
    low,
    high,
    across,
    relay1,
    relay2,
    enc0,
    enc1,
    enc2,
    enc3,
    codes,
    mask,
    full,
    active,
    bias,
):
    z, i = place[0], place[1]
    width = own.shape[1]
    for at, blocks in enumerate(
        (
            (own, high, relay1, relay2),
            (low, own, high, across),
            (across, low, own, high),
            (relay2, relay1, low, own),
        )
    ):

        @pl.when(z == at)
        def _(blocks=blocks):
            for b, block in enumerate(blocks):
                full[:, b * width : (b + 1) * width] = block[...]

    total = jnp.zeros(codes.shape, F32)
    piece = codes.shape[1] // 4
    for t, enc in enumerate((enc0, enc1, enc2, enc3)):
        b = i ^ t
        total += jnp.dot(
            full[:, columns(b * width, width)], enc[:width, :], preferred_element_type=F32
        )
        bias[:, columns(b * piece, piece)] = one_row(enc[width:, :piece])
    preact = total + bias[...]
    low_codes = jnp.maximum(preact, 0.0).astype(BF16)
    codes[...] = low_codes
    mask[...] = (preact > 0.0).astype(F32).astype(BF16)
    active[...] = jnp.sum(low_codes.astype(F32), axis=0, keepdims=True)


def onward_body(place, low, high, out):
    @pl.when(place[0] == 1)
    def _():
        out[...] = high[...]

    @pl.when(place[0] != 1)
    def _():
        out[...] = low[...]


def pieces_body(place, dec, up, down, across):
    z = place[0]
    half = up.shape[0]
    for out, second in ((up, z >= 1), (down, z >= 3), (across, z < 2)):
        out[...] = dec[pl.ds(pl.multiple_of(jnp.where(second, half, 0), half), half), :]


def turn_body(place, full, turned):
    turned[...] = full[...].T


def rebuilt_error(place, t, codes, dec, row, inputs):
    z, i = place[0], place[1]
    half = row.shape[0] // 3
    shift = pl.multiple_of(jnp.where(z >= 2, half, 0), half)
    below = pl.multiple_of(jnp.where(z == 1, 0, half), half)
    rights = [
        dec[pl.ds(shift, half), :],
        row[2 * half :, :],
        row[pl.ds(half - below, half), :],
        row[pl.ds(below, half), :],
    ]
    total = jnp.zeros((codes[0].shape[0], half), F32)
    for left, right in zip(codes, rights):
        total += lax.dot_general(
            left[...], right, (((1,), (1,)), ((), ())), preferred_element_type=F32
        )
    given = inputs[:, columns((i ^ t) * 2 * half + shift, half)].astype(F32)
    return (given - total).astype(BF16)


def own_error_body(place, own, across, middle, near, dec0, dec2, row0, row2, inputs, out):
    half = out.shape[1] // 2
    codes = (own, across, middle, near)
    out[:, :half] = rebuilt_error(place, 0, codes, dec0, row0, inputs)
    out[:, half:] = rebuilt_error(place, 2, codes, dec2, row2, inputs)


def error_body(place, own, across, middle, near, dec1, dec3, row1, row3, inputs, made, error):
    i = place[1]
    half = error.shape[1] // 4
    codes = (own, across, middle, near)
    error[:, columns(i * half, half)] = made[:, :half]
    error[:, columns((i ^ 2) * half, half)] = made[:, half:]
    error[:, columns((i ^ 1) * half, half)] = rebuilt_error(place, 1, codes, dec1, row1, inputs)
    error[:, columns((i ^ 3) * half, half)] = rebuilt_error(place, 3, codes, dec3, row3, inputs)


def pick(place, middle, end, out):
    z = place[0]
    is_middle = (z == 1) | (z == 2)

    @pl.when(is_middle)
    def _():
        out[...] = middle[...]

    @pl.when(jnp.logical_not(is_middle))
    def _():
        out[...] = end[...]


def decoder_grads(scale, i, error, codes, slots, outs):
    half = error.shape[1] // 4
    for slot, out in zip(slots, outs):
        out[:half] = scale * lax.dot_general(
            error[:, columns((i ^ slot) * half, half)],
            codes[...],
            (((0,), (0,)), ((), ())),
            preferred_element_type=F32,
        )


def back_through(i, error, decs, shift):
    half = error.shape[1] // 4
    return functools.reduce(
        jnp.add,
        [
            jnp.dot(
                error[:, columns((i ^ t) * half, half)],
                dec[pl.ds(pl.multiple_of(shift, half), half), :],
                preferred_element_type=F32,
            )
            for t, dec in enumerate(decs)
        ],
    )


def near_body(rows, place, mine, passed, codes, active, dec0, dec1, dec2, dec3, part, near, *outs):
    z, i = place[0], place[1]
    half = mine.shape[1] // 4
    pick(place, mine, passed, near)
    decoder_grads(-2.0 / rows, i, near, codes, (3, 1, 2, 0), outs)
    outs[0][half:] = jnp.broadcast_to(active[...], (outs[0].shape[0] - half, active.shape[1]))
    part[...] = back_through(i, near, (dec0, dec1, dec2, dec3), jnp.where(z >= 2, half, 0))


def far_error_body(rows, place, swapped, direct, codes, far, send, kept):
    pick(place, swapped, direct, far)
    decoder_grads(-2.0 / rows, place[1], far, codes, (3, 2), (send, kept))


def code_grad_body(
    rows, place, far, part, mask, dec0, dec1, dec2, dec3, turned, grad_low, bias_sum, norms, *sends
):
    z, i = place[0], place[1]
    half = far.shape[1] // 4
    width = 2 * half
    decs = (dec0, dec1, dec2, dec3)
    total = part[...] + back_through(i, far, decs, jnp.where(z >= 2, 0, half))
    squares = functools.reduce(jnp.add, [one_row(dec[width:, :]) for dec in decs])
    column_norms = jnp.sqrt(squares + 1e-06)
    norms[...] = column_norms
    code_grad = (-2.0 / rows) * total + column_norms / rows
    grad = jnp.where(mask[...] > 0, code_grad, 0.0)
    grad_low[...] = grad.astype(BF16)
    row = jnp.sum(grad, axis=0, keepdims=True)
    bias_sum[...] = row
    at = pl.multiple_of((i ^ 3) * width, width)
    block = jnp.dot(turned[pl.ds(at, width), :], grad_low[...], preferred_element_type=F32)
    sends[0][:half] = block[:half]
    sends[0][half:] = jnp.broadcast_to(row, (sends[0].shape[0] - half, row.shape[1]))
    sends[1][...] = block[half:]


def encoder_grads(i, turned, grad_low, slots, outs):
    width = turned.shape[0] // 4
    for slot, out in zip(slots, outs):
        at = pl.ds(pl.multiple_of((i ^ slot) * width, width), width)
        out[:width] = jnp.dot(turned[at, :], grad_low[...], preferred_element_type=F32)


def rest_body(rows, place, turned, grad_low, near, far, codes, home, send, kept_far, kept, *outs):
    z, i = place[0], place[1]
    half = far.shape[1] // 4
    shift = jnp.where(z >= 2, 0, half)
    encoder_grads(i, turned, grad_low, (2, 1, 0), (kept_far, send, kept))
    decoder_grads(-2.0 / rows, i, far, codes, (1, 0), outs)
    home[:, columns(half - shift, half)] = near[:, columns(z * half, half)]
    home[:, columns(shift, half)] = far[:, columns(z * half, half)]


def power(values):
    largest = jnp.max(jnp.abs(values), axis=0, keepdims=True)
    return jnp.ceil(jnp.log(jnp.maximum(largest, 1e-30)) * (1.0 / math.log(2.0)))


def scale_of(exponent):
    return jnp.exp(exponent * math.log(2.0))


def pack_body(place, kept, row, *refs):
    width = kept.shape[0]
    at = [ref.shape[0] == width + EXTRA for ref in refs].index(True)
    received, packed, row_sums = refs[:at], refs[at], refs[at + 1 :]
    block = width // len(received)
    total = jnp.concatenate([piece[:block] for piece in received], axis=0) + kept[...]
    exponent = power(total)
    packed[:width] = total * scale_of(14.0 - exponent)
    sums = row[...]
    if received[0].shape[0] > block:
        sums += received[0][block : block + 1]
    for row_sum in row_sums:
        row_sum[...] = sums
    row_exponent = power(sums)
    parts = three_rows(sums * scale_of(14.0 - row_exponent)).astype(F32)
    at = lax.broadcasted_iota(jnp.int32, parts.shape, 0)
    parts = jnp.where(at == 3, exponent, jnp.where(at == 4, row_exponent, parts))
    packed[width:] = parts


def unpack(packed):
    width = packed.shape[0] - EXTRA
    rows = packed[width:].astype(F32)
    block = packed[:width].astype(F32) * scale_of(rows[3:4] - 14.0)
    row = (rows[0:1] + rows[1:2] + rows[2:3]) * scale_of(rows[4:5] - 14.0)
    return block, row


def bias_step_body(place, param, moment, square, here, there, param_out, moment_out, square_out):
    width = param.shape[1]
    grad = here[...] + there[...]
    pieces = [grad[:, b * width : (b + 1) * width] for b in range(4)]
    own = functools.reduce(
        jnp.add, [jnp.where(place[1] == b, piece, 0.0) for b, piece in enumerate(pieces)]
    )
    param_out[...], moment_out[...], square_out[...] = adam_update(
        param[...], own, moment[...], square[...]
    )


def decoder_step_body(
    rows, place, param, moment, square, near, far, active, norms, param_out, moment_out, square_out
):
    is_near = (pl.program_id(0) < pl.num_programs(0) // 2) == (place[0] < 2)
    grad = jnp.where(is_near, near[...], far[...])
    grad += param[...] * (active[...] / norms[...]) / rows
    param_out[...], moment_out[...], square_out[...] = adam_update(
        param[...], grad, moment[...], square[...]
    )


def line_shards(
    activations,
    encoder,
    enc_bias,
    decoder,
    enc_moment,
    enc_square,
    bias_moment,
    bias_square,
    dec_moment,
    dec_square,
):
    rows = activations.shape[0] * 4
    count, width = activations.shape
    latents = encoder.shape[1]
    half = width // 2
    features = 4 * width
    z, i = lax.axis_index("latent"), lax.axis_index("dp")
    place = jnp.stack([z, i]).astype(jnp.int32)

    def along(value, pairs):
        return lax.ppermute(value, "latent", pairs)

    def flip(value, bits, planes=(0, 1, 2, 3)):
        pairs = [(4 * p + k, 4 * p + (k ^ bits)) for p in planes for k in range(4)]
        return lax.ppermute(value, ("latent", "dp"), pairs)

    ends = [(1, 0), (2, 3)]
    low = along(activations, [(0, 1), (1, 2), (2, 3)])
    high = along(activations, [(1, 0), (2, 1), (3, 2)])
    across = along(activations, [(0, 2), (3, 1)])

    (enc_own,) = local_kernel(
        encoder_body,
        [shape((width + EXTRA, latents), BF16)],
        place,
        encoder,
        enc_bias.reshape(1, -1),
    )
    enc_chip, enc_core = flip(enc_own, 2), flip(enc_own, 1)
    (dec_own,) = local_kernel(
        decoder_body,
        [shape((width + EXTRA, latents), BF16)],
        place,
        decoder,
        after=(enc_core,),
    )
    dec_chip, dec_core = flip(dec_own, 2), flip(dec_own, 1)
    (onward,) = local_kernel(
        onward_body, [shape((count, width), BF16)], place, low, high
    )
    relay1 = along(onward, ends)
    relay2 = along(across, ends)
    enc = [enc_own, enc_core, enc_chip, flip(behind(enc_chip, relay2), 1)]

    up, down, beyond = local_kernel(
        pieces_body, [shape((half, latents), BF16)] * 3, place, dec_own
    )
    dec_pieces = [
        along(up, [(0, 1), (1, 2)]),
        along(down, [(2, 1), (3, 2)]),
        along(beyond, [(0, 2), (3, 1)]),
    ]
    dec = [dec_own, dec_core, dec_chip, flip(dec_chip, 1)]

    rows_own = jnp.concatenate([behind(piece, dec_chip) for piece in dec_pieces], axis=0)
    codes, mask, inputs, active = local_kernel(
        codes_body,
        [
            shape((count, latents), BF16),
            shape((count, latents), BF16),
            shape((count, features), BF16),
            shape((1, latents), F32),
        ],
        place,
        activations,
        low,
        high,
        across,
        relay1,
        relay2,
        *enc,
        after=(rows_own, dec[1], dec[3]),
        scratch=[pltpu.VMEM((1, latents), F32)],
    )
    codes_near = along(codes, [(0, 1), (3, 2)])
    codes_middle = along(codes, [(1, 2), (2, 1)])
    codes_across = along(codes, [(0, 2), (3, 1)])
    (turned,) = local_kernel(
        turn_body, [shape((features, count), BF16)], place, inputs, after=(codes_across,)
    )
    rows_chip = flip(rows_own, 2, (1, 2))
    rows_core = flip(behind(rows_own, codes), 1, (1, 2))
    rows_both = flip(behind(rows_chip, codes_middle), 1, (1, 2))

    all_codes = codes, codes_across, codes_middle, codes_near
    (made,) = local_kernel(
        own_error_body,
        [shape((count, features // 4), BF16)],
        place,
        *all_codes,
        dec[0],
        dec[2],
        rows_own,
        rows_chip,
        inputs,
        cost=NOTABLE,
    )
    (own_error,) = local_kernel(
        error_body,
        [shape((count, features // 2), BF16)],
        place,
        *all_codes,
        dec[1],
        dec[3],
        rows_core,
        rows_both,
        inputs,
        made,
    )
    swapped = along(own_error, [(1, 2), (2, 1)])
    passed = along(own_error, [(1, 0), (2, 3)])
    direct = along(own_error, [(2, 0), (1, 3)])

    def across_chips(kept, row, *send, keep_row=True):
        packed, *row_sum = local_kernel(
            pack_body,
            [shape((kept.shape[0] + EXTRA, latents), F32)] + [shape((1, latents), F32)] * keep_row,
            place,
            kept,
            row,
            *[flip(piece, 1) for piece in send],
        )
        return packed, flip(packed.astype(jnp.float16), 2), *row_sum

    blocks = [shape((half + 8, latents), F32)] + [shape((half, latents), F32)] * 3
    part, near, *near_blocks = local_kernel(
        functools.partial(near_body, rows),
        [shape((count, latents), F32), shape((count, features // 2), BF16), *blocks],
        place,
        own_error,
        passed,
        codes,
        active,
        *dec,
        after=(swapped,),
    )
    send_far, send_near, keep_far, keep_near = near_blocks
    near_packed, near_received, active_sum = across_chips(keep_far, active, send_far)
    near_kept = keep_near, flip(send_near, 1)
    far, far_send, far_keep = local_kernel(
        functools.partial(far_error_body, rows),
        [shape((count, features // 2), BF16)] + [shape((half, latents), F32)] * 2,
        place,
        swapped,
        direct,
        codes,
        after=(near_packed, near_kept[1]),
        cost=NOTABLE,
    )
    grad_low, bias_sum, norms, *send_far_enc = local_kernel(
        functools.partial(code_grad_body, rows),
        [
            shape((count, latents), BF16),
            shape((1, latents), F32),
            shape((1, latents), F32),
            shape((half + 8, latents), F32),
            shape((half, latents), F32),
        ],
        place,
        far,
        behind(part, near_received),
        mask,
        *dec,
        turned,
        cost=NOTABLE,
    )
    far_packed, far_received = across_chips(far_keep, active, far_send, keep_row=False)
    error, enc_send_near, enc_keep_far, enc_keep_near, send_near, keep_near = local_kernel(
        functools.partial(rest_body, rows),
        [shape((count, width), BF16)]
        + [shape((width, latents), F32)] * 3
        + [shape((half, latents), F32)] * 2,
        place,
        turned,
        grad_low,
        near,
        far,
        codes,
        after=(far_packed,),
    )
    far_kept = keep_near, flip(send_near, 1)
    enc_packed, enc_received, bias_here = across_chips(enc_keep_far, bias_sum, *send_far_enc)
    enc_kept = enc_keep_near, flip(enc_send_near, 1)

    decoder, dec_moment, dec_square, encoder, enc_moment, enc_square = lax.optimization_barrier(
        (decoder, dec_moment, dec_square, encoder, enc_moment, enc_square, enc_packed)
    )[:6]
    near_block, active_there = unpack(near_received)
    far_block, _ = unpack(far_received)
    enc_block, bias_there = unpack(enc_received)
    near_grad = near_kept[0] + near_kept[1] + near_block
    far_grad = far_kept[0] + far_kept[1] + far_block
    active_sum = active_sum + active_there
    grad_encoder = enc_kept[0] + enc_kept[1] + enc_block
    new_enc_bias, new_bias_moment, new_bias_square = [
        value.reshape(-1)
        for value in local_kernel(
            bias_step_body,
            [shape((1, enc_bias.shape[0]), F32)] * 3,
            place,
            enc_bias.reshape(1, -1),
            bias_moment.reshape(1, -1),
            bias_square.reshape(1, -1),
            bias_here,
            bias_there,
        )
    ]
    new_encoder, new_enc_moment, new_enc_square = adam_update(
        encoder, grad_encoder, enc_moment, enc_square
    )
    step = width // 4
    block = pl.BlockSpec((step, latents), lambda r: (r, 0))
    in_half = pl.BlockSpec((step, latents), lambda r: (r % 2, 0))
    row = pl.BlockSpec((1, latents), lambda r: (0, 0))
    new_decoder, new_dec_moment, new_dec_square = pl.pallas_call(
        functools.partial(decoder_step_body, rows),
        grid=(4,),
        out_shape=[shape((width, latents), F32)] * 3,
        in_specs=[SMEM, block, block, block, in_half, in_half, row, row],
        out_specs=[block] * 3,
        compiler_params=pltpu.CompilerParams(vmem_limit_bytes=12 * 1024 * 1024),
        cost_estimate=pl.CostEstimate(flops=1, bytes_accessed=1, transcendentals=0),
    )(place, decoder, dec_moment, dec_square, near_grad, far_grad, active_sum, norms)
    return (
        error,
        new_encoder,
        new_enc_bias,
        new_decoder,
        new_enc_moment,
        new_enc_square,
        new_bias_moment,
        new_bias_square,
        new_dec_moment,
        new_dec_square,
    )


def solution(mesh):
    in_specs = (
        P(("groups", "dp"), "latent"),
        P(("groups", "dp"), "latent"),
        P(("groups", "latent", "dp")),
        P(("groups", "dp"), "latent"),
        P(("groups", "dp"), "latent"),
        P(("groups", "dp"), "latent"),
        P(("groups", "latent", "dp")),
        P(("groups", "latent", "dp")),
        P(("groups", "dp"), "latent"),
        P(("groups", "dp"), "latent"),
    )
    out_specs = (
        P(("groups", "dp"), "latent"),
        P(("groups", "dp"), "latent"),
        P(("groups", "latent", "dp")),
        P(("groups", "dp"), "latent"),
        P(("groups", "dp"), "latent"),
        P(("groups", "dp"), "latent"),
        P(("groups", "latent", "dp")),
        P(("groups", "latent", "dp")),
        P(("groups", "dp"), "latent"),
        P(("groups", "dp"), "latent"),
    )
    line = mesh.shape["latent"] == 4 and mesh.shape["dp"] == 4
    plan = line_shards if line else shards
    return jax.shard_map(plan, mesh=mesh, in_specs=in_specs, out_specs=out_specs, check_vma=False)
```

```python
import functools
import math

import jax
import jax.numpy as jnp
from jax import lax
from jax.experimental import pallas as pl
from jax.experimental.pallas import tpu as pltpu
from jax.sharding import PartitionSpec as P

ADAM_STEP = 1000


first_decay = 0.9
second_decay = 0.999
learn_rate = 0.001
epsilon = 1e-08

F32 = jnp.float32
BF16 = jnp.bfloat16


def adam_update(param, grad, moment, square):
    moment_new = first_decay * moment + (1.0 - first_decay) * grad
    square_new = second_decay * square + (1.0 - second_decay) * grad * grad
    first_fix = 1.0 - first_decay**ADAM_STEP
    second_fix = 1.0 - second_decay**ADAM_STEP
    param_new = param - learn_rate * (moment_new / first_fix) / (
        jnp.sqrt(square_new / second_fix) + epsilon
    )
    return (param_new, moment_new, square_new)


def shards(
    activations,
    encoder,
    enc_bias,
    decoder,
    enc_moment,
    enc_square,
    bias_moment,
    bias_square,
    dec_moment,
    dec_square,
):
    row_count = activations.shape[0] * lax.axis_size("dp")
    loss_scale = 2.0 / row_count
    inputs = lax.all_gather(activations, "latent", axis=1, tiled=True)
    enc_low, dec_low = (
        lax.all_gather(encoder.astype(jnp.bfloat16), "dp", axis=0, tiled=True),
        lax.all_gather(decoder.astype(jnp.bfloat16), "dp", axis=0, tiled=True),
    )
    bias_full = lax.all_gather(enc_bias, "dp", axis=0, tiled=True)
    square_sums = lax.psum(jnp.sum(decoder * decoder, axis=0), "dp")
    column_norms = jnp.sqrt(square_sums + 1e-06)
    preact = jnp.dot(inputs, enc_low, preferred_element_type=jnp.float32) + bias_full
    latent_codes = jnp.maximum(preact, 0.0).astype(jnp.bfloat16)
    partial_sums = lax.dot_general(
        latent_codes, dec_low, (((1,), (1,)), ((), ())), preferred_element_type=jnp.float32
    )
    rebuilt = lax.psum_scatter(partial_sums, "latent", scatter_dimension=1, tiled=True)
    error = (activations.astype(jnp.float32) - rebuilt).astype(jnp.bfloat16)
    full_error = lax.all_gather(error, "latent", axis=1, tiled=True)
    active_sum = lax.psum(jnp.sum(latent_codes.astype(jnp.float32), axis=0), "dp")
    grad_dec_rows = -loss_scale * lax.dot_general(
        full_error, latent_codes, (((0,), (0,)), ((), ())), preferred_element_type=jnp.float32
    )
    code_grad = (
        -loss_scale * jnp.dot(full_error, dec_low, preferred_element_type=jnp.float32)
        + column_norms / row_count
    )
    grad_preact = jnp.where(preact > 0.0, code_grad, 0.0)
    grad_encoder = lax.dot_general(
        inputs,
        grad_preact.astype(jnp.bfloat16),
        (((0,), (0,)), ((), ())),
        preferred_element_type=jnp.float32,
    )
    grad_bias = jnp.sum(grad_preact, axis=0)
    grad_encoder, grad_dec_rows, grad_bias = (
        lax.psum_scatter(grad_encoder, "dp", scatter_dimension=0, tiled=True),
        lax.psum_scatter(grad_dec_rows, "dp", scatter_dimension=0, tiled=True),
        lax.psum_scatter(grad_bias, "dp", scatter_dimension=0, tiled=True),
    )
    grad_decoder = grad_dec_rows + decoder * (active_sum / column_norms) / row_count
    new_encoder, new_enc_moment, new_enc_square = adam_update(
        encoder, grad_encoder, enc_moment, enc_square
    )
    new_enc_bias, new_bias_moment, new_bias_square = adam_update(
        enc_bias, grad_bias, bias_moment, bias_square
    )
    new_decoder, new_dec_moment, new_dec_square = adam_update(
        decoder, grad_decoder, dec_moment, dec_square
    )
    return (
        error,
        new_encoder,
        new_enc_bias,
        new_decoder,
        new_enc_moment,
        new_enc_square,
        new_bias_moment,
        new_bias_square,
        new_dec_moment,
        new_dec_square,
    )


VMEM = pl.BlockSpec(memory_space=pltpu.VMEM)
SMEM = pl.BlockSpec(memory_space=pltpu.SMEM)
ANY = pl.BlockSpec(memory_space=pl.ANY)
EXTRA = 16
NOTABLE = 10**10


def local_kernel(body, outs, place, *args, after=(), scratch=(), cost=1):
    def run(place, *refs):
        body(place, *refs[: len(args)], *refs[len(args) + len(after) :])

    held = sum(a.size * jnp.dtype(a.dtype).itemsize for a in (*args, *outs))
    return pl.pallas_call(
        run,
        out_shape=outs,
        in_specs=[SMEM] + [VMEM] * len(args) + [ANY] * len(after),
        out_specs=[VMEM] * len(outs),
        scratch_shapes=scratch,
        compiler_params=pltpu.CompilerParams(vmem_limit_bytes=held + 6 * 1024 * 1024),
        cost_estimate=pl.CostEstimate(flops=cost, bytes_accessed=1, transcendentals=0),
    )(place, *args, *after)


def shape(dims, dtype):
    return jax.ShapeDtypeStruct(dims, dtype)


def columns(start, width):
    return pl.ds(pl.multiple_of(start, width), width)


def three_rows(row):
    high = row.astype(BF16).astype(F32)
    middle = (row - high).astype(BF16).astype(F32)
    low = row - high - middle
    at = lax.broadcasted_iota(jnp.int32, (EXTRA, row.shape[1]), 0)
    rows = jnp.where(at == 0, high, jnp.where(at == 1, middle, jnp.where(at == 2, low, 0.0)))
    return rows.astype(BF16)


def behind(value, *others):
    return lax.optimization_barrier((value, *others))[0]


def one_row(rows):
    return jnp.sum(rows.astype(F32), axis=0, keepdims=True)


def encoder_body(place, encoder, bias, out):
    depth = encoder.shape[0]
    out[:depth] = encoder[...].astype(BF16)
    out[depth:] = three_rows(jnp.concatenate([bias[...]] * 4, axis=1))


def decoder_body(place, decoder, out):
    depth = decoder.shape[0]
    value = decoder[...]
    out[:depth] = value.astype(BF16)
    out[depth:] = three_rows(jnp.sum(value * value, axis=0, keepdims=True))


def codes_body(
    place,
    own,
    low,
    high,
    across,
    relay1,
    relay2,
    enc0,
    enc1,
    enc2,
    enc3,
    codes,
    mask,
    full,
    active,
    bias,
):
    z, i = place[0], place[1]
    width = own.shape[1]
    for at, blocks in enumerate(
        (
            (own, high, relay1, relay2),
            (low, own, high, across),
            (across, low, own, high),
            (relay2, relay1, low, own),
        )
    ):

        @pl.when(z == at)
        def _(blocks=blocks):
            for b, block in enumerate(blocks):
                full[:, b * width : (b + 1) * width] = block[...]

    total = jnp.zeros(codes.shape, F32)
    piece = codes.shape[1] // 4
    for t, enc in enumerate((enc0, enc1, enc2, enc3)):
        b = i ^ t
        total += jnp.dot(
            full[:, columns(b * width, width)], enc[:width, :], preferred_element_type=F32
        )
        bias[:, columns(b * piece, piece)] = one_row(enc[width:, :piece])
    preact = total + bias[...]
    low_codes = jnp.maximum(preact, 0.0).astype(BF16)
    codes[...] = low_codes
    mask[...] = (preact > 0.0).astype(F32).astype(BF16)
    active[...] = jnp.sum(low_codes.astype(F32), axis=0, keepdims=True)


def onward_body(place, low, high, out):
    @pl.when(place[0] == 1)
    def _():
        out[...] = high[...]

    @pl.when(place[0] != 1)
    def _():
        out[...] = low[...]


def pieces_body(place, dec, up, down, across):
    z = place[0]
    half = up.shape[0]
    for out, second in ((up, z >= 1), (down, z >= 3), (across, z < 2)):
        out[...] = dec[pl.ds(pl.multiple_of(jnp.where(second, half, 0), half), half), :]


def turn_body(place, full, turned):
    turned[...] = full[...].T


def rebuilt_error(place, t, codes, dec, row, inputs):
    z, i = place[0], place[1]
    half = row.shape[0] // 3
    shift = pl.multiple_of(jnp.where(z >= 2, half, 0), half)
    below = pl.multiple_of(jnp.where(z == 1, 0, half), half)
    rights = [
        dec[pl.ds(shift, half), :],
        row[pl.ds(below, half), :],
        row[2 * half :, :],
        row[pl.ds(half - below, half), :],
    ]
    total = jnp.zeros((codes[0].shape[0], half), F32)
    for left, right in zip(codes, rights):
        total += lax.dot_general(
            left[...], right, (((1,), (1,)), ((), ())), preferred_element_type=F32
        )
    given = inputs[:, columns((i ^ t) * 2 * half + shift, half)].astype(F32)
    return (given - total).astype(BF16)


def own_error_body(place, own, near, across, middle, dec0, dec2, row0, row2, inputs, out):
    half = out.shape[1] // 2
    codes = (own, near, across, middle)
    out[:, :half] = rebuilt_error(place, 0, codes, dec0, row0, inputs)
    out[:, half:] = rebuilt_error(place, 2, codes, dec2, row2, inputs)


def error_body(place, own, near, across, middle, dec1, dec3, row1, row3, inputs, made, error):
    i = place[1]
    half = error.shape[1] // 4
    codes = (own, near, across, middle)
    error[:, columns(i * half, half)] = made[:, :half]
    error[:, columns((i ^ 2) * half, half)] = made[:, half:]
    error[:, columns((i ^ 1) * half, half)] = rebuilt_error(place, 1, codes, dec1, row1, inputs)
    error[:, columns((i ^ 3) * half, half)] = rebuilt_error(place, 3, codes, dec3, row3, inputs)


def pick(place, middle, end, out):
    z = place[0]
    is_middle = (z == 1) | (z == 2)

    @pl.when(is_middle)
    def _():
        out[...] = middle[...]

    @pl.when(jnp.logical_not(is_middle))
    def _():
        out[...] = end[...]


def decoder_grads(scale, i, error, codes, slots, outs):
    half = error.shape[1] // 4
    for slot, out in zip(slots, outs):
        out[:half] = scale * lax.dot_general(
            error[:, columns((i ^ slot) * half, half)],
            codes[...],
            (((0,), (0,)), ((), ())),
            preferred_element_type=F32,
        )


def back_through(i, error, decs, shift):
    half = error.shape[1] // 4
    return functools.reduce(
        jnp.add,
        [
            jnp.dot(
                error[:, columns((i ^ t) * half, half)],
                dec[pl.ds(pl.multiple_of(shift, half), half), :],
                preferred_element_type=F32,
            )
            for t, dec in enumerate(decs)
        ],
    )


def near_body(rows, place, mine, passed, codes, active, dec0, dec1, dec2, dec3, part, near, *outs):
    z, i = place[0], place[1]
    half = mine.shape[1] // 4
    pick(place, mine, passed, near)
    decoder_grads(-2.0 / rows, i, near, codes, (3, 1, 2, 0), outs)
    outs[0][half:] = jnp.broadcast_to(active[...], (outs[0].shape[0] - half, active.shape[1]))
    part[...] = back_through(i, near, (dec0, dec1, dec2, dec3), jnp.where(z >= 2, half, 0))


def far_error_body(rows, place, swapped, direct, codes, far, send, kept):
    pick(place, swapped, direct, far)
    decoder_grads(-2.0 / rows, place[1], far, codes, (3, 2), (send, kept))


def code_grad_body(
    rows, place, far, part, mask, dec0, dec1, dec2, dec3, turned, grad_low, bias_sum, norms, *sends
):
    z, i = place[0], place[1]
    half = far.shape[1] // 4
    width = 2 * half
    decs = (dec0, dec1, dec2, dec3)
    total = part[...] + back_through(i, far, decs, jnp.where(z >= 2, 0, half))
    squares = functools.reduce(jnp.add, [one_row(dec[width:, :]) for dec in decs])
    column_norms = jnp.sqrt(squares + 1e-06)
    norms[...] = column_norms
    code_grad = (-2.0 / rows) * total + column_norms / rows
    grad = jnp.where(mask[...] > 0, code_grad, 0.0)
    grad_low[...] = grad.astype(BF16)
    row = jnp.sum(grad, axis=0, keepdims=True)
    bias_sum[...] = row
    at = pl.multiple_of((i ^ 3) * width, width)
    block = jnp.dot(turned[pl.ds(at, width), :], grad_low[...], preferred_element_type=F32)
    sends[0][:half] = block[:half]
    sends[0][half:] = jnp.broadcast_to(row, (sends[0].shape[0] - half, row.shape[1]))
    sends[1][...] = block[half:]


def encoder_grads(i, turned, grad_low, slots, outs):
    width = turned.shape[0] // 4
    for slot, out in zip(slots, outs):
        at = pl.ds(pl.multiple_of((i ^ slot) * width, width), width)
        out[:width] = jnp.dot(turned[at, :], grad_low[...], preferred_element_type=F32)


def rest_body(rows, place, turned, grad_low, near, far, codes, home, send, kept_far, kept, *outs):
    z, i = place[0], place[1]
    half = far.shape[1] // 4
    shift = jnp.where(z >= 2, 0, half)
    encoder_grads(i, turned, grad_low, (2, 1, 0), (kept_far, send, kept))
    decoder_grads(-2.0 / rows, i, far, codes, (1, 0), outs)
    home[:, columns(half - shift, half)] = near[:, columns(z * half, half)]
    home[:, columns(shift, half)] = far[:, columns(z * half, half)]


def power(values):
    largest = jnp.max(jnp.abs(values), axis=0, keepdims=True)
    return jnp.ceil(jnp.log(jnp.maximum(largest, 1e-30)) * (1.0 / math.log(2.0)))


def scale_of(exponent):
    return jnp.exp(exponent * math.log(2.0))


def pack_body(place, kept, row, *refs):
    width = kept.shape[0]
    at = [ref.shape[0] == width + EXTRA for ref in refs].index(True)
    received, packed, row_sums = refs[:at], refs[at], refs[at + 1 :]
    block = width // len(received)
    total = jnp.concatenate([piece[:block] for piece in received], axis=0) + kept[...]
    exponent = power(total)
    packed[:width] = total * scale_of(14.0 - exponent)
    sums = row[...]
    if received[0].shape[0] > block:
        sums += received[0][block : block + 1]
    for row_sum in row_sums:
        row_sum[...] = sums
    row_exponent = power(sums)
    parts = three_rows(sums * scale_of(14.0 - row_exponent)).astype(F32)
    at = lax.broadcasted_iota(jnp.int32, parts.shape, 0)
    parts = jnp.where(at == 3, exponent, jnp.where(at == 4, row_exponent, parts))
    packed[width:] = parts


def unpack(packed):
    width = packed.shape[0] - EXTRA
    rows = packed[width:].astype(F32)
    block = packed[:width].astype(F32) * scale_of(rows[3:4] - 14.0)
    row = (rows[0:1] + rows[1:2] + rows[2:3]) * scale_of(rows[4:5] - 14.0)
    return block, row


def bias_step_body(place, param, moment, square, here, there, param_out, moment_out, square_out):
    width = param.shape[1]
    grad = here[...] + there[...]
    pieces = [grad[:, b * width : (b + 1) * width] for b in range(4)]
    own = functools.reduce(
        jnp.add, [jnp.where(place[1] == b, piece, 0.0) for b, piece in enumerate(pieces)]
    )
    param_out[...], moment_out[...], square_out[...] = adam_update(
        param[...], own, moment[...], square[...]
    )


def decoder_step_body(
    rows, place, param, moment, square, near, far, active, norms, param_out, moment_out, square_out
):
    is_near = (pl.program_id(0) < pl.num_programs(0) // 2) == (place[0] < 2)
    grad = jnp.where(is_near, near[...], far[...])
    grad += param[...] * (active[...] / norms[...]) / rows
    param_out[...], moment_out[...], square_out[...] = adam_update(
        param[...], grad, moment[...], square[...]
    )


def line_shards(
    activations,
    encoder,
    enc_bias,
    decoder,
    enc_moment,
    enc_square,
    bias_moment,
    bias_square,
    dec_moment,
    dec_square,
):
    rows = activations.shape[0] * 4
    count, width = activations.shape
    latents = encoder.shape[1]
    half = width // 2
    features = 4 * width
    z, i = lax.axis_index("latent"), lax.axis_index("dp")
    place = jnp.stack([z, i]).astype(jnp.int32)

    def along(value, pairs):
        return lax.ppermute(value, "latent", pairs)

    def flip(value, bits, planes=(0, 1, 2, 3)):
        pairs = [(4 * p + k, 4 * p + (k ^ bits)) for p in planes for k in range(4)]
        return lax.ppermute(value, ("latent", "dp"), pairs)

    ends = [(1, 0), (2, 3)]
    low = along(activations, [(0, 1), (1, 2), (2, 3)])
    high = along(activations, [(1, 0), (2, 1), (3, 2)])
    across = along(activations, [(0, 2), (3, 1)])

    (enc_own,) = local_kernel(
        encoder_body,
        [shape((width + EXTRA, latents), BF16)],
        place,
        encoder,
        enc_bias.reshape(1, -1),
    )
    enc_chip, enc_core = flip(enc_own, 2), flip(enc_own, 1)
    (dec_own,) = local_kernel(
        decoder_body,
        [shape((width + EXTRA, latents), BF16)],
        place,
        decoder,
        after=(enc_core,),
    )
    dec_chip, dec_core = flip(dec_own, 2), flip(dec_own, 1)
    (onward,) = local_kernel(
        onward_body, [shape((count, width), BF16)], place, low, high
    )
    relay1 = along(onward, ends)
    relay2 = along(across, ends)
    enc = [enc_own, enc_core, enc_chip, flip(behind(enc_chip, relay2), 1)]

    up, down, beyond = local_kernel(
        pieces_body, [shape((half, latents), BF16)] * 3, place, dec_own
    )
    dec_pieces = [
        along(up, [(0, 1), (1, 2)]),
        along(down, [(2, 1), (3, 2)]),
        along(beyond, [(0, 2), (3, 1)]),
    ]
    dec = [dec_own, dec_core, dec_chip, flip(dec_chip, 1)]

    rows_own = jnp.concatenate([behind(piece, dec_chip) for piece in dec_pieces], axis=0)
    codes, mask, inputs, active = local_kernel(
        codes_body,
        [
            shape((count, latents), BF16),
            shape((count, latents), BF16),
            shape((count, features), BF16),
            shape((1, latents), F32),
        ],
        place,
        activations,
        low,
        high,
        across,
        relay1,
        relay2,
        *enc,
        after=(rows_own, dec[1], dec[3]),
        scratch=[pltpu.VMEM((1, latents), F32)],
    )
    codes_near = along(codes, [(0, 1), (3, 2)])
    codes_middle = along(codes, [(1, 2), (2, 1)])
    codes_across = along(codes, [(0, 2), (3, 1)])
    (turned,) = local_kernel(
        turn_body, [shape((features, count), BF16)], place, inputs, after=(codes_across,)
    )
    rows_chip = flip(rows_own, 2, (1, 2))
    rows_core = flip(behind(rows_own, codes), 1, (1, 2))
    rows_both = flip(behind(rows_chip, codes_across), 1, (1, 2))

    all_codes = codes, codes_near, codes_across, codes_middle
    (made,) = local_kernel(
        own_error_body,
        [shape((count, features // 4), BF16)],
        place,
        *all_codes,
        dec[0],
        dec[2],
        rows_own,
        rows_chip,
        inputs,
        cost=NOTABLE,
    )
    (own_error,) = local_kernel(
        error_body,
        [shape((count, features // 2), BF16)],
        place,
        *all_codes,
        dec[1],
        dec[3],
        rows_core,
        rows_both,
        inputs,
        made,
    )
    swapped = along(own_error, [(1, 2), (2, 1)])
    passed = along(own_error, [(1, 0), (2, 3)])
    direct = along(own_error, [(2, 0), (1, 3)])

    def across_chips(kept, row, *send, keep_row=True):
        packed, *row_sum = local_kernel(
            pack_body,
            [shape((kept.shape[0] + EXTRA, latents), F32)] + [shape((1, latents), F32)] * keep_row,
            place,
            kept,
            row,
            *[flip(piece, 1) for piece in send],
        )
        return packed, flip(packed.astype(jnp.float16), 2), *row_sum

    blocks = [shape((half + 8, latents), F32)] + [shape((half, latents), F32)] * 3
    part, near, *near_blocks = local_kernel(
        functools.partial(near_body, rows),
        [shape((count, latents), F32), shape((count, features // 2), BF16), *blocks],
        place,
        own_error,
        passed,
        codes,
        active,
        *dec,
        after=(swapped,),
    )
    send_far, send_near, keep_far, keep_near = near_blocks
    near_packed, near_received, active_sum = across_chips(keep_far, active, send_far)
    near_kept = keep_near, flip(send_near, 1)
    far, far_send, far_keep = local_kernel(
        functools.partial(far_error_body, rows),
        [shape((count, features // 2), BF16)] + [shape((half, latents), F32)] * 2,
        place,
        swapped,
        direct,
        codes,
        after=(near_packed, near_kept[1]),
        cost=NOTABLE,
    )
    grad_low, bias_sum, norms, *send_far_enc = local_kernel(
        functools.partial(code_grad_body, rows),
        [
            shape((count, latents), BF16),
            shape((1, latents), F32),
            shape((1, latents), F32),
            shape((half + 8, latents), F32),
            shape((half, latents), F32),
        ],
        place,
        far,
        behind(part, near_received),
        mask,
        *dec,
        turned,
        cost=NOTABLE,
    )
    far_packed, far_received = across_chips(far_keep, active, far_send, keep_row=False)
    error, enc_send_near, enc_keep_far, enc_keep_near, send_near, keep_near = local_kernel(
        functools.partial(rest_body, rows),
        [shape((count, width), BF16)]
        + [shape((width, latents), F32)] * 3
        + [shape((half, latents), F32)] * 2,
        place,
        turned,
        grad_low,
        near,
        far,
        codes,
        after=(far_packed,),
    )
    far_kept = keep_near, flip(send_near, 1)
    enc_packed, enc_received, bias_here = across_chips(enc_keep_far, bias_sum, *send_far_enc)
    enc_kept = enc_keep_near, flip(enc_send_near, 1)

    decoder, dec_moment, dec_square, encoder, enc_moment, enc_square = lax.optimization_barrier(
        (decoder, dec_moment, dec_square, encoder, enc_moment, enc_square, enc_packed)
    )[:6]
    near_block, active_there = unpack(near_received)
    far_block, _ = unpack(far_received)
    enc_block, bias_there = unpack(enc_received)
    near_grad = near_kept[0] + near_kept[1] + near_block
    far_grad = far_kept[0] + far_kept[1] + far_block
    active_sum = active_sum + active_there
    grad_encoder = enc_kept[0] + enc_kept[1] + enc_block
    new_enc_bias, new_bias_moment, new_bias_square = [
        value.reshape(-1)
        for value in local_kernel(
            bias_step_body,
            [shape((1, enc_bias.shape[0]), F32)] * 3,
            place,
            enc_bias.reshape(1, -1),
            bias_moment.reshape(1, -1),
            bias_square.reshape(1, -1),
            bias_here,
            bias_there,
        )
    ]
    new_encoder, new_enc_moment, new_enc_square = adam_update(
        encoder, grad_encoder, enc_moment, enc_square
    )
    step = width // 4
    block = pl.BlockSpec((step, latents), lambda r: (r, 0))
    in_half = pl.BlockSpec((step, latents), lambda r: (r % 2, 0))
    row = pl.BlockSpec((1, latents), lambda r: (0, 0))
    new_decoder, new_dec_moment, new_dec_square = pl.pallas_call(
        functools.partial(decoder_step_body, rows),
        grid=(4,),
        out_shape=[shape((width, latents), F32)] * 3,
        in_specs=[SMEM, block, block, block, in_half, in_half, row, row],
        out_specs=[block] * 3,
        compiler_params=pltpu.CompilerParams(vmem_limit_bytes=12 * 1024 * 1024),
        cost_estimate=pl.CostEstimate(flops=1, bytes_accessed=1, transcendentals=0),
    )(place, decoder, dec_moment, dec_square, near_grad, far_grad, active_sum, norms)
    return (
        error,
        new_encoder,
        new_enc_bias,
        new_decoder,
        new_enc_moment,
        new_enc_square,
        new_bias_moment,
        new_bias_square,
        new_dec_moment,
        new_dec_square,
    )


def solution(mesh):
    in_specs = (
        P(("groups", "dp"), "latent"),
        P(("groups", "dp"), "latent"),
        P(("groups", "latent", "dp")),
        P(("groups", "dp"), "latent"),
        P(("groups", "dp"), "latent"),
        P(("groups", "dp"), "latent"),
        P(("groups", "latent", "dp")),
        P(("groups", "latent", "dp")),
        P(("groups", "dp"), "latent"),
        P(("groups", "dp"), "latent"),
    )
    out_specs = (
        P(("groups", "dp"), "latent"),
        P(("groups", "dp"), "latent"),
        P(("groups", "latent", "dp")),
        P(("groups", "dp"), "latent"),
        P(("groups", "dp"), "latent"),
        P(("groups", "dp"), "latent"),
        P(("groups", "latent", "dp")),
        P(("groups", "latent", "dp")),
        P(("groups", "dp"), "latent"),
        P(("groups", "dp"), "latent"),
    )
    line = mesh.shape["latent"] == 4 and mesh.shape["dp"] == 4
    plan = line_shards if line else shards
    return jax.shard_map(plan, mesh=mesh, in_specs=in_specs, out_specs=out_specs, check_vma=False)
```

```python
import functools
import math

import jax
import jax.numpy as jnp
from jax import lax
from jax.experimental import pallas as pl
from jax.experimental.pallas import tpu as pltpu
from jax.sharding import PartitionSpec as P

ADAM_STEP = 1000


first_decay = 0.9
second_decay = 0.999
learn_rate = 0.001
epsilon = 1e-08

F32 = jnp.float32
BF16 = jnp.bfloat16


def adam_update(param, grad, moment, square):
    moment_new = first_decay * moment + (1.0 - first_decay) * grad
    square_new = second_decay * square + (1.0 - second_decay) * grad * grad
    first_fix = 1.0 - first_decay**ADAM_STEP
    second_fix = 1.0 - second_decay**ADAM_STEP
    param_new = param - learn_rate * (moment_new / first_fix) / (
        jnp.sqrt(square_new / second_fix) + epsilon
    )
    return (param_new, moment_new, square_new)


def shards(
    activations,
    encoder,
    enc_bias,
    decoder,
    enc_moment,
    enc_square,
    bias_moment,
    bias_square,
    dec_moment,
    dec_square,
):
    row_count = activations.shape[0] * lax.axis_size("dp")
    loss_scale = 2.0 / row_count
    inputs = lax.all_gather(activations, "latent", axis=1, tiled=True)
    enc_low, dec_low = (
        lax.all_gather(encoder.astype(jnp.bfloat16), "dp", axis=0, tiled=True),
        lax.all_gather(decoder.astype(jnp.bfloat16), "dp", axis=0, tiled=True),
    )
    bias_full = lax.all_gather(enc_bias, "dp", axis=0, tiled=True)
    square_sums = lax.psum(jnp.sum(decoder * decoder, axis=0), "dp")
    column_norms = jnp.sqrt(square_sums + 1e-06)
    preact = jnp.dot(inputs, enc_low, preferred_element_type=jnp.float32) + bias_full
    latent_codes = jnp.maximum(preact, 0.0).astype(jnp.bfloat16)
    partial_sums = lax.dot_general(
        latent_codes, dec_low, (((1,), (1,)), ((), ())), preferred_element_type=jnp.float32
    )
    rebuilt = lax.psum_scatter(partial_sums, "latent", scatter_dimension=1, tiled=True)
    error = (activations.astype(jnp.float32) - rebuilt).astype(jnp.bfloat16)
    full_error = lax.all_gather(error, "latent", axis=1, tiled=True)
    active_sum = lax.psum(jnp.sum(latent_codes.astype(jnp.float32), axis=0), "dp")
    grad_dec_rows = -loss_scale * lax.dot_general(
        full_error, latent_codes, (((0,), (0,)), ((), ())), preferred_element_type=jnp.float32
    )
    code_grad = (
        -loss_scale * jnp.dot(full_error, dec_low, preferred_element_type=jnp.float32)
        + column_norms / row_count
    )
    grad_preact = jnp.where(preact > 0.0, code_grad, 0.0)
    grad_encoder = lax.dot_general(
        inputs,
        grad_preact.astype(jnp.bfloat16),
        (((0,), (0,)), ((), ())),
        preferred_element_type=jnp.float32,
    )
    grad_bias = jnp.sum(grad_preact, axis=0)
    grad_encoder, grad_dec_rows, grad_bias = (
        lax.psum_scatter(grad_encoder, "dp", scatter_dimension=0, tiled=True),
        lax.psum_scatter(grad_dec_rows, "dp", scatter_dimension=0, tiled=True),
        lax.psum_scatter(grad_bias, "dp", scatter_dimension=0, tiled=True),
    )
    grad_decoder = grad_dec_rows + decoder * (active_sum / column_norms) / row_count
    new_encoder, new_enc_moment, new_enc_square = adam_update(
        encoder, grad_encoder, enc_moment, enc_square
    )
    new_enc_bias, new_bias_moment, new_bias_square = adam_update(
        enc_bias, grad_bias, bias_moment, bias_square
    )
    new_decoder, new_dec_moment, new_dec_square = adam_update(
        decoder, grad_decoder, dec_moment, dec_square
    )
    return (
        error,
        new_encoder,
        new_enc_bias,
        new_decoder,
        new_enc_moment,
        new_enc_square,
        new_bias_moment,
        new_bias_square,
        new_dec_moment,
        new_dec_square,
    )


VMEM = pl.BlockSpec(memory_space=pltpu.VMEM)
SMEM = pl.BlockSpec(memory_space=pltpu.SMEM)
ANY = pl.BlockSpec(memory_space=pl.ANY)
EXTRA = 16
NOTABLE = 10**10


def local_kernel(body, outs, place, *args, ahead=(), after=(), scratch=(), cost=1):
    def run(place, *refs):
        refs = refs[len(ahead) :]
        body(place, *refs[: len(args)], *refs[len(args) + len(after) :])

    held = sum(a.size * jnp.dtype(a.dtype).itemsize for a in (*args, *outs))
    return pl.pallas_call(
        run,
        out_shape=outs,
        in_specs=[SMEM] + [ANY] * len(ahead) + [VMEM] * len(args) + [ANY] * len(after),
        out_specs=[VMEM] * len(outs),
        scratch_shapes=scratch,
        compiler_params=pltpu.CompilerParams(vmem_limit_bytes=held + 6 * 1024 * 1024),
        cost_estimate=pl.CostEstimate(flops=cost, bytes_accessed=1, transcendentals=0),
    )(place, *ahead, *args, *after)


def shape(dims, dtype):
    return jax.ShapeDtypeStruct(dims, dtype)


def columns(start, width):
    return pl.ds(pl.multiple_of(start, width), width)


def three_rows(row):
    high = row.astype(BF16).astype(F32)
    middle = (row - high).astype(BF16).astype(F32)
    low = row - high - middle
    at = lax.broadcasted_iota(jnp.int32, (EXTRA, row.shape[1]), 0)
    rows = jnp.where(at == 0, high, jnp.where(at == 1, middle, jnp.where(at == 2, low, 0.0)))
    return rows.astype(BF16)


def behind(value, *others):
    return lax.optimization_barrier((value, *others))[0]


def one_row(rows):
    return jnp.sum(rows.astype(F32), axis=0, keepdims=True)


def encoder_body(place, encoder, bias, out):
    depth = encoder.shape[0]
    out[:depth] = encoder[...].astype(BF16)
    out[depth:] = three_rows(jnp.concatenate([bias[...]] * 4, axis=1))


def decoder_body(place, decoder, out):
    depth = decoder.shape[0]
    value = decoder[...]
    out[:depth] = value.astype(BF16)
    out[depth:] = three_rows(jnp.sum(value * value, axis=0, keepdims=True))


def codes_body(
    place,
    own,
    low,
    high,
    across,
    relay1,
    relay2,
    enc0,
    enc1,
    enc2,
    enc3,
    codes,
    mask,
    full,
    active,
    bias,
):
    z, i = place[0], place[1]
    width = own.shape[1]
    for at, blocks in enumerate(
        (
            (own, high, relay1, relay2),
            (low, own, high, across),
            (across, low, own, high),
            (relay2, relay1, low, own),
        )
    ):

        @pl.when(z == at)
        def _(blocks=blocks):
            for b, block in enumerate(blocks):
                full[:, b * width : (b + 1) * width] = block[...]

    total = jnp.zeros(codes.shape, F32)
    piece = codes.shape[1] // 4
    for t, enc in enumerate((enc0, enc1, enc2, enc3)):
        b = i ^ t
        total += jnp.dot(
            full[:, columns(b * width, width)], enc[:width, :], preferred_element_type=F32
        )
        bias[:, columns(b * piece, piece)] = one_row(enc[width:, :piece])
    preact = total + bias[...]
    low_codes = jnp.maximum(preact, 0.0).astype(BF16)
    codes[...] = low_codes
    mask[...] = (preact > 0.0).astype(F32).astype(BF16)
    active[...] = jnp.sum(low_codes.astype(F32), axis=0, keepdims=True)


def onward_body(place, low, high, out):
    @pl.when(place[0] == 1)
    def _():
        out[...] = high[...]

    @pl.when(place[0] != 1)
    def _():
        out[...] = low[...]


def pieces_body(place, dec, up, down, across):
    z = place[0]
    half = up.shape[0]
    for out, second in ((up, z >= 1), (down, z >= 3), (across, z < 2)):
        out[...] = dec[pl.ds(pl.multiple_of(jnp.where(second, half, 0), half), half), :]


def turn_body(place, full, turned):
    turned[...] = full[...].T


def rebuilt_error(place, t, codes, dec, row, inputs):
    z, i = place[0], place[1]
    half = row.shape[0] // 3
    shift = pl.multiple_of(jnp.where(z >= 2, half, 0), half)
    below = pl.multiple_of(jnp.where(z == 1, 0, half), half)
    rights = [
        dec[pl.ds(shift, half), :],
        row[pl.ds(below, half), :],
        row[2 * half :, :],
        row[pl.ds(half - below, half), :],
    ]
    total = jnp.zeros((codes[0].shape[0], half), F32)
    for left, right in zip(codes, rights):
        total += lax.dot_general(
            left[...], right, (((1,), (1,)), ((), ())), preferred_element_type=F32
        )
    given = inputs[:, columns((i ^ t) * 2 * half + shift, half)].astype(F32)
    return (given - total).astype(BF16)


def own_error_body(place, own, near, across, middle, dec0, dec2, row0, row2, inputs, out):
    half = out.shape[1] // 2
    codes = (own, near, across, middle)
    out[:, :half] = rebuilt_error(place, 0, codes, dec0, row0, inputs)
    out[:, half:] = rebuilt_error(place, 2, codes, dec2, row2, inputs)


def error_body(place, own, near, across, middle, dec1, dec3, row1, row3, inputs, made, error):
    i = place[1]
    half = error.shape[1] // 4
    codes = (own, near, across, middle)
    error[:, columns(i * half, half)] = made[:, :half]
    error[:, columns((i ^ 2) * half, half)] = made[:, half:]
    error[:, columns((i ^ 1) * half, half)] = rebuilt_error(place, 1, codes, dec1, row1, inputs)
    error[:, columns((i ^ 3) * half, half)] = rebuilt_error(place, 3, codes, dec3, row3, inputs)


def pick(place, middle, end, out):
    z = place[0]
    is_middle = (z == 1) | (z == 2)

    @pl.when(is_middle)
    def _():
        out[...] = middle[...]

    @pl.when(jnp.logical_not(is_middle))
    def _():
        out[...] = end[...]


def decoder_grads(scale, i, error, codes, slots, outs):
    half = error.shape[1] // 4
    for slot, out in zip(slots, outs):
        out[:half] = scale * lax.dot_general(
            error[:, columns((i ^ slot) * half, half)],
            codes[...],
            (((0,), (0,)), ((), ())),
            preferred_element_type=F32,
        )


def back_through(i, error, decs, shift):
    half = error.shape[1] // 4
    return functools.reduce(
        jnp.add,
        [
            jnp.dot(
                error[:, columns((i ^ t) * half, half)],
                dec[pl.ds(pl.multiple_of(shift, half), half), :],
                preferred_element_type=F32,
            )
            for t, dec in enumerate(decs)
        ],
    )


def near_body(rows, place, mine, passed, codes, active, dec0, dec1, dec2, dec3, part, near, *outs):
    z, i = place[0], place[1]
    half = mine.shape[1] // 4
    pick(place, mine, passed, near)
    decoder_grads(-2.0 / rows, i, near, codes, (3, 1, 2, 0), outs)
    outs[0][half:] = jnp.broadcast_to(active[...], (outs[0].shape[0] - half, active.shape[1]))
    part[...] = back_through(i, near, (dec0, dec1, dec2, dec3), jnp.where(z >= 2, half, 0))


def far_error_body(rows, place, swapped, direct, codes, far, send, kept):
    pick(place, swapped, direct, far)
    decoder_grads(-2.0 / rows, place[1], far, codes, (3, 2), (send, kept))


def code_grad_body(
    rows, place, far, part, mask, dec0, dec1, dec2, dec3, turned, grad_low, bias_sum, norms, *sends
):
    z, i = place[0], place[1]
    half = far.shape[1] // 4
    width = 2 * half
    decs = (dec0, dec1, dec2, dec3)
    total = part[...] + back_through(i, far, decs, jnp.where(z >= 2, 0, half))
    squares = functools.reduce(jnp.add, [one_row(dec[width:, :]) for dec in decs])
    column_norms = jnp.sqrt(squares + 1e-06)
    norms[...] = column_norms
    code_grad = (-2.0 / rows) * total + column_norms / rows
    grad = jnp.where(mask[...] > 0, code_grad, 0.0)
    grad_low[...] = grad.astype(BF16)
    row = jnp.sum(grad, axis=0, keepdims=True)
    bias_sum[...] = row
    at = pl.multiple_of((i ^ 3) * width, width)
    block = jnp.dot(turned[pl.ds(at, width), :], grad_low[...], preferred_element_type=F32)
    sends[0][:half] = block[:half]
    sends[0][half:] = jnp.broadcast_to(row, (sends[0].shape[0] - half, row.shape[1]))
    sends[1][...] = block[half:]


def encoder_grads(i, turned, grad_low, slots, outs):
    width = turned.shape[0] // 4
    for slot, out in zip(slots, outs):
        at = pl.ds(pl.multiple_of((i ^ slot) * width, width), width)
        out[:width] = jnp.dot(turned[at, :], grad_low[...], preferred_element_type=F32)


def rest_body(rows, place, turned, grad_low, near, far, codes, home, send, kept_far, kept, *outs):
    z, i = place[0], place[1]
    half = far.shape[1] // 4
    shift = jnp.where(z >= 2, 0, half)
    encoder_grads(i, turned, grad_low, (2, 1, 0), (kept_far, send, kept))
    decoder_grads(-2.0 / rows, i, far, codes, (1, 0), outs)
    home[:, columns(half - shift, half)] = near[:, columns(z * half, half)]
    home[:, columns(shift, half)] = far[:, columns(z * half, half)]


def power(values):
    largest = jnp.max(jnp.abs(values), axis=0, keepdims=True)
    return jnp.ceil(jnp.log(jnp.maximum(largest, 1e-30)) * (1.0 / math.log(2.0)))


def scale_of(exponent):
    return jnp.exp(exponent * math.log(2.0))


def pack_body(place, kept, row, *refs):
    width = kept.shape[0]
    at = [ref.shape[0] == width + EXTRA for ref in refs].index(True)
    received, packed, row_sums = refs[:at], refs[at], refs[at + 1 :]
    block = width // len(received)
    total = jnp.concatenate([piece[:block] for piece in received], axis=0) + kept[...]
    exponent = power(total)
    packed[:width] = total * scale_of(14.0 - exponent)
    sums = row[...]
    if received[0].shape[0] > block:
        sums += received[0][block : block + 1]
    for row_sum in row_sums:
        row_sum[...] = sums
    row_exponent = power(sums)
    parts = three_rows(sums * scale_of(14.0 - row_exponent)).astype(F32)
    at = lax.broadcasted_iota(jnp.int32, parts.shape, 0)
    parts = jnp.where(at == 3, exponent, jnp.where(at == 4, row_exponent, parts))
    packed[width:] = parts


def unpack(packed):
    width = packed.shape[0] - EXTRA
    rows = packed[width:].astype(F32)
    block = packed[:width].astype(F32) * scale_of(rows[3:4] - 14.0)
    row = (rows[0:1] + rows[1:2] + rows[2:3]) * scale_of(rows[4:5] - 14.0)
    return block, row


def bias_step_body(place, param, moment, square, here, there, param_out, moment_out, square_out):
    width = param.shape[1]
    grad = here[...] + there[...]
    pieces = [grad[:, b * width : (b + 1) * width] for b in range(4)]
    own = functools.reduce(
        jnp.add, [jnp.where(place[1] == b, piece, 0.0) for b, piece in enumerate(pieces)]
    )
    param_out[...], moment_out[...], square_out[...] = adam_update(
        param[...], own, moment[...], square[...]
    )


def decoder_step_body(
    rows, place, param, moment, square, near, far, active, norms, param_out, moment_out, square_out
):
    is_near = (pl.program_id(0) < pl.num_programs(0) // 2) == (place[0] < 2)
    grad = jnp.where(is_near, near[...], far[...])
    grad += param[...] * (active[...] / norms[...]) / rows
    param_out[...], moment_out[...], square_out[...] = adam_update(
        param[...], grad, moment[...], square[...]
    )


def line_shards(
    activations,
    encoder,
    enc_bias,
    decoder,
    enc_moment,
    enc_square,
    bias_moment,
    bias_square,
    dec_moment,
    dec_square,
):
    rows = activations.shape[0] * 4
    count, width = activations.shape
    latents = encoder.shape[1]
    half = width // 2
    features = 4 * width
    z, i = lax.axis_index("latent"), lax.axis_index("dp")
    place = jnp.stack([z, i]).astype(jnp.int32)

    def along(value, pairs):
        return lax.ppermute(value, "latent", pairs)

    def flip(value, bits, planes=(0, 1, 2, 3)):
        pairs = [(4 * p + k, 4 * p + (k ^ bits)) for p in planes for k in range(4)]
        return lax.ppermute(value, ("latent", "dp"), pairs)

    ends = [(1, 0), (2, 3)]
    low = along(activations, [(0, 1), (1, 2), (2, 3)])
    high = along(activations, [(1, 0), (2, 1), (3, 2)])
    across = along(activations, [(0, 2), (3, 1)])

    (enc_own,) = local_kernel(
        encoder_body,
        [shape((width + EXTRA, latents), BF16)],
        place,
        encoder,
        enc_bias.reshape(1, -1),
    )
    enc_chip, enc_core = flip(enc_own, 2), flip(enc_own, 1)
    (dec_own,) = local_kernel(
        decoder_body,
        [shape((width + EXTRA, latents), BF16)],
        place,
        decoder,
        after=(enc_core,),
    )
    dec_chip, dec_core = flip(dec_own, 2), flip(dec_own, 1)
    (onward,) = local_kernel(
        onward_body, [shape((count, width), BF16)], place, low, high
    )
    relay1 = along(onward, ends)
    relay2 = along(across, ends)
    enc = [enc_own, enc_core, enc_chip, flip(behind(enc_chip, relay2), 1)]

    up, down, beyond = local_kernel(
        pieces_body, [shape((half, latents), BF16)] * 3, place, dec_own
    )
    dec_pieces = [
        along(up, [(0, 1), (1, 2)]),
        along(down, [(2, 1), (3, 2)]),
        along(beyond, [(0, 2), (3, 1)]),
    ]
    dec = [dec_own, dec_core, dec_chip, flip(dec_chip, 1)]

    rows_own = jnp.concatenate([behind(piece, dec_chip) for piece in dec_pieces], axis=0)
    codes, mask, inputs, active = local_kernel(
        codes_body,
        [
            shape((count, latents), BF16),
            shape((count, latents), BF16),
            shape((count, features), BF16),
            shape((1, latents), F32),
        ],
        place,
        activations,
        low,
        high,
        across,
        relay1,
        relay2,
        *enc,
        after=(rows_own, dec[1], dec[3]),
        scratch=[pltpu.VMEM((1, latents), F32)],
    )
    codes_near = along(codes, [(0, 1), (3, 2)])
    codes_middle = along(codes, [(1, 2), (2, 1)])
    codes_across = along(codes, [(0, 2), (3, 1)])
    (turned,) = local_kernel(
        turn_body, [shape((features, count), BF16)], place, inputs, after=(codes_across,)
    )
    rows_chip = flip(rows_own, 2, (1, 2))
    rows_core = flip(behind(rows_own, codes), 1, (1, 2))
    rows_both = flip(behind(rows_chip, codes_across), 1, (1, 2))

    all_codes = codes, codes_near, codes_across, codes_middle
    (made,) = local_kernel(
        own_error_body,
        [shape((count, features // 4), BF16)],
        place,
        *all_codes,
        dec[0],
        dec[2],
        rows_own,
        rows_chip,
        inputs,
        cost=NOTABLE,
    )
    (own_error,) = local_kernel(
        error_body,
        [shape((count, features // 2), BF16)],
        place,
        *all_codes,
        dec[1],
        dec[3],
        rows_core,
        rows_both,
        inputs,
        made,
    )
    swapped = along(own_error, [(1, 2), (2, 1)])
    passed = along(own_error, [(1, 0), (2, 3)])
    direct = along(own_error, [(2, 0), (1, 3)])

    def across_chips(kept, row, *send, keep_row=True):
        packed, *row_sum = local_kernel(
            pack_body,
            [shape((kept.shape[0] + EXTRA, latents), F32)] + [shape((1, latents), F32)] * keep_row,
            place,
            kept,
            row,
            *[flip(piece, 1) for piece in send],
        )
        return packed, flip(packed.astype(jnp.float16), 2), *row_sum

    blocks = [shape((half + 8, latents), F32)] + [shape((half, latents), F32)] * 3
    part, near, *near_blocks = local_kernel(
        functools.partial(near_body, rows),
        [shape((count, latents), F32), shape((count, features // 2), BF16), *blocks],
        place,
        own_error,
        passed,
        codes,
        active,
        *dec,
        after=(swapped,),
    )
    send_far, send_near, keep_far, keep_near = near_blocks
    near_packed, near_received, active_sum = across_chips(keep_far, active, send_far)
    near_kept = keep_near, flip(send_near, 1)
    far, far_send, far_keep = local_kernel(
        functools.partial(far_error_body, rows),
        [shape((count, features // 2), BF16)] + [shape((half, latents), F32)] * 2,
        place,
        swapped,
        direct,
        codes,
        ahead=(near_packed, near_kept[1]),
        cost=NOTABLE,
    )
    grad_low, bias_sum, norms, *send_far_enc = local_kernel(
        functools.partial(code_grad_body, rows),
        [
            shape((count, latents), BF16),
            shape((1, latents), F32),
            shape((1, latents), F32),
            shape((half + 8, latents), F32),
            shape((half, latents), F32),
        ],
        place,
        far,
        behind(part, near_received),
        mask,
        *dec,
        turned,
        cost=NOTABLE,
    )
    far_packed, far_received = across_chips(far_keep, active, far_send, keep_row=False)
    error, enc_send_near, enc_keep_far, enc_keep_near, send_near, keep_near = local_kernel(
        functools.partial(rest_body, rows),
        [shape((count, width), BF16)]
        + [shape((width, latents), F32)] * 3
        + [shape((half, latents), F32)] * 2,
        place,
        turned,
        grad_low,
        near,
        far,
        codes,
        after=(far_packed,),
    )
    far_kept = keep_near, flip(send_near, 1)
    enc_packed, enc_received, bias_here = across_chips(enc_keep_far, bias_sum, *send_far_enc)
    enc_kept = enc_keep_near, flip(enc_send_near, 1)

    decoder, dec_moment, dec_square, encoder, enc_moment, enc_square = lax.optimization_barrier(
        (decoder, dec_moment, dec_square, encoder, enc_moment, enc_square, enc_packed)
    )[:6]
    near_block, active_there = unpack(near_received)
    far_block, _ = unpack(far_received)
    enc_block, bias_there = unpack(enc_received)
    near_grad = near_kept[0] + near_kept[1] + near_block
    far_grad = far_kept[0] + far_kept[1] + far_block
    active_sum = active_sum + active_there
    grad_encoder = enc_kept[0] + enc_kept[1] + enc_block
    new_enc_bias, new_bias_moment, new_bias_square = [
        value.reshape(-1)
        for value in local_kernel(
            bias_step_body,
            [shape((1, enc_bias.shape[0]), F32)] * 3,
            place,
            enc_bias.reshape(1, -1),
            bias_moment.reshape(1, -1),
            bias_square.reshape(1, -1),
            bias_here,
            bias_there,
        )
    ]
    new_encoder, new_enc_moment, new_enc_square = adam_update(
        encoder, grad_encoder, enc_moment, enc_square
    )
    step = width // 4
    block = pl.BlockSpec((step, latents), lambda r: (r, 0))
    in_half = pl.BlockSpec((step, latents), lambda r: (r % 2, 0))
    row = pl.BlockSpec((1, latents), lambda r: (0, 0))
    new_decoder, new_dec_moment, new_dec_square = pl.pallas_call(
        functools.partial(decoder_step_body, rows),
        grid=(4,),
        out_shape=[shape((width, latents), F32)] * 3,
        in_specs=[SMEM, block, block, block, in_half, in_half, row, row],
        out_specs=[block] * 3,
        compiler_params=pltpu.CompilerParams(vmem_limit_bytes=12 * 1024 * 1024),
        cost_estimate=pl.CostEstimate(flops=1, bytes_accessed=1, transcendentals=0),
    )(place, decoder, dec_moment, dec_square, near_grad, far_grad, active_sum, norms)
    return (
        error,
        new_encoder,
        new_enc_bias,
        new_decoder,
        new_enc_moment,
        new_enc_square,
        new_bias_moment,
        new_bias_square,
        new_dec_moment,
        new_dec_square,
    )


def solution(mesh):
    in_specs = (
        P(("groups", "dp"), "latent"),
        P(("groups", "dp"), "latent"),
        P(("groups", "latent", "dp")),
        P(("groups", "dp"), "latent"),
        P(("groups", "dp"), "latent"),
        P(("groups", "dp"), "latent"),
        P(("groups", "latent", "dp")),
        P(("groups", "latent", "dp")),
        P(("groups", "dp"), "latent"),
        P(("groups", "dp"), "latent"),
    )
    out_specs = (
        P(("groups", "dp"), "latent"),
        P(("groups", "dp"), "latent"),
        P(("groups", "latent", "dp")),
        P(("groups", "dp"), "latent"),
        P(("groups", "dp"), "latent"),
        P(("groups", "dp"), "latent"),
        P(("groups", "latent", "dp")),
        P(("groups", "latent", "dp")),
        P(("groups", "dp"), "latent"),
        P(("groups", "dp"), "latent"),
    )
    line = mesh.shape["latent"] == 4 and mesh.shape["dp"] == 4
    plan = line_shards if line else shards
    return jax.shard_map(plan, mesh=mesh, in_specs=in_specs, out_specs=out_specs, check_vma=False)
```

```python
import functools
import math

import jax
import jax.numpy as jnp
from jax import lax
from jax.experimental import pallas as pl
from jax.experimental.pallas import tpu as pltpu
from jax.sharding import PartitionSpec as P

ADAM_STEP = 1000


first_decay = 0.9
second_decay = 0.999
learn_rate = 0.001
epsilon = 1e-08

F32 = jnp.float32
BF16 = jnp.bfloat16


def adam_update(param, grad, moment, square):
    moment_new = first_decay * moment + (1.0 - first_decay) * grad
    square_new = second_decay * square + (1.0 - second_decay) * grad * grad
    first_fix = 1.0 - first_decay**ADAM_STEP
    second_fix = 1.0 - second_decay**ADAM_STEP
    param_new = param - learn_rate * (moment_new / first_fix) / (
        jnp.sqrt(square_new / second_fix) + epsilon
    )
    return (param_new, moment_new, square_new)


def shards(
    activations,
    encoder,
    enc_bias,
    decoder,
    enc_moment,
    enc_square,
    bias_moment,
    bias_square,
    dec_moment,
    dec_square,
):
    row_count = activations.shape[0] * lax.axis_size("dp")
    loss_scale = 2.0 / row_count
    inputs = lax.all_gather(activations, "latent", axis=1, tiled=True)
    enc_low, dec_low = (
        lax.all_gather(encoder.astype(jnp.bfloat16), "dp", axis=0, tiled=True),
        lax.all_gather(decoder.astype(jnp.bfloat16), "dp", axis=0, tiled=True),
    )
    bias_full = lax.all_gather(enc_bias, "dp", axis=0, tiled=True)
    square_sums = lax.psum(jnp.sum(decoder * decoder, axis=0), "dp")
    column_norms = jnp.sqrt(square_sums + 1e-06)
    preact = jnp.dot(inputs, enc_low, preferred_element_type=jnp.float32) + bias_full
    latent_codes = jnp.maximum(preact, 0.0).astype(jnp.bfloat16)
    partial_sums = lax.dot_general(
        latent_codes, dec_low, (((1,), (1,)), ((), ())), preferred_element_type=jnp.float32
    )
    rebuilt = lax.psum_scatter(partial_sums, "latent", scatter_dimension=1, tiled=True)
    error = (activations.astype(jnp.float32) - rebuilt).astype(jnp.bfloat16)
    full_error = lax.all_gather(error, "latent", axis=1, tiled=True)
    active_sum = lax.psum(jnp.sum(latent_codes.astype(jnp.float32), axis=0), "dp")
    grad_dec_rows = -loss_scale * lax.dot_general(
        full_error, latent_codes, (((0,), (0,)), ((), ())), preferred_element_type=jnp.float32
    )
    code_grad = (
        -loss_scale * jnp.dot(full_error, dec_low, preferred_element_type=jnp.float32)
        + column_norms / row_count
    )
    grad_preact = jnp.where(preact > 0.0, code_grad, 0.0)
    grad_encoder = lax.dot_general(
        inputs,
        grad_preact.astype(jnp.bfloat16),
        (((0,), (0,)), ((), ())),
        preferred_element_type=jnp.float32,
    )
    grad_bias = jnp.sum(grad_preact, axis=0)
    grad_encoder, grad_dec_rows, grad_bias = (
        lax.psum_scatter(grad_encoder, "dp", scatter_dimension=0, tiled=True),
        lax.psum_scatter(grad_dec_rows, "dp", scatter_dimension=0, tiled=True),
        lax.psum_scatter(grad_bias, "dp", scatter_dimension=0, tiled=True),
    )
    grad_decoder = grad_dec_rows + decoder * (active_sum / column_norms) / row_count
    new_encoder, new_enc_moment, new_enc_square = adam_update(
        encoder, grad_encoder, enc_moment, enc_square
    )
    new_enc_bias, new_bias_moment, new_bias_square = adam_update(
        enc_bias, grad_bias, bias_moment, bias_square
    )
    new_decoder, new_dec_moment, new_dec_square = adam_update(
        decoder, grad_decoder, dec_moment, dec_square
    )
    return (
        error,
        new_encoder,
        new_enc_bias,
        new_decoder,
        new_enc_moment,
        new_enc_square,
        new_bias_moment,
        new_bias_square,
        new_dec_moment,
        new_dec_square,
    )


VMEM = pl.BlockSpec(memory_space=pltpu.VMEM)
SMEM = pl.BlockSpec(memory_space=pltpu.SMEM)
ANY = pl.BlockSpec(memory_space=pl.ANY)
EXTRA = 16
NOTABLE = 10**10


def local_kernel(body, outs, place, *args, after=(), scratch=(), cost=1):
    def run(place, *refs):
        body(place, *refs[: len(args)], *refs[len(args) + len(after) :])

    held = sum(a.size * jnp.dtype(a.dtype).itemsize for a in (*args, *outs))
    return pl.pallas_call(
        run,
        out_shape=outs,
        in_specs=[SMEM] + [VMEM] * len(args) + [ANY] * len(after),
        out_specs=[VMEM] * len(outs),
        scratch_shapes=scratch,
        compiler_params=pltpu.CompilerParams(vmem_limit_bytes=held + 6 * 1024 * 1024),
        cost_estimate=pl.CostEstimate(flops=cost, bytes_accessed=1, transcendentals=0),
    )(place, *args, *after)


def shape(dims, dtype):
    return jax.ShapeDtypeStruct(dims, dtype)


def columns(start, width):
    return pl.ds(pl.multiple_of(start, width), width)


def three_rows(row):
    high = row.astype(BF16).astype(F32)
    middle = (row - high).astype(BF16).astype(F32)
    low = row - high - middle
    at = lax.broadcasted_iota(jnp.int32, (EXTRA, row.shape[1]), 0)
    rows = jnp.where(at == 0, high, jnp.where(at == 1, middle, jnp.where(at == 2, low, 0.0)))
    return rows.astype(BF16)


def behind(value, *others):
    return lax.optimization_barrier((value, *others))[0]


def one_row(rows):
    return jnp.sum(rows.astype(F32), axis=0, keepdims=True)


def encoder_body(place, encoder, out):
    depth = encoder.shape[0]
    out[:depth] = encoder[...].astype(BF16)
    out[depth:] = jnp.zeros((out.shape[0] - depth, out.shape[1]), BF16)


def decoder_body(place, decoder, bias, out):
    depth = decoder.shape[0]
    value = decoder[...]
    out[:depth] = value.astype(BF16)
    out[depth : depth + EXTRA] = three_rows(jnp.sum(value * value, axis=0, keepdims=True))
    out[depth + EXTRA :] = three_rows(jnp.concatenate([bias[...]] * 4, axis=1))


def codes_body(
    place,
    own,
    low,
    high,
    across,
    relay1,
    relay2,
    enc0,
    enc1,
    enc2,
    enc3,
    dec0,
    dec1,
    dec2,
    dec3,
    codes,
    mask,
    full,
    active,
    bias,
):
    z, i = place[0], place[1]
    width = own.shape[1]
    for at, blocks in enumerate(
        (
            (own, high, relay1, relay2),
            (low, own, high, across),
            (across, low, own, high),
            (relay2, relay1, low, own),
        )
    ):

        @pl.when(z == at)
        def _(blocks=blocks):
            for b, block in enumerate(blocks):
                full[:, b * width : (b + 1) * width] = block[...]

    total = jnp.zeros(codes.shape, F32)
    piece = codes.shape[1] // 4
    decs = (dec0, dec1, dec2, dec3)
    for t, enc in enumerate((enc0, enc1, enc2, enc3)):
        b = i ^ t
        total += jnp.dot(
            full[:, columns(b * width, width)], enc[:width, :], preferred_element_type=F32
        )
        bias[:, columns(b * piece, piece)] = one_row(decs[t][width + EXTRA :, :piece])
    preact = total + bias[...]
    low_codes = jnp.maximum(preact, 0.0).astype(BF16)
    codes[...] = low_codes
    mask[...] = (preact > 0.0).astype(F32).astype(BF16)
    active[...] = jnp.sum(low_codes.astype(F32), axis=0, keepdims=True)


def onward_body(place, low, high, out):
    @pl.when(place[0] == 1)
    def _():
        out[...] = high[...]

    @pl.when(place[0] != 1)
    def _():
        out[...] = low[...]


def pieces_body(place, dec, up, down, across):
    z = place[0]
    half = up.shape[0]
    for out, second in ((up, z >= 1), (down, z >= 3), (across, z < 2)):
        out[...] = dec[pl.ds(pl.multiple_of(jnp.where(second, half, 0), half), half), :]


def turn_body(place, full, turned):
    turned[...] = full[...].T


def rebuilt_error(place, t, codes, dec, row, inputs):
    z, i = place[0], place[1]
    half = row.shape[0] // 3
    shift = pl.multiple_of(jnp.where(z >= 2, half, 0), half)
    below = pl.multiple_of(jnp.where(z == 1, 0, half), half)
    rights = [
        dec[pl.ds(shift, half), :],
        row[pl.ds(below, half), :],
        row[2 * half :, :],
        row[pl.ds(half - below, half), :],
    ]
    total = jnp.zeros((codes[0].shape[0], half), F32)
    for left, right in zip(codes, rights):
        total += lax.dot_general(
            left[...], right, (((1,), (1,)), ((), ())), preferred_element_type=F32
        )
    given = inputs[:, columns((i ^ t) * 2 * half + shift, half)].astype(F32)
    return (given - total).astype(BF16)


def own_error_body(place, own, near, across, middle, dec0, dec2, row0, row2, inputs, out):
    half = out.shape[1] // 2
    codes = (own, near, across, middle)
    out[:, :half] = rebuilt_error(place, 0, codes, dec0, row0, inputs)
    out[:, half:] = rebuilt_error(place, 2, codes, dec2, row2, inputs)


def error_body(place, own, near, across, middle, dec1, dec3, row1, row3, inputs, made, error):
    i = place[1]
    half = error.shape[1] // 4
    codes = (own, near, across, middle)
    error[:, columns(i * half, half)] = made[:, :half]
    error[:, columns((i ^ 2) * half, half)] = made[:, half:]
    error[:, columns((i ^ 1) * half, half)] = rebuilt_error(place, 1, codes, dec1, row1, inputs)
    error[:, columns((i ^ 3) * half, half)] = rebuilt_error(place, 3, codes, dec3, row3, inputs)


def pick(place, middle, end, out):
    z = place[0]
    is_middle = (z == 1) | (z == 2)

    @pl.when(is_middle)
    def _():
        out[...] = middle[...]

    @pl.when(jnp.logical_not(is_middle))
    def _():
        out[...] = end[...]


def decoder_grads(scale, i, error, codes, slots, outs):
    half = error.shape[1] // 4
    for slot, out in zip(slots, outs):
        out[:half] = scale * lax.dot_general(
            error[:, columns((i ^ slot) * half, half)],
            codes[...],
            (((0,), (0,)), ((), ())),
            preferred_element_type=F32,
        )


def back_through(i, error, decs, shift):
    half = error.shape[1] // 4
    return functools.reduce(
        jnp.add,
        [
            jnp.dot(
                error[:, columns((i ^ t) * half, half)],
                dec[pl.ds(pl.multiple_of(shift, half), half), :],
                preferred_element_type=F32,
            )
            for t, dec in enumerate(decs)
        ],
    )


def near_body(rows, place, mine, passed, codes, active, dec0, dec1, dec2, dec3, part, near, *outs):
    z, i = place[0], place[1]
    half = mine.shape[1] // 4
    pick(place, mine, passed, near)
    decoder_grads(-2.0 / rows, i, near, codes, (3, 1, 2, 0), outs)
    outs[0][half:] = jnp.broadcast_to(active[...], (outs[0].shape[0] - half, active.shape[1]))
    part[...] = back_through(i, near, (dec0, dec1, dec2, dec3), jnp.where(z >= 2, half, 0))


def far_error_body(rows, place, swapped, direct, codes, far, send, kept):
    pick(place, swapped, direct, far)
    decoder_grads(-2.0 / rows, place[1], far, codes, (3, 2), (send, kept))


def code_grad_body(
    rows, place, far, part, mask, dec0, dec1, dec2, dec3, turned, grad_low, bias_sum, norms, *sends
):
    z, i = place[0], place[1]
    half = far.shape[1] // 4
    width = 2 * half
    decs = (dec0, dec1, dec2, dec3)
    total = part[...] + back_through(i, far, decs, jnp.where(z >= 2, 0, half))
    squares = functools.reduce(jnp.add, [one_row(dec[width : width + EXTRA, :]) for dec in decs])
    column_norms = jnp.sqrt(squares + 1e-06)
    norms[...] = column_norms
    code_grad = (-2.0 / rows) * total + column_norms / rows
    grad = jnp.where(mask[...] > 0, code_grad, 0.0)
    grad_low[...] = grad.astype(BF16)
    row = jnp.sum(grad, axis=0, keepdims=True)
    bias_sum[...] = row
    at = pl.multiple_of((i ^ 3) * width, width)
    block = jnp.dot(turned[pl.ds(at, width), :], grad_low[...], preferred_element_type=F32)
    sends[0][:half] = block[:half]
    sends[0][half:] = jnp.broadcast_to(row, (sends[0].shape[0] - half, row.shape[1]))
    sends[1][...] = block[half:]


def encoder_grads(i, turned, grad_low, slots, outs):
    width = turned.shape[0] // 4
    for slot, out in zip(slots, outs):
        at = pl.ds(pl.multiple_of((i ^ slot) * width, width), width)
        out[:width] = jnp.dot(turned[at, :], grad_low[...], preferred_element_type=F32)


def rest_body(rows, place, turned, grad_low, near, far, codes, home, send, kept_far, kept, *outs):
    z, i = place[0], place[1]
    half = far.shape[1] // 4
    shift = jnp.where(z >= 2, 0, half)
    encoder_grads(i, turned, grad_low, (2, 1, 0), (kept_far, send, kept))
    decoder_grads(-2.0 / rows, i, far, codes, (1, 0), outs)
    home[:, columns(half - shift, half)] = near[:, columns(z * half, half)]
    home[:, columns(shift, half)] = far[:, columns(z * half, half)]


def power(values):
    largest = jnp.max(jnp.abs(values), axis=0, keepdims=True)
    return jnp.ceil(jnp.log(jnp.maximum(largest, 1e-30)) * (1.0 / math.log(2.0)))


def scale_of(exponent):
    return jnp.exp(exponent * math.log(2.0))


def pack_body(place, kept, row, *refs):
    width = kept.shape[0]
    at = [ref.shape[0] == width + EXTRA for ref in refs].index(True)
    received, packed, row_sums = refs[:at], refs[at], refs[at + 1 :]
    block = width // len(received)
    total = jnp.concatenate([piece[:block] for piece in received], axis=0) + kept[...]
    exponent = power(total)
    packed[:width] = total * scale_of(14.0 - exponent)
    sums = row[...]
    if received[0].shape[0] > block:
        sums += received[0][block : block + 1]
    for row_sum in row_sums:
        row_sum[...] = sums
    row_exponent = power(sums)
    parts = three_rows(sums * scale_of(14.0 - row_exponent)).astype(F32)
    at = lax.broadcasted_iota(jnp.int32, parts.shape, 0)
    parts = jnp.where(at == 3, exponent, jnp.where(at == 4, row_exponent, parts))
    packed[width:] = parts


def unpack(packed):
    width = packed.shape[0] - EXTRA
    rows = packed[width:].astype(F32)
    block = packed[:width].astype(F32) * scale_of(rows[3:4] - 14.0)
    row = (rows[0:1] + rows[1:2] + rows[2:3]) * scale_of(rows[4:5] - 14.0)
    return block, row


def bias_step_body(place, param, moment, square, here, there, param_out, moment_out, square_out):
    width = param.shape[1]
    grad = here[...] + there[...]
    pieces = [grad[:, b * width : (b + 1) * width] for b in range(4)]
    own = functools.reduce(
        jnp.add, [jnp.where(place[1] == b, piece, 0.0) for b, piece in enumerate(pieces)]
    )
    param_out[...], moment_out[...], square_out[...] = adam_update(
        param[...], own, moment[...], square[...]
    )


def decoder_step_body(
    rows, place, param, moment, square, near, far, active, norms, param_out, moment_out, square_out
):
    is_near = (pl.program_id(0) < pl.num_programs(0) // 2) == (place[0] < 2)
    grad = jnp.where(is_near, near[...], far[...])
    grad += param[...] * (active[...] / norms[...]) / rows
    param_out[...], moment_out[...], square_out[...] = adam_update(
        param[...], grad, moment[...], square[...]
    )


def line_shards(
    activations,
    encoder,
    enc_bias,
    decoder,
    enc_moment,
    enc_square,
    bias_moment,
    bias_square,
    dec_moment,
    dec_square,
):
    rows = activations.shape[0] * 4
    count, width = activations.shape
    latents = encoder.shape[1]
    half = width // 2
    features = 4 * width
    z, i = lax.axis_index("latent"), lax.axis_index("dp")
    place = jnp.stack([z, i]).astype(jnp.int32)

    def along(value, pairs):
        return lax.ppermute(value, "latent", pairs)

    def flip(value, bits, planes=(0, 1, 2, 3)):
        pairs = [(4 * p + k, 4 * p + (k ^ bits)) for p in planes for k in range(4)]
        return lax.ppermute(value, ("latent", "dp"), pairs)

    ends = [(1, 0), (2, 3)]
    low = along(activations, [(0, 1), (1, 2), (2, 3)])
    high = along(activations, [(1, 0), (2, 1), (3, 2)])
    across = along(activations, [(0, 2), (3, 1)])

    (enc_own,) = local_kernel(
        encoder_body,
        [shape((width + 2 * EXTRA, latents), BF16)],
        place,
        encoder,
    )
    enc_chip, enc_core = flip(enc_own, 2), flip(enc_own, 1)
    (dec_own,) = local_kernel(
        decoder_body,
        [shape((width + 2 * EXTRA, latents), BF16)],
        place,
        decoder,
        enc_bias.reshape(1, -1),
        after=(enc_core,),
    )
    dec_chip, dec_core = flip(dec_own, 2), flip(dec_own, 1)
    (onward,) = local_kernel(
        onward_body, [shape((count, width), BF16)], place, low, high
    )
    relay1 = along(onward, ends)
    relay2 = along(across, ends)
    enc = [enc_own, enc_core, enc_chip, flip(behind(enc_chip, relay2), 1)]

    up, down, beyond = local_kernel(
        pieces_body, [shape((half, latents), BF16)] * 3, place, dec_own
    )
    dec_pieces = [
        along(up, [(0, 1), (1, 2)]),
        along(down, [(2, 1), (3, 2)]),
        along(beyond, [(0, 2), (3, 1)]),
    ]
    dec = [dec_own, dec_core, dec_chip, flip(dec_chip, 1)]

    rows_own = jnp.concatenate([behind(piece, dec_chip) for piece in dec_pieces], axis=0)
    codes, mask, inputs, active = local_kernel(
        codes_body,
        [
            shape((count, latents), BF16),
            shape((count, latents), BF16),
            shape((count, features), BF16),
            shape((1, latents), F32),
        ],
        place,
        activations,
        low,
        high,
        across,
        relay1,
        relay2,
        *enc,
        *dec,
        after=(rows_own,),
        scratch=[pltpu.VMEM((1, latents), F32)],
    )
    codes_near = along(codes, [(0, 1), (3, 2)])
    codes_middle = along(codes, [(1, 2), (2, 1)])
    codes_across = along(codes, [(0, 2), (3, 1)])
    (turned,) = local_kernel(
        turn_body, [shape((features, count), BF16)], place, inputs, after=(codes_across,)
    )
    rows_chip = flip(rows_own, 2, (1, 2))
    rows_core = flip(behind(rows_own, codes), 1, (1, 2))
    rows_both = flip(behind(rows_chip, codes_across), 1, (1, 2))

    all_codes = codes, codes_near, codes_across, codes_middle
    (made,) = local_kernel(
        own_error_body,
        [shape((count, features // 4), BF16)],
        place,
        *all_codes,
        dec[0],
        dec[2],
        rows_own,
        rows_chip,
        inputs,
        cost=NOTABLE,
    )
    (own_error,) = local_kernel(
        error_body,
        [shape((count, features // 2), BF16)],
        place,
        *all_codes,
        dec[1],
        dec[3],
        rows_core,
        rows_both,
        inputs,
        made,
    )
    swapped = along(own_error, [(1, 2), (2, 1)])
    passed = along(own_error, [(1, 0), (2, 3)])
    direct = along(own_error, [(2, 0), (1, 3)])

    def across_chips(kept, row, *send, keep_row=True):
        packed, *row_sum = local_kernel(
            pack_body,
            [shape((kept.shape[0] + EXTRA, latents), F32)] + [shape((1, latents), F32)] * keep_row,
            place,
            kept,
            row,
            *[flip(piece, 1) for piece in send],
        )
        return packed, flip(packed.astype(jnp.float16), 2), *row_sum

    blocks = [shape((half + 8, latents), F32)] + [shape((half, latents), F32)] * 3
    part, near, *near_blocks = local_kernel(
        functools.partial(near_body, rows),
        [shape((count, latents), F32), shape((count, features // 2), BF16), *blocks],
        place,
        own_error,
        passed,
        codes,
        active,
        *dec,
        after=(swapped,),
    )
    send_far, send_near, keep_far, keep_near = near_blocks
    near_packed, near_received, active_sum = across_chips(keep_far, active, send_far)
    near_kept = keep_near, flip(send_near, 1)
    far, far_send, far_keep = local_kernel(
        functools.partial(far_error_body, rows),
        [shape((count, features // 2), BF16)] + [shape((half, latents), F32)] * 2,
        place,
        swapped,
        direct,
        codes,
        after=(near_packed, near_kept[1]),
        cost=NOTABLE,
    )
    grad_low, bias_sum, norms, *send_far_enc = local_kernel(
        functools.partial(code_grad_body, rows),
        [
            shape((count, latents), BF16),
            shape((1, latents), F32),
            shape((1, latents), F32),
            shape((half + 8, latents), F32),
            shape((half, latents), F32),
        ],
        place,
        far,
        behind(part, near_received),
        mask,
        *dec,
        turned,
        cost=NOTABLE,
    )
    far_packed, far_received = across_chips(far_keep, active, far_send, keep_row=False)
    error, enc_send_near, enc_keep_far, enc_keep_near, send_near, keep_near = local_kernel(
        functools.partial(rest_body, rows),
        [shape((count, width), BF16)]
        + [shape((width, latents), F32)] * 3
        + [shape((half, latents), F32)] * 2,
        place,
        turned,
        grad_low,
        near,
        far,
        codes,
        after=(far_packed,),
    )
    far_kept = keep_near, flip(send_near, 1)
    enc_packed, enc_received, bias_here = across_chips(enc_keep_far, bias_sum, *send_far_enc)
    enc_kept = enc_keep_near, flip(enc_send_near, 1)

    decoder, dec_moment, dec_square, encoder, enc_moment, enc_square = lax.optimization_barrier(
        (decoder, dec_moment, dec_square, encoder, enc_moment, enc_square, enc_packed)
    )[:6]
    near_block, active_there = unpack(near_received)
    far_block, _ = unpack(far_received)
    enc_block, bias_there = unpack(enc_received)
    near_grad = near_kept[0] + near_kept[1] + near_block
    far_grad = far_kept[0] + far_kept[1] + far_block
    active_sum = active_sum + active_there
    grad_encoder = enc_kept[0] + enc_kept[1] + enc_block
    new_enc_bias, new_bias_moment, new_bias_square = [
        value.reshape(-1)
        for value in local_kernel(
            bias_step_body,
            [shape((1, enc_bias.shape[0]), F32)] * 3,
            place,
            enc_bias.reshape(1, -1),
            bias_moment.reshape(1, -1),
            bias_square.reshape(1, -1),
            bias_here,
            bias_there,
        )
    ]
    new_encoder, new_enc_moment, new_enc_square = adam_update(
        encoder, grad_encoder, enc_moment, enc_square
    )
    step = width // 4
    block = pl.BlockSpec((step, latents), lambda r: (r, 0))
    in_half = pl.BlockSpec((step, latents), lambda r: (r % 2, 0))
    row = pl.BlockSpec((1, latents), lambda r: (0, 0))
    new_decoder, new_dec_moment, new_dec_square = pl.pallas_call(
        functools.partial(decoder_step_body, rows),
        grid=(4,),
        out_shape=[shape((width, latents), F32)] * 3,
        in_specs=[SMEM, block, block, block, in_half, in_half, row, row],
        out_specs=[block] * 3,
        compiler_params=pltpu.CompilerParams(vmem_limit_bytes=12 * 1024 * 1024),
        cost_estimate=pl.CostEstimate(flops=1, bytes_accessed=1, transcendentals=0),
    )(place, decoder, dec_moment, dec_square, near_grad, far_grad, active_sum, norms)
    return (
        error,
        new_encoder,
        new_enc_bias,
        new_decoder,
        new_enc_moment,
        new_enc_square,
        new_bias_moment,
        new_bias_square,
        new_dec_moment,
        new_dec_square,
    )


def solution(mesh):
    in_specs = (
        P(("groups", "dp"), "latent"),
        P(("groups", "dp"), "latent"),
        P(("groups", "latent", "dp")),
        P(("groups", "dp"), "latent"),
        P(("groups", "dp"), "latent"),
        P(("groups", "dp"), "latent"),
        P(("groups", "latent", "dp")),
        P(("groups", "latent", "dp")),
        P(("groups", "dp"), "latent"),
        P(("groups", "dp"), "latent"),
    )
    out_specs = (
        P(("groups", "dp"), "latent"),
        P(("groups", "dp"), "latent"),
        P(("groups", "latent", "dp")),
        P(("groups", "dp"), "latent"),
        P(("groups", "dp"), "latent"),
        P(("groups", "dp"), "latent"),
        P(("groups", "latent", "dp")),
        P(("groups", "latent", "dp")),
        P(("groups", "dp"), "latent"),
        P(("groups", "dp"), "latent"),
    )
    line = mesh.shape["latent"] == 4 and mesh.shape["dp"] == 4
    plan = line_shards if line else shards
    return jax.shard_map(plan, mesh=mesh, in_specs=in_specs, out_specs=out_specs, check_vma=False)
```

```python
import functools
import math

import jax
import jax.numpy as jnp
from jax import lax
from jax.experimental import pallas as pl
from jax.experimental.pallas import tpu as pltpu
from jax.sharding import PartitionSpec as P

ADAM_STEP = 1000


first_decay = 0.9
second_decay = 0.999
learn_rate = 0.001
epsilon = 1e-08

F32 = jnp.float32
BF16 = jnp.bfloat16


def adam_update(param, grad, moment, square):
    moment_new = first_decay * moment + (1.0 - first_decay) * grad
    square_new = second_decay * square + (1.0 - second_decay) * grad * grad
    first_fix = 1.0 - first_decay**ADAM_STEP
    second_fix = 1.0 - second_decay**ADAM_STEP
    param_new = param - learn_rate * (moment_new / first_fix) / (
        jnp.sqrt(square_new / second_fix) + epsilon
    )
    return (param_new, moment_new, square_new)


def shards(
    activations,
    encoder,
    enc_bias,
    decoder,
    enc_moment,
    enc_square,
    bias_moment,
    bias_square,
    dec_moment,
    dec_square,
):
    row_count = activations.shape[0] * lax.axis_size("dp")
    loss_scale = 2.0 / row_count
    inputs = lax.all_gather(activations, "latent", axis=1, tiled=True)
    enc_low, dec_low = (
        lax.all_gather(encoder.astype(jnp.bfloat16), "dp", axis=0, tiled=True),
        lax.all_gather(decoder.astype(jnp.bfloat16), "dp", axis=0, tiled=True),
    )
    bias_full = lax.all_gather(enc_bias, "dp", axis=0, tiled=True)
    square_sums = lax.psum(jnp.sum(decoder * decoder, axis=0), "dp")
    column_norms = jnp.sqrt(square_sums + 1e-06)
    preact = jnp.dot(inputs, enc_low, preferred_element_type=jnp.float32) + bias_full
    latent_codes = jnp.maximum(preact, 0.0).astype(jnp.bfloat16)
    partial_sums = lax.dot_general(
        latent_codes, dec_low, (((1,), (1,)), ((), ())), preferred_element_type=jnp.float32
    )
    rebuilt = lax.psum_scatter(partial_sums, "latent", scatter_dimension=1, tiled=True)
    error = (activations.astype(jnp.float32) - rebuilt).astype(jnp.bfloat16)
    full_error = lax.all_gather(error, "latent", axis=1, tiled=True)
    active_sum = lax.psum(jnp.sum(latent_codes.astype(jnp.float32), axis=0), "dp")
    grad_dec_rows = -loss_scale * lax.dot_general(
        full_error, latent_codes, (((0,), (0,)), ((), ())), preferred_element_type=jnp.float32
    )
    code_grad = (
        -loss_scale * jnp.dot(full_error, dec_low, preferred_element_type=jnp.float32)
        + column_norms / row_count
    )
    grad_preact = jnp.where(preact > 0.0, code_grad, 0.0)
    grad_encoder = lax.dot_general(
        inputs,
        grad_preact.astype(jnp.bfloat16),
        (((0,), (0,)), ((), ())),
        preferred_element_type=jnp.float32,
    )
    grad_bias = jnp.sum(grad_preact, axis=0)
    grad_encoder, grad_dec_rows, grad_bias = (
        lax.psum_scatter(grad_encoder, "dp", scatter_dimension=0, tiled=True),
        lax.psum_scatter(grad_dec_rows, "dp", scatter_dimension=0, tiled=True),
        lax.psum_scatter(grad_bias, "dp", scatter_dimension=0, tiled=True),
    )
    grad_decoder = grad_dec_rows + decoder * (active_sum / column_norms) / row_count
    new_encoder, new_enc_moment, new_enc_square = adam_update(
        encoder, grad_encoder, enc_moment, enc_square
    )
    new_enc_bias, new_bias_moment, new_bias_square = adam_update(
        enc_bias, grad_bias, bias_moment, bias_square
    )
    new_decoder, new_dec_moment, new_dec_square = adam_update(
        decoder, grad_decoder, dec_moment, dec_square
    )
    return (
        error,
        new_encoder,
        new_enc_bias,
        new_decoder,
        new_enc_moment,
        new_enc_square,
        new_bias_moment,
        new_bias_square,
        new_dec_moment,
        new_dec_square,
    )


VMEM = pl.BlockSpec(memory_space=pltpu.VMEM)
SMEM = pl.BlockSpec(memory_space=pltpu.SMEM)
ANY = pl.BlockSpec(memory_space=pl.ANY)
EXTRA = 16
NOTABLE = 10**10


def local_kernel(body, outs, place, *args, after=(), scratch=(), cost=1):
    def run(place, *refs):
        body(place, *refs[: len(args)], *refs[len(args) + len(after) :])

    held = sum(a.size * jnp.dtype(a.dtype).itemsize for a in (*args, *outs))
    return pl.pallas_call(
        run,
        out_shape=outs,
        in_specs=[SMEM] + [VMEM] * len(args) + [ANY] * len(after),
        out_specs=[VMEM] * len(outs),
        scratch_shapes=scratch,
        compiler_params=pltpu.CompilerParams(vmem_limit_bytes=held + 6 * 1024 * 1024),
        cost_estimate=pl.CostEstimate(flops=cost, bytes_accessed=1, transcendentals=0),
    )(place, *args, *after)


def shape(dims, dtype):
    return jax.ShapeDtypeStruct(dims, dtype)


def columns(start, width):
    return pl.ds(pl.multiple_of(start, width), width)


def three_rows(row):
    high = row.astype(BF16).astype(F32)
    middle = (row - high).astype(BF16).astype(F32)
    low = row - high - middle
    at = lax.broadcasted_iota(jnp.int32, (EXTRA, row.shape[1]), 0)
    rows = jnp.where(at == 0, high, jnp.where(at == 1, middle, jnp.where(at == 2, low, 0.0)))
    return rows.astype(BF16)


def behind(value, *others):
    return lax.optimization_barrier((value, *others))[0]


def one_row(rows):
    return jnp.sum(rows.astype(F32), axis=0, keepdims=True)


def encoder_body(place, encoder, out):
    depth = encoder.shape[0]
    out[:depth] = encoder[...].astype(BF16)
    out[depth:] = jnp.zeros((out.shape[0] - depth, out.shape[1]), BF16)


def decoder_body(place, decoder, bias, out):
    depth = decoder.shape[0]
    value = decoder[...]
    out[:depth] = value.astype(BF16)
    out[depth : depth + EXTRA] = three_rows(jnp.sum(value * value, axis=0, keepdims=True))
    out[depth + EXTRA :] = three_rows(jnp.concatenate([bias[...]] * 4, axis=1))


def codes_body(
    place,
    own,
    low,
    high,
    across,
    relay1,
    relay2,
    enc0,
    enc1,
    enc2,
    enc3,
    dec0,
    dec1,
    dec2,
    dec3,
    codes,
    mask,
    full,
    active,
    bias,
):
    z, i = place[0], place[1]
    width = own.shape[1]
    for at, blocks in enumerate(
        (
            (own, high, relay1, relay2),
            (low, own, high, across),
            (across, low, own, high),
            (relay2, relay1, low, own),
        )
    ):

        @pl.when(z == at)
        def _(blocks=blocks):
            for b, block in enumerate(blocks):
                full[:, b * width : (b + 1) * width] = block[...]

    total = jnp.zeros(codes.shape, F32)
    piece = codes.shape[1] // 4
    decs = (dec0, dec1, dec2, dec3)
    for t, enc in enumerate((enc0, enc1, enc2, enc3)):
        b = i ^ t
        total += jnp.dot(
            full[:, columns(b * width, width)], enc[:width, :], preferred_element_type=F32
        )
        bias[:, columns(b * piece, piece)] = one_row(decs[t][width + EXTRA :, :piece])
    preact = total + bias[...]
    low_codes = jnp.maximum(preact, 0.0).astype(BF16)
    codes[...] = low_codes
    mask[...] = (preact > 0.0).astype(F32).astype(BF16)
    active[...] = jnp.sum(low_codes.astype(F32), axis=0, keepdims=True)


def onward_body(place, low, high, out):
    @pl.when(place[0] == 1)
    def _():
        out[...] = high[...]

    @pl.when(place[0] != 1)
    def _():
        out[...] = low[...]


def pieces_body(place, dec, up, down, across):
    z = place[0]
    half = up.shape[0]
    for out, second in ((up, z >= 1), (down, z >= 3), (across, z < 2)):
        out[...] = dec[pl.ds(pl.multiple_of(jnp.where(second, half, 0), half), half), :]


def turn_body(place, full, turned):
    turned[...] = full[...].T


def rebuilt_error(place, t, codes, dec, row, inputs):
    z, i = place[0], place[1]
    half = row.shape[0] // 3
    shift = pl.multiple_of(jnp.where(z >= 2, half, 0), half)
    below = pl.multiple_of(jnp.where(z == 1, 0, half), half)
    rights = [
        dec[pl.ds(shift, half), :],
        row[pl.ds(below, half), :],
        row[2 * half :, :],
        row[pl.ds(half - below, half), :],
    ]
    total = jnp.zeros((codes[0].shape[0], half), F32)
    for left, right in zip(codes, rights):
        total += lax.dot_general(
            left[...], right, (((1,), (1,)), ((), ())), preferred_element_type=F32
        )
    given = inputs[:, columns((i ^ t) * 2 * half + shift, half)].astype(F32)
    return (given - total).astype(BF16)


def own_error_body(place, own, near, across, middle, dec0, dec2, row0, row2, inputs, out):
    half = out.shape[1] // 2
    codes = (own, near, across, middle)
    out[:, :half] = rebuilt_error(place, 0, codes, dec0, row0, inputs)
    out[:, half:] = rebuilt_error(place, 2, codes, dec2, row2, inputs)


def error_body(place, own, near, across, middle, dec1, dec3, row1, row3, inputs, made, error):
    i = place[1]
    half = error.shape[1] // 4
    codes = (own, near, across, middle)
    error[:, columns(i * half, half)] = made[:, :half]
    error[:, columns((i ^ 2) * half, half)] = made[:, half:]
    error[:, columns((i ^ 1) * half, half)] = rebuilt_error(place, 1, codes, dec1, row1, inputs)
    error[:, columns((i ^ 3) * half, half)] = rebuilt_error(place, 3, codes, dec3, row3, inputs)


def pick(place, middle, end, out):
    z = place[0]
    is_middle = (z == 1) | (z == 2)

    @pl.when(is_middle)
    def _():
        out[...] = middle[...]

    @pl.when(jnp.logical_not(is_middle))
    def _():
        out[...] = end[...]


def decoder_grads(scale, i, error, codes, slots, outs):
    half = error.shape[1] // 4
    for slot, out in zip(slots, outs):
        out[:half] = scale * lax.dot_general(
            error[:, columns((i ^ slot) * half, half)],
            codes[...],
            (((0,), (0,)), ((), ())),
            preferred_element_type=F32,
        )


def back_through(i, error, decs, shift):
    half = error.shape[1] // 4
    return functools.reduce(
        jnp.add,
        [
            jnp.dot(
                error[:, columns((i ^ t) * half, half)],
                dec[pl.ds(pl.multiple_of(shift, half), half), :],
                preferred_element_type=F32,
            )
            for t, dec in enumerate(decs)
        ],
    )


def near_body(rows, place, mine, passed, codes, active, dec0, dec1, dec2, dec3, part, near, *outs):
    z, i = place[0], place[1]
    half = mine.shape[1] // 4
    pick(place, mine, passed, near)
    decoder_grads(-2.0 / rows, i, near, codes, (3, 1, 2, 0), outs)
    outs[0][half:] = jnp.broadcast_to(active[...], (outs[0].shape[0] - half, active.shape[1]))
    part[...] = back_through(i, near, (dec0, dec1, dec2, dec3), jnp.where(z >= 2, half, 0))


def far_error_body(rows, place, swapped, direct, codes, far, send, kept):
    pick(place, swapped, direct, far)
    decoder_grads(-2.0 / rows, place[1], far, codes, (3, 2), (send, kept))


def code_grad_body(
    rows, place, far, part, mask, dec0, dec1, dec2, dec3, turned, grad_low, bias_sum, norms, *sends
):
    z, i = place[0], place[1]
    half = far.shape[1] // 4
    width = 2 * half
    decs = (dec0, dec1, dec2, dec3)
    total = part[...] + back_through(i, far, decs, jnp.where(z >= 2, 0, half))
    squares = functools.reduce(jnp.add, [one_row(dec[width : width + EXTRA, :]) for dec in decs])
    column_norms = jnp.sqrt(squares + 1e-06)
    norms[...] = column_norms
    code_grad = (-2.0 / rows) * total + column_norms / rows
    grad = jnp.where(mask[...] > 0, code_grad, 0.0)
    grad_low[...] = grad.astype(BF16)
    bias_sum[...] = jnp.sum(grad, axis=0, keepdims=True)
    at = pl.multiple_of((i ^ 3) * width, width)
    block = jnp.dot(turned[pl.ds(at, width), :], grad_low[...], preferred_element_type=F32)
    sends[0][...] = block[:half]
    sends[1][...] = block[half:]


def encoder_grads(i, turned, grad_low, slots, outs):
    width = turned.shape[0] // 4
    for slot, out in zip(slots, outs):
        at = pl.ds(pl.multiple_of((i ^ slot) * width, width), width)
        out[:width] = jnp.dot(turned[at, :], grad_low[...], preferred_element_type=F32)


def rest_body(rows, place, turned, grad_low, near, far, codes, home, send, kept_far, kept, *outs):
    z, i = place[0], place[1]
    half = far.shape[1] // 4
    shift = jnp.where(z >= 2, 0, half)
    encoder_grads(i, turned, grad_low, (2, 1, 0), (kept_far, send, kept))
    decoder_grads(-2.0 / rows, i, far, codes, (1, 0), outs)
    home[:, columns(half - shift, half)] = near[:, columns(z * half, half)]
    home[:, columns(shift, half)] = far[:, columns(z * half, half)]


def power(values):
    largest = jnp.max(jnp.abs(values), axis=0, keepdims=True)
    return jnp.ceil(jnp.log(jnp.maximum(largest, 1e-30)) * (1.0 / math.log(2.0)))


def scale_of(exponent):
    return jnp.exp(exponent * math.log(2.0))


def pack_body(place, kept, row, *refs):
    width = kept.shape[0]
    at = [ref.shape[0] == width + EXTRA for ref in refs].index(True)
    received, packed, row_sums = refs[:at], refs[at], refs[at + 1 :]
    block = width // len(received)
    total = jnp.concatenate([piece[:block] for piece in received], axis=0) + kept[...]
    exponent = power(total)
    packed[:width] = total * scale_of(14.0 - exponent)
    sums = row[...]
    if received[0].shape[0] > block:
        sums += received[0][block : block + 1]
    for row_sum in row_sums:
        row_sum[...] = sums
    row_exponent = power(sums)
    parts = three_rows(sums * scale_of(14.0 - row_exponent)).astype(F32)
    at = lax.broadcasted_iota(jnp.int32, parts.shape, 0)
    parts = jnp.where(at == 3, exponent, jnp.where(at == 4, row_exponent, parts))
    packed[width:] = parts


def unpack(packed):
    width = packed.shape[0] - EXTRA
    rows = packed[width:].astype(F32)
    block = packed[:width].astype(F32) * scale_of(rows[3:4] - 14.0)
    row = (rows[0:1] + rows[1:2] + rows[2:3]) * scale_of(rows[4:5] - 14.0)
    return block, row


def bias_step_body(place, param, moment, square, here, there, param_out, moment_out, square_out):
    width = param.shape[1]
    grad = here[...] + there[...]
    pieces = [grad[:, b * width : (b + 1) * width] for b in range(4)]
    own = functools.reduce(
        jnp.add, [jnp.where(place[1] == b, piece, 0.0) for b, piece in enumerate(pieces)]
    )
    param_out[...], moment_out[...], square_out[...] = adam_update(
        param[...], own, moment[...], square[...]
    )


def decoder_step_body(
    rows, place, param, moment, square, near, far, active, norms, param_out, moment_out, square_out
):
    is_near = (pl.program_id(0) < pl.num_programs(0) // 2) == (place[0] < 2)
    grad = jnp.where(is_near, near[...], far[...])
    grad += param[...] * (active[...] / norms[...]) / rows
    param_out[...], moment_out[...], square_out[...] = adam_update(
        param[...], grad, moment[...], square[...]
    )


def line_shards(
    activations,
    encoder,
    enc_bias,
    decoder,
    enc_moment,
    enc_square,
    bias_moment,
    bias_square,
    dec_moment,
    dec_square,
):
    rows = activations.shape[0] * 4
    count, width = activations.shape
    latents = encoder.shape[1]
    half = width // 2
    features = 4 * width
    z, i = lax.axis_index("latent"), lax.axis_index("dp")
    place = jnp.stack([z, i]).astype(jnp.int32)

    def along(value, pairs):
        return lax.ppermute(value, "latent", pairs)

    def flip(value, bits, planes=(0, 1, 2, 3)):
        pairs = [(4 * p + k, 4 * p + (k ^ bits)) for p in planes for k in range(4)]
        return lax.ppermute(value, ("latent", "dp"), pairs)

    ends = [(1, 0), (2, 3)]
    low = along(activations, [(0, 1), (1, 2), (2, 3)])
    high = along(activations, [(1, 0), (2, 1), (3, 2)])
    across = along(activations, [(0, 2), (3, 1)])

    (enc_own,) = local_kernel(
        encoder_body,
        [shape((width + 2 * EXTRA, latents), BF16)],
        place,
        encoder,
    )
    enc_chip, enc_core = flip(enc_own, 2), flip(enc_own, 1)
    (dec_own,) = local_kernel(
        decoder_body,
        [shape((width + 2 * EXTRA, latents), BF16)],
        place,
        decoder,
        enc_bias.reshape(1, -1),
        after=(enc_core,),
    )
    dec_chip, dec_core = flip(dec_own, 2), flip(dec_own, 1)
    (onward,) = local_kernel(
        onward_body, [shape((count, width), BF16)], place, low, high
    )
    relay1 = along(onward, ends)
    relay2 = along(across, ends)
    enc = [enc_own, enc_core, enc_chip, flip(behind(enc_chip, relay2), 1)]

    up, down, beyond = local_kernel(
        pieces_body, [shape((half, latents), BF16)] * 3, place, dec_own
    )
    dec_pieces = [
        along(up, [(0, 1), (1, 2)]),
        along(down, [(2, 1), (3, 2)]),
        along(beyond, [(0, 2), (3, 1)]),
    ]
    dec = [dec_own, dec_core, dec_chip, flip(dec_chip, 1)]

    rows_own = jnp.concatenate([behind(piece, dec_chip) for piece in dec_pieces], axis=0)
    codes, mask, inputs, active = local_kernel(
        codes_body,
        [
            shape((count, latents), BF16),
            shape((count, latents), BF16),
            shape((count, features), BF16),
            shape((1, latents), F32),
        ],
        place,
        activations,
        low,
        high,
        across,
        relay1,
        relay2,
        *enc,
        *dec,
        after=(rows_own,),
        scratch=[pltpu.VMEM((1, latents), F32)],
    )
    codes_near = along(codes, [(0, 1), (3, 2)])
    codes_middle = along(codes, [(1, 2), (2, 1)])
    codes_across = along(codes, [(0, 2), (3, 1)])
    (turned,) = local_kernel(
        turn_body, [shape((features, count), BF16)], place, inputs, after=(codes_across,)
    )
    rows_chip = flip(rows_own, 2, (1, 2))
    rows_core = flip(behind(rows_own, codes), 1, (1, 2))
    rows_both = flip(behind(rows_chip, codes_across), 1, (1, 2))

    all_codes = codes, codes_near, codes_across, codes_middle
    (made,) = local_kernel(
        own_error_body,
        [shape((count, features // 4), BF16)],
        place,
        *all_codes,
        dec[0],
        dec[2],
        rows_own,
        rows_chip,
        inputs,
        cost=NOTABLE,
    )
    (own_error,) = local_kernel(
        error_body,
        [shape((count, features // 2), BF16)],
        place,
        *all_codes,
        dec[1],
        dec[3],
        rows_core,
        rows_both,
        inputs,
        made,
    )
    swapped = along(own_error, [(1, 2), (2, 1)])
    passed = along(own_error, [(1, 0), (2, 3)])
    direct = along(own_error, [(2, 0), (1, 3)])

    def across_chips(kept, row, *send, keep_row=True):
        packed, *row_sum = local_kernel(
            pack_body,
            [shape((kept.shape[0] + EXTRA, latents), F32)] + [shape((1, latents), F32)] * keep_row,
            place,
            kept,
            row,
            *[flip(piece, 1) for piece in send],
        )
        return packed, flip(packed.astype(jnp.float16), 2), *row_sum

    blocks = [shape((half + 8, latents), F32)] + [shape((half, latents), F32)] * 3
    part, near, *near_blocks = local_kernel(
        functools.partial(near_body, rows),
        [shape((count, latents), F32), shape((count, features // 2), BF16), *blocks],
        place,
        own_error,
        passed,
        codes,
        active,
        *dec,
        after=(swapped,),
    )
    send_far, send_near, keep_far, keep_near = near_blocks
    near_packed, near_received, active_sum = across_chips(keep_far, active, send_far)
    near_kept = keep_near, flip(send_near, 1)
    far, far_send, far_keep = local_kernel(
        functools.partial(far_error_body, rows),
        [shape((count, features // 2), BF16)] + [shape((half, latents), F32)] * 2,
        place,
        swapped,
        direct,
        codes,
        after=(near_packed, near_kept[1]),
        cost=NOTABLE,
    )
    grad_low, bias_sum, norms, *send_far_enc = local_kernel(
        functools.partial(code_grad_body, rows),
        [
            shape((count, latents), BF16),
            shape((1, latents), F32),
            shape((1, latents), F32),
            shape((half, latents), F32),
            shape((half, latents), F32),
        ],
        place,
        far,
        behind(part, near_received),
        mask,
        *dec,
        turned,
        cost=NOTABLE,
    )
    far_packed, far_received = across_chips(far_keep, bias_sum, far_send, keep_row=False)
    error, enc_send_near, enc_keep_far, enc_keep_near, send_near, keep_near = local_kernel(
        functools.partial(rest_body, rows),
        [shape((count, width), BF16)]
        + [shape((width, latents), F32)] * 3
        + [shape((half, latents), F32)] * 2,
        place,
        turned,
        grad_low,
        near,
        far,
        codes,
        after=(far_packed,),
    )
    far_kept = keep_near, flip(send_near, 1)
    enc_packed, enc_received = across_chips(enc_keep_far, bias_sum, *send_far_enc, keep_row=False)
    enc_kept = enc_keep_near, flip(enc_send_near, 1)

    decoder, dec_moment, dec_square, encoder, enc_moment, enc_square = lax.optimization_barrier(
        (decoder, dec_moment, dec_square, encoder, enc_moment, enc_square, enc_packed)
    )[:6]
    near_block, active_there = unpack(near_received)
    far_block, bias_there = unpack(far_received)
    enc_block, _ = unpack(enc_received)
    near_grad = near_kept[0] + near_kept[1] + near_block
    far_grad = far_kept[0] + far_kept[1] + far_block
    active_sum = active_sum + active_there
    grad_encoder = enc_kept[0] + enc_kept[1] + enc_block
    new_encoder, new_enc_moment, new_enc_square = adam_update(
        encoder, grad_encoder, enc_moment, enc_square
    )
    step = width // 4
    block = pl.BlockSpec((step, latents), lambda r: (r, 0))
    in_half = pl.BlockSpec((step, latents), lambda r: (r % 2, 0))
    row = pl.BlockSpec((1, latents), lambda r: (0, 0))
    new_decoder, new_dec_moment, new_dec_square = pl.pallas_call(
        functools.partial(decoder_step_body, rows),
        grid=(4,),
        out_shape=[shape((width, latents), F32)] * 3,
        in_specs=[SMEM, block, block, block, in_half, in_half, row, row],
        out_specs=[block] * 3,
        compiler_params=pltpu.CompilerParams(vmem_limit_bytes=12 * 1024 * 1024),
        cost_estimate=pl.CostEstimate(flops=1, bytes_accessed=1, transcendentals=0),
    )(place, decoder, dec_moment, dec_square, near_grad, far_grad, active_sum, norms)
    bias_chips = bias_sum + bias_there
    new_enc_bias, new_bias_moment, new_bias_square = [
        value.reshape(-1)
        for value in local_kernel(
            bias_step_body,
            [shape((1, enc_bias.shape[0]), F32)] * 3,
            place,
            enc_bias.reshape(1, -1),
            bias_moment.reshape(1, -1),
            bias_square.reshape(1, -1),
            bias_chips,
            flip(bias_chips, 1),
            after=(new_decoder,),
        )
    ]
    return (
        error,
        new_encoder,
        new_enc_bias,
        new_decoder,
        new_enc_moment,
        new_enc_square,
        new_bias_moment,
        new_bias_square,
        new_dec_moment,
        new_dec_square,
    )


def solution(mesh):
    in_specs = (
        P(("groups", "dp"), "latent"),
        P(("groups", "dp"), "latent"),
        P(("groups", "latent", "dp")),
        P(("groups", "dp"), "latent"),
        P(("groups", "dp"), "latent"),
        P(("groups", "dp"), "latent"),
        P(("groups", "latent", "dp")),
        P(("groups", "latent", "dp")),
        P(("groups", "dp"), "latent"),
        P(("groups", "dp"), "latent"),
    )
    out_specs = (
        P(("groups", "dp"), "latent"),
        P(("groups", "dp"), "latent"),
        P(("groups", "latent", "dp")),
        P(("groups", "dp"), "latent"),
        P(("groups", "dp"), "latent"),
        P(("groups", "dp"), "latent"),
        P(("groups", "latent", "dp")),
        P(("groups", "latent", "dp")),
        P(("groups", "dp"), "latent"),
        P(("groups", "dp"), "latent"),
    )
    line = mesh.shape["latent"] == 4 and mesh.shape["dp"] == 4
    plan = line_shards if line else shards
    return jax.shard_map(plan, mesh=mesh, in_specs=in_specs, out_specs=out_specs, check_vma=False)
```

```python
import functools
import math

import jax
import jax.numpy as jnp
from jax import lax
from jax.experimental import pallas as pl
from jax.experimental.pallas import tpu as pltpu
from jax.sharding import PartitionSpec as P

ADAM_STEP = 1000


first_decay = 0.9
second_decay = 0.999
learn_rate = 0.001
epsilon = 1e-08

F32 = jnp.float32
BF16 = jnp.bfloat16


def adam_update(param, grad, moment, square):
    moment_new = first_decay * moment + (1.0 - first_decay) * grad
    square_new = second_decay * square + (1.0 - second_decay) * grad * grad
    first_fix = 1.0 - first_decay**ADAM_STEP
    second_fix = 1.0 - second_decay**ADAM_STEP
    param_new = param - learn_rate * (moment_new / first_fix) / (
        jnp.sqrt(square_new / second_fix) + epsilon
    )
    return (param_new, moment_new, square_new)


def shards(
    activations,
    encoder,
    enc_bias,
    decoder,
    enc_moment,
    enc_square,
    bias_moment,
    bias_square,
    dec_moment,
    dec_square,
):
    row_count = activations.shape[0] * lax.axis_size("dp")
    loss_scale = 2.0 / row_count
    inputs = lax.all_gather(activations, "latent", axis=1, tiled=True)
    enc_low, dec_low = (
        lax.all_gather(encoder.astype(jnp.bfloat16), "dp", axis=0, tiled=True),
        lax.all_gather(decoder.astype(jnp.bfloat16), "dp", axis=0, tiled=True),
    )
    bias_full = lax.all_gather(enc_bias, "dp", axis=0, tiled=True)
    square_sums = lax.psum(jnp.sum(decoder * decoder, axis=0), "dp")
    column_norms = jnp.sqrt(square_sums + 1e-06)
    preact = jnp.dot(inputs, enc_low, preferred_element_type=jnp.float32) + bias_full
    latent_codes = jnp.maximum(preact, 0.0).astype(jnp.bfloat16)
    partial_sums = lax.dot_general(
        latent_codes, dec_low, (((1,), (1,)), ((), ())), preferred_element_type=jnp.float32
    )
    rebuilt = lax.psum_scatter(partial_sums, "latent", scatter_dimension=1, tiled=True)
    error = (activations.astype(jnp.float32) - rebuilt).astype(jnp.bfloat16)
    full_error = lax.all_gather(error, "latent", axis=1, tiled=True)
    active_sum = lax.psum(jnp.sum(latent_codes.astype(jnp.float32), axis=0), "dp")
    grad_dec_rows = -loss_scale * lax.dot_general(
        full_error, latent_codes, (((0,), (0,)), ((), ())), preferred_element_type=jnp.float32
    )
    code_grad = (
        -loss_scale * jnp.dot(full_error, dec_low, preferred_element_type=jnp.float32)
        + column_norms / row_count
    )
    grad_preact = jnp.where(preact > 0.0, code_grad, 0.0)
    grad_encoder = lax.dot_general(
        inputs,
        grad_preact.astype(jnp.bfloat16),
        (((0,), (0,)), ((), ())),
        preferred_element_type=jnp.float32,
    )
    grad_bias = jnp.sum(grad_preact, axis=0)
    grad_encoder, grad_dec_rows, grad_bias = (
        lax.psum_scatter(grad_encoder, "dp", scatter_dimension=0, tiled=True),
        lax.psum_scatter(grad_dec_rows, "dp", scatter_dimension=0, tiled=True),
        lax.psum_scatter(grad_bias, "dp", scatter_dimension=0, tiled=True),
    )
    grad_decoder = grad_dec_rows + decoder * (active_sum / column_norms) / row_count
    new_encoder, new_enc_moment, new_enc_square = adam_update(
        encoder, grad_encoder, enc_moment, enc_square
    )
    new_enc_bias, new_bias_moment, new_bias_square = adam_update(
        enc_bias, grad_bias, bias_moment, bias_square
    )
    new_decoder, new_dec_moment, new_dec_square = adam_update(
        decoder, grad_decoder, dec_moment, dec_square
    )
    return (
        error,
        new_encoder,
        new_enc_bias,
        new_decoder,
        new_enc_moment,
        new_enc_square,
        new_bias_moment,
        new_bias_square,
        new_dec_moment,
        new_dec_square,
    )


VMEM = pl.BlockSpec(memory_space=pltpu.VMEM)
SMEM = pl.BlockSpec(memory_space=pltpu.SMEM)
ANY = pl.BlockSpec(memory_space=pl.ANY)
EXTRA = 16
NOTABLE = 10**10


def local_kernel(body, outs, place, *args, after=(), scratch=(), cost=1):
    def run(place, *refs):
        body(place, *refs[: len(args)], *refs[len(args) + len(after) :])

    held = sum(a.size * jnp.dtype(a.dtype).itemsize for a in (*args, *outs))
    return pl.pallas_call(
        run,
        out_shape=outs,
        in_specs=[SMEM] + [VMEM] * len(args) + [ANY] * len(after),
        out_specs=[VMEM] * len(outs),
        scratch_shapes=scratch,
        compiler_params=pltpu.CompilerParams(vmem_limit_bytes=held + 6 * 1024 * 1024),
        cost_estimate=pl.CostEstimate(flops=cost, bytes_accessed=1, transcendentals=0),
    )(place, *args, *after)


def shape(dims, dtype):
    return jax.ShapeDtypeStruct(dims, dtype)


def columns(start, width):
    return pl.ds(pl.multiple_of(start, width), width)


def three_rows(row):
    high = row.astype(BF16).astype(F32)
    middle = (row - high).astype(BF16).astype(F32)
    low = row - high - middle
    at = lax.broadcasted_iota(jnp.int32, (EXTRA, row.shape[1]), 0)
    rows = jnp.where(at == 0, high, jnp.where(at == 1, middle, jnp.where(at == 2, low, 0.0)))
    return rows.astype(BF16)


def behind(value, *others):
    return lax.optimization_barrier((value, *others))[0]


def one_row(rows):
    return jnp.sum(rows.astype(F32), axis=0, keepdims=True)


def encoder_body(place, encoder, out):
    depth = encoder.shape[0]
    out[:depth] = encoder[...].astype(BF16)
    out[depth:] = jnp.zeros((out.shape[0] - depth, out.shape[1]), BF16)


def decoder_body(place, decoder, bias, out):
    depth = decoder.shape[0]
    value = decoder[...]
    out[:depth] = value.astype(BF16)
    out[depth : depth + EXTRA] = three_rows(jnp.sum(value * value, axis=0, keepdims=True))
    out[depth + EXTRA :] = three_rows(jnp.concatenate([bias[...]] * 4, axis=1))


def codes_body(
    place,
    own,
    low,
    high,
    across,
    relay1,
    relay2,
    enc0,
    enc1,
    enc2,
    enc3,
    dec0,
    dec1,
    dec2,
    dec3,
    codes,
    mask,
    full,
    active,
    bias,
):
    z, i = place[0], place[1]
    width = own.shape[1]
    for at, blocks in enumerate(
        (
            (own, high, relay1, relay2),
            (low, own, high, across),
            (across, low, own, high),
            (relay2, relay1, low, own),
        )
    ):

        @pl.when(z == at)
        def _(blocks=blocks):
            for b, block in enumerate(blocks):
                full[:, b * width : (b + 1) * width] = block[...]

    total = jnp.zeros(codes.shape, F32)
    piece = codes.shape[1] // 4
    decs = (dec0, dec1, dec2, dec3)
    for t, enc in enumerate((enc0, enc1, enc2, enc3)):
        b = i ^ t
        total += jnp.dot(
            full[:, columns(b * width, width)], enc[:width, :], preferred_element_type=F32
        )
        bias[:, columns(b * piece, piece)] = one_row(decs[t][width + EXTRA :, :piece])
    preact = total + bias[...]
    low_codes = jnp.maximum(preact, 0.0).astype(BF16)
    codes[...] = low_codes
    mask[...] = (preact > 0.0).astype(F32).astype(BF16)
    active[...] = jnp.sum(low_codes.astype(F32), axis=0, keepdims=True)


def onward_body(place, low, high, out):
    @pl.when(place[0] == 1)
    def _():
        out[...] = high[...]

    @pl.when(place[0] != 1)
    def _():
        out[...] = low[...]


def pieces_body(place, dec, up, down, across):
    z = place[0]
    half = up.shape[0]
    for out, second in ((up, z >= 1), (down, z >= 3), (across, z < 2)):
        out[...] = dec[pl.ds(pl.multiple_of(jnp.where(second, half, 0), half), half), :]


def turn_body(place, full, turned):
    turned[...] = full[...].T


def rebuilt_error(place, t, codes, dec, row, inputs):
    z, i = place[0], place[1]
    half = row.shape[0] // 3
    shift = pl.multiple_of(jnp.where(z >= 2, half, 0), half)
    below = pl.multiple_of(jnp.where(z == 1, 0, half), half)
    rights = [
        dec[pl.ds(shift, half), :],
        row[pl.ds(below, half), :],
        row[2 * half :, :],
        row[pl.ds(half - below, half), :],
    ]
    total = jnp.zeros((codes[0].shape[0], half), F32)
    for left, right in zip(codes, rights):
        total += lax.dot_general(
            left[...], right, (((1,), (1,)), ((), ())), preferred_element_type=F32
        )
    given = inputs[:, columns((i ^ t) * 2 * half + shift, half)].astype(F32)
    return (given - total).astype(BF16)


def met_body(place, out):
    out[...] = jnp.zeros(out.shape, F32)


def error_body(
    place, own, near, across, middle, dec0, dec1, dec2, dec3, row0, row1, row2, row3, inputs, error
):
    half = error.shape[1] // 4
    codes = (own, near, across, middle)
    decs, rows = (dec0, dec1, dec2, dec3), (row0, row1, row2, row3)
    for t in range(4):
        block = rebuilt_error(place, t, codes, decs[t], rows[t], inputs)
        error[:, columns((place[1] ^ t) * half, half)] = block


def pick(place, middle, end, out):
    z = place[0]
    is_middle = (z == 1) | (z == 2)

    @pl.when(is_middle)
    def _():
        out[...] = middle[...]

    @pl.when(jnp.logical_not(is_middle))
    def _():
        out[...] = end[...]


def decoder_grads(scale, i, error, codes, slots, outs):
    half = error.shape[1] // 4
    for slot, out in zip(slots, outs):
        out[:half] = scale * lax.dot_general(
            error[:, columns((i ^ slot) * half, half)],
            codes[...],
            (((0,), (0,)), ((), ())),
            preferred_element_type=F32,
        )


def back_through(i, error, decs, shift):
    half = error.shape[1] // 4
    return functools.reduce(
        jnp.add,
        [
            jnp.dot(
                error[:, columns((i ^ t) * half, half)],
                dec[pl.ds(pl.multiple_of(shift, half), half), :],
                preferred_element_type=F32,
            )
            for t, dec in enumerate(decs)
        ],
    )


def near_body(rows, place, mine, passed, codes, active, dec0, dec1, dec2, dec3, part, near, *outs):
    z, i = place[0], place[1]
    half = mine.shape[1] // 4
    pick(place, mine, passed, near)
    decoder_grads(-2.0 / rows, i, near, codes, (3, 1, 2, 0), outs)
    outs[0][half:] = jnp.broadcast_to(active[...], (outs[0].shape[0] - half, active.shape[1]))
    part[...] = back_through(i, near, (dec0, dec1, dec2, dec3), jnp.where(z >= 2, half, 0))


def far_error_body(rows, place, swapped, direct, codes, far, send, kept):
    pick(place, swapped, direct, far)
    decoder_grads(-2.0 / rows, place[1], far, codes, (3, 2), (send, kept))


def code_grad_body(
    rows, place, far, part, mask, dec0, dec1, dec2, dec3, turned, grad_low, bias_sum, norms, *sends
):
    z, i = place[0], place[1]
    half = far.shape[1] // 4
    width = 2 * half
    decs = (dec0, dec1, dec2, dec3)
    total = part[...] + back_through(i, far, decs, jnp.where(z >= 2, 0, half))
    squares = functools.reduce(jnp.add, [one_row(dec[width : width + EXTRA, :]) for dec in decs])
    column_norms = jnp.sqrt(squares + 1e-06)
    norms[...] = column_norms
    code_grad = (-2.0 / rows) * total + column_norms / rows
    grad = jnp.where(mask[...] > 0, code_grad, 0.0)
    grad_low[...] = grad.astype(BF16)
    bias_sum[...] = jnp.sum(grad, axis=0, keepdims=True)
    at = pl.multiple_of((i ^ 3) * width, width)
    block = jnp.dot(turned[pl.ds(at, width), :], grad_low[...], preferred_element_type=F32)
    sends[0][...] = block[:half]
    sends[1][...] = block[half:]


def encoder_grads(i, turned, grad_low, slots, outs):
    width = turned.shape[0] // 4
    for slot, out in zip(slots, outs):
        at = pl.ds(pl.multiple_of((i ^ slot) * width, width), width)
        out[:width] = jnp.dot(turned[at, :], grad_low[...], preferred_element_type=F32)


def rest_body(rows, place, turned, grad_low, near, far, codes, home, send, kept_far, kept, *outs):
    z, i = place[0], place[1]
    half = far.shape[1] // 4
    shift = jnp.where(z >= 2, 0, half)
    encoder_grads(i, turned, grad_low, (2, 1, 0), (kept_far, send, kept))
    decoder_grads(-2.0 / rows, i, far, codes, (1, 0), outs)
    home[:, columns(half - shift, half)] = near[:, columns(z * half, half)]
    home[:, columns(shift, half)] = far[:, columns(z * half, half)]


def power(values):
    largest = jnp.max(jnp.abs(values), axis=0, keepdims=True)
    return jnp.ceil(jnp.log(jnp.maximum(largest, 1e-30)) * (1.0 / math.log(2.0)))


def scale_of(exponent):
    return jnp.exp(exponent * math.log(2.0))


def pack_body(place, kept, row, *refs):
    width = kept.shape[0]
    at = [ref.shape[0] == width + EXTRA for ref in refs].index(True)
    received, packed, row_sums = refs[:at], refs[at], refs[at + 1 :]
    block = width // len(received)
    total = jnp.concatenate([piece[:block] for piece in received], axis=0) + kept[...]
    exponent = power(total)
    packed[:width] = total * scale_of(14.0 - exponent)
    sums = row[...]
    if received[0].shape[0] > block:
        sums += received[0][block : block + 1]
    for row_sum in row_sums:
        row_sum[...] = sums
    row_exponent = power(sums)
    parts = three_rows(sums * scale_of(14.0 - row_exponent)).astype(F32)
    at = lax.broadcasted_iota(jnp.int32, parts.shape, 0)
    parts = jnp.where(at == 3, exponent, jnp.where(at == 4, row_exponent, parts))
    packed[width:] = parts


def unpack(packed):
    width = packed.shape[0] - EXTRA
    rows = packed[width:].astype(F32)
    block = packed[:width].astype(F32) * scale_of(rows[3:4] - 14.0)
    row = (rows[0:1] + rows[1:2] + rows[2:3]) * scale_of(rows[4:5] - 14.0)
    return block, row


def bias_step_body(place, param, moment, square, here, there, param_out, moment_out, square_out):
    width = param.shape[1]
    grad = here[...] + there[...]
    pieces = [grad[:, b * width : (b + 1) * width] for b in range(4)]
    own = functools.reduce(
        jnp.add, [jnp.where(place[1] == b, piece, 0.0) for b, piece in enumerate(pieces)]
    )
    param_out[...], moment_out[...], square_out[...] = adam_update(
        param[...], own, moment[...], square[...]
    )


def decoder_step_body(
    rows, place, param, moment, square, near, far, active, norms, param_out, moment_out, square_out
):
    is_near = (pl.program_id(0) < pl.num_programs(0) // 2) == (place[0] < 2)
    grad = jnp.where(is_near, near[...], far[...])
    grad += param[...] * (active[...] / norms[...]) / rows
    param_out[...], moment_out[...], square_out[...] = adam_update(
        param[...], grad, moment[...], square[...]
    )


def line_shards(
    activations,
    encoder,
    enc_bias,
    decoder,
    enc_moment,
    enc_square,
    bias_moment,
    bias_square,
    dec_moment,
    dec_square,
):
    rows = activations.shape[0] * 4
    count, width = activations.shape
    latents = encoder.shape[1]
    half = width // 2
    features = 4 * width
    z, i = lax.axis_index("latent"), lax.axis_index("dp")
    place = jnp.stack([z, i]).astype(jnp.int32)

    def along(value, pairs):
        return lax.ppermute(value, "latent", pairs)

    def flip(value, bits, planes=(0, 1, 2, 3)):
        pairs = [(4 * p + k, 4 * p + (k ^ bits)) for p in planes for k in range(4)]
        return lax.ppermute(value, ("latent", "dp"), pairs)

    ends = [(1, 0), (2, 3)]
    low = along(activations, [(0, 1), (1, 2), (2, 3)])
    high = along(activations, [(1, 0), (2, 1), (3, 2)])
    across = along(activations, [(0, 2), (3, 1)])

    (enc_own,) = local_kernel(
        encoder_body,
        [shape((width + 2 * EXTRA, latents), BF16)],
        place,
        encoder,
    )
    enc_chip, enc_core = flip(enc_own, 2), flip(enc_own, 1)
    (dec_own,) = local_kernel(
        decoder_body,
        [shape((width + 2 * EXTRA, latents), BF16)],
        place,
        decoder,
        enc_bias.reshape(1, -1),
        after=(enc_core,),
    )
    dec_chip, dec_core = flip(dec_own, 2), flip(dec_own, 1)
    (onward,) = local_kernel(
        onward_body, [shape((count, width), BF16)], place, low, high
    )
    relay1 = along(onward, ends)
    relay2 = along(across, ends)
    enc = [enc_own, enc_core, enc_chip, flip(behind(enc_chip, relay2), 1)]

    up, down, beyond = local_kernel(
        pieces_body, [shape((half, latents), BF16)] * 3, place, dec_own
    )
    dec_pieces = [
        along(up, [(0, 1), (1, 2)]),
        along(down, [(2, 1), (3, 2)]),
        along(beyond, [(0, 2), (3, 1)]),
    ]
    dec = [dec_own, dec_core, dec_chip, flip(dec_chip, 1)]

    rows_own = jnp.concatenate([behind(piece, dec_chip) for piece in dec_pieces], axis=0)
    codes, mask, inputs, active = local_kernel(
        codes_body,
        [
            shape((count, latents), BF16),
            shape((count, latents), BF16),
            shape((count, features), BF16),
            shape((1, latents), F32),
        ],
        place,
        activations,
        low,
        high,
        across,
        relay1,
        relay2,
        *enc,
        *dec,
        after=(rows_own,),
        scratch=[pltpu.VMEM((1, latents), F32)],
    )
    codes_near = along(codes, [(0, 1), (3, 2)])
    codes_middle = along(codes, [(1, 2), (2, 1)])
    codes_across = along(codes, [(0, 2), (3, 1)])
    (turned,) = local_kernel(
        turn_body, [shape((features, count), BF16)], place, inputs, after=(codes_across,)
    )
    rows_chip = flip(rows_own, 2, (1, 2))
    rows_core = flip(behind(rows_own, codes), 1, (1, 2))
    rows_both = flip(behind(rows_chip, codes_across), 1, (1, 2))

    all_codes = codes, codes_near, codes_across, codes_middle
    (met,) = local_kernel(
        met_body, [shape((8, 128), F32)], place, after=(*all_codes, rows_chip), cost=NOTABLE
    )
    (own_error,) = local_kernel(
        error_body,
        [shape((count, features // 2), BF16)],
        place,
        *all_codes,
        *dec,
        rows_own,
        rows_core,
        rows_chip,
        rows_both,
        inputs,
        after=(met,),
    )
    swapped = along(own_error, [(1, 2), (2, 1)])
    passed = along(own_error, [(1, 0), (2, 3)])
    direct = along(own_error, [(2, 0), (1, 3)])

    def across_chips(kept, row, *send, keep_row=True):
        packed, *row_sum = local_kernel(
            pack_body,
            [shape((kept.shape[0] + EXTRA, latents), F32)] + [shape((1, latents), F32)] * keep_row,
            place,
            kept,
            row,
            *[flip(piece, 1) for piece in send],
        )
        return packed, flip(packed.astype(jnp.float16), 2), *row_sum

    blocks = [shape((half + 8, latents), F32)] + [shape((half, latents), F32)] * 3
    part, near, *near_blocks = local_kernel(
        functools.partial(near_body, rows),
        [shape((count, latents), F32), shape((count, features // 2), BF16), *blocks],
        place,
        own_error,
        passed,
        codes,
        active,
        *dec,
        after=(swapped,),
    )
    send_far, send_near, keep_far, keep_near = near_blocks
    near_packed, near_received, active_sum = across_chips(keep_far, active, send_far)
    near_kept = keep_near, flip(send_near, 1)
    far, far_send, far_keep = local_kernel(
        functools.partial(far_error_body, rows),
        [shape((count, features // 2), BF16)] + [shape((half, latents), F32)] * 2,
        place,
        swapped,
        direct,
        codes,
        after=(near_packed, near_kept[1]),
        cost=NOTABLE,
    )
    grad_low, bias_sum, norms, *send_far_enc = local_kernel(
        functools.partial(code_grad_body, rows),
        [
            shape((count, latents), BF16),
            shape((1, latents), F32),
            shape((1, latents), F32),
            shape((half, latents), F32),
            shape((half, latents), F32),
        ],
        place,
        far,
        behind(part, near_received),
        mask,
        *dec,
        turned,
        cost=NOTABLE,
    )
    far_packed, far_received = across_chips(far_keep, bias_sum, far_send, keep_row=False)
    error, enc_send_near, enc_keep_far, enc_keep_near, send_near, keep_near = local_kernel(
        functools.partial(rest_body, rows),
        [shape((count, width), BF16)]
        + [shape((width, latents), F32)] * 3
        + [shape((half, latents), F32)] * 2,
        place,
        turned,
        grad_low,
        near,
        far,
        codes,
        after=(far_packed,),
    )
    far_kept = keep_near, flip(send_near, 1)
    enc_packed, enc_received = across_chips(enc_keep_far, bias_sum, *send_far_enc, keep_row=False)
    enc_kept = enc_keep_near, flip(enc_send_near, 1)

    decoder, dec_moment, dec_square, encoder, enc_moment, enc_square = lax.optimization_barrier(
        (decoder, dec_moment, dec_square, encoder, enc_moment, enc_square, enc_packed)
    )[:6]
    near_block, active_there = unpack(near_received)
    far_block, bias_there = unpack(far_received)
    enc_block, _ = unpack(enc_received)
    near_grad = near_kept[0] + near_kept[1] + near_block
    far_grad = far_kept[0] + far_kept[1] + far_block
    active_sum = active_sum + active_there
    grad_encoder = enc_kept[0] + enc_kept[1] + enc_block
    new_encoder, new_enc_moment, new_enc_square = adam_update(
        encoder, grad_encoder, enc_moment, enc_square
    )
    step = width // 4
    block = pl.BlockSpec((step, latents), lambda r: (r, 0))
    in_half = pl.BlockSpec((step, latents), lambda r: (r % 2, 0))
    row = pl.BlockSpec((1, latents), lambda r: (0, 0))
    new_decoder, new_dec_moment, new_dec_square = pl.pallas_call(
        functools.partial(decoder_step_body, rows),
        grid=(4,),
        out_shape=[shape((width, latents), F32)] * 3,
        in_specs=[SMEM, block, block, block, in_half, in_half, row, row],
        out_specs=[block] * 3,
        compiler_params=pltpu.CompilerParams(vmem_limit_bytes=12 * 1024 * 1024),
        cost_estimate=pl.CostEstimate(flops=1, bytes_accessed=1, transcendentals=0),
    )(place, decoder, dec_moment, dec_square, near_grad, far_grad, active_sum, norms)
    bias_chips = bias_sum + bias_there
    new_enc_bias, new_bias_moment, new_bias_square = [
        value.reshape(-1)
        for value in local_kernel(
            bias_step_body,
            [shape((1, enc_bias.shape[0]), F32)] * 3,
            place,
            enc_bias.reshape(1, -1),
            bias_moment.reshape(1, -1),
            bias_square.reshape(1, -1),
            bias_chips,
            flip(bias_chips, 1),
            after=(new_decoder,),
        )
    ]
    return (
        error,
        new_encoder,
        new_enc_bias,
        new_decoder,
        new_enc_moment,
        new_enc_square,
        new_bias_moment,
        new_bias_square,
        new_dec_moment,
        new_dec_square,
    )


def solution(mesh):
    in_specs = (
        P(("groups", "dp"), "latent"),
        P(("groups", "dp"), "latent"),
        P(("groups", "latent", "dp")),
        P(("groups", "dp"), "latent"),
        P(("groups", "dp"), "latent"),
        P(("groups", "dp"), "latent"),
        P(("groups", "latent", "dp")),
        P(("groups", "latent", "dp")),
        P(("groups", "dp"), "latent"),
        P(("groups", "dp"), "latent"),
    )
    out_specs = (
        P(("groups", "dp"), "latent"),
        P(("groups", "dp"), "latent"),
        P(("groups", "latent", "dp")),
        P(("groups", "dp"), "latent"),
        P(("groups", "dp"), "latent"),
        P(("groups", "dp"), "latent"),
        P(("groups", "latent", "dp")),
        P(("groups", "latent", "dp")),
        P(("groups", "dp"), "latent"),
        P(("groups", "dp"), "latent"),
    )
    line = mesh.shape["latent"] == 4 and mesh.shape["dp"] == 4
    plan = line_shards if line else shards
    return jax.shard_map(plan, mesh=mesh, in_specs=in_specs, out_specs=out_specs, check_vma=False)
```

```python
import functools
import math

import jax
import jax.numpy as jnp
from jax import lax
from jax.experimental import pallas as pl
from jax.experimental.pallas import tpu as pltpu
from jax.sharding import PartitionSpec as P

ADAM_STEP = 1000


first_decay = 0.9
second_decay = 0.999
learn_rate = 0.001
epsilon = 1e-08

F32 = jnp.float32
BF16 = jnp.bfloat16


def adam_update(param, grad, moment, square):
    moment_new = first_decay * moment + (1.0 - first_decay) * grad
    square_new = second_decay * square + (1.0 - second_decay) * grad * grad
    first_fix = 1.0 - first_decay**ADAM_STEP
    second_fix = 1.0 - second_decay**ADAM_STEP
    param_new = param - learn_rate * (moment_new / first_fix) / (
        jnp.sqrt(square_new / second_fix) + epsilon
    )
    return (param_new, moment_new, square_new)


def shards(
    activations,
    encoder,
    enc_bias,
    decoder,
    enc_moment,
    enc_square,
    bias_moment,
    bias_square,
    dec_moment,
    dec_square,
):
    row_count = activations.shape[0] * lax.axis_size("dp")
    loss_scale = 2.0 / row_count
    inputs = lax.all_gather(activations, "latent", axis=1, tiled=True)
    enc_low, dec_low = (
        lax.all_gather(encoder.astype(jnp.bfloat16), "dp", axis=0, tiled=True),
        lax.all_gather(decoder.astype(jnp.bfloat16), "dp", axis=0, tiled=True),
    )
    bias_full = lax.all_gather(enc_bias, "dp", axis=0, tiled=True)
    square_sums = lax.psum(jnp.sum(decoder * decoder, axis=0), "dp")
    column_norms = jnp.sqrt(square_sums + 1e-06)
    preact = jnp.dot(inputs, enc_low, preferred_element_type=jnp.float32) + bias_full
    latent_codes = jnp.maximum(preact, 0.0).astype(jnp.bfloat16)
    partial_sums = lax.dot_general(
        latent_codes, dec_low, (((1,), (1,)), ((), ())), preferred_element_type=jnp.float32
    )
    rebuilt = lax.psum_scatter(partial_sums, "latent", scatter_dimension=1, tiled=True)
    error = (activations.astype(jnp.float32) - rebuilt).astype(jnp.bfloat16)
    full_error = lax.all_gather(error, "latent", axis=1, tiled=True)
    active_sum = lax.psum(jnp.sum(latent_codes.astype(jnp.float32), axis=0), "dp")
    grad_dec_rows = -loss_scale * lax.dot_general(
        full_error, latent_codes, (((0,), (0,)), ((), ())), preferred_element_type=jnp.float32
    )
    code_grad = (
        -loss_scale * jnp.dot(full_error, dec_low, preferred_element_type=jnp.float32)
        + column_norms / row_count
    )
    grad_preact = jnp.where(preact > 0.0, code_grad, 0.0)
    grad_encoder = lax.dot_general(
        inputs,
        grad_preact.astype(jnp.bfloat16),
        (((0,), (0,)), ((), ())),
        preferred_element_type=jnp.float32,
    )
    grad_bias = jnp.sum(grad_preact, axis=0)
    grad_encoder, grad_dec_rows, grad_bias = (
        lax.psum_scatter(grad_encoder, "dp", scatter_dimension=0, tiled=True),
        lax.psum_scatter(grad_dec_rows, "dp", scatter_dimension=0, tiled=True),
        lax.psum_scatter(grad_bias, "dp", scatter_dimension=0, tiled=True),
    )
    grad_decoder = grad_dec_rows + decoder * (active_sum / column_norms) / row_count
    new_encoder, new_enc_moment, new_enc_square = adam_update(
        encoder, grad_encoder, enc_moment, enc_square
    )
    new_enc_bias, new_bias_moment, new_bias_square = adam_update(
        enc_bias, grad_bias, bias_moment, bias_square
    )
    new_decoder, new_dec_moment, new_dec_square = adam_update(
        decoder, grad_decoder, dec_moment, dec_square
    )
    return (
        error,
        new_encoder,
        new_enc_bias,
        new_decoder,
        new_enc_moment,
        new_enc_square,
        new_bias_moment,
        new_bias_square,
        new_dec_moment,
        new_dec_square,
    )


VMEM = pl.BlockSpec(memory_space=pltpu.VMEM)
SMEM = pl.BlockSpec(memory_space=pltpu.SMEM)
ANY = pl.BlockSpec(memory_space=pl.ANY)
EXTRA = 16
NOTABLE = 10**10


def local_kernel(body, outs, place, *args, after=(), scratch=(), cost=1):
    def run(place, *refs):
        body(place, *refs[: len(args)], *refs[len(args) + len(after) :])

    held = sum(a.size * jnp.dtype(a.dtype).itemsize for a in (*args, *outs))
    return pl.pallas_call(
        run,
        out_shape=outs,
        in_specs=[SMEM] + [VMEM] * len(args) + [ANY] * len(after),
        out_specs=[VMEM] * len(outs),
        scratch_shapes=scratch,
        compiler_params=pltpu.CompilerParams(vmem_limit_bytes=held + 6 * 1024 * 1024),
        cost_estimate=pl.CostEstimate(flops=cost, bytes_accessed=1, transcendentals=0),
    )(place, *args, *after)


def shape(dims, dtype):
    return jax.ShapeDtypeStruct(dims, dtype)


def columns(start, width):
    return pl.ds(pl.multiple_of(start, width), width)


def three_rows(row):
    high = row.astype(BF16).astype(F32)
    middle = (row - high).astype(BF16).astype(F32)
    low = row - high - middle
    at = lax.broadcasted_iota(jnp.int32, (EXTRA, row.shape[1]), 0)
    rows = jnp.where(at == 0, high, jnp.where(at == 1, middle, jnp.where(at == 2, low, 0.0)))
    return rows.astype(BF16)


def behind(value, *others):
    return lax.optimization_barrier((value, *others))[0]


def one_row(rows):
    return jnp.sum(rows.astype(F32), axis=0, keepdims=True)


def encoder_body(place, encoder, out):
    depth = encoder.shape[0]
    out[:depth] = encoder[...].astype(BF16)
    out[depth:] = jnp.zeros((out.shape[0] - depth, out.shape[1]), BF16)


def decoder_body(place, decoder, bias, out):
    depth = decoder.shape[0]
    value = decoder[...]
    out[:depth] = value.astype(BF16)
    out[depth : depth + EXTRA] = three_rows(jnp.sum(value * value, axis=0, keepdims=True))
    out[depth + EXTRA :] = three_rows(jnp.concatenate([bias[...]] * 4, axis=1))


def codes_body(
    place,
    own,
    low,
    high,
    across,
    relay1,
    relay2,
    enc0,
    enc1,
    enc2,
    enc3,
    dec0,
    dec1,
    dec2,
    dec3,
    codes,
    mask,
    full,
    active,
    bias,
):
    z, i = place[0], place[1]
    width = own.shape[1]
    for at, blocks in enumerate(
        (
            (own, high, relay1, relay2),
            (low, own, high, across),
            (across, low, own, high),
            (relay2, relay1, low, own),
        )
    ):

        @pl.when(z == at)
        def _(blocks=blocks):
            for b, block in enumerate(blocks):
                full[:, b * width : (b + 1) * width] = block[...]

    total = jnp.zeros(codes.shape, F32)
    piece = codes.shape[1] // 4
    decs = (dec0, dec1, dec2, dec3)
    for t, enc in enumerate((enc0, enc1, enc2, enc3)):
        b = i ^ t
        total += jnp.dot(
            full[:, columns(b * width, width)], enc[:width, :], preferred_element_type=F32
        )
        bias[:, columns(b * piece, piece)] = one_row(decs[t][width + EXTRA :, :piece])
    preact = total + bias[...]
    low_codes = jnp.maximum(preact, 0.0).astype(BF16)
    codes[...] = low_codes
    mask[...] = (preact > 0.0).astype(F32).astype(BF16)
    active[...] = jnp.sum(low_codes.astype(F32), axis=0, keepdims=True)


def onward_body(place, low, high, out):
    @pl.when(place[0] == 1)
    def _():
        out[...] = high[...]

    @pl.when(place[0] != 1)
    def _():
        out[...] = low[...]


def pieces_body(place, dec, up, down, across):
    z = place[0]
    half = up.shape[0]
    for out, second in ((up, z >= 1), (down, z >= 3), (across, z < 2)):
        out[...] = dec[pl.ds(pl.multiple_of(jnp.where(second, half, 0), half), half), :]


def turn_body(place, full, turned):
    turned[...] = full[...].T


def rebuilt_error(place, t, codes, dec, row, inputs):
    z, i = place[0], place[1]
    half = row.shape[0] // 3
    shift = pl.multiple_of(jnp.where(z >= 2, half, 0), half)
    below = pl.multiple_of(jnp.where(z == 1, 0, half), half)
    rights = [
        dec[pl.ds(shift, half), :],
        row[pl.ds(below, half), :],
        row[2 * half :, :],
        row[pl.ds(half - below, half), :],
    ]
    total = jnp.zeros((codes[0].shape[0], half), F32)
    for left, right in zip(codes, rights):
        total += lax.dot_general(
            left[...], right, (((1,), (1,)), ((), ())), preferred_element_type=F32
        )
    given = inputs[:, columns((i ^ t) * 2 * half + shift, half)].astype(F32)
    return (given - total).astype(BF16)


def met_body(place, out):
    out[...] = jnp.zeros(out.shape, F32)


def error_body(
    place, own, near, across, middle, dec0, dec1, dec2, dec3, row0, row1, row2, row3, inputs, error
):
    half = error.shape[1] // 4
    codes = (own, near, across, middle)
    decs, rows = (dec0, dec1, dec2, dec3), (row0, row1, row2, row3)
    for t in range(4):
        block = rebuilt_error(place, t, codes, decs[t], rows[t], inputs)
        error[:, columns((place[1] ^ t) * half, half)] = block


def pick(place, middle, end, out):
    z = place[0]
    is_middle = (z == 1) | (z == 2)

    @pl.when(is_middle)
    def _():
        out[...] = middle[...]

    @pl.when(jnp.logical_not(is_middle))
    def _():
        out[...] = end[...]


def decoder_grads(scale, i, error, codes, slots, outs):
    half = error.shape[1] // 4
    for slot, out in zip(slots, outs):
        out[:half] = scale * lax.dot_general(
            error[:, columns((i ^ slot) * half, half)],
            codes[...],
            (((0,), (0,)), ((), ())),
            preferred_element_type=F32,
        )


def back_through(i, error, decs, shift):
    half = error.shape[1] // 4
    return functools.reduce(
        jnp.add,
        [
            jnp.dot(
                error[:, columns((i ^ t) * half, half)],
                dec[pl.ds(pl.multiple_of(shift, half), half), :],
                preferred_element_type=F32,
            )
            for t, dec in enumerate(decs)
        ],
    )


def near_body(rows, place, mine, passed, codes, active, dec0, dec1, dec2, dec3, part, near, *outs):
    z, i = place[0], place[1]
    half = mine.shape[1] // 4
    pick(place, mine, passed, near)
    decoder_grads(-2.0 / rows, i, near, codes, (3, 1, 2, 0), outs)
    outs[0][half:] = jnp.broadcast_to(active[...], (outs[0].shape[0] - half, active.shape[1]))
    part[...] = back_through(i, near, (dec0, dec1, dec2, dec3), jnp.where(z >= 2, half, 0))


def far_error_body(rows, place, swapped, direct, codes, far, send, kept):
    pick(place, swapped, direct, far)
    decoder_grads(-2.0 / rows, place[1], far, codes, (3, 2), (send, kept))


def code_grad_body(
    rows, place, far, part, mask, dec0, dec1, dec2, dec3, turned, grad_low, bias_sum, norms, *sends
):
    z, i = place[0], place[1]
    half = far.shape[1] // 4
    width = 2 * half
    decs = (dec0, dec1, dec2, dec3)
    total = part[...] + back_through(i, far, decs, jnp.where(z >= 2, 0, half))
    squares = functools.reduce(jnp.add, [one_row(dec[width : width + EXTRA, :]) for dec in decs])
    column_norms = jnp.sqrt(squares + 1e-06)
    norms[...] = column_norms
    code_grad = (-2.0 / rows) * total + column_norms / rows
    grad = jnp.where(mask[...] > 0, code_grad, 0.0)
    grad_low[...] = grad.astype(BF16)
    bias_sum[...] = jnp.sum(grad, axis=0, keepdims=True)
    at = pl.multiple_of((i ^ 3) * width, width)
    block = jnp.dot(turned[pl.ds(at, width), :], grad_low[...], preferred_element_type=F32)
    sends[0][...] = block[:half]
    sends[1][...] = block[half:]


def encoder_grads(i, turned, grad_low, slots, outs):
    width = turned.shape[0] // 4
    for slot, out in zip(slots, outs):
        at = pl.ds(pl.multiple_of((i ^ slot) * width, width), width)
        out[:width] = jnp.dot(turned[at, :], grad_low[...], preferred_element_type=F32)


def rest_body(rows, place, turned, grad_low, near, far, codes, home, send, kept_far, kept, *outs):
    z, i = place[0], place[1]
    half = far.shape[1] // 4
    shift = jnp.where(z >= 2, 0, half)
    encoder_grads(i, turned, grad_low, (2, 1, 0), (kept_far, send, kept))
    decoder_grads(-2.0 / rows, i, far, codes, (1, 0), outs)
    home[:, columns(half - shift, half)] = near[:, columns(z * half, half)]
    home[:, columns(shift, half)] = far[:, columns(z * half, half)]


def power(values):
    largest = jnp.max(jnp.abs(values), axis=0, keepdims=True)
    return jnp.ceil(jnp.log(jnp.maximum(largest, 1e-30)) * (1.0 / math.log(2.0)))


def scale_of(exponent):
    return jnp.exp(exponent * math.log(2.0))


def pack_body(place, kept, row, *refs):
    width = kept.shape[0]
    at = [ref.shape[0] == width + EXTRA for ref in refs].index(True)
    received, packed, row_sums = refs[:at], refs[at], refs[at + 1 :]
    block = width // len(received)
    total = jnp.concatenate([piece[:block] for piece in received], axis=0) + kept[...]
    exponent = power(total)
    packed[:width] = total * scale_of(14.0 - exponent)
    sums = row[...]
    if received[0].shape[0] > block:
        sums += received[0][block : block + 1]
    for row_sum in row_sums:
        row_sum[...] = sums
    row_exponent = power(sums)
    parts = three_rows(sums * scale_of(14.0 - row_exponent)).astype(F32)
    at = lax.broadcasted_iota(jnp.int32, parts.shape, 0)
    parts = jnp.where(at == 3, exponent, jnp.where(at == 4, row_exponent, parts))
    packed[width:] = parts


def unpack(packed):
    width = packed.shape[0] - EXTRA
    rows = packed[width:].astype(F32)
    block = packed[:width].astype(F32) * scale_of(rows[3:4] - 14.0)
    row = (rows[0:1] + rows[1:2] + rows[2:3]) * scale_of(rows[4:5] - 14.0)
    return block, row


def bias_step_body(place, param, moment, square, here, there, param_out, moment_out, square_out):
    width = param.shape[1]
    grad = here[...] + there[...]
    pieces = [grad[:, b * width : (b + 1) * width] for b in range(4)]
    own = functools.reduce(
        jnp.add, [jnp.where(place[1] == b, piece, 0.0) for b, piece in enumerate(pieces)]
    )
    param_out[...], moment_out[...], square_out[...] = adam_update(
        param[...], own, moment[...], square[...]
    )


def decoder_step_body(
    rows, place, param, moment, square, near, far, active, norms, param_out, moment_out, square_out
):
    is_near = (pl.program_id(0) < pl.num_programs(0) // 2) == (place[0] < 2)
    grad = jnp.where(is_near, near[...], far[...])
    grad += param[...] * (active[...] / norms[...]) / rows
    param_out[...], moment_out[...], square_out[...] = adam_update(
        param[...], grad, moment[...], square[...]
    )


def line_shards(
    activations,
    encoder,
    enc_bias,
    decoder,
    enc_moment,
    enc_square,
    bias_moment,
    bias_square,
    dec_moment,
    dec_square,
):
    rows = activations.shape[0] * 4
    count, width = activations.shape
    latents = encoder.shape[1]
    half = width // 2
    features = 4 * width
    z, i = lax.axis_index("latent"), lax.axis_index("dp")
    place = jnp.stack([z, i]).astype(jnp.int32)

    def along(value, pairs):
        return lax.ppermute(value, "latent", pairs)

    def flip(value, bits, planes=(0, 1, 2, 3)):
        pairs = [(4 * p + k, 4 * p + (k ^ bits)) for p in planes for k in range(4)]
        return lax.ppermute(value, ("latent", "dp"), pairs)

    ends = [(1, 0), (2, 3)]
    low = along(activations, [(0, 1), (1, 2), (2, 3)])
    high = along(activations, [(1, 0), (2, 1), (3, 2)])
    across = along(activations, [(0, 2), (3, 1)])

    (enc_own,) = local_kernel(
        encoder_body,
        [shape((width + 2 * EXTRA, latents), BF16)],
        place,
        encoder,
    )
    enc_chip, enc_core = flip(enc_own, 2), flip(enc_own, 1)
    (dec_own,) = local_kernel(
        decoder_body,
        [shape((width + 2 * EXTRA, latents), BF16)],
        place,
        decoder,
        enc_bias.reshape(1, -1),
        after=(enc_core,),
    )
    dec_chip, dec_core = flip(dec_own, 2), flip(dec_own, 1)
    (onward,) = local_kernel(
        onward_body, [shape((count, width), BF16)], place, low, high
    )
    relay1 = along(onward, ends)
    relay2 = along(across, ends)
    enc = [enc_own, enc_core, enc_chip, flip(behind(enc_chip, relay2), 1)]

    up, down, beyond = local_kernel(
        pieces_body, [shape((half, latents), BF16)] * 3, place, dec_own
    )
    dec_pieces = [
        along(up, [(0, 1), (1, 2)]),
        along(down, [(2, 1), (3, 2)]),
        along(beyond, [(0, 2), (3, 1)]),
    ]
    dec = [dec_own, dec_core, dec_chip, flip(dec_chip, 1)]

    rows_own = jnp.concatenate([behind(piece, dec_chip) for piece in dec_pieces], axis=0)
    codes, mask, inputs, active = local_kernel(
        codes_body,
        [
            shape((count, latents), BF16),
            shape((count, latents), BF16),
            shape((count, features), BF16),
            shape((1, latents), F32),
        ],
        place,
        activations,
        low,
        high,
        across,
        relay1,
        relay2,
        *enc,
        *dec,
        after=(rows_own,),
        scratch=[pltpu.VMEM((1, latents), F32)],
    )
    codes_near = along(codes, [(0, 1), (3, 2)])
    codes_middle = along(codes, [(1, 2), (2, 1)])
    codes_across = along(codes, [(0, 2), (3, 1)])
    (turned,) = local_kernel(
        turn_body, [shape((features, count), BF16)], place, inputs, after=(codes_across,)
    )
    rows_chip = flip(rows_own, 2, (1, 2))
    rows_core = flip(behind(rows_own, codes), 1, (1, 2))
    rows_both = flip(behind(rows_chip, codes_across), 1, (1, 2))

    all_codes = codes, codes_near, codes_across, codes_middle
    (met,) = local_kernel(
        met_body, [shape((8, 128), F32)], place, after=(*all_codes, rows_chip), cost=NOTABLE
    )
    (own_error,) = local_kernel(
        error_body,
        [shape((count, features // 2), BF16)],
        place,
        *all_codes,
        *dec,
        rows_own,
        rows_core,
        rows_chip,
        rows_both,
        inputs,
        after=(met,),
    )
    swapped = along(own_error, [(1, 2), (2, 1)])
    passed = along(own_error, [(1, 0), (2, 3)])
    direct = along(own_error, [(2, 0), (1, 3)])

    def across_chips(kept, row, *send, keep_row=True):
        packed, *row_sum = local_kernel(
            pack_body,
            [shape((kept.shape[0] + EXTRA, latents), F32)] + [shape((1, latents), F32)] * keep_row,
            place,
            kept,
            row,
            *[flip(piece, 1) for piece in send],
        )
        return packed, flip(packed.astype(jnp.float16), 2), *row_sum

    blocks = [shape((half + 8, latents), F32)] + [shape((half, latents), F32)] * 3
    part, near, *near_blocks = local_kernel(
        functools.partial(near_body, rows),
        [shape((count, latents), F32), shape((count, features // 2), BF16), *blocks],
        place,
        own_error,
        passed,
        codes,
        active,
        *dec,
        after=(swapped,),
    )
    send_far, send_near, keep_far, keep_near = near_blocks
    near_packed, near_received, active_sum = across_chips(keep_far, active, send_far)
    near_kept = keep_near, flip(send_near, 1)
    far, far_send, far_keep = local_kernel(
        functools.partial(far_error_body, rows),
        [shape((count, features // 2), BF16)] + [shape((half, latents), F32)] * 2,
        place,
        swapped,
        direct,
        codes,
        after=(near_packed, near_kept[1]),
        cost=NOTABLE,
    )
    grad_low, bias_sum, norms, *send_far_enc = local_kernel(
        functools.partial(code_grad_body, rows),
        [
            shape((count, latents), BF16),
            shape((1, latents), F32),
            shape((1, latents), F32),
            shape((half, latents), F32),
            shape((half, latents), F32),
        ],
        place,
        far,
        behind(part, near_received),
        mask,
        *dec,
        turned,
        cost=NOTABLE,
    )
    far_packed, far_received = across_chips(far_keep, bias_sum, far_send, keep_row=False)
    error, enc_send_near, enc_keep_far, enc_keep_near, send_near, keep_near = local_kernel(
        functools.partial(rest_body, rows),
        [shape((count, width), BF16)]
        + [shape((width, latents), F32)] * 3
        + [shape((half, latents), F32)] * 2,
        place,
        turned,
        grad_low,
        near,
        far,
        codes,
        after=(far_packed,),
    )
    far_kept = keep_near, flip(send_near, 1)
    enc_packed, enc_received = across_chips(enc_keep_far, bias_sum, *send_far_enc, keep_row=False)
    enc_kept = enc_keep_near, flip(enc_send_near, 1)

    decoder, dec_moment, dec_square, encoder, enc_moment, enc_square = lax.optimization_barrier(
        (decoder, dec_moment, dec_square, encoder, enc_moment, enc_square, enc_packed)
    )[:6]
    near_block, active_there = unpack(behind(near_received, enc_packed))
    far_block, bias_there = unpack(far_received)
    enc_block, _ = unpack(enc_received)
    near_grad = near_kept[0] + near_kept[1] + near_block
    far_grad = far_kept[0] + far_kept[1] + far_block
    active_sum = active_sum + active_there
    grad_encoder = enc_kept[0] + enc_kept[1] + enc_block
    new_encoder, new_enc_moment, new_enc_square = adam_update(
        encoder, grad_encoder, enc_moment, enc_square
    )
    step = width // 4
    block = pl.BlockSpec((step, latents), lambda r: (r, 0))
    in_half = pl.BlockSpec((step, latents), lambda r: (r % 2, 0))
    row = pl.BlockSpec((1, latents), lambda r: (0, 0))
    new_decoder, new_dec_moment, new_dec_square = pl.pallas_call(
        functools.partial(decoder_step_body, rows),
        grid=(4,),
        out_shape=[shape((width, latents), F32)] * 3,
        in_specs=[SMEM, block, block, block, in_half, in_half, row, row],
        out_specs=[block] * 3,
        compiler_params=pltpu.CompilerParams(vmem_limit_bytes=12 * 1024 * 1024),
        cost_estimate=pl.CostEstimate(flops=1, bytes_accessed=1, transcendentals=0),
    )(place, decoder, dec_moment, dec_square, near_grad, far_grad, active_sum, norms)
    bias_chips = bias_sum + bias_there
    new_enc_bias, new_bias_moment, new_bias_square = [
        value.reshape(-1)
        for value in local_kernel(
            bias_step_body,
            [shape((1, enc_bias.shape[0]), F32)] * 3,
            place,
            enc_bias.reshape(1, -1),
            bias_moment.reshape(1, -1),
            bias_square.reshape(1, -1),
            bias_chips,
            flip(bias_chips, 1),
            after=(new_decoder,),
        )
    ]
    return (
        error,
        new_encoder,
        new_enc_bias,
        new_decoder,
        new_enc_moment,
        new_enc_square,
        new_bias_moment,
        new_bias_square,
        new_dec_moment,
        new_dec_square,
    )


def solution(mesh):
    in_specs = (
        P(("groups", "dp"), "latent"),
        P(("groups", "dp"), "latent"),
        P(("groups", "latent", "dp")),
        P(("groups", "dp"), "latent"),
        P(("groups", "dp"), "latent"),
        P(("groups", "dp"), "latent"),
        P(("groups", "latent", "dp")),
        P(("groups", "latent", "dp")),
        P(("groups", "dp"), "latent"),
        P(("groups", "dp"), "latent"),
    )
    out_specs = (
        P(("groups", "dp"), "latent"),
        P(("groups", "dp"), "latent"),
        P(("groups", "latent", "dp")),
        P(("groups", "dp"), "latent"),
        P(("groups", "dp"), "latent"),
        P(("groups", "dp"), "latent"),
        P(("groups", "latent", "dp")),
        P(("groups", "latent", "dp")),
        P(("groups", "dp"), "latent"),
        P(("groups", "dp"), "latent"),
    )
    line = mesh.shape["latent"] == 4 and mesh.shape["dp"] == 4
    plan = line_shards if line else shards
    return jax.shard_map(plan, mesh=mesh, in_specs=in_specs, out_specs=out_specs, check_vma=False)
```
